32 devices in a mesh: gx: 8 (over y, x, core), gy: 4 (over z).
Axes of the slice: x: 2, y: 2, z: 4, core: 2. Of those that a mesh axis runs over, the one named last changes fastest.
Arguments:
- log_density: float32 [256, 256, 512], P('gx', 'gy'), may hold values from -3 to 3
- weights: bfloat16 [2048, 32, 32, 128], P(('gx', 'gy')), may hold values from -0.09375 to 0.09375
- observed: float32 [2048, 32], P(('gx', 'gy')), may hold values from -6 to 6
- inverse_var: float32 [2048, 32], P(('gx', 'gy')), may hold values from 0.25 to 4
- star_counts: int32 [2048], P(('gx', 'gy')), may hold values from 1 to 32
- block_ids: int32 [2048, 32], P(('gx', 'gy')), may hold values from 0 to 262143, as said below
Outputs:
- new_log_density: float32 [256, 256, 512], P('gx', 'gy')
- extinction: float32 [2048, 32], P(('gx', 'gy'))
The draws below stay inside these ranges and needn't reach their ends.
Inputs may be any that keep to these rules, and one draw needn't show every extreme that they name: `block_ids`: among the 2048 ids of one device's rows (rows d * 64 to (d + 1) * 64 - 1), at most 128 name blocks of any one tile (blocks t * 8192 to (t + 1) * 8192 - 1), and exactly 128 name blocks of tile d.
All inputs are finite; a program needn't handle non-finite values.
Results may differ from the reference program's by a relative error of at most 0.0029.
Values may be sent and summed in bfloat16 or wider, within the bound.
No kernel may reach another device: no remote copies, remote signals or barrier semaphores. Data moves between devices by JAX's collectives and lax.ppermute only.
A program may use at most 128 MiB of HBM per device.

```python
import math
import jax
import jax.numpy as jnp
from jax import lax

CX = 32
CY = 64
NZ = 512
VB = 128
SB = 32
K = 32
SBD = 64
NDEV = 32
ZB = 4
VBD = 8192
CAP = 128
NX = 256
NY = 256
N_GX = 8
N_GY = 4


def draw_block_ids(key, part):
    total = SBD * K

    def one_device(device):
        dev_key = jax.random.fold_in(key, device)
        key_a, key_b, key_c = jax.random.split(dev_key, 3)
        others = jax.random.permutation(key_a, (NDEV - 1) * CAP)[:total - CAP]
        target_other = (device + 1 + others // CAP) % NDEV
        target = jnp.concatenate([jnp.full((CAP,), device, jnp.int32), target_other.astype(jnp.int32)])
        order = jax.random.permutation(key_b, total)
        target = target[order]
        within = jax.random.randint(key_c, (total,), 0, VBD, jnp.int32)
        return (target * VBD + within).reshape(SBD, K)
    return jax.vmap(one_device)(jnp.arange(NDEV, dtype=jnp.int32)).reshape(NDEV * SBD, K)


def with_ends(drawn, own_key, low, top_value):
    index_at = [jax.random.randint(jax.random.fold_in(own_key, axis), (), 0, length) for axis, length in enumerate(drawn.shape)]
    main_axis = drawn.shape.index(max(drawn.shape))
    next_to = index_at[:main_axis] + [(index_at[main_axis] + 1) % drawn.shape[main_axis]] + index_at[main_axis + 1:]
    return drawn.at[tuple(index_at)].set(low).at[tuple(next_to)].set(top_value)


def steps_of(rng, dims, pieces, least, top_value):
    factor_of, own = 1.0, jax.random.fold_in(rng, 6)
    for axis_at, parts in pieces:
        steps = jnp.exp(jax.random.uniform(jax.random.fold_in(own, axis_at), (parts,), jnp.float32, least / len(pieces), top_value / len(pieces)))
        factor_of = factor_of * jnp.repeat(steps, dims[axis_at] // parts).reshape([-1 if axis == axis_at else 1 for axis in range(len(dims))])
    return factor_of


def gaussian(own_key, extent, spread, most, pieces=(), kind=jnp.bfloat16):
    array = jax.random.normal(own_key, extent, jnp.float32) * spread
    if len(pieces) > 0:
        array = steps_of(own_key, extent, pieces, -0.22, 0.18) * array
    return jnp.clip(array, min=-most, max=most).astype(kind)


def setup_inputs(seed: int = 0) -> dict:
    streams_of = jax.random.split(jax.random.key(seed), 7)
    return {
        "log_density": gaussian(streams_of[0], (NX, NY, NZ), 0.5, 3.0, ((0, 8), (1, 4)), jnp.float32),
        "weights": gaussian(streams_of[1], (NDEV * SBD, K, SB, VB), (K * VB) ** -0.5, 0.09375, ((0, 32),)),
        "observed": gaussian(streams_of[2], (NDEV * SBD, SB), 1.0, 6.0, ((0, 32),), jnp.float32),
        "inverse_var": jnp.clip(jnp.exp(math.log(4.0) - 2.7725887 * jax.random.uniform(streams_of[3], (NDEV * SBD, SB), jnp.float32) ** steps_of(streams_of[3], (NDEV * SBD, SB), ((0, 32),), -0.2, 0.2)), 0.25, 4.0),
        "star_counts": with_ends(jax.random.randint(streams_of[4], (NDEV * SBD,), 1, SB + 1), jax.random.fold_in(streams_of[4], 1), 1, SB).astype(jnp.int32),
        "block_ids": draw_block_ids(jax.random.fold_in(streams_of[6], 71), 0),
    }


shift_kappa = 0.5
prior_weight = 0.05
step_rate = 2.0


def operate(field):
    padded = jnp.pad(field, 1)
    beside = padded[2:, 1:-1, 1:-1] + padded[:-2, 1:-1, 1:-1]
    beside = beside + padded[1:-1, 2:, 1:-1] + padded[1:-1, :-2, 1:-1]
    beside = beside + padded[1:-1, 1:-1, 2:] + padded[1:-1, 1:-1, :-2]
    return (shift_kappa + 6.0) * field - beside


def reference(log_density, weights, observed, inverse_var, star_counts, block_ids):
    dens_field = jnp.exp(log_density)
    table = dens_field.astype(jnp.bfloat16).reshape(N_GX, CX, N_GY, CY, ZB, VB)
    table = table.transpose(0, 2, 1, 3, 4, 5).reshape(NDEV * VBD, VB)
    fetched = table[block_ids]

    def per_device(packed):
        w_dev, f_dev, obs_dev, inv_dev, cnt_dev = packed
        w_full = w_dev.astype(jnp.float32)
        ext = jnp.einsum("bksv,bkv->bs", w_full, f_dev.astype(jnp.float32))
        live = jnp.arange(SB)[None, :] < cnt_dev[:, None]
        weighted = jnp.where(live, inv_dev * (ext - obs_dev), 0.0).astype(jnp.bfloat16)
        sens = jnp.einsum("bksv,bs->bkv", w_full, weighted.astype(jnp.float32))
        return ext, sens

    ext, sens = lax.map(per_device, (weights.reshape(NDEV, SBD, K, SB, VB),
                                      fetched.reshape(NDEV, SBD, K, VB),
                                      observed.reshape(NDEV, SBD, SB),
                                      inverse_var.reshape(NDEV, SBD, SB),
                                      star_counts.reshape(NDEV, SBD)))
    collected = jnp.zeros((NDEV * VBD, VB), jnp.float32).at[block_ids.reshape(-1)].add(sens.reshape(-1, VB))
    collected = collected.reshape(N_GX, N_GY, CX, CY, ZB, VB).transpose(0, 2, 1, 3, 4, 5)
    data_grad = collected.reshape(NX, NY, NZ) * dens_field
    smooth = operate(log_density)
    prior_grad = operate(smooth)
    new_log_density = log_density - step_rate * (data_grad + prior_weight * prior_grad)
    return new_log_density, ext.reshape(NDEV * SBD, SB)
```

```python
import functools

import jax
import jax.numpy as jnp
from jax import lax
from jax.experimental import pallas as pl
from jax.experimental.pallas import tpu as pltpu
from jax.sharding import PartitionSpec as P

shift_kappa = 0.5
prior_weight = 0.05
step_rate = 2.0

LANES = 128
GROUP = 16
MIB = 1 << 20

CONTRACT_LANES = (((1,), (1,)), ((), ()))


def split_by(value, size):
    if size & (size - 1) == 0:
        high = value >> (size.bit_length() - 1)
        return high, value & (size - 1)
    high = value // size
    return high, value - high * size


def route_kernel(ids_ref, outgoing_ref, position_ref, *, devices, capacity, blocks, per_column):
    lane = lax.broadcasted_iota(jnp.int32, (LANES, LANES), 1)
    row = lax.broadcasted_iota(jnp.int32, (LANES, LANES), 0)
    upper = jnp.where(row <= lane, 1.0, 0.0).astype(jnp.bfloat16)
    tile_no = lax.broadcasted_iota(jnp.int32, (devices, LANES), 0)
    slot_no = lax.broadcasted_iota(jnp.int32, (capacity, LANES), 0)
    before = jnp.zeros((devices, 1), jnp.float32)
    lists = jnp.zeros((2 * devices, capacity), jnp.float32)
    for chunk in range(ids_ref.shape[0]):
        target, local = split_by(ids_ref[chunk : chunk + 1, :], blocks)
        column, part = split_by(local, per_column)
        local = ((column >> 3) * per_column + part) * 8 + (column & 7)
        hit = tile_no == target
        onehot = jnp.where(hit, 1.0, 0.0)
        upto = before + jnp.dot(
            onehot.astype(jnp.bfloat16), upper, preferred_element_type=jnp.float32
        )
        before = upto[:, LANES - 1 :]
        rank = jnp.sum(onehot * upto, axis=0, keepdims=True).astype(jnp.int32) - 1
        in_slot = jnp.where(slot_no == rank, 1.0, 0.0).astype(jnp.bfloat16)
        high = ((local >> 7) + 1).astype(jnp.float32)
        low = (local & 127).astype(jnp.float32)
        digits = jnp.concatenate([jnp.where(hit, high, 0.0), jnp.where(hit, low, 0.0)], axis=0)
        lists = lists + lax.dot_general(
            digits.astype(jnp.bfloat16),
            in_slot,
            CONTRACT_LANES,
            preferred_element_type=jnp.float32,
        )
        position_ref[chunk : chunk + 1, :] = target * capacity + rank
    high, low = lists[:devices], lists[devices:]
    wanted = ((high - 1.0) * 128.0 + low).astype(jnp.int32)
    outgoing_ref[...] = jnp.where(high > 0.5, wanted, blocks + before.astype(jnp.int32))


def filled_groups(incoming_ref, source, capacity, blocks):
    last = incoming_ref[source, capacity - 1]
    filled = jnp.where(last < blocks, capacity, last - blocks)
    return (filled + GROUP - 1) // GROUP


def serve_kernel(incoming_ref, table_ref, served_ref, rows_ref, *, capacity, blocks):
    sources = incoming_ref.shape[0]

    def one_source(source, carry):
        base = pl.multiple_of(source * capacity, capacity)

        def one_group(group, carry):
            first = pl.multiple_of(group * GROUP, GROUP)
            for j in range(GROUP):
                at = jnp.minimum(incoming_ref[source, first + j], blocks - 1)
                rows_ref[pl.ds(base + first + j, 1), :] = table_ref[pl.ds(at, 1), :]
            return carry

        lax.fori_loop(0, filled_groups(incoming_ref, source, capacity, blocks), one_group, 0)
        span = pl.ds(base, capacity)
        served_ref[span, :] = jnp.exp(rows_ref[span, :]).astype(jnp.bfloat16)
        return carry

    lax.fori_loop(0, sources, one_source, 0)


def match_kernel(incoming_ref, match_ref):
    lane = lax.broadcasted_iota(jnp.int32, (LANES, LANES), 1)
    row = lax.broadcasted_iota(jnp.int32, (LANES, LANES), 0)
    ones = jnp.ones((LANES, LANES), jnp.bfloat16)
    same_group = (lane // GROUP) == (row // GROUP)

    def one_row(i, carry):
        wanted = incoming_ref[pl.ds(i, 1), :]
        high = jnp.where(lane == row, (wanted >> 7).astype(jnp.float32), 0.0).astype(jnp.bfloat16)
        low = jnp.where(lane == row, (wanted & 127).astype(jnp.float32), 0.0).astype(jnp.bfloat16)
        down = 128.0 * jnp.dot(high, ones, preferred_element_type=jnp.float32)
        down = down + jnp.dot(low, ones, preferred_element_type=jnp.float32)
        same = (down == wanted.astype(jnp.float32)) & same_group
        match_ref[pl.ds(pl.multiple_of(i * LANES, LANES), LANES), :] = jnp.where(
            same, 1.0, 0.0
        ).astype(jnp.bfloat16)
        return carry

    lax.fori_loop(0, incoming_ref.shape[0], one_row, 0)


def star_kernel(
    position_ref,
    returned_ref,
    observed_ref,
    inverse_ref,
    weights_hbm,
    extinction_ref,
    parcel_ref,
    weights_ref,
    fetched_ref,
    sens_ref,
    sems,
):
    blocks_dev, slots, stars, width = weights_ref.shape
    chunks = extinction_ref.shape[0]
    per = blocks_dev // chunks

    def load(chunk):
        span = pl.ds(chunk * per, per)
        return pltpu.make_async_copy(weights_hbm.at[span], weights_ref.at[span], sems.at[chunk])

    for chunk in range(chunks):
        load(chunk).start()
    fetched_ref[...] = returned_ref[...].astype(jnp.float32)
    sens_ref[...] = jnp.zeros_like(sens_ref)
    lane = lax.broadcasted_iota(jnp.int32, (8, LANES), 1)
    row = lax.broadcasted_iota(jnp.int32, (8, LANES), 0)
    star_group = lane // stars

    def extinctions(chunk):
        sums = []
        for b in range(per):
            total = jnp.zeros((stars, width), jnp.float32)
            for k in range(slots):
                at = position_ref[chunk, b * slots + k]
                total = total + weights_ref[chunk * per + b, k].astype(jnp.float32) * fetched_ref[
                    pl.ds(at, 1), :
                ]
            sums.append(total)
        extinction = lax.dot_general(
            jnp.ones((8, width), jnp.float32),
            jnp.concatenate(sums, axis=0),
            CONTRACT_LANES,
            precision=lax.Precision.HIGHEST,
            preferred_element_type=jnp.float32,
        )
        extinction_ref[pl.ds(chunk, 1), :] = extinction[:1]
        here = pl.ds(chunk, 1)
        return inverse_ref[here, :] * (extinction - observed_ref[here, :])

    def sensitivities(chunk, weighted):
        for b in range(per):
            spread = jnp.where(star_group == b, weighted, 0.0)
            shift = stars
            while shift < LANES:
                spread = spread + pltpu.roll(spread, shift, 1)
                shift *= 2
            left = jnp.concatenate(
                [jnp.where(row == star_group + per * h, spread, 0.0) for h in range(8 // per)],
                axis=1,
            ).astype(jnp.bfloat16)
            for j in range(slots // 8):
                right = weights_ref[chunk * per + b, 8 * j : 8 * j + 8].reshape(8 * stars, width)
                sens = jnp.dot(left, right, preferred_element_type=jnp.float32)
                for r in range(8):
                    at = position_ref[chunk, b * slots + 8 * j + r]
                    sens_ref[pl.ds(at, 1), :] = sens[r : r + 1, :]

    load(0).wait()
    first = extinctions(0)

    def step(chunk, weighted):
        load(chunk).wait()
        following = extinctions(chunk)
        sensitivities(chunk - 1, weighted)
        return following

    last = lax.fori_loop(1, chunks, step, first)
    sensitivities(chunks - 1, last)
    parcel_ref[...] = sens_ref[...].astype(jnp.bfloat16)


def prior_kernel(field_ref, xlo_ref, xhi_ref, ylo_ref, yhi_ref, out_ref, padded, smooth):
    cells_x, cells_y, depth = field_ref.shape
    rows = padded.shape[1]
    gx, gy = lax.axis_index("gx"), lax.axis_index("gy")
    last_gx, last_gy = lax.axis_size("gx") - 1, lax.axis_size("gy") - 1
    z = lax.broadcasted_iota(jnp.int32, (rows, depth), 1)
    y = lax.broadcasted_iota(jnp.int32, (rows, depth), 0) - 8
    inside_y = ((y >= 0) | (gy > 0)) & ((y < cells_y) | (gy < last_gy))

    def operate(center, below, above):
        beside = below + above
        beside = beside + pltpu.roll(center, 1, 0) + pltpu.roll(center, rows - 1, 0)
        beside = beside + jnp.where(z == 0, 0.0, pltpu.roll(center, 1, 1))
        beside = beside + jnp.where(z == depth - 1, 0.0, pltpu.roll(center, depth - 1, 1))
        return (shift_kappa + 6.0) * center - beside

    def fill(plane, source):
        padded[plane, 8 : 8 + cells_y, :] = source
        padded[plane, 0:8, :] = jnp.zeros((8, depth), jnp.float32)
        padded[plane, 8 + cells_y :, :] = jnp.zeros((8, depth), jnp.float32)
        for h in range(2):
            padded[plane, 6 + h : 7 + h, :] = ylo_ref[h, pl.ds(plane, 1), :]
            padded[plane, 8 + cells_y + h : 9 + cells_y + h, :] = yhi_ref[h, pl.ds(plane, 1), :]

    for h in range(2):
        fill(h, xlo_ref[h])
        fill(cells_x + 2 + h, xhi_ref[h])

    def fill_own(x, carry):
        fill(x + 2, field_ref[x])
        return carry

    lax.fori_loop(0, cells_x, fill_own, 0)

    def smooth_plane(plane, carry):
        value = operate(padded[plane], padded[plane - 1], padded[plane + 1])
        inside = ((plane > 1) | (gx > 0)) & ((plane < cells_x + 2) | (gx < last_gx))
        smooth[plane - 1] = jnp.where(inside_y & inside, value, 0.0)
        return carry

    lax.fori_loop(1, cells_x + 3, smooth_plane, 0)

    def out_plane(x, carry):
        prior = operate(smooth[x + 1], smooth[x], smooth[x + 2])
        out_ref[x] = field_ref[x] - (step_rate * prior_weight) * prior[8 : 8 + cells_y]
        return carry

    lax.fori_loop(0, cells_x, out_plane, 0)


def finish_kernel(
    incoming_ref,
    match_ref,
    arrived_ref,
    field_hbm,
    base_hbm,
    out_hbm,
    collected,
    rows_ref,
    field_ref,
    base_ref,
    out_ref,
    in_sems,
    out_sems,
    *,
    capacity,
    blocks,
):
    cells_x, cells_y, depth = field_ref.shape
    sources = incoming_ref.shape[0]
    parts = out_sems.shape[0]
    planes = cells_x // parts
    loads = [
        pltpu.make_async_copy(field_hbm, field_ref, in_sems.at[0]),
        pltpu.make_async_copy(base_hbm, base_ref, in_sems.at[1]),
    ]
    for load in loads:
        load.start()

    def clear(i, carry):
        collected[pl.ds(pl.multiple_of(i * LANES, LANES), LANES), :] = jnp.zeros(
            (LANES, LANES), jnp.float32
        )
        return carry

    lax.fori_loop(0, blocks // LANES, clear, 0)

    def merge(i, carry):
        span = pl.ds(pl.multiple_of(i * LANES, LANES), LANES)
        rows_ref[span, :] = jnp.dot(
            match_ref[span, :], arrived_ref[span, :], preferred_element_type=jnp.float32
        )
        return carry

    lax.fori_loop(0, rows_ref.shape[0] // LANES, merge, 0)

    def one_source(source, carry):
        def one_group(group, carry):
            first = pl.multiple_of(group * GROUP, GROUP)
            places = [
                pl.ds(jnp.minimum(incoming_ref[source, first + j], blocks), 1)
                for j in range(GROUP)
            ]
            start = source * capacity + first
            sums = [
                collected[places[j], :] + rows_ref[pl.ds(start + j, 1), :] for j in range(GROUP)
            ]
            for j in range(GROUP):
                collected[places[j], :] = sums[j]
            return carry

        return lax.fori_loop(
            0, filled_groups(incoming_ref, source, capacity, blocks), one_group, carry
        )

    lax.fori_loop(0, sources, one_source, 0)
    for load in loads:
        load.wait()
    per_column = depth // LANES

    def store(part):
        span = pl.ds(part * planes, planes)
        return pltpu.make_async_copy(out_ref.at[span], out_hbm.at[span], out_sems.at[part])

    def one_plane(x, carry):
        for yb in range(cells_y // 8):
            for part in range(per_column):
                at = ((x * (cells_y // 8) + yb) * per_column + part) * 8
                grad = collected[pl.ds(pl.multiple_of(at, 8), 8), :]
                where = (x, slice(8 * yb, 8 * yb + 8), slice(part * LANES, (part + 1) * LANES))
                out_ref[where] = base_ref[where] - step_rate * (grad * jnp.exp(field_ref[where]))
        return carry

    for part in range(parts):
        lax.fori_loop(part * planes, (part + 1) * planes, one_plane, 0)
        store(part).start()
    for part in range(parts):
        store(part).wait()


def halo(field):
    def both_ways(first, last, axis):
        peers = lax.axis_size(axis)
        up = [(i, i + 1) for i in range(peers - 1)]
        down = [(j, i) for i, j in up]
        return lax.ppermute(last, axis, up), lax.ppermute(first, axis, down)

    xlo, xhi = both_ways(field[:2], field[-2:], "gx")

    def rows(at):
        return jnp.concatenate([xlo[:, at], field[:, at], xhi[:, at]], axis=0).transpose(1, 0, 2)

    ylo, yhi = both_ways(rows(slice(0, 2)), rows(slice(-2, None)), "gy")
    return xlo, xhi, ylo, yhi


VMEM = pl.BlockSpec(memory_space=pltpu.VMEM)
SMEM = pl.BlockSpec(memory_space=pltpu.SMEM)
ANY = pl.BlockSpec(memory_space=pl.ANY)


def on_device(log_density, weights, observed, inverse_var, star_counts, block_ids):
    cells_x, cells_y, depth = log_density.shape
    blocks_dev, slots, stars, width = weights.shape
    devices = lax.axis_size("gx") * lax.axis_size("gy")
    requests = blocks_dev * slots
    capacity = 2 * requests // devices
    all_slots = devices * capacity
    per_column = depth // width
    blocks = cells_x * cells_y * per_column
    cells = log_density.size
    mesh_axes = ("gx", "gy")
    f32, bf16, i32 = jnp.float32, jnp.bfloat16, jnp.int32
    shape = jax.ShapeDtypeStruct

    def exchange(x):
        return lax.all_to_all(x, mesh_axes, split_axis=0, concat_axis=0, tiled=True)

    outgoing, position = pl.pallas_call(
        functools.partial(
            route_kernel,
            devices=devices,
            capacity=capacity,
            blocks=blocks,
            per_column=per_column,
        ),
        out_shape=[shape((devices, capacity), i32), shape((requests // LANES, LANES), i32)],
        in_specs=[VMEM],
        out_specs=[VMEM, VMEM],
        name="route",
    )(block_ids.reshape(requests // LANES, LANES))
    incoming = exchange(outgoing)

    table = (
        log_density.reshape(cells_x, cells_y // 8, 8, per_column, width)
        .transpose(0, 1, 3, 2, 4)
        .reshape(blocks, width)
    )
    served = pl.pallas_call(
        functools.partial(serve_kernel, capacity=capacity, blocks=blocks),
        out_shape=shape((all_slots, width), bf16),
        in_specs=[SMEM, VMEM],
        out_specs=VMEM,
        scratch_shapes=[pltpu.VMEM((all_slots, width), f32)],
        compiler_params=pltpu.CompilerParams(vmem_limit_bytes=16 * MIB),
        cost_estimate=pl.CostEstimate(flops=0, bytes_accessed=5 * MIB, transcendentals=0),
        name="serve",
    )(incoming, table)
    returned = exchange(served.reshape(devices, capacity, width)).reshape(all_slots, width)

    field, incoming_late, _ = lax.optimization_barrier((log_density, incoming, served))
    match = pl.pallas_call(
        match_kernel,
        out_shape=shape((all_slots, LANES), bf16),
        in_specs=[VMEM],
        out_specs=VMEM,
        compiler_params=pltpu.CompilerParams(vmem_limit_bytes=8 * MIB),
        cost_estimate=pl.CostEstimate(flops=10**9, bytes_accessed=MIB, transcendentals=0),
        name="match",
    )(incoming_late.reshape(all_slots // LANES, LANES))
    xlo, xhi, ylo, yhi = halo(field)
    base = pl.pallas_call(
        prior_kernel,
        out_shape=shape((cells_x, cells_y, depth), f32),
        in_specs=[VMEM] * 5,
        out_specs=VMEM,
        scratch_shapes=[
            pltpu.VMEM((cells_x + 4, cells_y + 16, depth), f32),
            pltpu.VMEM((cells_x + 2, cells_y + 16, depth), f32),
        ],
        compiler_params=pltpu.CompilerParams(vmem_limit_bytes=32 * MIB),
        cost_estimate=pl.CostEstimate(
            flops=30 * cells, bytes_accessed=8 * cells, transcendentals=0
        ),
        name="prior",
    )(field, xlo, xhi, ylo, yhi)

    chunks = blocks_dev * stars // LANES
    live = jnp.arange(stars)[None, :] < star_counts[:, None]
    live_inverse = jnp.where(live, inverse_var, 0.0).reshape(chunks, LANES)
    extinction, parcel = pl.pallas_call(
        star_kernel,
        out_shape=[shape((chunks, LANES), f32), shape((all_slots, width), bf16)],
        in_specs=[SMEM, VMEM, VMEM, VMEM, ANY],
        out_specs=[VMEM, VMEM],
        scratch_shapes=[
            pltpu.VMEM(weights.shape, bf16),
            pltpu.VMEM((all_slots, width), f32),
            pltpu.VMEM((all_slots, width), f32),
            pltpu.SemaphoreType.DMA((chunks,)),
        ],
        compiler_params=pltpu.CompilerParams(vmem_limit_bytes=32 * MIB),
        cost_estimate=pl.CostEstimate(
            flops=4 * weights.size, bytes_accessed=2 * weights.size, transcendentals=0
        ),
        name="stars",
    )(position, returned, observed.reshape(chunks, LANES), live_inverse, weights)
    arrived = exchange(parcel.reshape(devices, capacity, width)).reshape(all_slots, width)

    parts = 8
    new_log_density = pl.pallas_call(
        functools.partial(finish_kernel, capacity=capacity, blocks=blocks),
        out_shape=shape((cells_x, cells_y, depth), f32),
        in_specs=[SMEM, VMEM, VMEM, ANY, ANY],
        out_specs=ANY,
        scratch_shapes=[
            pltpu.VMEM((blocks + 8, width), f32),
            pltpu.VMEM((all_slots, width), f32),
            pltpu.VMEM((cells_x, cells_y, depth), f32),
            pltpu.VMEM((cells_x, cells_y, depth), f32),
            pltpu.VMEM((cells_x, cells_y, depth), f32),
            pltpu.SemaphoreType.DMA((2,)),
            pltpu.SemaphoreType.DMA((parts,)),
        ],
        compiler_params=pltpu.CompilerParams(vmem_limit_bytes=32 * MIB),
        cost_estimate=pl.CostEstimate(
            flops=4 * cells, bytes_accessed=12 * cells, transcendentals=cells
        ),
        name="finish",
    )(incoming, match, arrived, log_density, base)
    return new_log_density, extinction.reshape(blocks_dev, stars)


def solution(mesh):
    placed = (
        P("gx", "gy", None),
        P(("gx", "gy"), None, None, None),
        P(("gx", "gy"), None),
        P(("gx", "gy"), None),
        P(("gx", "gy")),
        P(("gx", "gy"), None),
    )
    return jax.shard_map(
        on_device,
        mesh=mesh,
        in_specs=placed,
        out_specs=(P("gx", "gy", None), P(("gx", "gy"), None)),
        check_vma=False,
    )
```

```python
import functools

import jax
import jax.numpy as jnp
from jax import lax
from jax.experimental import pallas as pl
from jax.experimental.pallas import tpu as pltpu
from jax.sharding import PartitionSpec as P

shift_kappa = 0.5
prior_weight = 0.05
step_rate = 2.0

LANES = 128
GROUP = 16
MIB = 1 << 20

CONTRACT_LANES = (((1,), (1,)), ((), ()))


def split_by(value, size):
    if size & (size - 1) == 0:
        high = value >> (size.bit_length() - 1)
        return high, value & (size - 1)
    high = value // size
    return high, value - high * size


def route_kernel(ids_ref, outgoing_ref, position_ref, *, devices, capacity, blocks, per_column):
    half = ids_ref.shape[0] // 2
    ids = jnp.concatenate([ids_ref[:half, :], ids_ref[half:, :]], axis=1)
    lane = lax.broadcasted_iota(jnp.int32, (LANES, LANES), 1)
    row = lax.broadcasted_iota(jnp.int32, (LANES, LANES), 0)
    upper = jnp.where(row <= lane, 1.0, 0.0).astype(jnp.bfloat16)
    tile_no = lax.broadcasted_iota(jnp.int32, (devices, LANES), 0)
    slot_no = lax.broadcasted_iota(jnp.int32, (capacity, LANES), 0)
    before = jnp.zeros((devices, 1), jnp.float32)
    lists = jnp.zeros((2 * devices, capacity), jnp.float32)
    for chunk in range(half):
        target, local = split_by(ids[chunk : chunk + 1, :], blocks)
        column, part = split_by(local, per_column)
        local = ((column >> 3) * per_column + part) * 8 + (column & 7)
        hit = tile_no == target
        onehot = jnp.where(hit, 1.0, 0.0)
        upto = before + jnp.dot(
            onehot.astype(jnp.bfloat16), upper, preferred_element_type=jnp.float32
        )
        before = upto[:, LANES - 1 :]
        rank = jnp.sum(onehot * upto, axis=0, keepdims=True).astype(jnp.int32) - 1
        in_slot = jnp.where(slot_no == rank, 1.0, 0.0).astype(jnp.bfloat16)
        high = ((local >> 7) + 1).astype(jnp.float32)
        low = (local & 127).astype(jnp.float32)
        digits = jnp.concatenate([jnp.where(hit, high, 0.0), jnp.where(hit, low, 0.0)], axis=0)
        lists = lists + lax.dot_general(
            digits.astype(jnp.bfloat16),
            in_slot,
            CONTRACT_LANES,
            preferred_element_type=jnp.float32,
        )
        position_ref[chunk : chunk + 1, :] = target * capacity + rank
    high, low = lists[:devices], lists[devices:]
    wanted = ((high - 1.0) * 128.0 + low).astype(jnp.int32)
    outgoing_ref[...] = jnp.where(high > 0.5, wanted, blocks + before.astype(jnp.int32))


def table_kernel(field_ref, table_ref, xfirst_ref, xlast_ref, yfirst_ref, ylast_ref):
    cells_x, cells_y, depth = field_ref.shape
    per_column = depth // LANES
    xfirst_ref[...] = field_ref[:2]
    xlast_ref[...] = field_ref[cells_x - 2 :]

    def one_plane(x, carry):
        for yb in range(cells_y // 8):
            for part in range(per_column):
                at = pl.multiple_of(((x * (cells_y // 8) + yb) * per_column + part) * 8, 8)
                table_ref[pl.ds(at, 8), :] = jnp.exp(
                    field_ref[x, 8 * yb : 8 * yb + 8, part * LANES : (part + 1) * LANES]
                )
        for h in range(2):
            yfirst_ref[h, pl.ds(x, 1), :] = field_ref[x, h : h + 1, :]
            ylast_ref[h, pl.ds(x, 1), :] = field_ref[x, cells_y - 2 + h : cells_y - 1 + h, :]
        return carry

    lax.fori_loop(0, cells_x, one_plane, 0)
    pad = table_ref.shape[0] - cells_x * cells_y * per_column
    table_ref[cells_x * cells_y * per_column :, :] = jnp.zeros((pad, LANES), jnp.float32)


def filled_groups(incoming_ref, source, capacity, blocks):
    last = incoming_ref[source, capacity - 1]
    filled = jnp.where(last < blocks, capacity, last - blocks)
    return (filled + GROUP - 1) // GROUP


def serve_kernel(incoming_ref, table_ref, served_ref, rows_ref, *, capacity, blocks):
    def one_source(source, carry):
        def one_group(group, carry):
            first = pl.multiple_of(group * GROUP, GROUP)
            rows = [
                table_ref[pl.ds(incoming_ref[source, first + j], 1), :] for j in range(GROUP)
            ]
            start = source * capacity + first
            for j in range(GROUP):
                rows_ref[pl.ds(start + j, 1), :] = rows[j]
            return carry

        return lax.fori_loop(
            0, filled_groups(incoming_ref, source, capacity, blocks), one_group, carry
        )

    lax.fori_loop(0, incoming_ref.shape[0], one_source, 0)
    served_ref[...] = rows_ref[...].astype(jnp.bfloat16)


def match_kernel(incoming_ref, match_ref):
    lane = lax.broadcasted_iota(jnp.int32, (LANES, LANES), 1)
    row = lax.broadcasted_iota(jnp.int32, (LANES, LANES), 0)
    ones = jnp.ones((LANES, LANES), jnp.bfloat16)
    same_group = (lane // GROUP) == (row // GROUP)

    def one_row(i, carry):
        wanted = incoming_ref[pl.ds(i, 1), :]
        high = jnp.where(lane == row, (wanted >> 7).astype(jnp.float32), 0.0).astype(jnp.bfloat16)
        low = jnp.where(lane == row, (wanted & 127).astype(jnp.float32), 0.0).astype(jnp.bfloat16)
        down = 128.0 * jnp.dot(high, ones, preferred_element_type=jnp.float32)
        down = down + jnp.dot(low, ones, preferred_element_type=jnp.float32)
        same = (down == wanted.astype(jnp.float32)) & same_group
        match_ref[pl.ds(pl.multiple_of(i * LANES, LANES), LANES), :] = jnp.where(
            same, 1.0, 0.0
        ).astype(jnp.bfloat16)
        return carry

    lax.fori_loop(0, incoming_ref.shape[0], one_row, 0)


def star_kernel(
    position_ref,
    returned_ref,
    observed_ref,
    inverse_ref,
    weights_hbm,
    extinction_ref,
    parcel_ref,
    weights_ref,
    fetched_ref,
    sens_ref,
    sems,
):
    blocks_dev, slots, stars, width = weights_ref.shape
    chunks = extinction_ref.shape[0]
    per = blocks_dev // chunks
    half = position_ref.shape[0]

    def place(block, slot):
        return position_ref[slot % half, (slot // half) * blocks_dev + block]

    def load(chunk):
        span = pl.ds(chunk * per, per)
        return pltpu.make_async_copy(weights_hbm.at[span], weights_ref.at[span], sems.at[chunk])

    for chunk in range(chunks):
        load(chunk).start()
    fetched_ref[...] = returned_ref[...].astype(jnp.float32)
    sens_ref[...] = jnp.zeros_like(sens_ref)
    lane = lax.broadcasted_iota(jnp.int32, (8, LANES), 1)
    row = lax.broadcasted_iota(jnp.int32, (8, LANES), 0)
    star_group = lane // stars

    def extinctions(chunk):
        sums = []
        for b in range(per):
            total = jnp.zeros((stars, width), jnp.float32)
            for k in range(slots):
                at = place(chunk * per + b, k)
                total = total + weights_ref[chunk * per + b, k].astype(jnp.float32) * fetched_ref[
                    pl.ds(at, 1), :
                ]
            sums.append(total)
        extinction = lax.dot_general(
            jnp.ones((8, width), jnp.float32),
            jnp.concatenate(sums, axis=0),
            CONTRACT_LANES,
            precision=lax.Precision.HIGHEST,
            preferred_element_type=jnp.float32,
        )
        extinction_ref[pl.ds(chunk, 1), :] = extinction[:1]
        here = pl.ds(chunk, 1)
        return inverse_ref[here, :] * (extinction - observed_ref[here, :])

    def sensitivities(chunk, weighted):
        for b in range(per):
            spread = jnp.where(star_group == b, weighted, 0.0)
            shift = stars
            while shift < LANES:
                spread = spread + pltpu.roll(spread, shift, 1)
                shift *= 2
            left = jnp.concatenate(
                [jnp.where(row == star_group + per * h, spread, 0.0) for h in range(8 // per)],
                axis=1,
            ).astype(jnp.bfloat16)
            for j in range(slots // 8):
                right = weights_ref[chunk * per + b, 8 * j : 8 * j + 8].reshape(8 * stars, width)
                sens = jnp.dot(left, right, preferred_element_type=jnp.float32)
                for r in range(8):
                    at = place(chunk * per + b, 8 * j + r)
                    sens_ref[pl.ds(at, 1), :] = sens[r : r + 1, :]

    load(0).wait()
    first = extinctions(0)

    def step(chunk, weighted):
        load(chunk).wait()
        following = extinctions(chunk)
        sensitivities(chunk - 1, weighted)
        return following

    last = lax.fori_loop(1, chunks, step, first)
    sensitivities(chunks - 1, last)
    parcel_ref[...] = sens_ref[...].astype(jnp.bfloat16)


def prior_kernel(field_ref, xlo_ref, xhi_ref, ylo_ref, yhi_ref, out_ref, padded, smooth):
    cells_x, cells_y, depth = field_ref.shape
    rows = padded.shape[1]
    gx, gy = lax.axis_index("gx"), lax.axis_index("gy")
    last_gx, last_gy = lax.axis_size("gx") - 1, lax.axis_size("gy") - 1
    z = lax.broadcasted_iota(jnp.int32, (rows, depth), 1)
    y = lax.broadcasted_iota(jnp.int32, (rows, depth), 0) - 8
    inside_y = ((y >= 0) | (gy > 0)) & ((y < cells_y) | (gy < last_gy))

    def operate(center, below, above):
        beside = below + above
        beside = beside + pltpu.roll(center, 1, 0) + pltpu.roll(center, rows - 1, 0)
        beside = beside + jnp.where(z == 0, 0.0, pltpu.roll(center, 1, 1))
        beside = beside + jnp.where(z == depth - 1, 0.0, pltpu.roll(center, depth - 1, 1))
        return (shift_kappa + 6.0) * center - beside

    def fill(plane, source):
        padded[plane, 8 : 8 + cells_y, :] = source
        padded[plane, 0:8, :] = jnp.zeros((8, depth), jnp.float32)
        padded[plane, 8 + cells_y :, :] = jnp.zeros((8, depth), jnp.float32)
        for h in range(2):
            padded[plane, 6 + h : 7 + h, :] = ylo_ref[h, pl.ds(plane, 1), :]
            padded[plane, 8 + cells_y + h : 9 + cells_y + h, :] = yhi_ref[h, pl.ds(plane, 1), :]

    for h in range(2):
        fill(h, xlo_ref[h])
        fill(cells_x + 2 + h, xhi_ref[h])

    def fill_own(x, carry):
        fill(x + 2, field_ref[x])
        return carry

    lax.fori_loop(0, cells_x, fill_own, 0)

    def smooth_plane(plane, carry):
        value = operate(padded[plane], padded[plane - 1], padded[plane + 1])
        inside = ((plane > 1) | (gx > 0)) & ((plane < cells_x + 2) | (gx < last_gx))
        smooth[plane - 1] = jnp.where(inside_y & inside, value, 0.0)
        return carry

    lax.fori_loop(1, cells_x + 3, smooth_plane, 0)

    def out_plane(x, carry):
        prior = operate(smooth[x + 1], smooth[x], smooth[x + 2])
        out_ref[x] = field_ref[x] - (step_rate * prior_weight) * prior[8 : 8 + cells_y]
        return carry

    lax.fori_loop(0, cells_x, out_plane, 0)


def finish_kernel(
    incoming_ref,
    match_ref,
    arrived_ref,
    table_hbm,
    base_hbm,
    out_hbm,
    rows_ref,
    table_ref,
    out_ref,
    sems,
    *,
    capacity,
    blocks,
):
    own = pl.ds(0, blocks)
    loads = [
        pltpu.make_async_copy(table_hbm, table_ref, sems.at[0]),
        pltpu.make_async_copy(base_hbm, out_ref.at[own], sems.at[1]),
    ]
    for load in loads:
        load.start()
    for i in range(rows_ref.shape[0] // LANES):
        span = slice(i * LANES, (i + 1) * LANES)
        rows_ref[span, :] = -step_rate * jnp.dot(
            match_ref[span, :], arrived_ref[span, :], preferred_element_type=jnp.float32
        )
    for load in loads:
        load.wait()

    def one_source(source, carry):
        def one_group(group, carry):
            first = pl.multiple_of(group * GROUP, GROUP)
            places = [pl.ds(incoming_ref[source, first + j], 1) for j in range(GROUP)]
            start = source * capacity + first
            sums = [
                out_ref[places[j], :] + table_ref[places[j], :] * rows_ref[pl.ds(start + j, 1), :]
                for j in range(GROUP)
            ]
            for j in range(GROUP):
                out_ref[places[j], :] = sums[j]
            return carry

        return lax.fori_loop(
            0, filled_groups(incoming_ref, source, capacity, blocks), one_group, carry
        )

    lax.fori_loop(0, incoming_ref.shape[0], one_source, 0)
    store = pltpu.make_async_copy(out_ref.at[own], out_hbm, sems.at[2])
    store.start()
    store.wait()


def halo(xfirst, xlast, yfirst, ylast):
    def both_ways(first, last, axis):
        peers = lax.axis_size(axis)
        up = [(i, i + 1) for i in range(peers - 1)]
        down = [(j, i) for i, j in up]
        return lax.ppermute(last, axis, up), lax.ppermute(first, axis, down)

    xlo, xhi = both_ways(xfirst, xlast, "gx")

    def rows(own, at):
        return jnp.concatenate(
            [xlo[:, at].transpose(1, 0, 2), own, xhi[:, at].transpose(1, 0, 2)], axis=1
        )

    ylo, yhi = both_ways(rows(yfirst, slice(0, 2)), rows(ylast, slice(-2, None)), "gy")
    return xlo, xhi, ylo, yhi


VMEM = pl.BlockSpec(memory_space=pltpu.VMEM)
SMEM = pl.BlockSpec(memory_space=pltpu.SMEM)
ANY = pl.BlockSpec(memory_space=pl.ANY)


def on_device(log_density, weights, observed, inverse_var, star_counts, block_ids):
    cells_x, cells_y, depth = log_density.shape
    blocks_dev, slots, stars, width = weights.shape
    devices = lax.axis_size("gx") * lax.axis_size("gy")
    requests = blocks_dev * slots
    capacity = 2 * requests // devices
    all_slots = devices * capacity
    per_column = depth // width
    blocks = cells_x * cells_y * per_column
    cells = log_density.size
    mesh_axes = ("gx", "gy")
    f32, bf16, i32 = jnp.float32, jnp.bfloat16, jnp.int32
    shape = jax.ShapeDtypeStruct

    def to_rows(x):
        x = x.reshape(cells_x, cells_y // 8, 8, per_column, width)
        return x.transpose(0, 1, 3, 2, 4).reshape(blocks, width)

    def to_field(rows):
        x = rows.reshape(cells_x, cells_y // 8, per_column, 8, width)
        return x.transpose(0, 1, 3, 2, 4).reshape(cells_x, cells_y, depth)

    def exchange(x):
        return lax.all_to_all(x, mesh_axes, split_axis=0, concat_axis=0, tiled=True)

    outgoing, position = pl.pallas_call(
        functools.partial(
            route_kernel,
            devices=devices,
            capacity=capacity,
            blocks=blocks,
            per_column=per_column,
        ),
        out_shape=[shape((devices, capacity), i32), shape((requests // LANES, LANES), i32)],
        in_specs=[VMEM],
        out_specs=[VMEM, VMEM],
        name="route",
    )(block_ids.T)
    incoming = exchange(outgoing)

    field, _ = lax.optimization_barrier((log_density, outgoing))
    table, xfirst, xlast, yfirst, ylast = pl.pallas_call(
        table_kernel,
        out_shape=[
            shape((blocks + capacity, width), f32),
            shape((2, cells_y, depth), f32),
            shape((2, cells_y, depth), f32),
            shape((2, cells_x, depth), f32),
            shape((2, cells_x, depth), f32),
        ],
        in_specs=[VMEM],
        out_specs=[VMEM] * 5,
        compiler_params=pltpu.CompilerParams(vmem_limit_bytes=16 * MIB),
        cost_estimate=pl.CostEstimate(
            flops=8 * cells, bytes_accessed=8 * cells, transcendentals=cells
        ),
        name="table",
    )(field)

    served = pl.pallas_call(
        functools.partial(serve_kernel, capacity=capacity, blocks=blocks),
        out_shape=shape((all_slots, width), bf16),
        in_specs=[SMEM, VMEM],
        out_specs=VMEM,
        scratch_shapes=[pltpu.VMEM((all_slots, width), f32)],
        compiler_params=pltpu.CompilerParams(vmem_limit_bytes=16 * MIB),
        cost_estimate=pl.CostEstimate(flops=0, bytes_accessed=5 * MIB, transcendentals=0),
        name="serve",
    )(incoming, table)
    returned = exchange(served.reshape(devices, capacity, width)).reshape(all_slots, width)

    *edges, _ = lax.optimization_barrier((xfirst, xlast, yfirst, ylast, served))
    sides = halo(*edges)
    returned, *sides = lax.optimization_barrier((returned, *sides))

    chunks = blocks_dev * stars // LANES
    live = jnp.arange(stars)[None, :] < star_counts[:, None]
    live_inverse = jnp.where(live, inverse_var, 0.0).reshape(chunks, LANES)
    extinction, parcel = pl.pallas_call(
        star_kernel,
        out_shape=[shape((chunks, LANES), f32), shape((all_slots, width), bf16)],
        in_specs=[SMEM, VMEM, VMEM, VMEM, ANY],
        out_specs=[VMEM, VMEM],
        scratch_shapes=[
            pltpu.VMEM(weights.shape, bf16),
            pltpu.VMEM((all_slots, width), f32),
            pltpu.VMEM((all_slots, width), f32),
            pltpu.SemaphoreType.DMA((chunks,)),
        ],
        compiler_params=pltpu.CompilerParams(vmem_limit_bytes=56 * MIB),
        cost_estimate=pl.CostEstimate(
            flops=4 * weights.size, bytes_accessed=2 * weights.size, transcendentals=0
        ),
        name="stars",
    )(position, returned, observed.reshape(chunks, LANES), live_inverse, weights)
    arrived = exchange(parcel.reshape(devices, capacity, width)).reshape(all_slots, width)

    field_late, incoming_late, _ = lax.optimization_barrier((log_density, incoming, parcel))
    match = pl.pallas_call(
        match_kernel,
        out_shape=shape((all_slots, LANES), bf16),
        in_specs=[VMEM],
        out_specs=VMEM,
        compiler_params=pltpu.CompilerParams(vmem_limit_bytes=8 * MIB),
        cost_estimate=pl.CostEstimate(flops=10**9, bytes_accessed=MIB, transcendentals=0),
        name="match",
    )(incoming_late.reshape(all_slots // LANES, LANES))
    base = pl.pallas_call(
        prior_kernel,
        out_shape=shape((cells_x, cells_y, depth), f32),
        in_specs=[VMEM] * 5,
        out_specs=VMEM,
        scratch_shapes=[
            pltpu.VMEM((cells_x + 4, cells_y + 16, depth), f32),
            pltpu.VMEM((cells_x + 2, cells_y + 16, depth), f32),
        ],
        compiler_params=pltpu.CompilerParams(vmem_limit_bytes=32 * MIB),
        cost_estimate=pl.CostEstimate(
            flops=30 * cells, bytes_accessed=8 * cells, transcendentals=0
        ),
        name="prior",
    )(field_late, *sides)

    new_rows = pl.pallas_call(
        functools.partial(finish_kernel, capacity=capacity, blocks=blocks),
        out_shape=shape((blocks, width), f32),
        in_specs=[SMEM, VMEM, VMEM, ANY, ANY],
        out_specs=ANY,
        scratch_shapes=[
            pltpu.VMEM((all_slots, width), f32),
            pltpu.VMEM((blocks + capacity, width), f32),
            pltpu.VMEM((blocks + capacity, width), f32),
            pltpu.SemaphoreType.DMA((3,)),
        ],
        compiler_params=pltpu.CompilerParams(vmem_limit_bytes=56 * MIB),
        cost_estimate=pl.CostEstimate(
            flops=4 * cells, bytes_accessed=12 * cells, transcendentals=0
        ),
        name="finish",
    )(incoming, match, arrived, table, to_rows(base))
    return to_field(new_rows), extinction.reshape(blocks_dev, stars)


def solution(mesh):
    placed = (
        P("gx", "gy", None),
        P(("gx", "gy"), None, None, None),
        P(("gx", "gy"), None),
        P(("gx", "gy"), None),
        P(("gx", "gy")),
        P(("gx", "gy"), None),
    )
    return jax.shard_map(
        on_device,
        mesh=mesh,
        in_specs=placed,
        out_specs=(P("gx", "gy", None), P(("gx", "gy"), None)),
        check_vma=False,
    )
```

```python
import functools

import jax
import jax.numpy as jnp
from jax import lax
from jax.experimental import pallas as pl
from jax.experimental.pallas import tpu as pltpu
from jax.sharding import PartitionSpec as P

shift_kappa = 0.5
prior_weight = 0.05
step_rate = 2.0

LANES = 128
GROUP = 16
MIB = 1 << 20

CONTRACT_LANES = (((1,), (1,)), ((), ()))


def split_by(value, size):
    if size & (size - 1) == 0:
        high = value >> (size.bit_length() - 1)
        return high, value & (size - 1)
    high = value // size
    return high, value - high * size


def route_kernel(ids_ref, outgoing_ref, position_ref, *, devices, capacity, blocks, per_column):
    half = ids_ref.shape[0] // 2
    ids = jnp.concatenate([ids_ref[:half, :], ids_ref[half:, :]], axis=1)
    lane = lax.broadcasted_iota(jnp.int32, (LANES, LANES), 1)
    row = lax.broadcasted_iota(jnp.int32, (LANES, LANES), 0)
    upper = jnp.where(row <= lane, 1.0, 0.0).astype(jnp.bfloat16)
    tile_no = lax.broadcasted_iota(jnp.int32, (devices, LANES), 0)
    slot_no = lax.broadcasted_iota(jnp.int32, (capacity, LANES), 0)
    before = jnp.zeros((devices, 1), jnp.float32)
    lists = jnp.zeros((2 * devices, capacity), jnp.float32)
    for chunk in range(half):
        target, local = split_by(ids[chunk : chunk + 1, :], blocks)
        column, part = split_by(local, per_column)
        local = ((column >> 3) * per_column + part) * 8 + (column & 7)
        hit = tile_no == target
        onehot = jnp.where(hit, 1.0, 0.0)
        upto = before + jnp.dot(
            onehot.astype(jnp.bfloat16), upper, preferred_element_type=jnp.float32
        )
        before = upto[:, LANES - 1 :]
        rank = jnp.sum(onehot * upto, axis=0, keepdims=True).astype(jnp.int32) - 1
        in_slot = jnp.where(slot_no == rank, 1.0, 0.0).astype(jnp.bfloat16)
        high = ((local >> 7) + 1).astype(jnp.float32)
        low = (local & 127).astype(jnp.float32)
        digits = jnp.concatenate([jnp.where(hit, high, 0.0), jnp.where(hit, low, 0.0)], axis=0)
        lists = lists + lax.dot_general(
            digits.astype(jnp.bfloat16),
            in_slot,
            CONTRACT_LANES,
            preferred_element_type=jnp.float32,
        )
        position_ref[chunk : chunk + 1, :] = target * capacity + rank
    high, low = lists[:devices], lists[devices:]
    wanted = ((high - 1.0) * 128.0 + low).astype(jnp.int32)
    outgoing_ref[...] = jnp.where(high > 0.5, wanted, blocks + before.astype(jnp.int32))


def table_kernel(field_ref, table_ref, xfirst_ref, xlast_ref, yfirst_ref, ylast_ref):
    cells_x, cells_y, depth = field_ref.shape
    per_column = depth // LANES
    rows_ref = table_ref.reshape(table_ref.shape[0], LANES)
    xfirst_ref[...] = field_ref[:2]
    xlast_ref[...] = field_ref[cells_x - 2 :]

    def one_plane(x, carry):
        for yb in range(cells_y // 8):
            for part in range(per_column):
                at = pl.multiple_of(((x * (cells_y // 8) + yb) * per_column + part) * 8, 8)
                rows_ref[pl.ds(at, 8), :] = jnp.exp(
                    field_ref[x, 8 * yb : 8 * yb + 8, part * LANES : (part + 1) * LANES]
                )
        for h in range(2):
            yfirst_ref[h, pl.ds(x, 1), :] = field_ref[x, h : h + 1, :]
            ylast_ref[h, pl.ds(x, 1), :] = field_ref[x, cells_y - 2 + h : cells_y - 1 + h, :]
        return carry

    lax.fori_loop(0, cells_x, one_plane, 0)
    blocks = cells_x * cells_y * per_column
    rows_ref[blocks:, :] = jnp.zeros((table_ref.shape[0] - blocks, LANES), jnp.float32)


def filled_groups(incoming_ref, source, capacity, blocks):
    last = incoming_ref[source, capacity - 1]
    filled = jnp.where(last < blocks, capacity, last - blocks)
    return (filled + GROUP - 1) // GROUP


def serve_kernel(incoming_ref, table_ref, served_ref, rows_ref, *, capacity, blocks):
    def one_source(source, carry):
        def one_group(group, carry):
            first = pl.multiple_of(group * GROUP, GROUP)
            rows = [table_ref[incoming_ref[source, first + j]] for j in range(GROUP)]
            start = pl.multiple_of(source * capacity + first, GROUP)
            for j in range(GROUP):
                rows_ref[pl.ds(start + j, 1), :] = rows[j]
            return carry

        return lax.fori_loop(
            0, filled_groups(incoming_ref, source, capacity, blocks), one_group, carry
        )

    lax.fori_loop(0, incoming_ref.shape[0], one_source, 0)
    served_ref[...] = rows_ref[...].astype(jnp.bfloat16)


def match_kernel(incoming_ref, match_ref):
    lane = lax.broadcasted_iota(jnp.int32, (LANES, LANES), 1)
    row = lax.broadcasted_iota(jnp.int32, (LANES, LANES), 0)
    ones = jnp.ones((LANES, LANES), jnp.bfloat16)
    same_group = (lane // GROUP) == (row // GROUP)

    def one_row(i):
        wanted = incoming_ref[pl.ds(i, 1), :]
        high = jnp.where(lane == row, (wanted >> 7).astype(jnp.float32), 0.0).astype(jnp.bfloat16)
        low = jnp.where(lane == row, (wanted & 127).astype(jnp.float32), 0.0).astype(jnp.bfloat16)
        down = 128.0 * jnp.dot(high, ones, preferred_element_type=jnp.float32)
        down = down + jnp.dot(low, ones, preferred_element_type=jnp.float32)
        same = (down == wanted.astype(jnp.float32)) & same_group
        match_ref[pl.ds(pl.multiple_of(i * LANES, LANES), LANES), :] = jnp.where(
            same, 1.0, 0.0
        ).astype(jnp.bfloat16)

    def some_rows(i, carry):
        for j in range(4):
            one_row(4 * i + j)
        return carry

    lax.fori_loop(0, incoming_ref.shape[0] // 4, some_rows, 0)


def star_kernel(
    position_ref,
    returned_ref,
    observed_ref,
    inverse_ref,
    weights_hbm,
    extinction_ref,
    parcel_ref,
    weights_ref,
    returned_rows,
    fetched_ref,
    sens_ref,
    parcel_rows,
    sems,
):
    blocks_dev, slots, stars, width = weights_ref.shape
    chunks = sems.shape[0]
    per = blocks_dev // chunks
    half = position_ref.shape[0]
    fold = LANES // stars
    all_slots = parcel_rows.shape[0]
    lane = lax.broadcasted_iota(jnp.int32, (8, LANES), 1)
    row = lax.broadcasted_iota(jnp.int32, (8, LANES), 0)
    own_slot = [row == lane // stars + fold * h for h in range(8 // fold)]

    def load(chunk):
        span = pl.ds(chunk * per, per)
        return pltpu.make_async_copy(weights_hbm.at[span], weights_ref.at[span], sems.at[chunk])

    def place(block, slot):
        return position_ref[slot % half, (slot // half) * blocks_dev + block]

    def start_of(chunk):
        return pl.multiple_of(chunk * per * slots, per * slots)

    def eight_slots(chunk, b, j):
        return weights_ref[chunk * per + b, 8 * j : 8 * j + 8].reshape(8 * stars, width)

    def gather(chunk):
        rows = [returned_rows[place(chunk * per + b, k)] for b in range(per) for k in range(slots)]
        for i, value in enumerate(rows):
            fetched_ref[pl.ds(start_of(chunk) + i, 1), :] = value

    def extinctions(chunk):
        weighted = []
        for b in range(per):
            total = jnp.zeros((8, 8 * stars), jnp.float32)
            for j in range(slots // 8):
                eight = fetched_ref[pl.ds(start_of(chunk) + b * slots + 8 * j, 8), :]
                total = total + lax.dot_general(
                    eight.astype(jnp.bfloat16),
                    eight_slots(chunk, b, j),
                    CONTRACT_LANES,
                    preferred_element_type=jnp.float32,
                )
            folded = jnp.zeros((8, LANES), jnp.float32)
            for h, own in enumerate(own_slot):
                folded = folded + jnp.where(own, total[:, h * LANES : (h + 1) * LANES], 0.0)
            extinction = jnp.sum(folded, axis=0, keepdims=True)
            shift = stars
            while shift < LANES:
                extinction = extinction + pltpu.roll(extinction, shift, 1)
                shift *= 2
            here = pl.ds(chunk * per + b, 1)
            extinction_ref[here, :] = extinction
            weighted.append(inverse_ref[here, :] * (extinction - observed_ref[here, :]))
        return weighted

    def sensitivities(chunk, weighted):
        for b in range(per):
            left = jnp.concatenate(
                [jnp.where(own, weighted[b], 0.0) for own in own_slot], axis=1
            ).astype(jnp.bfloat16)
            for j in range(slots // 8):
                sens_ref[pl.ds(start_of(chunk) + b * slots + 8 * j, 8), :] = jnp.dot(
                    left, eight_slots(chunk, b, j), preferred_element_type=jnp.float32
                )

    def scatter(chunk):
        for b in range(per):
            for k in range(slots):
                at = pl.ds(start_of(chunk) + b * slots + k, 1)
                parcel_rows[place(chunk * per + b, k)] = sens_ref[at, :]

    for chunk in range(chunks):
        load(chunk).start()
    returned_rows.reshape(all_slots, width)[...] = returned_ref[...].astype(jnp.float32)
    parcel_rows.reshape(all_slots, width)[...] = jnp.zeros((all_slots, width), jnp.float32)
    gather(0)
    load(0).wait()
    weighted = extinctions(0)
    gather(1)
    load(1).wait()
    following = extinctions(1)
    sensitivities(0, weighted)
    gather(2)

    def step(chunk, weighted):
        load(chunk).wait()
        following = extinctions(chunk)
        sensitivities(chunk - 1, weighted)
        scatter(chunk - 2)
        gather(jnp.minimum(chunk + 1, chunks - 1))
        return following

    weighted = lax.fori_loop(2, chunks, step, following)
    sensitivities(chunks - 1, weighted)
    scatter(chunks - 2)
    scatter(chunks - 1)
    parcel_ref[...] = parcel_rows.reshape(all_slots, width)[...].astype(jnp.bfloat16)


def prior_kernel(field_ref, xlo_ref, xhi_ref, ylo_ref, yhi_ref, out_ref, exp_ref, padded, smooth):
    cells_x, cells_y, depth = field_ref.shape
    rows = padded.shape[1]
    gx, gy = lax.axis_index("gx"), lax.axis_index("gy")
    last_gx, last_gy = lax.axis_size("gx") - 1, lax.axis_size("gy") - 1
    z = lax.broadcasted_iota(jnp.int32, (rows, depth), 1)
    y = lax.broadcasted_iota(jnp.int32, (rows, depth), 0) - 8
    inside_y = ((y >= 0) | (gy > 0)) & ((y < cells_y) | (gy < last_gy))

    def operate(center, below, above):
        beside = below + above
        beside = beside + pltpu.roll(center, 1, 0) + pltpu.roll(center, rows - 1, 0)
        beside = beside + jnp.where(z == 0, 0.0, pltpu.roll(center, 1, 1))
        beside = beside + jnp.where(z == depth - 1, 0.0, pltpu.roll(center, depth - 1, 1))
        return (shift_kappa + 6.0) * center - beside

    def fill(plane, source):
        padded[plane, 8 : 8 + cells_y, :] = source
        padded[plane, 0:8, :] = jnp.zeros((8, depth), jnp.float32)
        padded[plane, 8 + cells_y :, :] = jnp.zeros((8, depth), jnp.float32)
        for h in range(2):
            padded[plane, 6 + h : 7 + h, :] = ylo_ref[h, pl.ds(plane, 1), :]
            padded[plane, 8 + cells_y + h : 9 + cells_y + h, :] = yhi_ref[h, pl.ds(plane, 1), :]

    for h in range(2):
        fill(h, xlo_ref[h])
        fill(cells_x + 2 + h, xhi_ref[h])

    def fill_own(x, carry):
        fill(x + 2, field_ref[x])
        return carry

    lax.fori_loop(0, cells_x, fill_own, 0)

    def smooth_plane(plane, carry):
        value = operate(padded[plane], padded[plane - 1], padded[plane + 1])
        inside = ((plane > 1) | (gx > 0)) & ((plane < cells_x + 2) | (gx < last_gx))
        smooth[plane - 1] = jnp.where(inside_y & inside, value, 0.0)
        return carry

    lax.fori_loop(1, cells_x + 3, smooth_plane, 0)

    def out_plane(x, carry):
        prior = operate(smooth[x + 1], smooth[x], smooth[x + 2])
        out_ref[x] = field_ref[x] - (step_rate * prior_weight) * prior[8 : 8 + cells_y]
        exp_ref[x] = jnp.exp(field_ref[x])
        return carry

    lax.fori_loop(0, cells_x, out_plane, 0)


def finish_kernel(
    incoming_ref,
    match_ref,
    arrived_ref,
    exp_hbm,
    base_hbm,
    out_hbm,
    rows_ref,
    exp_ref,
    out_ref,
    sems,
    *,
    capacity,
    blocks,
):
    own = pl.ds(0, blocks)
    loads = [
        pltpu.make_async_copy(exp_hbm, exp_ref.at[own], sems.at[0]),
        pltpu.make_async_copy(base_hbm, out_ref.at[own], sems.at[1]),
    ]
    for load in loads:
        load.start()
    for i in range(rows_ref.shape[0] // LANES):
        span = slice(i * LANES, (i + 1) * LANES)
        rows_ref[span, :] = -step_rate * jnp.dot(
            match_ref[span, :], arrived_ref[span, :], preferred_element_type=jnp.float32
        )
    for load in loads:
        load.wait()

    def one_source(source, carry):
        def one_group(group, carry):
            first = pl.multiple_of(group * GROUP, GROUP)
            places = [incoming_ref[source, first + j] for j in range(GROUP)]
            start = pl.multiple_of(source * capacity + first, GROUP)
            sums = [
                out_ref[places[j]] + exp_ref[places[j]] * rows_ref[pl.ds(start + j, 1), :]
                for j in range(GROUP)
            ]
            for j in range(GROUP):
                out_ref[places[j]] = sums[j]
            return carry

        return lax.fori_loop(
            0, filled_groups(incoming_ref, source, capacity, blocks), one_group, carry
        )

    lax.fori_loop(0, incoming_ref.shape[0], one_source, 0)
    store = pltpu.make_async_copy(out_ref.at[own], out_hbm, sems.at[2])
    store.start()
    store.wait()


def halo(xfirst, xlast, yfirst, ylast):
    def both_ways(first, last, axis):
        peers = lax.axis_size(axis)
        up = [(i, i + 1) for i in range(peers - 1)]
        down = [(j, i) for i, j in up]
        return lax.ppermute(last, axis, up), lax.ppermute(first, axis, down)

    xlo, xhi = both_ways(xfirst, xlast, "gx")

    def rows(own, at):
        return jnp.concatenate(
            [xlo[:, at].transpose(1, 0, 2), own, xhi[:, at].transpose(1, 0, 2)], axis=1
        )

    ylo, yhi = both_ways(rows(yfirst, slice(0, 2)), rows(ylast, slice(-2, None)), "gy")
    return xlo, xhi, ylo, yhi


VMEM = pl.BlockSpec(memory_space=pltpu.VMEM)
SMEM = pl.BlockSpec(memory_space=pltpu.SMEM)
ANY = pl.BlockSpec(memory_space=pl.ANY)


def on_device(log_density, weights, observed, inverse_var, star_counts, block_ids):
    cells_x, cells_y, depth = log_density.shape
    blocks_dev, slots, stars, width = weights.shape
    devices = lax.axis_size("gx") * lax.axis_size("gy")
    requests = blocks_dev * slots
    capacity = 2 * requests // devices
    all_slots = devices * capacity
    per_column = depth // width
    blocks = cells_x * cells_y * per_column
    cells = log_density.size
    mesh_axes = ("gx", "gy")
    f32, bf16, i32 = jnp.float32, jnp.bfloat16, jnp.int32
    shape = jax.ShapeDtypeStruct

    def to_rows(x):
        x = x.reshape(cells_x, cells_y // 8, 8, per_column, width)
        return x.transpose(0, 1, 3, 2, 4).reshape(blocks, 1, width)

    def to_field(rows):
        x = rows.reshape(cells_x, cells_y // 8, per_column, 8, width)
        return x.transpose(0, 1, 3, 2, 4).reshape(cells_x, cells_y, depth)

    def exchange(x):
        return lax.all_to_all(x, mesh_axes, split_axis=0, concat_axis=0, tiled=True)

    outgoing, position = pl.pallas_call(
        functools.partial(
            route_kernel,
            devices=devices,
            capacity=capacity,
            blocks=blocks,
            per_column=per_column,
        ),
        out_shape=[shape((devices, capacity), i32), shape((requests // LANES, LANES), i32)],
        in_specs=[VMEM],
        out_specs=[VMEM, VMEM],
        name="route",
    )(block_ids.T)
    incoming = exchange(outgoing)

    field, _ = lax.optimization_barrier((log_density, outgoing))
    table, xfirst, xlast, yfirst, ylast = pl.pallas_call(
        table_kernel,
        out_shape=[
            shape((blocks + capacity, 1, width), f32),
            shape((2, cells_y, depth), f32),
            shape((2, cells_y, depth), f32),
            shape((2, cells_x, depth), f32),
            shape((2, cells_x, depth), f32),
        ],
        in_specs=[VMEM],
        out_specs=[VMEM] * 5,
        compiler_params=pltpu.CompilerParams(vmem_limit_bytes=16 * MIB),
        cost_estimate=pl.CostEstimate(
            flops=8 * cells, bytes_accessed=8 * cells, transcendentals=cells
        ),
        name="table",
    )(field)

    served = pl.pallas_call(
        functools.partial(serve_kernel, capacity=capacity, blocks=blocks),
        out_shape=shape((all_slots, width), bf16),
        in_specs=[SMEM, VMEM],
        out_specs=VMEM,
        scratch_shapes=[pltpu.VMEM((all_slots, width), f32)],
        compiler_params=pltpu.CompilerParams(vmem_limit_bytes=16 * MIB),
        cost_estimate=pl.CostEstimate(flops=0, bytes_accessed=5 * MIB, transcendentals=0),
        name="serve",
    )(incoming, table)
    returned = exchange(served.reshape(devices, capacity, width)).reshape(all_slots, width)

    *edges, incoming_late, _ = lax.optimization_barrier(
        (xfirst, xlast, yfirst, ylast, incoming, served)
    )
    sides = halo(*edges)
    match = pl.pallas_call(
        match_kernel,
        out_shape=shape((all_slots, LANES), bf16),
        in_specs=[VMEM],
        out_specs=VMEM,
        compiler_params=pltpu.CompilerParams(vmem_limit_bytes=8 * MIB),
        cost_estimate=pl.CostEstimate(flops=10**9, bytes_accessed=MIB, transcendentals=0),
        name="match",
    )(incoming_late.reshape(all_slots // LANES, LANES))
    returned, match, *sides = lax.optimization_barrier((returned, match, *sides))

    chunks = blocks_dev * stars // LANES
    live = jnp.arange(stars)[None, :] < star_counts[:, None]
    live_inverse = jnp.where(live, inverse_var, 0.0)
    extinction, parcel = pl.pallas_call(
        star_kernel,
        out_shape=[shape((blocks_dev, LANES), f32), shape((all_slots, width), bf16)],
        in_specs=[SMEM, VMEM, VMEM, VMEM, ANY],
        out_specs=[VMEM, VMEM],
        scratch_shapes=[
            pltpu.VMEM(weights.shape, bf16),
            pltpu.VMEM((all_slots, 1, width), f32),
            pltpu.VMEM((requests, width), f32),
            pltpu.VMEM((requests, width), f32),
            pltpu.VMEM((all_slots, 1, width), f32),
            pltpu.SemaphoreType.DMA((chunks,)),
        ],
        compiler_params=pltpu.CompilerParams(vmem_limit_bytes=50 * MIB),
        cost_estimate=pl.CostEstimate(
            flops=4 * weights.size, bytes_accessed=2 * weights.size, transcendentals=0
        ),
        name="stars",
    )(
        position,
        returned,
        jnp.tile(observed, (1, LANES // stars)),
        jnp.tile(live_inverse, (1, LANES // stars)),
        weights,
    )
    arrived = exchange(parcel.reshape(devices, capacity, width)).reshape(all_slots, width)

    field_late, _ = lax.optimization_barrier((log_density, parcel))
    base, scale = pl.pallas_call(
        prior_kernel,
        out_shape=[shape((cells_x, cells_y, depth), f32)] * 2,
        in_specs=[VMEM] * 5,
        out_specs=[VMEM] * 2,
        scratch_shapes=[
            pltpu.VMEM((cells_x + 4, cells_y + 16, depth), f32),
            pltpu.VMEM((cells_x + 2, cells_y + 16, depth), f32),
        ],
        compiler_params=pltpu.CompilerParams(vmem_limit_bytes=32 * MIB),
        cost_estimate=pl.CostEstimate(
            flops=30 * cells, bytes_accessed=12 * cells, transcendentals=cells
        ),
        name="prior",
    )(field_late, *sides)

    new_rows = pl.pallas_call(
        functools.partial(finish_kernel, capacity=capacity, blocks=blocks),
        out_shape=shape((blocks, 1, width), f32),
        in_specs=[SMEM, VMEM, VMEM, ANY, ANY],
        out_specs=ANY,
        scratch_shapes=[
            pltpu.VMEM((all_slots, width), f32),
            pltpu.VMEM((blocks + capacity, 1, width), f32),
            pltpu.VMEM((blocks + capacity, 1, width), f32),
            pltpu.SemaphoreType.DMA((3,)),
        ],
        compiler_params=pltpu.CompilerParams(vmem_limit_bytes=50 * MIB),
        cost_estimate=pl.CostEstimate(
            flops=4 * cells, bytes_accessed=12 * cells, transcendentals=0
        ),
        name="finish",
    )(incoming, match, arrived, to_rows(scale), to_rows(base))
    return to_field(new_rows), extinction[:, :stars]


def solution(mesh):
    placed = (
        P("gx", "gy", None),
        P(("gx", "gy"), None, None, None),
        P(("gx", "gy"), None),
        P(("gx", "gy"), None),
        P(("gx", "gy")),
        P(("gx", "gy"), None),
    )
    return jax.shard_map(
        on_device,
        mesh=mesh,
        in_specs=placed,
        out_specs=(P("gx", "gy", None), P(("gx", "gy"), None)),
        check_vma=False,
    )
```

```python
import functools

import jax
import jax.numpy as jnp
from jax import lax
from jax.experimental import pallas as pl
from jax.experimental.pallas import tpu as pltpu
from jax.sharding import PartitionSpec as P

shift_kappa = 0.5
prior_weight = 0.05
step_rate = 2.0

LANES = 128
GROUP = 16
MIB = 1 << 20
MARK = 1 << 16

CONTRACT_LANES = (((1,), (1,)), ((), ()))


def split_by(value, size):
    if size & (size - 1) == 0:
        high = value >> (size.bit_length() - 1)
        return high, value & (size - 1)
    high = value // size
    return high, value - high * size


def route_kernel(
    ids_ref, outgoing_ref, position_ref, *, devices, capacity, first_slots, blocks, per_column
):
    half = ids_ref.shape[0] // 2
    ids = jnp.concatenate([ids_ref[:half, :], ids_ref[half:, :]], axis=1)
    lane = lax.broadcasted_iota(jnp.int32, (LANES, LANES), 1)
    row = lax.broadcasted_iota(jnp.int32, (LANES, LANES), 0)
    upper = jnp.where(row <= lane, 1.0, 0.0).astype(jnp.bfloat16)
    tile_no = lax.broadcasted_iota(jnp.int32, (devices, LANES), 0)
    slot_no = lax.broadcasted_iota(jnp.int32, (capacity, LANES), 0)
    before = jnp.zeros((devices, 1), jnp.float32)
    lists = jnp.zeros((2 * devices, capacity), jnp.float32)
    for chunk in range(half):
        target, local = split_by(ids[chunk : chunk + 1, :], blocks)
        column, part = split_by(local, per_column)
        local = ((column >> 3) * per_column + part) * 8 + (column & 7)
        hit = tile_no == target
        onehot = jnp.where(hit, 1.0, 0.0)
        upto = before + jnp.dot(
            onehot.astype(jnp.bfloat16), upper, preferred_element_type=jnp.float32
        )
        before = upto[:, LANES - 1 :]
        rank = jnp.sum(onehot * upto, axis=0, keepdims=True).astype(jnp.int32) - 1
        in_slot = jnp.where(slot_no == rank, 1.0, 0.0).astype(jnp.bfloat16)
        high = ((local >> 7) + 1).astype(jnp.float32)
        low = (local & 127).astype(jnp.float32)
        digits = jnp.concatenate([jnp.where(hit, high, 0.0), jnp.where(hit, low, 0.0)], axis=0)
        lists = lists + lax.dot_general(
            digits.astype(jnp.bfloat16),
            in_slot,
            CONTRACT_LANES,
            preferred_element_type=jnp.float32,
        )
        last_slots = capacity - first_slots
        position_ref[chunk : chunk + 1, :] = jnp.where(
            rank < first_slots,
            target * first_slots + rank,
            devices * first_slots + target * last_slots + rank - first_slots,
        )
    high, low = lists[:devices], lists[devices:]
    wanted = ((high - 1.0) * 128.0 + low).astype(jnp.int32)
    filled = before.astype(jnp.int32)
    me = lax.axis_index("gx") * lax.axis_size("gy") + lax.axis_index("gy")
    fullest = jnp.max(jnp.where(tile_no[:, :1] == me, 0.0, before), axis=0, keepdims=True)
    listed = jnp.where(high > 0.5, wanted, blocks + filled)
    if first_slots < capacity:
        slot = lax.broadcasted_iota(jnp.int32, (devices, capacity), 1)
        mark = fullest.astype(jnp.int32) * MARK
        listed = listed + jnp.where(slot == capacity - 1, mark, 0)
    outgoing_ref[...] = listed


def edges_kernel(field_ref, xfirst_ref, xlast_ref, yfirst_ref, ylast_ref):
    cells_x, cells_y, _ = field_ref.shape
    xfirst_ref[...] = field_ref[:2]
    xlast_ref[...] = field_ref[cells_x - 2 :]
    for h in range(2):
        for x in range(cells_x):
            yfirst_ref[h, x : x + 1, :] = field_ref[x, h : h + 1, :]
            ylast_ref[h, x : x + 1, :] = field_ref[x, cells_y - 2 + h : cells_y - 1 + h, :]


def for_each_group(incoming_ref, visit, capacity, first_slots, blocks):
    sources = incoming_ref.shape[0]
    last_slots = capacity - first_slots
    together = 4

    def groups_of(source):
        last = incoming_ref[source, capacity - 1] & (MARK - 1)
        return (jnp.where(last < blocks, capacity, last - blocks) + GROUP - 1) // GROUP

    def some_sources(quad, carry):
        own = [quad * together + i for i in range(together)]
        most = functools.reduce(jnp.maximum, [groups_of(source) for source in own])

        def one_group(group, carry):
            slot = pl.multiple_of(group * GROUP, GROUP)
            for source in own:
                wanted = [incoming_ref[source, slot + j] for j in range(GROUP)]
                visit(wanted, pl.multiple_of(source * first_slots + slot, GROUP))
            return carry

        return lax.fori_loop(0, jnp.minimum(most, first_slots // GROUP), one_group, carry)

    lax.fori_loop(0, sources // together, some_sources, 0)
    if last_slots == 0:
        return

    def one_source(source, carry):
        def one_group(group, carry):
            slot = pl.multiple_of(group * GROUP, GROUP)
            row = (sources - 1) * first_slots + source * last_slots + slot
            wanted = [incoming_ref[source, slot + j] & (MARK - 1) for j in range(GROUP)]
            visit(wanted, pl.multiple_of(row, GROUP))
            return carry

        return lax.fori_loop(first_slots // GROUP, groups_of(source), one_group, carry)

    lax.fori_loop(0, sources, one_source, 0)


def serve_kernel(incoming_ref, field_ref, *refs, capacity, first_slots):
    *served_refs, table_ref, rows_ref = refs
    cells_x, cells_y, depth = field_ref.shape
    per_column = depth // LANES
    table_rows = table_ref.reshape(table_ref.shape[0], LANES)
    blocks = cells_x * cells_y * per_column
    table_rows[blocks:, :] = jnp.zeros((table_ref.shape[0] - blocks, LANES), jnp.float32)

    def one_plane(x, carry):
        for yb in range(cells_y // 8):
            for part in range(per_column):
                at = pl.multiple_of(((x * (cells_y // 8) + yb) * per_column + part) * 8, 8)
                table_rows[pl.ds(at, 8), :] = jnp.exp(
                    field_ref[x, 8 * yb : 8 * yb + 8, part * LANES : (part + 1) * LANES]
                )
        return carry

    lax.fori_loop(0, cells_x, one_plane, 0)

    def visit(wanted, row):
        rows = [table_ref[at] for at in wanted]
        for j in range(GROUP):
            rows_ref[pl.ds(row + j, 1), :] = rows[j]

    for_each_group(incoming_ref, visit, capacity, first_slots, blocks)
    start = 0
    for served_ref in served_refs:
        size = served_ref.shape[0]
        served_ref[...] = rows_ref[start : start + size, :].astype(jnp.bfloat16)
        start += size


def match_kernel(incoming_ref, match_ref):
    lane = lax.broadcasted_iota(jnp.int32, (LANES, LANES), 1)
    row = lax.broadcasted_iota(jnp.int32, (LANES, LANES), 0)
    ones = jnp.ones((LANES, LANES), jnp.bfloat16)
    same_group = (lane // GROUP) == (row // GROUP)

    def one_row(i):
        wanted = incoming_ref[pl.ds(i, 1), :]
        high = jnp.where(lane == row, (wanted >> 7).astype(jnp.float32), 0.0).astype(jnp.bfloat16)
        low = jnp.where(lane == row, (wanted & 127).astype(jnp.float32), 0.0).astype(jnp.bfloat16)
        down = 128.0 * jnp.dot(high, ones, preferred_element_type=jnp.float32)
        down = down + jnp.dot(low, ones, preferred_element_type=jnp.float32)
        same = (down == wanted.astype(jnp.float32)) & same_group
        match_ref[pl.ds(pl.multiple_of(i * LANES, LANES), LANES), :] = jnp.where(
            same, 1.0, 0.0
        ).astype(jnp.bfloat16)

    def some_rows(i, carry):
        for j in range(4):
            one_row(4 * i + j)
        return carry

    lax.fori_loop(0, incoming_ref.shape[0] // 4, some_rows, 0)


def star_kernel(position_ref, observed_ref, inverse_ref, weights_hbm, *refs, exchanges):
    returned_refs, refs = refs[:exchanges], refs[exchanges:]
    extinction_ref, refs = refs[0], refs[1:]
    parcel_refs, refs = refs[:exchanges], refs[exchanges:]
    weights_ref, returned_rows, fetched_ref, sens_ref, parcel_rows, sems = refs
    blocks_dev, slots, stars, width = weights_ref.shape
    chunks = sems.shape[0]
    per = blocks_dev // chunks
    half = position_ref.shape[0]
    fold = LANES // stars
    all_slots = parcel_rows.shape[0]
    lane = lax.broadcasted_iota(jnp.int32, (8, LANES), 1)
    row = lax.broadcasted_iota(jnp.int32, (8, LANES), 0)
    own_slot = [row == lane // stars + fold * h for h in range(8 // fold)]

    def load(chunk):
        span = pl.ds(chunk * per, per)
        return pltpu.make_async_copy(weights_hbm.at[span], weights_ref.at[span], sems.at[chunk])

    def place(block, slot):
        return position_ref[slot % half, (slot // half) * blocks_dev + block]

    def start_of(chunk):
        return pl.multiple_of(chunk * per * slots, per * slots)

    def matrix_of(chunk, b):
        eights = [weights_ref[chunk * per + b, 8 * j : 8 * j + 8] for j in range(slots // 8)]
        return jnp.concatenate([x.reshape(8 * stars, width) for x in eights], axis=1)

    def gather(chunk):
        rows = [returned_rows[place(chunk * per + b, k)] for b in range(per) for k in range(slots)]
        for i, value in enumerate(rows):
            fetched_ref[pl.ds(start_of(chunk) + i, 1), :] = value

    def extinctions(chunk):
        weighted = []
        for b in range(per):
            left = jnp.concatenate(
                [
                    fetched_ref[pl.ds(start_of(chunk) + b * slots + 8 * j, 8), :]
                    for j in range(slots // 8)
                ],
                axis=1,
            )
            total = lax.dot_general(
                left.astype(jnp.bfloat16),
                matrix_of(chunk, b),
                CONTRACT_LANES,
                preferred_element_type=jnp.float32,
            )
            folded = jnp.zeros((8, LANES), jnp.float32)
            for h, own in enumerate(own_slot):
                folded = folded + jnp.where(own, total[:, h * LANES : (h + 1) * LANES], 0.0)
            extinction = jnp.sum(folded, axis=0, keepdims=True)
            shift = stars
            while shift < LANES:
                extinction = extinction + pltpu.roll(extinction, shift, 1)
                shift *= 2
            here = pl.ds(chunk * per + b, 1)
            extinction_ref[here, :] = extinction
            weighted.append(inverse_ref[here, :] * (extinction - observed_ref[here, :]))
        return weighted

    def sensitivities(chunk, weighted):
        for b in range(per):
            left = jnp.concatenate(
                [jnp.where(own, weighted[b], 0.0) for own in own_slot], axis=1
            ).astype(jnp.bfloat16)
            sens = jnp.dot(left, matrix_of(chunk, b), preferred_element_type=jnp.float32)
            for j in range(slots // 8):
                sens_ref[pl.ds(start_of(chunk) + b * slots + 8 * j, 8), :] = sens[
                    :, j * width : (j + 1) * width
                ]

    def scatter(chunk):
        for b in range(per):
            for k in range(slots):
                at = pl.ds(start_of(chunk) + b * slots + k, 1)
                parcel_rows[place(chunk * per + b, k)] = sens_ref[at, :]

    for chunk in range(chunks):
        load(chunk).start()
    start = 0
    for returned_ref in returned_refs:
        span = slice(start, start + returned_ref.shape[0])
        returned_rows.reshape(all_slots, width)[span, :] = returned_ref[...].astype(jnp.float32)
        start = span.stop
    parcel_rows.reshape(all_slots, width)[...] = jnp.zeros((all_slots, width), jnp.float32)
    gather(0)
    load(0).wait()
    weighted = extinctions(0)
    gather(1)
    load(1).wait()
    following = extinctions(1)
    sensitivities(0, weighted)
    gather(2)

    def step(chunk, weighted):
        load(chunk).wait()
        following = extinctions(chunk)
        sensitivities(chunk - 1, weighted)
        scatter(chunk - 2)
        gather(jnp.minimum(chunk + 1, chunks - 1))
        return following

    weighted = lax.fori_loop(2, chunks, step, following)
    sensitivities(chunks - 1, weighted)
    scatter(chunks - 2)
    scatter(chunks - 1)
    start = 0
    for parcel_ref in parcel_refs:
        span = slice(start, start + parcel_ref.shape[0])
        parcel_ref[...] = parcel_rows.reshape(all_slots, width)[span, :].astype(jnp.bfloat16)
        start = span.stop


def prior_kernel(field_ref, xlo_ref, xhi_ref, ylo_ref, yhi_ref, out_ref, padded, smooth):
    cells_x, cells_y, depth = field_ref.shape
    rows = padded.shape[1]
    gx, gy = lax.axis_index("gx"), lax.axis_index("gy")
    last_gx, last_gy = lax.axis_size("gx") - 1, lax.axis_size("gy") - 1
    z = lax.broadcasted_iota(jnp.int32, (rows, depth), 1)
    y = lax.broadcasted_iota(jnp.int32, (rows, depth), 0) - 8
    inside_y = ((y >= 0) | (gy > 0)) & ((y < cells_y) | (gy < last_gy))

    def operate(center, below, above):
        beside = below + above
        beside = beside + pltpu.roll(center, 1, 0) + pltpu.roll(center, rows - 1, 0)
        beside = beside + jnp.where(z == 0, 0.0, pltpu.roll(center, 1, 1))
        beside = beside + jnp.where(z == depth - 1, 0.0, pltpu.roll(center, depth - 1, 1))
        return (shift_kappa + 6.0) * center - beside

    def fill(plane, source):
        padded[plane, 8 : 8 + cells_y, :] = source
        padded[plane, 0:8, :] = jnp.zeros((8, depth), jnp.float32)
        padded[plane, 8 + cells_y :, :] = jnp.zeros((8, depth), jnp.float32)
        for h in range(2):
            padded[plane, 6 + h : 7 + h, :] = ylo_ref[h, pl.ds(plane, 1), :]
            padded[plane, 8 + cells_y + h : 9 + cells_y + h, :] = yhi_ref[h, pl.ds(plane, 1), :]

    for h in range(2):
        fill(h, xlo_ref[h])
        fill(cells_x + 2 + h, xhi_ref[h])

    def fill_own(x, carry):
        fill(x + 2, field_ref[x])
        return carry

    lax.fori_loop(0, cells_x, fill_own, 0)

    def smooth_plane(plane, carry):
        value = operate(padded[plane], padded[plane - 1], padded[plane + 1])
        inside = ((plane > 1) | (gx > 0)) & ((plane < cells_x + 2) | (gx < last_gx))
        smooth[plane - 1] = jnp.where(inside_y & inside, value, 0.0)
        return carry

    lax.fori_loop(1, cells_x + 3, smooth_plane, 0)

    def out_plane(x, carry):
        prior = operate(smooth[x + 1], smooth[x], smooth[x + 2])
        out_ref[x] = field_ref[x] - (step_rate * prior_weight) * prior[8 : 8 + cells_y]
        return carry

    lax.fori_loop(0, cells_x, out_plane, 0)


def finish_kernel(
    incoming_ref, match_ref, field_hbm, base_hbm, *refs, exchanges, capacity, first_slots
):
    arrived_refs, refs = refs[:exchanges], refs[exchanges:]
    out_hbm, collected, rows_ref, field_ref, base_ref, out_ref, in_sems, out_sems = refs
    cells_x, cells_y, depth = field_ref.shape
    per_column = depth // LANES
    parts = out_sems.shape[0]
    planes = cells_x // parts
    blocks = cells_x * cells_y * per_column
    loads = [
        pltpu.make_async_copy(field_hbm, field_ref, in_sems.at[0]),
        pltpu.make_async_copy(base_hbm, base_ref, in_sems.at[1]),
    ]
    for load in loads:
        load.start()
    collected_rows = collected.reshape(collected.shape[0], LANES)
    start = 0
    for arrived_ref in arrived_refs:
        for i in range(arrived_ref.shape[0] // LANES):
            span = slice(start + i * LANES, start + (i + 1) * LANES)
            rows_ref[span, :] = -step_rate * jnp.dot(
                match_ref[span, :],
                arrived_ref[i * LANES : (i + 1) * LANES, :],
                preferred_element_type=jnp.float32,
            )
        start += arrived_ref.shape[0]
    collected_rows[...] = jnp.zeros_like(collected_rows)

    def visit(wanted, row):
        sums = [collected[wanted[j]] + rows_ref[pl.ds(row + j, 1), :] for j in range(GROUP)]
        for j in range(GROUP):
            collected[wanted[j]] = sums[j]

    for_each_group(incoming_ref, visit, capacity, first_slots, blocks)
    for load in loads:
        load.wait()

    def store(part):
        span = pl.ds(part * planes, planes)
        return pltpu.make_async_copy(out_ref.at[span], out_hbm.at[span], out_sems.at[part])

    def one_plane(x, carry):
        for yb in range(cells_y // 8):
            for part in range(per_column):
                at = pl.multiple_of(((x * (cells_y // 8) + yb) * per_column + part) * 8, 8)
                here = (x, slice(8 * yb, 8 * yb + 8), slice(part * LANES, (part + 1) * LANES))
                out_ref[here] = base_ref[here] + collected_rows[pl.ds(at, 8), :] * jnp.exp(
                    field_ref[here]
                )
        return carry

    for part in range(parts):
        lax.fori_loop(part * planes, (part + 1) * planes, one_plane, 0)
        store(part).start()
    for part in range(parts):
        store(part).wait()


def both_ways(first, last, axis):
    peers = lax.axis_size(axis)
    up = [(i, i + 1) for i in range(peers - 1)]
    down = [(j, i) for i, j in up]
    return lax.ppermute(last, axis, up), lax.ppermute(first, axis, down)


def halo_y(xlo, xhi, yfirst, ylast):
    def rows(own, at):
        return jnp.concatenate(
            [xlo[:, at].transpose(1, 0, 2), own, xhi[:, at].transpose(1, 0, 2)], axis=1
        )

    return both_ways(rows(yfirst, slice(0, 2)), rows(ylast, slice(-2, None)), "gy")


VMEM = pl.BlockSpec(memory_space=pltpu.VMEM)
SMEM = pl.BlockSpec(memory_space=pltpu.SMEM)
ANY = pl.BlockSpec(memory_space=pl.ANY)


def on_device(log_density, weights, observed, inverse_var, star_counts, block_ids):
    cells_x, cells_y, depth = log_density.shape
    blocks_dev, slots, stars, width = weights.shape
    devices = lax.axis_size("gx") * lax.axis_size("gy")
    requests = blocks_dev * slots
    capacity = 2 * requests // devices
    first_slots = min(capacity, -(-3 * capacity // (4 * GROUP)) * GROUP)
    slots_of = [n for n in (first_slots, capacity - first_slots) if n > 0]
    exchanges = len(slots_of)
    all_slots = devices * capacity
    per_column = depth // width
    blocks = cells_x * cells_y * per_column
    cells = log_density.size
    field_shape = (cells_x, cells_y, depth)
    mesh_axes = ("gx", "gy")
    f32, bf16, i32 = jnp.float32, jnp.bfloat16, jnp.int32
    shape = jax.ShapeDtypeStruct

    def exchange(x):
        return lax.all_to_all(x, mesh_axes, split_axis=0, concat_axis=0, tiled=True)

    def exchange_rows(parts, crowded):
        moved = [parts[0].reshape(devices, first_slots, width)]
        moved[0] = exchange(moved[0])
        for part in parts[1:]:
            part = part.reshape(devices, capacity - first_slots, width)
            moved.append(lax.cond(crowded, exchange, lambda x: x, part))
        return [x.reshape(-1, width) for x in moved]

    outgoing, position = pl.pallas_call(
        functools.partial(
            route_kernel,
            devices=devices,
            capacity=capacity,
            first_slots=first_slots,
            blocks=blocks,
            per_column=per_column,
        ),
        out_shape=[shape((devices, capacity), i32), shape((requests // LANES, LANES), i32)],
        in_specs=[VMEM],
        out_specs=[VMEM, VMEM],
        name="route",
    )(block_ids.T)
    incoming = exchange(outgoing)

    field, _ = lax.optimization_barrier((log_density, outgoing))
    xfirst, xlast, yfirst, ylast = pl.pallas_call(
        edges_kernel,
        out_shape=[
            shape((2, cells_y, depth), f32),
            shape((2, cells_y, depth), f32),
            shape((2, cells_x, depth), f32),
            shape((2, cells_x, depth), f32),
        ],
        in_specs=[VMEM],
        out_specs=[VMEM] * 4,
        compiler_params=pltpu.CompilerParams(vmem_limit_bytes=8 * MIB),
        cost_estimate=pl.CostEstimate(flops=0, bytes_accessed=2 * MIB, transcendentals=0),
        name="edges",
    )(field)
    xlo, xhi = both_ways(xfirst, xlast, "gx")

    served = pl.pallas_call(
        functools.partial(serve_kernel, capacity=capacity, first_slots=first_slots),
        out_shape=[shape((devices * n, width), bf16) for n in slots_of],
        in_specs=[SMEM, VMEM],
        out_specs=[VMEM] * exchanges,
        scratch_shapes=[
            pltpu.VMEM((blocks + capacity, 1, width), f32),
            pltpu.VMEM((all_slots, width), f32),
        ],
        compiler_params=pltpu.CompilerParams(vmem_limit_bytes=24 * MIB),
        cost_estimate=pl.CostEstimate(
            flops=cells, bytes_accessed=6 * MIB, transcendentals=cells
        ),
        name="serve",
    )(incoming, field)
    crowded = jnp.max(incoming[:, capacity - 1]) >= (first_slots + 1) * MARK
    returned = exchange_rows(served, crowded)

    incoming_late, xlo, xhi, yfirst, ylast, _ = lax.optimization_barrier(
        (incoming, xlo, xhi, yfirst, ylast, served[0])
    )
    sides = halo_y(xlo, xhi, yfirst, ylast)
    slot_lists = [
        incoming_late[:, :first_slots].reshape(-1, LANES),
        (incoming_late[:, first_slots:] & (MARK - 1)).reshape(-1, LANES),
    ][:exchanges]
    match = pl.pallas_call(
        match_kernel,
        out_shape=shape((all_slots, LANES), bf16),
        in_specs=[VMEM],
        out_specs=VMEM,
        compiler_params=pltpu.CompilerParams(vmem_limit_bytes=8 * MIB),
        cost_estimate=pl.CostEstimate(flops=10**9, bytes_accessed=MIB, transcendentals=0),
        name="match",
    )(jnp.concatenate(slot_lists, axis=0))
    *returned, match, xlo, xhi, ylo, yhi = lax.optimization_barrier(
        (*returned, match, xlo, xhi, *sides)
    )

    chunks = blocks_dev * stars // LANES
    live = jnp.arange(stars)[None, :] < star_counts[:, None]
    live_inverse = jnp.where(live, inverse_var, 0.0)
    extinction, *parcel = pl.pallas_call(
        functools.partial(star_kernel, exchanges=exchanges),
        out_shape=[shape((blocks_dev, LANES), f32)]
        + [shape((devices * n, width), bf16) for n in slots_of],
        in_specs=[SMEM, VMEM, VMEM, ANY] + [VMEM] * exchanges,
        out_specs=[VMEM] * (1 + exchanges),
        scratch_shapes=[
            pltpu.VMEM(weights.shape, bf16),
            pltpu.VMEM((all_slots, 1, width), f32),
            pltpu.VMEM((requests, width), f32),
            pltpu.VMEM((requests, width), f32),
            pltpu.VMEM((all_slots, 1, width), f32),
            pltpu.SemaphoreType.DMA((chunks,)),
        ],
        compiler_params=pltpu.CompilerParams(vmem_limit_bytes=50 * MIB),
        cost_estimate=pl.CostEstimate(
            flops=4 * weights.size, bytes_accessed=2 * weights.size, transcendentals=0
        ),
        name="stars",
    )(
        position,
        jnp.tile(observed, (1, LANES // stars)),
        jnp.tile(live_inverse, (1, LANES // stars)),
        weights,
        *returned,
    )
    arrived = exchange_rows(parcel, crowded)

    field_late, _ = lax.optimization_barrier((log_density, parcel[0]))
    base = pl.pallas_call(
        prior_kernel,
        out_shape=shape(field_shape, f32),
        in_specs=[VMEM] * 5,
        out_specs=VMEM,
        scratch_shapes=[
            pltpu.VMEM((cells_x + 4, cells_y + 16, depth), f32),
            pltpu.VMEM((cells_x + 2, cells_y + 16, depth), f32),
        ],
        compiler_params=pltpu.CompilerParams(vmem_limit_bytes=32 * MIB),
        cost_estimate=pl.CostEstimate(
            flops=30 * cells, bytes_accessed=8 * cells, transcendentals=0
        ),
        name="prior",
    )(field_late, xlo, xhi, ylo, yhi)

    parts = 8
    new_log_density = pl.pallas_call(
        functools.partial(
            finish_kernel, exchanges=exchanges, capacity=capacity, first_slots=first_slots
        ),
        out_shape=shape(field_shape, f32),
        in_specs=[SMEM, VMEM, ANY, ANY] + [VMEM] * exchanges,
        out_specs=ANY,
        scratch_shapes=[
            pltpu.VMEM((blocks + capacity, 1, width), f32),
            pltpu.VMEM((all_slots, width), f32),
            pltpu.VMEM(field_shape, f32),
            pltpu.VMEM(field_shape, f32),
            pltpu.VMEM(field_shape, f32),
            pltpu.SemaphoreType.DMA((2,)),
            pltpu.SemaphoreType.DMA((parts,)),
        ],
        compiler_params=pltpu.CompilerParams(vmem_limit_bytes=50 * MIB),
        cost_estimate=pl.CostEstimate(
            flops=4 * cells, bytes_accessed=12 * cells, transcendentals=cells
        ),
        name="finish",
    )(incoming, match, log_density, base, *arrived)
    return new_log_density, extinction[:, :stars]


def solution(mesh):
    placed = (
        P("gx", "gy", None),
        P(("gx", "gy"), None, None, None),
        P(("gx", "gy"), None),
        P(("gx", "gy"), None),
        P(("gx", "gy")),
        P(("gx", "gy"), None),
    )
    return jax.shard_map(
        on_device,
        mesh=mesh,
        in_specs=placed,
        out_specs=(P("gx", "gy", None), P(("gx", "gy"), None)),
        check_vma=False,
    )
```

```python
import functools

import jax
import jax.numpy as jnp
from jax import lax
from jax.experimental import pallas as pl
from jax.experimental.pallas import tpu as pltpu
from jax.sharding import PartitionSpec as P

shift_kappa = 0.5
prior_weight = 0.05
step_rate = 2.0

LANES = 128
GROUP = 16
MIB = 1 << 20
MARK = 1 << 16

CONTRACT_LANES = (((1,), (1,)), ((), ()))


def split_by(value, size):
    if size & (size - 1) == 0:
        high = value >> (size.bit_length() - 1)
        return high, value & (size - 1)
    high = value // size
    return high, value - high * size


def route_kernel(
    ids_ref, outgoing_ref, position_ref, *, devices, capacity, first_slots, blocks, per_column
):
    half = ids_ref.shape[0] // 2
    ids = jnp.concatenate([ids_ref[:half, :], ids_ref[half:, :]], axis=1)
    lane = lax.broadcasted_iota(jnp.int32, (LANES, LANES), 1)
    row = lax.broadcasted_iota(jnp.int32, (LANES, LANES), 0)
    upper = jnp.where(row <= lane, 1.0, 0.0).astype(jnp.bfloat16)
    tile_no = lax.broadcasted_iota(jnp.int32, (devices, LANES), 0)
    slot_no = lax.broadcasted_iota(jnp.int32, (capacity, LANES), 0)
    before = jnp.zeros((devices, 1), jnp.float32)
    lists = jnp.zeros((2 * devices, capacity), jnp.float32)
    for chunk in range(half):
        target, local = split_by(ids[chunk : chunk + 1, :], blocks)
        column, part = split_by(local, per_column)
        local = ((column >> 3) * per_column + part) * 8 + (column & 7)
        hit = tile_no == target
        onehot = jnp.where(hit, 1.0, 0.0)
        upto = before + jnp.dot(
            onehot.astype(jnp.bfloat16), upper, preferred_element_type=jnp.float32
        )
        before = upto[:, LANES - 1 :]
        rank = jnp.sum(onehot * upto, axis=0, keepdims=True).astype(jnp.int32) - 1
        in_slot = jnp.where(slot_no == rank, 1.0, 0.0).astype(jnp.bfloat16)
        high = ((local >> 7) + 1).astype(jnp.float32)
        low = (local & 127).astype(jnp.float32)
        digits = jnp.concatenate([jnp.where(hit, high, 0.0), jnp.where(hit, low, 0.0)], axis=0)
        lists = lists + lax.dot_general(
            digits.astype(jnp.bfloat16),
            in_slot,
            CONTRACT_LANES,
            preferred_element_type=jnp.float32,
        )
        last_slots = capacity - first_slots
        position = jnp.where(
            rank < first_slots,
            target * first_slots + rank,
            devices * first_slots + target * last_slots + rank - first_slots,
        )
        position_ref[chunk : chunk + 1, :] = position + MARK * pltpu.roll(position, LANES // 2, 1)
    high, low = lists[:devices], lists[devices:]
    wanted = ((high - 1.0) * 128.0 + low).astype(jnp.int32)
    filled = before.astype(jnp.int32)
    me = lax.axis_index("gx") * lax.axis_size("gy") + lax.axis_index("gy")
    fullest = jnp.max(jnp.where(tile_no[:, :1] == me, 0.0, before), axis=0, keepdims=True)
    listed = jnp.where(high > 0.5, wanted, blocks + filled)
    if first_slots < capacity:
        slot = lax.broadcasted_iota(jnp.int32, (devices, capacity), 1)
        mark = fullest.astype(jnp.int32) * MARK
        listed = listed + jnp.where(slot == capacity - 1, mark, 0)
    outgoing_ref[...] = listed


def edges_kernel(field_ref, xfirst_ref, xlast_ref, yfirst_ref, ylast_ref):
    cells_x, cells_y, _ = field_ref.shape
    xfirst_ref[...] = field_ref[:2]
    xlast_ref[...] = field_ref[cells_x - 2 :]
    for h in range(2):
        for x in range(cells_x):
            yfirst_ref[h, x : x + 1, :] = field_ref[x, h : h + 1, :]
            ylast_ref[h, x : x + 1, :] = field_ref[x, cells_y - 2 + h : cells_y - 1 + h, :]


def for_each_group(incoming_ref, visit, capacity, first_slots, blocks):
    sources = incoming_ref.shape[0] // capacity
    last_slots = capacity - first_slots
    together = 4

    def groups_of(source):
        last = incoming_ref[source * capacity + capacity - 1] & (MARK - 1)
        return (jnp.where(last < blocks, capacity, last - blocks) + GROUP - 1) // GROUP

    def some_sources(quad, carry):
        own = [quad * together + i for i in range(together)]
        most = functools.reduce(jnp.maximum, [groups_of(source) for source in own])

        def one_group(group, carry):
            slot = group * GROUP
            for source in own:
                wanted = [incoming_ref[source * capacity + slot + j] for j in range(GROUP)]
                visit(wanted, pl.multiple_of(source * first_slots + slot, GROUP), 0)
            return carry

        return lax.fori_loop(0, jnp.minimum(most, first_slots // GROUP), one_group, carry)

    lax.fori_loop(0, sources // together, some_sources, 0)
    if last_slots == 0:
        return

    def one_source(source, carry):
        def one_group(group, carry):
            slot = group * GROUP
            wanted = [
                incoming_ref[source * capacity + slot + j] & (MARK - 1) for j in range(GROUP)
            ]
            visit(wanted, pl.multiple_of(source * last_slots + slot - first_slots, GROUP), 1)
            return carry

        return lax.fori_loop(first_slots // GROUP, groups_of(source), one_group, carry)

    lax.fori_loop(0, sources, one_source, 0)


def serve_kernel(incoming_ref, field_ref, *refs, capacity, first_slots):
    *served_refs, table_ref = refs
    cells_x, cells_y, depth = field_ref.shape
    per_column = depth // LANES
    table_rows = table_ref.reshape(table_ref.shape[0], LANES)
    blocks = cells_x * cells_y * per_column
    table_rows[blocks:, :] = jnp.zeros((table_ref.shape[0] - blocks, LANES), jnp.float32)

    def one_plane(x, carry):
        for yb in range(cells_y // 8):
            for part in range(per_column):
                at = pl.multiple_of(((x * (cells_y // 8) + yb) * per_column + part) * 8, 8)
                table_rows[pl.ds(at, 8), :] = jnp.exp(
                    field_ref[x, 8 * yb : 8 * yb + 8, part * LANES : (part + 1) * LANES]
                )
        return carry

    lax.fori_loop(0, cells_x, one_plane, 0)

    def visit(wanted, row, list_part):
        rows = jnp.concatenate([table_ref[at] for at in wanted], axis=0)
        served_refs[list_part][pl.ds(row, GROUP), :] = rows.astype(jnp.bfloat16)

    for_each_group(incoming_ref, visit, capacity, first_slots, blocks)


def match_kernel(incoming_ref, match_ref):
    lane = lax.broadcasted_iota(jnp.int32, (LANES, LANES), 1)
    row = lax.broadcasted_iota(jnp.int32, (LANES, LANES), 0)
    ones = jnp.ones((LANES, LANES), jnp.bfloat16)
    same_group = (lane // GROUP) == (row // GROUP)

    def one_row(i):
        wanted = incoming_ref[pl.ds(i, 1), :]
        high = jnp.where(lane == row, (wanted >> 7).astype(jnp.float32), 0.0).astype(jnp.bfloat16)
        low = jnp.where(lane == row, (wanted & 127).astype(jnp.float32), 0.0).astype(jnp.bfloat16)
        down = 128.0 * jnp.dot(high, ones, preferred_element_type=jnp.float32)
        down = down + jnp.dot(low, ones, preferred_element_type=jnp.float32)
        same = (down == wanted.astype(jnp.float32)) & same_group
        match_ref[pl.ds(pl.multiple_of(i * LANES, LANES), LANES), :] = jnp.where(
            same, 1.0, 0.0
        ).astype(jnp.bfloat16)

    def some_rows(i, carry):
        for j in range(4):
            one_row(4 * i + j)
        return carry

    lax.fori_loop(0, incoming_ref.shape[0] // 4, some_rows, 0)


def star_kernel(position_ref, observed_ref, inverse_ref, weights_hbm, *refs, exchanges):
    returned_refs, refs = refs[:exchanges], refs[exchanges:]
    extinction_ref, refs = refs[0], refs[1:]
    parcel_refs, refs = refs[:exchanges], refs[exchanges:]
    weights_ref, returned_rows, fetched_ref, sens_ref, parcel_rows, sems = refs
    blocks_dev, slots, stars, width = weights_ref.shape
    chunks = sems.shape[0]
    per = blocks_dev // chunks
    half = slots // 2
    fold = LANES // stars
    all_slots = parcel_rows.shape[0]
    lane = lax.broadcasted_iota(jnp.int32, (8, LANES), 1)
    row = lax.broadcasted_iota(jnp.int32, (8, LANES), 0)
    own_slot = [row == lane // stars + fold * h for h in range(8 // fold)]

    def load(chunk):
        span = pl.ds(chunk * per, per)
        return pltpu.make_async_copy(weights_hbm.at[span], weights_ref.at[span], sems.at[chunk])

    def places(chunk):
        found = {}
        for b in range(per):
            for k in range(half):
                both = position_ref[k * 2 * blocks_dev + chunk * per + b]
                found[b, k] = both & (MARK - 1)
                found[b, k + half] = both >> 16
        return found

    def start_of(chunk):
        return pl.multiple_of(chunk * per * slots, per * slots)

    def matrix_of(chunk, b):
        eights = [weights_ref[chunk * per + b, 8 * j : 8 * j + 8] for j in range(slots // 8)]
        return jnp.concatenate([x.reshape(8 * stars, width) for x in eights], axis=1)

    def gather(chunk):
        for (b, k), at in places(chunk).items():
            fetched_ref[pl.ds(start_of(chunk) + b * slots + k, 1), :] = returned_rows[at]

    def extinctions(chunk):
        weighted = []
        for b in range(per):
            left = jnp.concatenate(
                [
                    fetched_ref[pl.ds(start_of(chunk) + b * slots + 8 * j, 8), :]
                    for j in range(slots // 8)
                ],
                axis=1,
            )
            total = lax.dot_general(
                left.astype(jnp.bfloat16),
                matrix_of(chunk, b),
                CONTRACT_LANES,
                preferred_element_type=jnp.float32,
            )
            folded = jnp.zeros((8, LANES), jnp.float32)
            for h, own in enumerate(own_slot):
                folded = folded + jnp.where(own, total[:, h * LANES : (h + 1) * LANES], 0.0)
            extinction = jnp.sum(folded, axis=0, keepdims=True)
            shift = stars
            while shift < LANES:
                extinction = extinction + pltpu.roll(extinction, shift, 1)
                shift *= 2
            here = pl.ds(chunk * per + b, 1)
            extinction_ref[here, :] = extinction
            weighted.append(inverse_ref[here, :] * (extinction - observed_ref[here, :]))
        return weighted

    def sensitivities(chunk, weighted):
        for b in range(per):
            left = jnp.concatenate(
                [jnp.where(own, weighted[b], 0.0) for own in own_slot], axis=1
            ).astype(jnp.bfloat16)
            sens = jnp.dot(left, matrix_of(chunk, b), preferred_element_type=jnp.float32)
            for j in range(slots // 8):
                sens_ref[pl.ds(start_of(chunk) + b * slots + 8 * j, 8), :] = sens[
                    :, j * width : (j + 1) * width
                ]

    def scatter(chunk):
        for (b, k), at in places(chunk).items():
            parcel_rows[at] = sens_ref[pl.ds(start_of(chunk) + b * slots + k, 1), :]

    for chunk in range(chunks):
        load(chunk).start()
    start = 0
    for returned_ref in returned_refs:
        span = slice(start, start + returned_ref.shape[0])
        returned_rows.reshape(all_slots, width)[span, :] = returned_ref[...].astype(jnp.float32)
        start = span.stop
    parcel_rows.reshape(all_slots, width)[...] = jnp.zeros((all_slots, width), jnp.float32)
    gather(0)
    load(0).wait()
    weighted = extinctions(0)
    gather(1)
    load(1).wait()
    following = extinctions(1)
    sensitivities(0, weighted)
    gather(2)

    def step(chunk, weighted):
        load(chunk).wait()
        following = extinctions(chunk)
        sensitivities(chunk - 1, weighted)
        scatter(chunk - 2)
        gather(jnp.minimum(chunk + 1, chunks - 1))
        return following

    weighted = lax.fori_loop(2, chunks, step, following)
    sensitivities(chunks - 1, weighted)
    scatter(chunks - 2)
    scatter(chunks - 1)
    start = 0
    for parcel_ref in parcel_refs:
        span = slice(start, start + parcel_ref.shape[0])
        parcel_ref[...] = parcel_rows.reshape(all_slots, width)[span, :].astype(jnp.bfloat16)
        start = span.stop


def prior_kernel(field_ref, xlo_ref, xhi_ref, ylo_ref, yhi_ref, out_ref, padded, smooth):
    cells_x, cells_y, depth = field_ref.shape
    rows = padded.shape[1]
    gx, gy = lax.axis_index("gx"), lax.axis_index("gy")
    last_gx, last_gy = lax.axis_size("gx") - 1, lax.axis_size("gy") - 1
    z = lax.broadcasted_iota(jnp.int32, (rows, depth), 1)
    y = lax.broadcasted_iota(jnp.int32, (rows, depth), 0) - 8
    inside_y = ((y >= 0) | (gy > 0)) & ((y < cells_y) | (gy < last_gy))

    def operate(center, below, above):
        beside = below + above
        beside = beside + pltpu.roll(center, 1, 0) + pltpu.roll(center, rows - 1, 0)
        beside = beside + jnp.where(z == 0, 0.0, pltpu.roll(center, 1, 1))
        beside = beside + jnp.where(z == depth - 1, 0.0, pltpu.roll(center, depth - 1, 1))
        return (shift_kappa + 6.0) * center - beside

    def fill(plane, source):
        padded[plane, 8 : 8 + cells_y, :] = source
        padded[plane, 0:8, :] = jnp.zeros((8, depth), jnp.float32)
        padded[plane, 8 + cells_y :, :] = jnp.zeros((8, depth), jnp.float32)
        for h in range(2):
            padded[plane, 6 + h : 7 + h, :] = ylo_ref[h, pl.ds(plane, 1), :]
            padded[plane, 8 + cells_y + h : 9 + cells_y + h, :] = yhi_ref[h, pl.ds(plane, 1), :]

    for h in range(2):
        fill(h, xlo_ref[h])
        fill(cells_x + 2 + h, xhi_ref[h])

    def fill_own(x, carry):
        fill(x + 2, field_ref[x])
        return carry

    lax.fori_loop(0, cells_x, fill_own, 0)

    def smooth_plane(plane, carry):
        value = operate(padded[plane], padded[plane - 1], padded[plane + 1])
        inside = ((plane > 1) | (gx > 0)) & ((plane < cells_x + 2) | (gx < last_gx))
        smooth[plane - 1] = jnp.where(inside_y & inside, value, 0.0)
        return carry

    lax.fori_loop(1, cells_x + 3, smooth_plane, 0)

    def out_plane(x, carry):
        prior = operate(smooth[x + 1], smooth[x], smooth[x + 2])
        out_ref[x] = field_ref[x] - (step_rate * prior_weight) * prior[8 : 8 + cells_y]
        return carry

    lax.fori_loop(0, cells_x, out_plane, 0)


def finish_kernel(
    incoming_ref, match_ref, field_hbm, base_hbm, *refs, exchanges, capacity, first_slots
):
    arrived_refs, refs = refs[:exchanges], refs[exchanges:]
    out_hbm, collected, rows_ref, field_ref, base_ref, out_ref, in_sems, out_sems = refs
    cells_x, cells_y, depth = field_ref.shape
    per_column = depth // LANES
    parts = out_sems.shape[0]
    planes = cells_x // parts
    blocks = cells_x * cells_y * per_column
    loads = [
        pltpu.make_async_copy(field_hbm, field_ref, in_sems.at[0]),
        pltpu.make_async_copy(base_hbm, base_ref, in_sems.at[1]),
    ]
    for load in loads:
        load.start()
    collected_rows = collected.reshape(collected.shape[0], LANES)
    start = 0
    for arrived_ref in arrived_refs:
        for i in range(arrived_ref.shape[0] // LANES):
            span = slice(start + i * LANES, start + (i + 1) * LANES)
            rows_ref[span, :] = -step_rate * jnp.dot(
                match_ref[span, :],
                arrived_ref[i * LANES : (i + 1) * LANES, :],
                preferred_element_type=jnp.float32,
            )
        start += arrived_ref.shape[0]
    collected_rows[...] = jnp.zeros_like(collected_rows)

    part_starts = [0, arrived_refs[0].shape[0]]

    def visit(wanted, row, list_part):
        row = row + part_starts[list_part]
        sums = [collected[wanted[j]] + rows_ref[pl.ds(row + j, 1), :] for j in range(GROUP)]
        for j in range(GROUP):
            collected[wanted[j]] = sums[j]

    for_each_group(incoming_ref, visit, capacity, first_slots, blocks)
    for load in loads:
        load.wait()

    def store(part):
        span = pl.ds(part * planes, planes)
        return pltpu.make_async_copy(out_ref.at[span], out_hbm.at[span], out_sems.at[part])

    def one_plane(x, carry):
        for yb in range(cells_y // 8):
            for part in range(per_column):
                at = pl.multiple_of(((x * (cells_y // 8) + yb) * per_column + part) * 8, 8)
                here = (x, slice(8 * yb, 8 * yb + 8), slice(part * LANES, (part + 1) * LANES))
                out_ref[here] = base_ref[here] + collected_rows[pl.ds(at, 8), :] * jnp.exp(
                    field_ref[here]
                )
        return carry

    for part in range(parts):
        lax.fori_loop(part * planes, (part + 1) * planes, one_plane, 0)
        store(part).start()
    for part in range(parts):
        store(part).wait()


def both_ways(first, last, axis):
    peers = lax.axis_size(axis)
    up = [(i, i + 1) for i in range(peers - 1)]
    down = [(j, i) for i, j in up]
    return lax.ppermute(last, axis, up), lax.ppermute(first, axis, down)


def halo_y(xlo, xhi, yfirst, ylast):
    def rows(own, at):
        return jnp.concatenate(
            [xlo[:, at].transpose(1, 0, 2), own, xhi[:, at].transpose(1, 0, 2)], axis=1
        )

    return both_ways(rows(yfirst, slice(0, 2)), rows(ylast, slice(-2, None)), "gy")


VMEM = pl.BlockSpec(memory_space=pltpu.VMEM)
SMEM = pl.BlockSpec(memory_space=pltpu.SMEM)
ANY = pl.BlockSpec(memory_space=pl.ANY)


def on_device(log_density, weights, observed, inverse_var, star_counts, block_ids):
    cells_x, cells_y, depth = log_density.shape
    blocks_dev, slots, stars, width = weights.shape
    devices = lax.axis_size("gx") * lax.axis_size("gy")
    requests = blocks_dev * slots
    capacity = 2 * requests // devices
    first_slots = min(capacity, -(-3 * capacity // (4 * GROUP)) * GROUP)
    slots_of = [n for n in (first_slots, capacity - first_slots) if n > 0]
    exchanges = len(slots_of)
    all_slots = devices * capacity
    per_column = depth // width
    blocks = cells_x * cells_y * per_column
    cells = log_density.size
    field_shape = (cells_x, cells_y, depth)
    mesh_axes = ("gx", "gy")
    f32, bf16, i32 = jnp.float32, jnp.bfloat16, jnp.int32
    shape = jax.ShapeDtypeStruct

    def exchange(x):
        return lax.all_to_all(x, mesh_axes, split_axis=0, concat_axis=0, tiled=True)

    def exchange_rows(parts, crowded):
        moved = [parts[0].reshape(devices, first_slots, width)]
        moved[0] = exchange(moved[0])
        for part in parts[1:]:
            part = part.reshape(devices, capacity - first_slots, width)
            moved.append(lax.cond(crowded, exchange, lambda x: x, part))
        return [x.reshape(-1, width) for x in moved]

    outgoing, position = pl.pallas_call(
        functools.partial(
            route_kernel,
            devices=devices,
            capacity=capacity,
            first_slots=first_slots,
            blocks=blocks,
            per_column=per_column,
        ),
        out_shape=[shape((devices, capacity), i32), shape((requests // LANES, LANES), i32)],
        in_specs=[VMEM],
        out_specs=[VMEM, VMEM],
        name="route",
    )(block_ids.T)
    incoming = exchange(outgoing)

    field, _ = lax.optimization_barrier((log_density, outgoing))
    xfirst, xlast, yfirst, ylast = pl.pallas_call(
        edges_kernel,
        out_shape=[
            shape((2, cells_y, depth), f32),
            shape((2, cells_y, depth), f32),
            shape((2, cells_x, depth), f32),
            shape((2, cells_x, depth), f32),
        ],
        in_specs=[VMEM],
        out_specs=[VMEM] * 4,
        compiler_params=pltpu.CompilerParams(vmem_limit_bytes=8 * MIB),
        cost_estimate=pl.CostEstimate(flops=0, bytes_accessed=2 * MIB, transcendentals=0),
        name="edges",
    )(field)
    xlo, xhi = both_ways(xfirst, xlast, "gx")
    incoming, yfirst, ylast = lax.optimization_barrier((incoming, yfirst, ylast))
    wanted = incoming.reshape(-1)

    served = pl.pallas_call(
        functools.partial(serve_kernel, capacity=capacity, first_slots=first_slots),
        out_shape=[shape((devices * n, width), bf16) for n in slots_of],
        in_specs=[SMEM, VMEM],
        out_specs=[VMEM] * exchanges,
        scratch_shapes=[
            pltpu.VMEM((blocks + capacity, 1, width), f32),
        ],
        compiler_params=pltpu.CompilerParams(vmem_limit_bytes=24 * MIB),
        cost_estimate=pl.CostEstimate(
            flops=cells, bytes_accessed=6 * MIB, transcendentals=cells
        ),
        name="serve",
    )(wanted, field)

    incoming_late, xlo, xhi, yfirst, ylast, _ = lax.optimization_barrier(
        (incoming, xlo, xhi, yfirst, ylast, served[0])
    )
    crowded = jnp.max(incoming_late[:, capacity - 1]) >= (first_slots + 1) * MARK
    returned = exchange_rows(served, crowded)
    ylo, yhi = halo_y(xlo, xhi, yfirst, ylast)
    slot_lists = [
        incoming_late[:, :first_slots].reshape(-1, LANES),
        (incoming_late[:, first_slots:] & (MARK - 1)).reshape(-1, LANES),
    ][:exchanges]
    match = pl.pallas_call(
        match_kernel,
        out_shape=shape((all_slots, LANES), bf16),
        in_specs=[VMEM],
        out_specs=VMEM,
        compiler_params=pltpu.CompilerParams(vmem_limit_bytes=8 * MIB),
        cost_estimate=pl.CostEstimate(flops=10**9, bytes_accessed=MIB, transcendentals=0),
        name="match",
    )(jnp.concatenate(slot_lists, axis=0))
    *returned, match, xlo, xhi = lax.optimization_barrier((*returned, match, xlo, xhi))

    chunks = blocks_dev * stars // LANES
    live = jnp.arange(stars)[None, :] < star_counts[:, None]
    live_inverse = jnp.where(live, inverse_var, 0.0)
    extinction, *parcel = pl.pallas_call(
        functools.partial(star_kernel, exchanges=exchanges),
        out_shape=[shape((blocks_dev, LANES), f32)]
        + [shape((devices * n, width), bf16) for n in slots_of],
        in_specs=[SMEM, VMEM, VMEM, ANY] + [VMEM] * exchanges,
        out_specs=[VMEM] * (1 + exchanges),
        scratch_shapes=[
            pltpu.VMEM(weights.shape, bf16),
            pltpu.VMEM((all_slots, 1, width), f32),
            pltpu.VMEM((requests, width), f32),
            pltpu.VMEM((requests, width), f32),
            pltpu.VMEM((all_slots, 1, width), f32),
            pltpu.SemaphoreType.DMA((chunks,)),
        ],
        compiler_params=pltpu.CompilerParams(vmem_limit_bytes=50 * MIB),
        cost_estimate=pl.CostEstimate(
            flops=4 * weights.size, bytes_accessed=2 * weights.size, transcendentals=0
        ),
        name="stars",
    )(
        position.reshape(requests),
        jnp.tile(observed, (1, LANES // stars)),
        jnp.tile(live_inverse, (1, LANES // stars)),
        weights,
        *returned,
    )
    arrived = exchange_rows(parcel, crowded)

    field_late, _ = lax.optimization_barrier((log_density, parcel[0]))
    base = pl.pallas_call(
        prior_kernel,
        out_shape=shape(field_shape, f32),
        in_specs=[VMEM] * 5,
        out_specs=VMEM,
        scratch_shapes=[
            pltpu.VMEM((cells_x + 4, cells_y + 16, depth), f32),
            pltpu.VMEM((cells_x + 2, cells_y + 16, depth), f32),
        ],
        compiler_params=pltpu.CompilerParams(vmem_limit_bytes=32 * MIB),
        cost_estimate=pl.CostEstimate(
            flops=30 * cells, bytes_accessed=8 * cells, transcendentals=0
        ),
        name="prior",
    )(field_late, xlo, xhi, ylo, yhi)

    parts = 8
    new_log_density = pl.pallas_call(
        functools.partial(
            finish_kernel, exchanges=exchanges, capacity=capacity, first_slots=first_slots
        ),
        out_shape=shape(field_shape, f32),
        in_specs=[SMEM, VMEM, ANY, ANY] + [VMEM] * exchanges,
        out_specs=ANY,
        scratch_shapes=[
            pltpu.VMEM((blocks + capacity, 1, width), f32),
            pltpu.VMEM((all_slots, width), f32),
            pltpu.VMEM(field_shape, f32),
            pltpu.VMEM(field_shape, f32),
            pltpu.VMEM(field_shape, f32),
            pltpu.SemaphoreType.DMA((2,)),
            pltpu.SemaphoreType.DMA((parts,)),
        ],
        compiler_params=pltpu.CompilerParams(vmem_limit_bytes=50 * MIB),
        cost_estimate=pl.CostEstimate(
            flops=4 * cells, bytes_accessed=12 * cells, transcendentals=cells
        ),
        name="finish",
    )(wanted, match, log_density, base, *arrived)
    return new_log_density, extinction[:, :stars]


def solution(mesh):
    placed = (
        P("gx", "gy", None),
        P(("gx", "gy"), None, None, None),
        P(("gx", "gy"), None),
        P(("gx", "gy"), None),
        P(("gx", "gy")),
        P(("gx", "gy"), None),
    )
    return jax.shard_map(
        on_device,
        mesh=mesh,
        in_specs=placed,
        out_specs=(P("gx", "gy", None), P(("gx", "gy"), None)),
        check_vma=False,
    )
```

```python
import functools

import jax
import jax.numpy as jnp
from jax import lax
from jax.experimental import pallas as pl
from jax.experimental.pallas import tpu as pltpu
from jax.sharding import PartitionSpec as P

shift_kappa = 0.5
prior_weight = 0.05
step_rate = 2.0

LANES = 128
GROUP = 16
MIB = 1 << 20
MARK = 1 << 16

CONTRACT_LANES = (((1,), (1,)), ((), ()))


def split_by(value, size):
    if size & (size - 1) == 0:
        high = value >> (size.bit_length() - 1)
        return high, value & (size - 1)
    high = value // size
    return high, value - high * size


def route_kernel(
    ids_ref, outgoing_ref, position_ref, *, devices, capacity, first_slots, blocks, per_column
):
    half = ids_ref.shape[0] // 2
    ids = jnp.concatenate([ids_ref[:half, :], ids_ref[half:, :]], axis=1)
    lane = lax.broadcasted_iota(jnp.int32, (LANES, LANES), 1)
    row = lax.broadcasted_iota(jnp.int32, (LANES, LANES), 0)
    upper = jnp.where(row <= lane, 1.0, 0.0).astype(jnp.bfloat16)
    tile_no = lax.broadcasted_iota(jnp.int32, (devices, LANES), 0)
    slot_no = lax.broadcasted_iota(jnp.int32, (capacity, LANES), 0)
    before = jnp.zeros((devices, 1), jnp.float32)
    lists = jnp.zeros((2 * devices, capacity), jnp.float32)
    for chunk in range(half):
        target, local = split_by(ids[chunk : chunk + 1, :], blocks)
        column, part = split_by(local, per_column)
        local = ((column >> 3) * per_column + part) * 8 + (column & 7)
        hit = tile_no == target
        onehot = jnp.where(hit, 1.0, 0.0)
        upto = before + jnp.dot(
            onehot.astype(jnp.bfloat16), upper, preferred_element_type=jnp.float32
        )
        before = upto[:, LANES - 1 :]
        rank = jnp.sum(onehot * upto, axis=0, keepdims=True).astype(jnp.int32) - 1
        in_slot = jnp.where(slot_no == rank, 1.0, 0.0).astype(jnp.bfloat16)
        high = ((local >> 7) + 1).astype(jnp.float32)
        low = (local & 127).astype(jnp.float32)
        digits = jnp.concatenate([jnp.where(hit, high, 0.0), jnp.where(hit, low, 0.0)], axis=0)
        lists = lists + lax.dot_general(
            digits.astype(jnp.bfloat16),
            in_slot,
            CONTRACT_LANES,
            preferred_element_type=jnp.float32,
        )
        last_slots = capacity - first_slots
        position_ref[chunk : chunk + 1, :] = jnp.where(
            rank < first_slots,
            target * first_slots + rank,
            devices * first_slots + target * last_slots + rank - first_slots,
        )
    high, low = lists[:devices], lists[devices:]
    wanted = ((high - 1.0) * 128.0 + low).astype(jnp.int32)
    filled = before.astype(jnp.int32)
    me = lax.axis_index("gx") * lax.axis_size("gy") + lax.axis_index("gy")
    fullest = jnp.max(jnp.where(tile_no[:, :1] == me, 0.0, before), axis=0, keepdims=True)
    listed = jnp.where(high > 0.5, wanted, blocks + filled)
    if first_slots < capacity:
        slot = lax.broadcasted_iota(jnp.int32, (devices, capacity), 1)
        mark = fullest.astype(jnp.int32) * MARK
        listed = listed + jnp.where(slot == capacity - 1, mark, 0)
    outgoing_ref[...] = listed


def edges_kernel(field_ref, xfirst_ref, xlast_ref, yfirst_ref, ylast_ref):
    cells_x, cells_y, _ = field_ref.shape
    xfirst_ref[...] = field_ref[:2].astype(xfirst_ref.dtype)
    xlast_ref[...] = field_ref[cells_x - 2 :].astype(xlast_ref.dtype)
    for h in range(2):
        for x in range(cells_x):
            yfirst_ref[h, x : x + 1, :] = field_ref[x, h : h + 1, :]
            ylast_ref[h, x : x + 1, :] = field_ref[x, cells_y - 2 + h : cells_y - 1 + h, :]


def for_each_group(incoming_ref, visit, capacity, first_slots, blocks):
    sources = incoming_ref.shape[0] // capacity
    last_slots = capacity - first_slots
    together = 4

    def groups_of(source):
        last = incoming_ref[source * capacity + capacity - 1] & (MARK - 1)
        return (jnp.where(last < blocks, capacity, last - blocks) + GROUP - 1) // GROUP

    def some_sources(quad, carry):
        own = [quad * together + i for i in range(together)]
        most = functools.reduce(jnp.maximum, [groups_of(source) for source in own])

        def one_group(group, carry):
            slot = group * GROUP
            for source in own:
                listed = incoming_ref.at[pl.ds(source * capacity + slot, GROUP)]
                wanted = [listed[j] for j in range(GROUP)]
                visit(wanted, pl.multiple_of(source * first_slots + slot, GROUP), 0)
            return carry

        return lax.fori_loop(0, jnp.minimum(most, first_slots // GROUP), one_group, carry)

    lax.fori_loop(0, sources // together, some_sources, 0)
    if last_slots == 0:
        return

    def one_source(source, carry):
        def one_group(group, carry):
            slot = group * GROUP
            listed = incoming_ref.at[pl.ds(source * capacity + slot, GROUP)]
            wanted = [listed[j] & (MARK - 1) for j in range(GROUP)]
            visit(wanted, pl.multiple_of(source * last_slots + slot - first_slots, GROUP), 1)
            return carry

        return lax.fori_loop(first_slots // GROUP, groups_of(source), one_group, carry)

    lax.fori_loop(0, sources, one_source, 0)


def serve_kernel(incoming_ref, field_ref, *refs, capacity, first_slots):
    *served_refs, table_ref = refs
    cells_x, cells_y, depth = field_ref.shape
    per_column = depth // LANES
    table_rows = table_ref.reshape(table_ref.shape[0], LANES)
    blocks = cells_x * cells_y * per_column
    table_rows[blocks:, :] = jnp.zeros((table_ref.shape[0] - blocks, LANES), jnp.float32)

    def one_plane(x, carry):
        for yb in range(cells_y // 8):
            for part in range(per_column):
                at = pl.multiple_of(((x * (cells_y // 8) + yb) * per_column + part) * 8, 8)
                table_rows[pl.ds(at, 8), :] = jnp.exp(
                    field_ref[x, 8 * yb : 8 * yb + 8, part * LANES : (part + 1) * LANES]
                )
        return carry

    lax.fori_loop(0, cells_x, one_plane, 0)

    def visit(wanted, row, list_part):
        rows = jnp.concatenate([table_ref[at] for at in wanted], axis=0)
        served_refs[list_part][pl.ds(row, GROUP), :] = rows.astype(jnp.bfloat16)

    for_each_group(incoming_ref, visit, capacity, first_slots, blocks)


def match_kernel(incoming_ref, marked_ref, match_ref, fullest_ref):
    marks = marked_ref[:, marked_ref.shape[1] - 1 :] >> 16
    fullest = jnp.max(marks, axis=0, keepdims=True)
    fullest_ref[...] = jnp.broadcast_to(fullest, fullest_ref.shape)
    lane = lax.broadcasted_iota(jnp.int32, (LANES, LANES), 1)
    row = lax.broadcasted_iota(jnp.int32, (LANES, LANES), 0)
    ones = jnp.ones((LANES, LANES), jnp.bfloat16)
    same_group = (lane // GROUP) == (row // GROUP)

    def one_row(i):
        wanted = incoming_ref[pl.ds(i, 1), :]
        high = jnp.where(lane == row, (wanted >> 7).astype(jnp.float32), 0.0).astype(jnp.bfloat16)
        low = jnp.where(lane == row, (wanted & 127).astype(jnp.float32), 0.0).astype(jnp.bfloat16)
        down = 128.0 * jnp.dot(high, ones, preferred_element_type=jnp.float32)
        down = down + jnp.dot(low, ones, preferred_element_type=jnp.float32)
        same = (down == wanted.astype(jnp.float32)) & same_group
        match_ref[pl.ds(pl.multiple_of(i * LANES, LANES), LANES), :] = jnp.where(
            same, 1.0, 0.0
        ).astype(jnp.bfloat16)

    def some_rows(i, carry):
        for j in range(4):
            one_row(4 * i + j)
        return carry

    lax.fori_loop(0, incoming_ref.shape[0] // 4, some_rows, 0)


def star_kernel(position_ref, observed_ref, inverse_ref, weights_hbm, *refs, exchanges):
    returned_refs, refs = refs[:exchanges], refs[exchanges:]
    extinction_ref, refs = refs[0], refs[1:]
    parcel_refs, refs = refs[:exchanges], refs[exchanges:]
    weights_ref, returned_rows, sens_ref, parcel_rows, sems = refs
    blocks_dev, slots, stars, width = weights_ref.shape
    chunks = sems.shape[0]
    per = blocks_dev // chunks
    fold = LANES // stars
    all_slots = parcel_rows.shape[0]
    lane = lax.broadcasted_iota(jnp.int32, (8, LANES), 1)
    row = lax.broadcasted_iota(jnp.int32, (8, LANES), 0)
    star_group = lane // stars
    own_slot = [row == star_group + fold * h for h in range(8 // fold)]

    def load(chunk):
        span = pl.ds(chunk * per, per)
        return pltpu.make_async_copy(weights_hbm.at[span], weights_ref.at[span], sems.at[chunk])

    def start_of(chunk):
        return pl.multiple_of(chunk * per * slots, per * slots)

    def positions(chunk):
        return position_ref.at[pl.ds(start_of(chunk), per * slots)]

    def extinctions(chunk):
        places = positions(chunk)
        sums = []
        for b in range(per):
            total = jnp.zeros((stars, width), jnp.float32)
            for k in range(slots):
                fetched = returned_rows[places[b * slots + k]]
                total = total + weights_ref[chunk * per + b, k].astype(jnp.float32) * fetched
            sums.append(total)
        extinction = lax.dot_general(
            jnp.ones((8, width), jnp.float32),
            jnp.concatenate(sums, axis=0),
            CONTRACT_LANES,
            precision=lax.Precision.HIGHEST,
            preferred_element_type=jnp.float32,
        )
        here = pl.ds(chunk, 1)
        extinction_ref[here, :] = extinction[:1]
        return inverse_ref[here, :] * (extinction - observed_ref[here, :])

    def sensitivities(chunk, weighted):
        for b in range(per):
            spread = jnp.where(star_group == b, weighted, 0.0)
            shift = stars
            while shift < LANES:
                spread = spread + pltpu.roll(spread, shift, 1)
                shift *= 2
            left = jnp.concatenate(
                [jnp.where(own, spread, 0.0) for own in own_slot], axis=1
            ).astype(jnp.bfloat16)
            eights = [weights_ref[chunk * per + b, 8 * j : 8 * j + 8] for j in range(slots // 8)]
            right = jnp.concatenate([x.reshape(8 * stars, width) for x in eights], axis=1)
            sens = jnp.dot(left, right, preferred_element_type=jnp.float32)
            for j in range(slots // 8):
                sens_ref[pl.ds(start_of(chunk) + b * slots + 8 * j, 8), :] = sens[
                    :, j * width : (j + 1) * width
                ]

    def scatter(chunk):
        places = positions(chunk)
        rows = sens_ref.at[pl.ds(start_of(chunk), per * slots)]
        for i in range(per * slots):
            parcel_rows[places[i]] = rows[i : i + 1, :]

    for chunk in range(chunks):
        load(chunk).start()
    start = 0
    for returned_ref in returned_refs:
        span = slice(start, start + returned_ref.shape[0])
        returned_rows.reshape(all_slots, width)[span, :] = returned_ref[...].astype(jnp.float32)
        start = span.stop
    parcel_rows.reshape(all_slots, width)[...] = jnp.zeros((all_slots, width), jnp.float32)
    load(0).wait()
    weighted = extinctions(0)
    load(1).wait()
    following = extinctions(1)
    sensitivities(0, weighted)

    def step(chunk, weighted):
        load(chunk).wait()
        following = extinctions(chunk)
        sensitivities(chunk - 1, weighted)
        scatter(chunk - 2)
        return following

    weighted = lax.fori_loop(2, chunks, step, following)
    sensitivities(chunks - 1, weighted)
    scatter(chunks - 2)
    scatter(chunks - 1)
    start = 0
    for parcel_ref in parcel_refs:
        span = slice(start, start + parcel_ref.shape[0])
        parcel_ref[...] = parcel_rows.reshape(all_slots, width)[span, :].astype(jnp.bfloat16)
        start = span.stop


def prior_kernel(field_ref, xlo_ref, xhi_ref, ylo_ref, yhi_ref, out_ref, padded, smooth):
    cells_x, cells_y, depth = field_ref.shape
    rows = padded.shape[1]
    gx, gy = lax.axis_index("gx"), lax.axis_index("gy")
    last_gx, last_gy = lax.axis_size("gx") - 1, lax.axis_size("gy") - 1
    z = lax.broadcasted_iota(jnp.int32, (rows, depth), 1)
    y = lax.broadcasted_iota(jnp.int32, (rows, depth), 0) - 8
    inside_y = ((y >= 0) | (gy > 0)) & ((y < cells_y) | (gy < last_gy))

    def operate(center, below, above):
        beside = below + above
        beside = beside + pltpu.roll(center, 1, 0) + pltpu.roll(center, rows - 1, 0)
        beside = beside + jnp.where(z == 0, 0.0, pltpu.roll(center, 1, 1))
        beside = beside + jnp.where(z == depth - 1, 0.0, pltpu.roll(center, depth - 1, 1))
        return (shift_kappa + 6.0) * center - beside

    def fill(plane, source):
        padded[plane, 8 : 8 + cells_y, :] = source
        padded[plane, 0:8, :] = jnp.zeros((8, depth), jnp.float32)
        padded[plane, 8 + cells_y :, :] = jnp.zeros((8, depth), jnp.float32)
        for h in range(2):
            padded[plane, 6 + h : 7 + h, :] = ylo_ref[h, pl.ds(plane, 1), :]
            padded[plane, 8 + cells_y + h : 9 + cells_y + h, :] = yhi_ref[h, pl.ds(plane, 1), :]

    for h in range(2):
        fill(h, xlo_ref[h].astype(jnp.float32))
        fill(cells_x + 2 + h, xhi_ref[h].astype(jnp.float32))

    def fill_own(x, carry):
        fill(x + 2, field_ref[x])
        return carry

    lax.fori_loop(0, cells_x, fill_own, 0)

    def smooth_plane(plane, carry):
        value = operate(padded[plane], padded[plane - 1], padded[plane + 1])
        inside = ((plane > 1) | (gx > 0)) & ((plane < cells_x + 2) | (gx < last_gx))
        smooth[plane - 1] = jnp.where(inside_y & inside, value, 0.0)
        return carry

    lax.fori_loop(1, cells_x + 3, smooth_plane, 0)

    def out_plane(x, carry):
        prior = operate(smooth[x + 1], smooth[x], smooth[x + 2])
        out_ref[x] = field_ref[x] - (step_rate * prior_weight) * prior[8 : 8 + cells_y]
        return carry

    lax.fori_loop(0, cells_x, out_plane, 0)


def finish_kernel(
    incoming_ref, match_ref, field_hbm, base_hbm, *refs, exchanges, capacity, first_slots
):
    arrived_refs, refs = refs[:exchanges], refs[exchanges:]
    out_hbm, collected, rows_ref, field_ref, base_ref, out_ref, in_sems, out_sems = refs
    cells_x, cells_y, depth = field_ref.shape
    per_column = depth // LANES
    parts = out_sems.shape[0]
    planes = cells_x // parts
    blocks = cells_x * cells_y * per_column
    loads = [
        pltpu.make_async_copy(field_hbm, field_ref, in_sems.at[0]),
        pltpu.make_async_copy(base_hbm, base_ref, in_sems.at[1]),
    ]
    for load in loads:
        load.start()
    collected_rows = collected.reshape(collected.shape[0], LANES)
    start = 0
    for arrived_ref in arrived_refs:
        for i in range(arrived_ref.shape[0] // LANES):
            span = slice(start + i * LANES, start + (i + 1) * LANES)
            rows_ref[span, :] = -step_rate * jnp.dot(
                match_ref[span, :],
                arrived_ref[i * LANES : (i + 1) * LANES, :],
                preferred_element_type=jnp.float32,
            )
        start += arrived_ref.shape[0]
    collected_rows[...] = jnp.zeros_like(collected_rows)

    part_starts = [0, arrived_refs[0].shape[0]]

    def visit(wanted, row, list_part):
        row = pl.multiple_of(row + part_starts[list_part], GROUP)
        rows = rows_ref.at[pl.ds(row, GROUP)]
        sums = [collected[wanted[j]] + rows[j : j + 1, :] for j in range(GROUP)]
        for j in range(GROUP):
            collected[wanted[j]] = sums[j]

    for_each_group(incoming_ref, visit, capacity, first_slots, blocks)
    for load in loads:
        load.wait()

    def store(part):
        span = pl.ds(part * planes, planes)
        return pltpu.make_async_copy(out_ref.at[span], out_hbm.at[span], out_sems.at[part])

    def one_plane(x, carry):
        for yb in range(cells_y // 8):
            for part in range(per_column):
                at = pl.multiple_of(((x * (cells_y // 8) + yb) * per_column + part) * 8, 8)
                here = (x, slice(8 * yb, 8 * yb + 8), slice(part * LANES, (part + 1) * LANES))
                out_ref[here] = base_ref[here] + collected_rows[pl.ds(at, 8), :] * jnp.exp(
                    field_ref[here]
                )
        return carry

    for part in range(parts):
        lax.fori_loop(part * planes, (part + 1) * planes, one_plane, 0)
        store(part).start()
    for part in range(parts):
        store(part).wait()


def both_ways(first, last, axis):
    peers = lax.axis_size(axis)
    up = [(i, i + 1) for i in range(peers - 1)]
    down = [(j, i) for i, j in up]
    return lax.ppermute(last, axis, up), lax.ppermute(first, axis, down)


def halo(xfirst, xlast, yfirst, ylast):
    xlo, xhi = both_ways(xfirst, xlast, "gx")

    def rows(own, at):
        ends = [x[:, at].transpose(1, 0, 2) for x in (xlo, xhi)]
        return jnp.concatenate([ends[0], own.astype(xlo.dtype), ends[1]], axis=1)

    ylo, yhi = both_ways(rows(yfirst, slice(0, 2)), rows(ylast, slice(-2, None)), "gy")
    return xlo, xhi, ylo.astype(jnp.float32), yhi.astype(jnp.float32)


VMEM = pl.BlockSpec(memory_space=pltpu.VMEM)
SMEM = pl.BlockSpec(memory_space=pltpu.SMEM)
ANY = pl.BlockSpec(memory_space=pl.ANY)


def on_device(log_density, weights, observed, inverse_var, star_counts, block_ids):
    cells_x, cells_y, depth = log_density.shape
    blocks_dev, slots, stars, width = weights.shape
    devices = lax.axis_size("gx") * lax.axis_size("gy")
    requests = blocks_dev * slots
    capacity = 2 * requests // devices
    first_slots = min(capacity, -(-3 * capacity // (4 * GROUP)) * GROUP)
    slots_of = [n for n in (first_slots, capacity - first_slots) if n > 0]
    exchanges = len(slots_of)
    all_slots = devices * capacity
    per_column = depth // width
    blocks = cells_x * cells_y * per_column
    cells = log_density.size
    field_shape = (cells_x, cells_y, depth)
    mesh_axes = ("gx", "gy")
    f32, bf16, i32 = jnp.float32, jnp.bfloat16, jnp.int32
    shape = jax.ShapeDtypeStruct

    def exchange(x):
        return lax.all_to_all(x, mesh_axes, split_axis=0, concat_axis=0, tiled=True)

    def exchange_rows(parts, crowded):
        moved = [parts[0].reshape(devices, first_slots, width)]
        moved[0] = exchange(moved[0])
        for part in parts[1:]:
            part = part.reshape(devices, capacity - first_slots, width)
            moved.append(lax.cond(crowded, exchange, lambda x: x, part))
        return [x.reshape(-1, width) for x in moved]

    outgoing, position = pl.pallas_call(
        functools.partial(
            route_kernel,
            devices=devices,
            capacity=capacity,
            first_slots=first_slots,
            blocks=blocks,
            per_column=per_column,
        ),
        out_shape=[shape((devices, capacity), i32), shape((requests // LANES, LANES), i32)],
        in_specs=[VMEM],
        out_specs=[VMEM, VMEM],
        name="route",
    )(block_ids.T)
    incoming = exchange(outgoing)

    field, _ = lax.optimization_barrier((log_density, outgoing))
    xfirst, xlast, yfirst, ylast = pl.pallas_call(
        edges_kernel,
        out_shape=[
            shape((2, cells_y, depth), bf16),
            shape((2, cells_y, depth), bf16),
            shape((2, cells_x, depth), f32),
            shape((2, cells_x, depth), f32),
        ],
        in_specs=[VMEM],
        out_specs=[VMEM] * 4,
        compiler_params=pltpu.CompilerParams(vmem_limit_bytes=8 * MIB),
        cost_estimate=pl.CostEstimate(flops=0, bytes_accessed=2 * MIB, transcendentals=0),
        name="edges",
    )(field)
    incoming, *edges = lax.optimization_barrier((incoming, xfirst, xlast, yfirst, ylast))
    wanted = incoming.reshape(-1)

    served = pl.pallas_call(
        functools.partial(serve_kernel, capacity=capacity, first_slots=first_slots),
        out_shape=[shape((devices * n, width), bf16) for n in slots_of],
        in_specs=[SMEM, VMEM],
        out_specs=[VMEM] * exchanges,
        scratch_shapes=[
            pltpu.VMEM((blocks + capacity, 1, width), f32),
        ],
        compiler_params=pltpu.CompilerParams(vmem_limit_bytes=24 * MIB),
        cost_estimate=pl.CostEstimate(
            flops=cells, bytes_accessed=6 * MIB, transcendentals=cells
        ),
        name="serve",
    )(wanted, field)

    incoming_late, *edges, _ = lax.optimization_barrier((incoming, *edges, served[0]))
    slot_lists = [
        incoming_late[:, :first_slots].reshape(-1, LANES),
        (incoming_late[:, first_slots:] & (MARK - 1)).reshape(-1, LANES),
    ][:exchanges]
    match, fullest = pl.pallas_call(
        match_kernel,
        out_shape=[shape((all_slots, LANES), bf16), shape((8, LANES), i32)],
        in_specs=[VMEM] * 2,
        out_specs=[VMEM] * 2,
        compiler_params=pltpu.CompilerParams(vmem_limit_bytes=8 * MIB),
        cost_estimate=pl.CostEstimate(flops=10**9, bytes_accessed=MIB, transcendentals=0),
        name="match",
    )(jnp.concatenate(slot_lists, axis=0), incoming_late)
    crowded = fullest[0, 0] > first_slots
    returned = exchange_rows(served, crowded)
    xlo, xhi, ylo, yhi = halo(*edges)
    *returned, match, ylo, yhi = lax.optimization_barrier((*returned, match, ylo, yhi))

    chunks = blocks_dev * stars // LANES
    live = jnp.arange(stars)[None, :] < star_counts[:, None]
    live_inverse = jnp.where(live, inverse_var, 0.0)
    extinction, *parcel = pl.pallas_call(
        functools.partial(star_kernel, exchanges=exchanges),
        out_shape=[shape((chunks, LANES), f32)]
        + [shape((devices * n, width), bf16) for n in slots_of],
        in_specs=[SMEM, VMEM, VMEM, ANY] + [VMEM] * exchanges,
        out_specs=[VMEM] * (1 + exchanges),
        scratch_shapes=[
            pltpu.VMEM(weights.shape, bf16),
            pltpu.VMEM((all_slots, 1, width), f32),
            pltpu.VMEM((requests, width), f32),
            pltpu.VMEM((all_slots, 1, width), f32),
            pltpu.SemaphoreType.DMA((chunks,)),
        ],
        compiler_params=pltpu.CompilerParams(vmem_limit_bytes=50 * MIB),
        cost_estimate=pl.CostEstimate(
            flops=4 * weights.size, bytes_accessed=2 * weights.size, transcendentals=0
        ),
        name="stars",
    )(
        position.reshape(slots // 2, 2, blocks_dev).transpose(2, 1, 0).reshape(requests),
        observed.reshape(chunks, LANES),
        live_inverse.reshape(chunks, LANES),
        weights,
        *returned,
    )
    arrived = exchange_rows(parcel, crowded)

    field_late, _ = lax.optimization_barrier((log_density, parcel[0]))
    base = pl.pallas_call(
        prior_kernel,
        out_shape=shape(field_shape, f32),
        in_specs=[VMEM] * 5,
        out_specs=VMEM,
        scratch_shapes=[
            pltpu.VMEM((cells_x + 4, cells_y + 16, depth), f32),
            pltpu.VMEM((cells_x + 2, cells_y + 16, depth), f32),
        ],
        compiler_params=pltpu.CompilerParams(vmem_limit_bytes=32 * MIB),
        cost_estimate=pl.CostEstimate(
            flops=30 * cells, bytes_accessed=8 * cells, transcendentals=0
        ),
        name="prior",
    )(field_late, xlo, xhi, ylo, yhi)

    parts = 8
    new_log_density = pl.pallas_call(
        functools.partial(
            finish_kernel, exchanges=exchanges, capacity=capacity, first_slots=first_slots
        ),
        out_shape=shape(field_shape, f32),
        in_specs=[SMEM, VMEM, ANY, ANY] + [VMEM] * exchanges,
        out_specs=ANY,
        scratch_shapes=[
            pltpu.VMEM((blocks + capacity, 1, width), f32),
            pltpu.VMEM((all_slots, width), f32),
            pltpu.VMEM(field_shape, f32),
            pltpu.VMEM(field_shape, f32),
            pltpu.VMEM(field_shape, f32),
            pltpu.SemaphoreType.DMA((2,)),
            pltpu.SemaphoreType.DMA((parts,)),
        ],
        compiler_params=pltpu.CompilerParams(vmem_limit_bytes=50 * MIB),
        cost_estimate=pl.CostEstimate(
            flops=4 * cells, bytes_accessed=12 * cells, transcendentals=cells
        ),
        name="finish",
    )(wanted, match, log_density, base, *arrived)
    return new_log_density, extinction.reshape(blocks_dev, stars)


def solution(mesh):
    placed = (
        P("gx", "gy", None),
        P(("gx", "gy"), None, None, None),
        P(("gx", "gy"), None),
        P(("gx", "gy"), None),
        P(("gx", "gy")),
        P(("gx", "gy"), None),
    )
    return jax.shard_map(
        on_device,
        mesh=mesh,
        in_specs=placed,
        out_specs=(P("gx", "gy", None), P(("gx", "gy"), None)),
        check_vma=False,
    )
```

```python
import functools

import jax
import jax.numpy as jnp
from jax import lax
from jax.experimental import pallas as pl
from jax.experimental.pallas import tpu as pltpu
from jax.sharding import PartitionSpec as P

shift_kappa = 0.5
prior_weight = 0.05
step_rate = 2.0

LANES = 128
GROUP = 16
MIB = 1 << 20
MARK = 1 << 16

CONTRACT_LANES = (((1,), (1,)), ((), ()))


def split_by(value, size):
    if size & (size - 1) == 0:
        high = value >> (size.bit_length() - 1)
        return high, value & (size - 1)
    high = value // size
    return high, value - high * size


def route_kernel(
    ids_ref, outgoing_ref, position_ref, *, devices, capacity, first_slots, blocks, per_column
):
    half = ids_ref.shape[0] // 2
    ids = jnp.concatenate([ids_ref[:half, :], ids_ref[half:, :]], axis=1)
    lane = lax.broadcasted_iota(jnp.int32, (LANES, LANES), 1)
    row = lax.broadcasted_iota(jnp.int32, (LANES, LANES), 0)
    upper = jnp.where(row <= lane, 1.0, 0.0).astype(jnp.bfloat16)
    tile_no = lax.broadcasted_iota(jnp.int32, (devices, LANES), 0)
    slot_no = lax.broadcasted_iota(jnp.int32, (capacity, LANES), 0)
    before = jnp.zeros((devices, 1), jnp.float32)
    lists = jnp.zeros((2 * devices, capacity), jnp.float32)
    for chunk in range(half):
        target, local = split_by(ids[chunk : chunk + 1, :], blocks)
        column, part = split_by(local, per_column)
        local = ((column >> 3) * per_column + part) * 8 + (column & 7)
        hit = tile_no == target
        onehot = jnp.where(hit, 1.0, 0.0)
        upto = before + jnp.dot(
            onehot.astype(jnp.bfloat16), upper, preferred_element_type=jnp.float32
        )
        before = upto[:, LANES - 1 :]
        rank = jnp.sum(onehot * upto, axis=0, keepdims=True).astype(jnp.int32) - 1
        in_slot = jnp.where(slot_no == rank, 1.0, 0.0).astype(jnp.bfloat16)
        high = ((local >> 7) + 1).astype(jnp.float32)
        low = (local & 127).astype(jnp.float32)
        digits = jnp.concatenate([jnp.where(hit, high, 0.0), jnp.where(hit, low, 0.0)], axis=0)
        lists = lists + lax.dot_general(
            digits.astype(jnp.bfloat16),
            in_slot,
            CONTRACT_LANES,
            preferred_element_type=jnp.float32,
        )
        last_slots = capacity - first_slots
        position_ref[chunk : chunk + 1, :] = jnp.where(
            rank < first_slots,
            target * first_slots + rank,
            devices * first_slots + target * last_slots + rank - first_slots,
        )
    high, low = lists[:devices], lists[devices:]
    wanted = ((high - 1.0) * 128.0 + low).astype(jnp.int32)
    filled = before.astype(jnp.int32)
    me = lax.axis_index("gx") * lax.axis_size("gy") + lax.axis_index("gy")
    fullest = jnp.max(jnp.where(tile_no[:, :1] == me, 0.0, before), axis=0, keepdims=True)
    listed = jnp.where(high > 0.5, wanted, blocks + filled)
    if first_slots < capacity:
        slot = lax.broadcasted_iota(jnp.int32, (devices, capacity), 1)
        mark = fullest.astype(jnp.int32) * MARK
        listed = listed + jnp.where(slot == capacity - 1, mark, 0)
    outgoing_ref[...] = listed


def edges_kernel(
    field_hbm, xfirst_ref, xlast_ref, yfirst_ref, ylast_ref, planes_ref, strips_ref, sems
):
    cells_x, cells_y, _ = field_hbm.shape
    copies = [
        pltpu.make_async_copy(field_hbm.at[pl.ds(0, 2)], planes_ref.at[0], sems.at[0]),
        pltpu.make_async_copy(field_hbm.at[pl.ds(cells_x - 2, 2)], planes_ref.at[1], sems.at[1]),
        pltpu.make_async_copy(field_hbm.at[:, pl.ds(0, 8)], strips_ref.at[0], sems.at[2]),
        pltpu.make_async_copy(
            field_hbm.at[:, pl.ds(cells_y - 8, 8)], strips_ref.at[1], sems.at[3]
        ),
    ]
    for copy in copies:
        copy.start()
    for copy in copies:
        copy.wait()
    xfirst_ref[...] = planes_ref[0].astype(xfirst_ref.dtype)
    xlast_ref[...] = planes_ref[1].astype(xlast_ref.dtype)
    for h in range(2):
        for x in range(cells_x):
            yfirst_ref[h, x : x + 1, :] = strips_ref[0, x, h : h + 1, :]
            ylast_ref[h, x : x + 1, :] = strips_ref[1, x, 6 + h : 7 + h, :]


def for_each_group(incoming_ref, visit, capacity, first_slots, blocks):
    sources = incoming_ref.shape[0] // capacity
    last_slots = capacity - first_slots
    together = 4

    def groups_of(source):
        last = incoming_ref[source * capacity + capacity - 1] & (MARK - 1)
        return (jnp.where(last < blocks, capacity, last - blocks) + GROUP - 1) // GROUP

    def some_sources(quad, carry):
        own = [quad * together + i for i in range(together)]
        most = functools.reduce(jnp.maximum, [groups_of(source) for source in own])

        def one_group(group, carry):
            slot = group * GROUP
            for source in own:
                listed = incoming_ref.at[pl.ds(source * capacity + slot, GROUP)]
                wanted = [listed[j] for j in range(GROUP)]
                visit(wanted, pl.multiple_of(source * first_slots + slot, GROUP), 0)
            return carry

        return lax.fori_loop(0, jnp.minimum(most, first_slots // GROUP), one_group, carry)

    lax.fori_loop(0, sources // together, some_sources, 0)
    if last_slots == 0:
        return

    def one_source(source, carry):
        def one_group(group, carry):
            slot = group * GROUP
            listed = incoming_ref.at[pl.ds(source * capacity + slot, GROUP)]
            wanted = [listed[j] & (MARK - 1) for j in range(GROUP)]
            visit(wanted, pl.multiple_of(source * last_slots + slot - first_slots, GROUP), 1)
            return carry

        return lax.fori_loop(first_slots // GROUP, groups_of(source), one_group, carry)

    lax.fori_loop(0, sources, one_source, 0)


def serve_kernel(incoming_ref, field_hbm, *refs, capacity, first_slots):
    *served_refs, crowded_ref, field_ref, table_ref, sems = refs
    cells_x, cells_y, depth = field_ref.shape
    per_column = depth // LANES
    parts = sems.shape[0]
    planes = cells_x // parts

    def load(part):
        span = pl.ds(part * planes, planes)
        return pltpu.make_async_copy(field_hbm.at[span], field_ref.at[span], sems.at[part])

    for part in range(parts):
        load(part).start()

    def mark_of(source, most):
        return jnp.maximum(most, incoming_ref[source * capacity + capacity - 1] >> 16)

    fullest = lax.fori_loop(0, incoming_ref.shape[0] // capacity, mark_of, jnp.int32(0))
    crowded_ref[0] = jnp.where(fullest > first_slots, 1, 0)
    table_rows = table_ref.reshape(table_ref.shape[0], LANES)
    blocks = cells_x * cells_y * per_column
    table_rows[blocks:, :] = jnp.zeros((table_ref.shape[0] - blocks, LANES), jnp.float32)

    def one_plane(x, carry):
        for yb in range(cells_y // 8):
            for part in range(per_column):
                at = pl.multiple_of(((x * (cells_y // 8) + yb) * per_column + part) * 8, 8)
                table_rows[pl.ds(at, 8), :] = jnp.exp(
                    field_ref[x, 8 * yb : 8 * yb + 8, part * LANES : (part + 1) * LANES]
                )
        return carry

    for part in range(parts):
        load(part).wait()
        lax.fori_loop(part * planes, (part + 1) * planes, one_plane, 0)

    def visit(wanted, row, list_part):
        rows = jnp.concatenate([table_ref[at] for at in wanted], axis=0)
        served_refs[list_part][pl.ds(row, GROUP), :] = rows.astype(jnp.bfloat16)

    for_each_group(incoming_ref, visit, capacity, first_slots, blocks)


def match_kernel(incoming_ref, match_ref):
    lane = lax.broadcasted_iota(jnp.int32, (LANES, LANES), 1)
    row = lax.broadcasted_iota(jnp.int32, (LANES, LANES), 0)
    ones = jnp.ones((LANES, LANES), jnp.bfloat16)
    same_group = (lane // GROUP) == (row // GROUP)

    def one_row(i):
        wanted = incoming_ref[pl.ds(i, 1), :]
        high = jnp.where(lane == row, (wanted >> 7).astype(jnp.float32), 0.0).astype(jnp.bfloat16)
        low = jnp.where(lane == row, (wanted & 127).astype(jnp.float32), 0.0).astype(jnp.bfloat16)
        down = 128.0 * jnp.dot(high, ones, preferred_element_type=jnp.float32)
        down = down + jnp.dot(low, ones, preferred_element_type=jnp.float32)
        same = (down == wanted.astype(jnp.float32)) & same_group
        match_ref[pl.ds(pl.multiple_of(i * LANES, LANES), LANES), :] = jnp.where(
            same, 1.0, 0.0
        ).astype(jnp.bfloat16)

    def some_rows(i, carry):
        for j in range(4):
            one_row(4 * i + j)
        return carry

    lax.fori_loop(0, incoming_ref.shape[0] // 4, some_rows, 0)


def star_kernel(position_ref, observed_ref, inverse_ref, weights_hbm, *refs, exchanges):
    returned_refs, refs = refs[:exchanges], refs[exchanges:]
    extinction_ref, refs = refs[0], refs[1:]
    parcel_refs, refs = refs[:exchanges], refs[exchanges:]
    weights_ref, returned_rows, sens_ref, parcel_rows, sems = refs
    sets, in_set, per, slots, stars, width = weights_ref.shape
    chunks = extinction_ref.shape[0]
    rounds = chunks // (sets * in_set)
    per_chunk = per * slots
    fold = LANES // stars
    all_slots = parcel_rows.shape[0]
    lane = lax.broadcasted_iota(jnp.int32, (8, LANES), 1)
    row = lax.broadcasted_iota(jnp.int32, (8, LANES), 0)
    star_group = lane // stars
    own_slot = [row == star_group + fold * h for h in range(8 // fold)]

    def load(one_round, one_set):
        return [
            pltpu.make_async_copy(
                weights_hbm.at[pl.ds(((one_round * sets + one_set) * in_set + u) * per, per)],
                weights_ref.at[one_set, u],
                sems.at[one_set, u],
            )
            for u in range(in_set)
        ]

    def extinctions(one_set, u, chunk, places):
        sums = []
        for b in range(per):
            total = jnp.zeros((stars, width), jnp.float32)
            for k in range(slots):
                fetched = returned_rows[places[u * per_chunk + b * slots + k]]
                total = total + weights_ref[one_set, u, b, k].astype(jnp.float32) * fetched
            sums.append(total)
        extinction = lax.dot_general(
            jnp.ones((8, width), jnp.float32),
            jnp.concatenate(sums, axis=0),
            CONTRACT_LANES,
            precision=lax.Precision.HIGHEST,
            preferred_element_type=jnp.float32,
        )
        here = pl.ds(chunk, 1)
        extinction_ref[here, :] = extinction[:1]
        return inverse_ref[here, :] * (extinction - observed_ref[here, :])

    def sensitivities(one_set, u, weighted):
        for b in range(per):
            spread = jnp.where(star_group == b, weighted, 0.0)
            shift = stars
            while shift < LANES:
                spread = spread + pltpu.roll(spread, shift, 1)
                shift *= 2
            left = jnp.concatenate(
                [jnp.where(own, spread, 0.0) for own in own_slot], axis=1
            ).astype(jnp.bfloat16)
            eights = [weights_ref[one_set, u, b, 8 * j : 8 * j + 8] for j in range(slots // 8)]
            right = jnp.concatenate([x.reshape(8 * stars, width) for x in eights], axis=1)
            sens = jnp.dot(left, right, preferred_element_type=jnp.float32)
            for j in range(slots // 8):
                first = u * per_chunk + b * slots + 8 * j
                sens_ref[first : first + 8, :] = sens[:, j * width : (j + 1) * width]

    def scatter(u, places):
        for i in range(u * per_chunk, (u + 1) * per_chunk):
            parcel_rows[places[i]] = sens_ref[i : i + 1, :]

    def work(one_round, one_set):
        first = (one_round * sets + one_set) * in_set
        size = in_set * per_chunk
        places = position_ref.at[pl.ds(pl.multiple_of(first * per_chunk, size), size)]
        weighted = {}
        for u in range(in_set + 2):
            if u < in_set:
                weighted[u] = extinctions(one_set, u, first + u, places)
            if 1 <= u <= in_set:
                sensitivities(one_set, u - 1, weighted[u - 1])
            if u >= 2:
                scatter(u - 2, places)

    for one_set in range(sets):
        for copy in load(0, one_set):
            copy.start()
    start = 0
    for returned_ref in returned_refs:
        span = slice(start, start + returned_ref.shape[0])
        returned_rows.reshape(all_slots, width)[span, :] = returned_ref[...].astype(jnp.float32)
        start = span.stop
    parcel_rows.reshape(all_slots, width)[...] = jnp.zeros((all_slots, width), jnp.float32)

    def one_round(i, carry):
        for one_set in range(sets):
            for copy in load(i, one_set):
                copy.wait()
            work(i, one_set)

            @pl.when(i + 1 < rounds)
            def _():
                for copy in load(i + 1, one_set):
                    copy.start()

        return carry

    lax.fori_loop(0, rounds, one_round, 0)
    start = 0
    for parcel_ref in parcel_refs:
        span = slice(start, start + parcel_ref.shape[0])
        parcel_ref[...] = parcel_rows.reshape(all_slots, width)[span, :].astype(jnp.bfloat16)
        start = span.stop


def prior_kernel(field_ref, xlo_ref, xhi_ref, ylo_ref, yhi_ref, out_ref, padded, smooth):
    cells_x, cells_y, depth = field_ref.shape
    rows = padded.shape[1]
    gx, gy = lax.axis_index("gx"), lax.axis_index("gy")
    last_gx, last_gy = lax.axis_size("gx") - 1, lax.axis_size("gy") - 1
    z = lax.broadcasted_iota(jnp.int32, (rows, depth), 1)
    y = lax.broadcasted_iota(jnp.int32, (rows, depth), 0) - 8
    inside_y = ((y >= 0) | (gy > 0)) & ((y < cells_y) | (gy < last_gy))

    def operate(center, below, above):
        beside = below + above
        beside = beside + pltpu.roll(center, 1, 0) + pltpu.roll(center, rows - 1, 0)
        beside = beside + jnp.where(z == 0, 0.0, pltpu.roll(center, 1, 1))
        beside = beside + jnp.where(z == depth - 1, 0.0, pltpu.roll(center, depth - 1, 1))
        return (shift_kappa + 6.0) * center - beside

    def fill(plane, source):
        padded[plane, 8 : 8 + cells_y, :] = source
        padded[plane, 0:8, :] = jnp.zeros((8, depth), jnp.float32)
        padded[plane, 8 + cells_y :, :] = jnp.zeros((8, depth), jnp.float32)
        for h in range(2):
            padded[plane, 6 + h : 7 + h, :] = ylo_ref[h, pl.ds(plane, 1), :]
            padded[plane, 8 + cells_y + h : 9 + cells_y + h, :] = yhi_ref[h, pl.ds(plane, 1), :]

    for h in range(2):
        fill(h, xlo_ref[h].astype(jnp.float32))
        fill(cells_x + 2 + h, xhi_ref[h].astype(jnp.float32))

    def fill_own(x, carry):
        fill(x + 2, field_ref[x])
        return carry

    lax.fori_loop(0, cells_x, fill_own, 0)

    def smooth_plane(plane, carry):
        value = operate(padded[plane], padded[plane - 1], padded[plane + 1])
        inside = ((plane > 1) | (gx > 0)) & ((plane < cells_x + 2) | (gx < last_gx))
        smooth[plane - 1] = jnp.where(inside_y & inside, value, 0.0)
        return carry

    lax.fori_loop(1, cells_x + 3, smooth_plane, 0)

    def out_plane(x, carry):
        prior = operate(smooth[x + 1], smooth[x], smooth[x + 2])
        out_ref[x] = field_ref[x] - (step_rate * prior_weight) * prior[8 : 8 + cells_y]
        return carry

    lax.fori_loop(0, cells_x, out_plane, 0)


def finish_kernel(
    incoming_ref, match_ref, field_hbm, base_hbm, *refs, exchanges, capacity, first_slots
):
    arrived_refs, refs = refs[:exchanges], refs[exchanges:]
    out_hbm, collected, rows_ref, field_ref, base_ref, out_ref, in_sems, out_sems = refs
    cells_x, cells_y, depth = field_ref.shape
    per_column = depth // LANES
    parts = out_sems.shape[0]
    planes = cells_x // parts
    blocks = cells_x * cells_y * per_column
    loads = [
        pltpu.make_async_copy(field_hbm, field_ref, in_sems.at[0]),
        pltpu.make_async_copy(base_hbm, base_ref, in_sems.at[1]),
    ]
    for load in loads:
        load.start()
    collected_rows = collected.reshape(collected.shape[0], LANES)
    start = 0
    for arrived_ref in arrived_refs:
        for i in range(arrived_ref.shape[0] // LANES):
            span = slice(start + i * LANES, start + (i + 1) * LANES)
            rows_ref[span, :] = -step_rate * jnp.dot(
                match_ref[span, :],
                arrived_ref[i * LANES : (i + 1) * LANES, :],
                preferred_element_type=jnp.float32,
            )
        start += arrived_ref.shape[0]
    collected_rows[...] = jnp.zeros_like(collected_rows)

    part_starts = [0, arrived_refs[0].shape[0]]

    def visit(wanted, row, list_part):
        row = pl.multiple_of(row + part_starts[list_part], GROUP)
        rows = rows_ref.at[pl.ds(row, GROUP)]
        sums = [collected[wanted[j]] + rows[j : j + 1, :] for j in range(GROUP)]
        for j in range(GROUP):
            collected[wanted[j]] = sums[j]

    for_each_group(incoming_ref, visit, capacity, first_slots, blocks)
    for load in loads:
        load.wait()

    def store(part):
        span = pl.ds(part * planes, planes)
        return pltpu.make_async_copy(out_ref.at[span], out_hbm.at[span], out_sems.at[part])

    def one_plane(x, carry):
        for yb in range(cells_y // 8):
            for part in range(per_column):
                at = pl.multiple_of(((x * (cells_y // 8) + yb) * per_column + part) * 8, 8)
                here = (x, slice(8 * yb, 8 * yb + 8), slice(part * LANES, (part + 1) * LANES))
                out_ref[here] = base_ref[here] + collected_rows[pl.ds(at, 8), :] * jnp.exp(
                    field_ref[here]
                )
        return carry

    for part in range(parts):
        lax.fori_loop(part * planes, (part + 1) * planes, one_plane, 0)
        store(part).start()
    for part in range(parts):
        store(part).wait()


def both_ways(first, last, axis):
    peers = lax.axis_size(axis)
    up = [(i, i + 1) for i in range(peers - 1)]
    down = [(j, i) for i, j in up]
    return lax.ppermute(last, axis, up), lax.ppermute(first, axis, down)


def halo(xfirst, xlast, yfirst, ylast):
    xlo, xhi = both_ways(xfirst, xlast, "gx")

    def rows(own, at):
        ends = [x[:, at].transpose(1, 0, 2) for x in (xlo, xhi)]
        return jnp.concatenate([ends[0], own.astype(xlo.dtype), ends[1]], axis=1)

    ylo, yhi = both_ways(rows(yfirst, slice(0, 2)), rows(ylast, slice(-2, None)), "gy")
    return xlo, xhi, ylo.astype(jnp.float32), yhi.astype(jnp.float32)


VMEM = pl.BlockSpec(memory_space=pltpu.VMEM)
SMEM = pl.BlockSpec(memory_space=pltpu.SMEM)
ANY = pl.BlockSpec(memory_space=pl.ANY)


def on_device(log_density, weights, observed, inverse_var, star_counts, block_ids):
    cells_x, cells_y, depth = log_density.shape
    blocks_dev, slots, stars, width = weights.shape
    devices = lax.axis_size("gx") * lax.axis_size("gy")
    requests = blocks_dev * slots
    capacity = 2 * requests // devices
    first_slots = min(capacity, -(-3 * capacity // (4 * GROUP)) * GROUP)
    slots_of = [n for n in (first_slots, capacity - first_slots) if n > 0]
    exchanges = len(slots_of)
    all_slots = devices * capacity
    per_column = depth // width
    blocks = cells_x * cells_y * per_column
    cells = log_density.size
    field_shape = (cells_x, cells_y, depth)
    mesh_axes = ("gx", "gy")
    f32, bf16, i32 = jnp.float32, jnp.bfloat16, jnp.int32
    shape = jax.ShapeDtypeStruct

    def exchange(x):
        return lax.all_to_all(x, mesh_axes, split_axis=0, concat_axis=0, tiled=True)

    def exchange_rows(parts, crowded):
        moved = [parts[0].reshape(devices, first_slots, width)]
        moved[0] = exchange(moved[0])
        for part in parts[1:]:
            part = part.reshape(devices, capacity - first_slots, width)
            moved.append(lax.cond(crowded, exchange, lambda x: x, part))
        return [x.reshape(-1, width) for x in moved]

    outgoing, position = pl.pallas_call(
        functools.partial(
            route_kernel,
            devices=devices,
            capacity=capacity,
            first_slots=first_slots,
            blocks=blocks,
            per_column=per_column,
        ),
        out_shape=[shape((devices, capacity), i32), shape((requests // LANES, LANES), i32)],
        in_specs=[VMEM],
        out_specs=[VMEM, VMEM],
        name="route",
    )(block_ids.T)
    incoming = exchange(outgoing)

    field, _ = lax.optimization_barrier((log_density, outgoing))
    xfirst, xlast, yfirst, ylast = pl.pallas_call(
        edges_kernel,
        out_shape=[
            shape((2, cells_y, depth), bf16),
            shape((2, cells_y, depth), bf16),
            shape((2, cells_x, depth), f32),
            shape((2, cells_x, depth), f32),
        ],
        in_specs=[ANY],
        out_specs=[VMEM] * 4,
        scratch_shapes=[
            pltpu.VMEM((2, 2, cells_y, depth), f32),
            pltpu.VMEM((2, cells_x, 8, depth), f32),
            pltpu.SemaphoreType.DMA((4,)),
        ],
        compiler_params=pltpu.CompilerParams(vmem_limit_bytes=56 * MIB),
        cost_estimate=pl.CostEstimate(flops=0, bytes_accessed=2 * MIB, transcendentals=0),
        name="edges",
    )(field)
    incoming, *edges = lax.optimization_barrier((incoming, xfirst, xlast, yfirst, ylast))
    wanted = incoming.reshape(-1)

    parts = 8
    *served, crowded = pl.pallas_call(
        functools.partial(serve_kernel, capacity=capacity, first_slots=first_slots),
        out_shape=[shape((devices * n, width), bf16) for n in slots_of] + [shape((1,), i32)],
        in_specs=[SMEM, ANY],
        out_specs=[VMEM] * exchanges + [SMEM],
        scratch_shapes=[
            pltpu.VMEM(field_shape, f32),
            pltpu.VMEM((blocks + capacity, 1, width), f32),
            pltpu.SemaphoreType.DMA((parts,)),
        ],
        compiler_params=pltpu.CompilerParams(vmem_limit_bytes=56 * MIB),
        cost_estimate=pl.CostEstimate(
            flops=cells, bytes_accessed=6 * MIB, transcendentals=cells
        ),
        name="serve",
    )(wanted, log_density)
    crowded = crowded[0] != 0

    incoming_late, *edges, _ = lax.optimization_barrier((incoming, *edges, served[0]))
    slot_lists = [
        incoming_late[:, :first_slots].reshape(-1, LANES),
        (incoming_late[:, first_slots:] & (MARK - 1)).reshape(-1, LANES),
    ][:exchanges]
    match = pl.pallas_call(
        match_kernel,
        out_shape=shape((all_slots, LANES), bf16),
        in_specs=[VMEM],
        out_specs=VMEM,
        compiler_params=pltpu.CompilerParams(vmem_limit_bytes=8 * MIB),
        cost_estimate=pl.CostEstimate(flops=10**9, bytes_accessed=MIB, transcendentals=0),
        name="match",
    )(jnp.concatenate(slot_lists, axis=0))
    returned = exchange_rows(served, crowded)
    xlo, xhi, ylo, yhi = halo(*edges)
    *returned, match, ylo, yhi = lax.optimization_barrier((*returned, match, ylo, yhi))

    chunks = blocks_dev * stars // LANES
    in_set = chunks // 4
    live = jnp.arange(stars)[None, :] < star_counts[:, None]
    live_inverse = jnp.where(live, inverse_var, 0.0)
    extinction, *parcel = pl.pallas_call(
        functools.partial(star_kernel, exchanges=exchanges),
        out_shape=[shape((chunks, LANES), f32)]
        + [shape((devices * n, width), bf16) for n in slots_of],
        in_specs=[SMEM, VMEM, VMEM, ANY] + [VMEM] * exchanges,
        out_specs=[VMEM] * (1 + exchanges),
        scratch_shapes=[
            pltpu.VMEM((2, in_set, blocks_dev // chunks, slots, stars, width), bf16),
            pltpu.VMEM((all_slots, 1, width), f32),
            pltpu.VMEM((in_set * LANES // stars * slots, width), f32),
            pltpu.VMEM((all_slots, 1, width), f32),
            pltpu.SemaphoreType.DMA((2, in_set)),
        ],
        compiler_params=pltpu.CompilerParams(vmem_limit_bytes=50 * MIB),
        cost_estimate=pl.CostEstimate(
            flops=4 * weights.size, bytes_accessed=2 * weights.size, transcendentals=0
        ),
        name="stars",
    )(
        position.reshape(slots // 2, 2, blocks_dev).transpose(2, 1, 0).reshape(requests),
        observed.reshape(chunks, LANES),
        live_inverse.reshape(chunks, LANES),
        weights,
        *returned,
    )
    arrived = exchange_rows(parcel, crowded)

    field_late, _ = lax.optimization_barrier((log_density, parcel[0]))
    base = pl.pallas_call(
        prior_kernel,
        out_shape=shape(field_shape, f32),
        in_specs=[VMEM] * 5,
        out_specs=VMEM,
        scratch_shapes=[
            pltpu.VMEM((cells_x + 4, cells_y + 16, depth), f32),
            pltpu.VMEM((cells_x + 2, cells_y + 16, depth), f32),
        ],
        compiler_params=pltpu.CompilerParams(vmem_limit_bytes=32 * MIB),
        cost_estimate=pl.CostEstimate(
            flops=30 * cells, bytes_accessed=8 * cells, transcendentals=0
        ),
        name="prior",
    )(field_late, xlo, xhi, ylo, yhi)

    new_log_density = pl.pallas_call(
        functools.partial(
            finish_kernel, exchanges=exchanges, capacity=capacity, first_slots=first_slots
        ),
        out_shape=shape(field_shape, f32),
        in_specs=[SMEM, VMEM, ANY, ANY] + [VMEM] * exchanges,
        out_specs=ANY,
        scratch_shapes=[
            pltpu.VMEM((blocks + capacity, 1, width), f32),
            pltpu.VMEM((all_slots, width), f32),
            pltpu.VMEM(field_shape, f32),
            pltpu.VMEM(field_shape, f32),
            pltpu.VMEM(field_shape, f32),
            pltpu.SemaphoreType.DMA((2,)),
            pltpu.SemaphoreType.DMA((parts,)),
        ],
        compiler_params=pltpu.CompilerParams(vmem_limit_bytes=50 * MIB),
        cost_estimate=pl.CostEstimate(
            flops=4 * cells, bytes_accessed=12 * cells, transcendentals=cells
        ),
        name="finish",
    )(wanted, match, log_density, base, *arrived)
    return new_log_density, extinction.reshape(blocks_dev, stars)


def solution(mesh):
    placed = (
        P("gx", "gy", None),
        P(("gx", "gy"), None, None, None),
        P(("gx", "gy"), None),
        P(("gx", "gy"), None),
        P(("gx", "gy")),
        P(("gx", "gy"), None),
    )
    return jax.shard_map(
        on_device,
        mesh=mesh,
        in_specs=placed,
        out_specs=(P("gx", "gy", None), P(("gx", "gy"), None)),
        check_vma=False,
    )
```

```python
import functools

import jax
import jax.numpy as jnp
from jax import lax
from jax.experimental import pallas as pl
from jax.experimental.pallas import tpu as pltpu
from jax.sharding import PartitionSpec as P

shift_kappa = 0.5
prior_weight = 0.05
step_rate = 2.0

LANES = 128
GROUP = 16
MIB = 1 << 20
MARK = 1 << 16

CONTRACT_LANES = (((1,), (1,)), ((), ()))


def split_by(value, size):
    if size & (size - 1) == 0:
        high = value >> (size.bit_length() - 1)
        return high, value & (size - 1)
    high = value // size
    return high, value - high * size


def route_kernel(
    ids_ref, outgoing_ref, position_ref, *, devices, capacity, first_slots, blocks, per_column
):
    half = ids_ref.shape[0] // 2
    ids = jnp.concatenate([ids_ref[:half, :], ids_ref[half:, :]], axis=1)
    lane = lax.broadcasted_iota(jnp.int32, (LANES, LANES), 1)
    row = lax.broadcasted_iota(jnp.int32, (LANES, LANES), 0)
    upper = jnp.where(row <= lane, 1.0, 0.0).astype(jnp.bfloat16)
    size_x, size_y = lax.axis_size("gx"), lax.axis_size("gy")
    along_y, along_x = split_by(lax.broadcasted_iota(jnp.int32, (devices, LANES), 0), size_x)
    tile_no = along_x * size_y + along_y
    slot_no = lax.broadcasted_iota(jnp.int32, (capacity, LANES), 0)
    before = jnp.zeros((devices, 1), jnp.float32)
    lists = jnp.zeros((2 * devices, capacity), jnp.float32)
    for chunk in range(half):
        target, local = split_by(ids[chunk : chunk + 1, :], blocks)
        column, part = split_by(local, per_column)
        local = ((column >> 3) * per_column + part) * 8 + (column & 7)
        hit = tile_no == target
        onehot = jnp.where(hit, 1.0, 0.0)
        upto = before + jnp.dot(
            onehot.astype(jnp.bfloat16), upper, preferred_element_type=jnp.float32
        )
        before = upto[:, LANES - 1 :]
        rank = jnp.sum(onehot * upto, axis=0, keepdims=True).astype(jnp.int32) - 1
        in_slot = jnp.where(slot_no == rank, 1.0, 0.0).astype(jnp.bfloat16)
        high = ((local >> 7) + 1).astype(jnp.float32)
        low = (local & 127).astype(jnp.float32)
        digits = jnp.concatenate([jnp.where(hit, high, 0.0), jnp.where(hit, low, 0.0)], axis=0)
        lists = lists + lax.dot_general(
            digits.astype(jnp.bfloat16),
            in_slot,
            CONTRACT_LANES,
            preferred_element_type=jnp.float32,
        )
        last_slots = capacity - first_slots
        position_ref[chunk : chunk + 1, :] = jnp.where(
            rank < first_slots,
            target * first_slots + rank,
            devices * first_slots + target * last_slots + rank - first_slots,
        )
    high, low = lists[:devices], lists[devices:]
    wanted = ((high - 1.0) * 128.0 + low).astype(jnp.int32)
    filled = before.astype(jnp.int32)
    me = lax.axis_index("gx") * size_y + lax.axis_index("gy")
    fullest = jnp.max(jnp.where(tile_no[:, :1] == me, 0.0, before), axis=0, keepdims=True)
    listed = jnp.where(high > 0.5, wanted, blocks + filled)
    if first_slots < capacity:
        slot = lax.broadcasted_iota(jnp.int32, (devices, capacity), 1)
        mark = fullest.astype(jnp.int32) * MARK
        listed = listed + jnp.where(slot == capacity - 1, mark, 0)
    outgoing_ref[...] = listed


def edges_kernel(
    field_hbm, xfirst_ref, xlast_ref, yfirst_ref, ylast_ref, planes_ref, strips_ref, sems
):
    cells_x, cells_y, _ = field_hbm.shape
    copies = [
        pltpu.make_async_copy(field_hbm.at[pl.ds(0, 2)], planes_ref.at[0], sems.at[0]),
        pltpu.make_async_copy(field_hbm.at[pl.ds(cells_x - 2, 2)], planes_ref.at[1], sems.at[1]),
        pltpu.make_async_copy(field_hbm.at[:, pl.ds(0, 8)], strips_ref.at[0], sems.at[2]),
        pltpu.make_async_copy(
            field_hbm.at[:, pl.ds(cells_y - 8, 8)], strips_ref.at[1], sems.at[3]
        ),
    ]
    for copy in copies:
        copy.start()
    for copy in copies:
        copy.wait()
    xfirst_ref[...] = planes_ref[0].astype(xfirst_ref.dtype)
    xlast_ref[...] = planes_ref[1].astype(xlast_ref.dtype)
    for h in range(2):
        for x in range(cells_x):
            yfirst_ref[h, x : x + 1, :] = strips_ref[0, x, h : h + 1, :]
            ylast_ref[h, x : x + 1, :] = strips_ref[1, x, 6 + h : 7 + h, :]


def for_each_group(incoming_ref, visit, capacity, first_slots, blocks):
    sources = incoming_ref.shape[0] // capacity
    last_slots = capacity - first_slots
    together = 4

    def groups_of(source):
        last = incoming_ref[source * capacity + capacity - 1] & (MARK - 1)
        return (jnp.where(last < blocks, capacity, last - blocks) + GROUP - 1) // GROUP

    def some_sources(quad, carry):
        own = [quad * together + i for i in range(together)]
        most = functools.reduce(jnp.maximum, [groups_of(source) for source in own])

        def one_group(group, carry):
            slot = group * GROUP
            for source in own:
                listed = incoming_ref.at[pl.ds(source * capacity + slot, GROUP)]
                wanted = [listed[j] for j in range(GROUP)]
                visit(wanted, pl.multiple_of(source * first_slots + slot, GROUP), 0)
            return carry

        return lax.fori_loop(0, jnp.minimum(most, first_slots // GROUP), one_group, carry)

    lax.fori_loop(0, sources // together, some_sources, 0)
    if last_slots == 0:
        return

    def one_source(source, carry):
        def one_group(group, carry):
            slot = group * GROUP
            listed = incoming_ref.at[pl.ds(source * capacity + slot, GROUP)]
            wanted = [listed[j] & (MARK - 1) for j in range(GROUP)]
            visit(wanted, pl.multiple_of(source * last_slots + slot - first_slots, GROUP), 1)
            return carry

        return lax.fori_loop(first_slots // GROUP, groups_of(source), one_group, carry)

    lax.fori_loop(0, sources, one_source, 0)


def serve_kernel(incoming_ref, field_hbm, *refs, capacity, first_slots):
    *served_refs, crowded_ref, rows_ref, sems = refs
    blocks = field_hbm.shape[0]
    load = pltpu.make_async_copy(field_hbm, rows_ref.at[pl.ds(0, blocks)], sems.at[0])
    load.start()

    def mark_of(source, most):
        return jnp.maximum(most, incoming_ref[source * capacity + capacity - 1] >> 16)

    fullest = lax.fori_loop(0, incoming_ref.shape[0] // capacity, mark_of, jnp.int32(0))
    crowded_ref[0] = jnp.where(fullest > first_slots, 1, 0)
    rows_ref[blocks:] = jnp.zeros((rows_ref.shape[0] - blocks, 1, LANES), jnp.float32)
    load.wait()

    def visit(wanted, row, list_part):
        rows = jnp.concatenate([rows_ref[at] for at in wanted], axis=0)
        served_refs[list_part][pl.ds(row, GROUP), :] = jnp.exp(rows).astype(jnp.bfloat16)

    for_each_group(incoming_ref, visit, capacity, first_slots, blocks)


def match_kernel(incoming_ref, match_ref):
    lane = lax.broadcasted_iota(jnp.int32, (LANES, LANES), 1)
    row = lax.broadcasted_iota(jnp.int32, (LANES, LANES), 0)
    ones = jnp.ones((LANES, LANES), jnp.bfloat16)
    same_group = (lane // GROUP) == (row // GROUP)

    def one_row(i):
        wanted = incoming_ref[pl.ds(i, 1), :]
        high = jnp.where(lane == row, (wanted >> 7).astype(jnp.float32), 0.0).astype(jnp.bfloat16)
        low = jnp.where(lane == row, (wanted & 127).astype(jnp.float32), 0.0).astype(jnp.bfloat16)
        down = 128.0 * jnp.dot(high, ones, preferred_element_type=jnp.float32)
        down = down + jnp.dot(low, ones, preferred_element_type=jnp.float32)
        same = (down == wanted.astype(jnp.float32)) & same_group
        match_ref[pl.ds(pl.multiple_of(i * LANES, LANES), LANES), :] = jnp.where(
            same, 1.0, 0.0
        ).astype(jnp.bfloat16)

    def some_rows(i, carry):
        for j in range(4):
            one_row(4 * i + j)
        return carry

    lax.fori_loop(0, incoming_ref.shape[0] // 4, some_rows, 0)


def star_kernel(position_ref, observed_ref, inverse_ref, weights_hbm, *refs, exchanges):
    returned_refs, refs = refs[:exchanges], refs[exchanges:]
    extinction_ref, refs = refs[0], refs[1:]
    parcel_refs, refs = refs[:exchanges], refs[exchanges:]
    weights_ref, returned_rows, sens_ref, parcel_rows, sems = refs
    held, per, slots, stars, width = weights_ref.shape
    chunks = extinction_ref.shape[0]
    per_chunk = per * slots
    fold = LANES // stars
    all_slots = parcel_rows.shape[0]
    ahead = 2
    lane = lax.broadcasted_iota(jnp.int32, (8, LANES), 1)
    row = lax.broadcasted_iota(jnp.int32, (8, LANES), 0)
    star_group = lane // stars
    own_slot = [row == star_group + fold * h for h in range(8 // fold)]

    def load(chunk, u):
        source = weights_hbm.at[pl.ds(chunk * per, per)]
        return pltpu.make_async_copy(source, weights_ref.at[u], sems.at[u])

    def extinctions(u, chunk, places):
        sums = []
        for b in range(per):
            total = jnp.zeros((stars, width), jnp.float32)
            for k in range(slots):
                fetched = returned_rows[places[u * per_chunk + b * slots + k]]
                total = total + weights_ref[u, b, k].astype(jnp.float32) * fetched
            sums.append(total)
        extinction = lax.dot_general(
            jnp.ones((8, width), jnp.float32),
            jnp.concatenate(sums, axis=0),
            CONTRACT_LANES,
            precision=lax.Precision.HIGHEST,
            preferred_element_type=jnp.float32,
        )
        here = pl.ds(chunk, 1)
        extinction_ref[here, :] = extinction[:1]
        return inverse_ref[here, :] * (extinction - observed_ref[here, :])

    def sensitivities(u, weighted):
        for b in range(per):
            spread = jnp.where(star_group == b, weighted, 0.0)
            shift = stars
            while shift < LANES:
                spread = spread + pltpu.roll(spread, shift, 1)
                shift *= 2
            left = jnp.concatenate(
                [jnp.where(own, spread, 0.0) for own in own_slot], axis=1
            ).astype(jnp.bfloat16)
            eights = [weights_ref[u, b, 8 * j : 8 * j + 8] for j in range(slots // 8)]
            right = jnp.concatenate([x.reshape(8 * stars, width) for x in eights], axis=1)
            sens = jnp.dot(left, right, preferred_element_type=jnp.float32)
            for j in range(slots // 8):
                first = u * per_chunk + b * slots + 8 * j
                sens_ref[first : first + 8, :] = sens[:, j * width : (j + 1) * width]

    def scatter(u, places):
        for i in range(u * per_chunk, (u + 1) * per_chunk):
            parcel_rows[places[i]] = sens_ref[i : i + 1, :]

    for u in range(ahead):
        load(u, u).start()
    start = 0
    for returned_ref in returned_refs:
        span = slice(start, start + returned_ref.shape[0])
        returned_rows.reshape(all_slots, width)[span, :] = returned_ref[...].astype(jnp.float32)
        start = span.stop
    parcel_rows.reshape(all_slots, width)[...] = jnp.zeros((all_slots, width), jnp.float32)

    def one_round(i, carry):
        first = i * held
        size = held * per_chunk
        places = position_ref.at[pl.ds(pl.multiple_of(first * per_chunk, size), size)]
        weighted = {}
        for u in range(held + 2):
            if u < held:
                load(first + u, u).wait()
                if u + ahead < held:
                    load(first + u + ahead, u + ahead).start()
                else:

                    @pl.when(first + u + ahead < chunks)
                    def _():
                        load(first + u + ahead, u + ahead - held).start()

                weighted[u] = extinctions(u, first + u, places)
            if 1 <= u <= held:
                sensitivities(u - 1, weighted[u - 1])
            if u >= 2:
                scatter(u - 2, places)
        return carry

    lax.fori_loop(0, chunks // held, one_round, 0)
    start = 0
    for parcel_ref in parcel_refs:
        span = slice(start, start + parcel_ref.shape[0])
        parcel_ref[...] = parcel_rows.reshape(all_slots, width)[span, :].astype(jnp.bfloat16)
        start = span.stop


def prior_kernel(field_ref, xlo_ref, xhi_ref, ylo_ref, yhi_ref, out_ref, padded, smooth):
    cells_x, cells_y, depth = field_ref.shape
    rows = padded.shape[1]
    gx, gy = lax.axis_index("gx"), lax.axis_index("gy")
    last_gx, last_gy = lax.axis_size("gx") - 1, lax.axis_size("gy") - 1
    z = lax.broadcasted_iota(jnp.int32, (rows, depth), 1)
    y = lax.broadcasted_iota(jnp.int32, (rows, depth), 0) - 8
    inside_y = ((y >= 0) | (gy > 0)) & ((y < cells_y) | (gy < last_gy))

    def operate(center, below, above):
        beside = below + above
        beside = beside + pltpu.roll(center, 1, 0) + pltpu.roll(center, rows - 1, 0)
        beside = beside + jnp.where(z == 0, 0.0, pltpu.roll(center, 1, 1))
        beside = beside + jnp.where(z == depth - 1, 0.0, pltpu.roll(center, depth - 1, 1))
        return (shift_kappa + 6.0) * center - beside

    def fill(plane, source):
        padded[plane, 8 : 8 + cells_y, :] = source
        padded[plane, 0:8, :] = jnp.zeros((8, depth), jnp.float32)
        padded[plane, 8 + cells_y :, :] = jnp.zeros((8, depth), jnp.float32)
        for h in range(2):
            padded[plane, 6 + h : 7 + h, :] = ylo_ref[h, pl.ds(plane, 1), :]
            padded[plane, 8 + cells_y + h : 9 + cells_y + h, :] = yhi_ref[h, pl.ds(plane, 1), :]

    for h in range(2):
        fill(h, xlo_ref[h].astype(jnp.float32))
        fill(cells_x + 2 + h, xhi_ref[h].astype(jnp.float32))

    def fill_own(x, carry):
        fill(x + 2, field_ref[x])
        return carry

    lax.fori_loop(0, cells_x, fill_own, 0)

    def smooth_plane(plane, carry):
        value = operate(padded[plane], padded[plane - 1], padded[plane + 1])
        inside = ((plane > 1) | (gx > 0)) & ((plane < cells_x + 2) | (gx < last_gx))
        smooth[plane - 1] = jnp.where(inside_y & inside, value, 0.0)
        return carry

    lax.fori_loop(1, cells_x + 3, smooth_plane, 0)

    def out_plane(x, carry):
        prior = operate(smooth[x + 1], smooth[x], smooth[x + 2])
        out_ref[x] = field_ref[x] - (step_rate * prior_weight) * prior[8 : 8 + cells_y]
        return carry

    lax.fori_loop(0, cells_x, out_plane, 0)


def finish_kernel(
    incoming_ref, match_ref, field_hbm, base_hbm, *refs, exchanges, capacity, first_slots
):
    arrived_refs, refs = refs[:exchanges], refs[exchanges:]
    out_hbm, collected, rows_ref, field_ref, base_ref, out_ref, in_sems, out_sems = refs
    cells_x, cells_y, depth = field_ref.shape
    per_column = depth // LANES
    parts = out_sems.shape[0]
    planes = cells_x // parts
    blocks = cells_x * cells_y * per_column
    loads = [
        pltpu.make_async_copy(field_hbm, field_ref, in_sems.at[0]),
        pltpu.make_async_copy(base_hbm, base_ref, in_sems.at[1]),
    ]
    for load in loads:
        load.start()
    collected_rows = collected.reshape(collected.shape[0], LANES)
    start = 0
    for arrived_ref in arrived_refs:
        for i in range(arrived_ref.shape[0] // LANES):
            span = slice(start + i * LANES, start + (i + 1) * LANES)
            rows_ref[span, :] = -step_rate * jnp.dot(
                match_ref[span, :],
                arrived_ref[i * LANES : (i + 1) * LANES, :],
                preferred_element_type=jnp.float32,
            )
        start += arrived_ref.shape[0]
    collected_rows[...] = jnp.zeros_like(collected_rows)

    part_starts = [0, arrived_refs[0].shape[0]]

    def visit(wanted, row, list_part):
        row = pl.multiple_of(row + part_starts[list_part], GROUP)
        rows = rows_ref.at[pl.ds(row, GROUP)]
        sums = [collected[wanted[j]] + rows[j : j + 1, :] for j in range(GROUP)]
        for j in range(GROUP):
            collected[wanted[j]] = sums[j]

    for_each_group(incoming_ref, visit, capacity, first_slots, blocks)
    for load in loads:
        load.wait()

    def store(part):
        span = pl.ds(part * planes, planes)
        return pltpu.make_async_copy(out_ref.at[span], out_hbm.at[span], out_sems.at[part])

    def one_plane(x, carry):
        for yb in range(cells_y // 8):
            for part in range(per_column):
                at = pl.multiple_of(((x * (cells_y // 8) + yb) * per_column + part) * 8, 8)
                here = (x, slice(8 * yb, 8 * yb + 8), slice(part * LANES, (part + 1) * LANES))
                out_ref[here] = base_ref[here] + collected_rows[pl.ds(at, 8), :] * jnp.exp(
                    field_ref[here]
                )
        return carry

    for part in range(parts):
        lax.fori_loop(part * planes, (part + 1) * planes, one_plane, 0)
        store(part).start()
    for part in range(parts):
        store(part).wait()


def both_ways(first, last, axis):
    peers = lax.axis_size(axis)
    up = [(i, i + 1) for i in range(peers - 1)]
    down = [(j, i) for i, j in up]
    return lax.ppermute(last, axis, up), lax.ppermute(first, axis, down)


def halo(xfirst, xlast, yfirst, ylast):
    xlo, xhi = both_ways(xfirst, xlast, "gx")

    def rows(own, at):
        ends = [x[:, at].transpose(1, 0, 2) for x in (xlo, xhi)]
        return jnp.concatenate([ends[0], own.astype(xlo.dtype), ends[1]], axis=1)

    ylo, yhi = both_ways(rows(yfirst, slice(0, 2)), rows(ylast, slice(-2, None)), "gy")
    return xlo, xhi, ylo.astype(jnp.float32), yhi.astype(jnp.float32)


VMEM = pl.BlockSpec(memory_space=pltpu.VMEM)
SMEM = pl.BlockSpec(memory_space=pltpu.SMEM)
ANY = pl.BlockSpec(memory_space=pl.ANY)


def on_device(log_density, weights, observed, inverse_var, star_counts, block_ids):
    cells_x, cells_y, depth = log_density.shape
    blocks_dev, slots, stars, width = weights.shape
    devices = lax.axis_size("gx") * lax.axis_size("gy")
    requests = blocks_dev * slots
    capacity = 2 * requests // devices
    first_slots = min(capacity, -(-3 * capacity // (4 * GROUP)) * GROUP)
    slots_of = [n for n in (first_slots, capacity - first_slots) if n > 0]
    exchanges = len(slots_of)
    all_slots = devices * capacity
    per_column = depth // width
    blocks = cells_x * cells_y * per_column
    cells = log_density.size
    field_shape = (cells_x, cells_y, depth)
    mesh_axes = ("gx", "gy")
    f32, bf16, i32 = jnp.float32, jnp.bfloat16, jnp.int32
    shape = jax.ShapeDtypeStruct

    def to_rows(x):
        x = x.reshape(cells_x, cells_y // 8, 8, per_column, width)
        return x.transpose(0, 1, 3, 2, 4).reshape(blocks, 1, width)

    def exchange(x):
        return lax.all_to_all(x, mesh_axes, split_axis=0, concat_axis=0, tiled=True)

    def exchange_rows(parts, crowded):
        moved = [parts[0].reshape(devices, first_slots, width)]
        moved[0] = exchange(moved[0])
        for part in parts[1:]:
            part = part.reshape(devices, capacity - first_slots, width)
            moved.append(lax.cond(crowded, exchange, lambda x: x, part))
        return [x.reshape(-1, width) for x in moved]

    outgoing, position = pl.pallas_call(
        functools.partial(
            route_kernel,
            devices=devices,
            capacity=capacity,
            first_slots=first_slots,
            blocks=blocks,
            per_column=per_column,
        ),
        out_shape=[shape((devices, capacity), i32), shape((requests // LANES, LANES), i32)],
        in_specs=[VMEM],
        out_specs=[VMEM, VMEM],
        name="route",
    )(block_ids.T)
    incoming = lax.all_to_all(outgoing, "gy", split_axis=0, concat_axis=0, tiled=True)
    incoming = incoming.reshape(lax.axis_size("gy"), lax.axis_size("gx"), capacity)
    incoming = incoming.transpose(1, 0, 2).reshape(devices, capacity)
    incoming = lax.all_to_all(incoming, "gx", split_axis=0, concat_axis=0, tiled=True)

    field, _ = lax.optimization_barrier((log_density, outgoing))
    xfirst, xlast, yfirst, ylast = pl.pallas_call(
        edges_kernel,
        out_shape=[
            shape((2, cells_y, depth), bf16),
            shape((2, cells_y, depth), bf16),
            shape((2, cells_x, depth), f32),
            shape((2, cells_x, depth), f32),
        ],
        in_specs=[ANY],
        out_specs=[VMEM] * 4,
        scratch_shapes=[
            pltpu.VMEM((2, 2, cells_y, depth), f32),
            pltpu.VMEM((2, cells_x, 8, depth), f32),
            pltpu.SemaphoreType.DMA((4,)),
        ],
        compiler_params=pltpu.CompilerParams(vmem_limit_bytes=56 * MIB),
        cost_estimate=pl.CostEstimate(flops=0, bytes_accessed=2 * MIB, transcendentals=0),
        name="edges",
    )(field)
    incoming, *edges = lax.optimization_barrier((incoming, xfirst, xlast, yfirst, ylast))
    wanted = incoming.reshape(-1)

    *served, crowded = pl.pallas_call(
        functools.partial(serve_kernel, capacity=capacity, first_slots=first_slots),
        out_shape=[shape((devices * n, width), bf16) for n in slots_of] + [shape((1,), i32)],
        in_specs=[SMEM, ANY],
        out_specs=[VMEM] * exchanges + [SMEM],
        scratch_shapes=[
            pltpu.VMEM((blocks + capacity, 1, width), f32),
            pltpu.SemaphoreType.DMA((1,)),
        ],
        compiler_params=pltpu.CompilerParams(vmem_limit_bytes=56 * MIB),
        cost_estimate=pl.CostEstimate(
            flops=cells, bytes_accessed=6 * MIB, transcendentals=cells
        ),
        name="serve",
    )(wanted, to_rows(log_density))
    crowded = crowded[0] != 0

    incoming_late, *edges, _ = lax.optimization_barrier((incoming, *edges, served[0]))
    slot_lists = [
        incoming_late[:, :first_slots].reshape(-1, LANES),
        (incoming_late[:, first_slots:] & (MARK - 1)).reshape(-1, LANES),
    ][:exchanges]
    match = pl.pallas_call(
        match_kernel,
        out_shape=shape((all_slots, LANES), bf16),
        in_specs=[VMEM],
        out_specs=VMEM,
        compiler_params=pltpu.CompilerParams(vmem_limit_bytes=8 * MIB),
        cost_estimate=pl.CostEstimate(flops=10**9, bytes_accessed=MIB, transcendentals=0),
        name="match",
    )(jnp.concatenate(slot_lists, axis=0))
    returned = exchange_rows(served, crowded)
    xlo, xhi, ylo, yhi = halo(*edges)
    *returned, match, ylo, yhi = lax.optimization_barrier((*returned, match, ylo, yhi))

    chunks = blocks_dev * stars // LANES
    held = chunks // 2
    live = jnp.arange(stars)[None, :] < star_counts[:, None]
    live_inverse = jnp.where(live, inverse_var, 0.0)
    extinction, *parcel = pl.pallas_call(
        functools.partial(star_kernel, exchanges=exchanges),
        out_shape=[shape((chunks, LANES), f32)]
        + [shape((devices * n, width), bf16) for n in slots_of],
        in_specs=[SMEM, VMEM, VMEM, ANY] + [VMEM] * exchanges,
        out_specs=[VMEM] * (1 + exchanges),
        scratch_shapes=[
            pltpu.VMEM((held, blocks_dev // chunks, slots, stars, width), bf16),
            pltpu.VMEM((all_slots, 1, width), f32),
            pltpu.VMEM((held * (blocks_dev // chunks) * slots, width), f32),
            pltpu.VMEM((all_slots, 1, width), f32),
            pltpu.SemaphoreType.DMA((held,)),
        ],
        compiler_params=pltpu.CompilerParams(vmem_limit_bytes=50 * MIB),
        cost_estimate=pl.CostEstimate(
            flops=4 * weights.size, bytes_accessed=2 * weights.size, transcendentals=0
        ),
        name="stars",
    )(
        position.reshape(slots // 2, 2, blocks_dev).transpose(2, 1, 0).reshape(requests),
        observed.reshape(chunks, LANES),
        live_inverse.reshape(chunks, LANES),
        weights,
        *returned,
    )
    arrived = exchange_rows(parcel, crowded)

    field_late, _ = lax.optimization_barrier((log_density, parcel[0]))
    base = pl.pallas_call(
        prior_kernel,
        out_shape=shape(field_shape, f32),
        in_specs=[VMEM] * 5,
        out_specs=VMEM,
        scratch_shapes=[
            pltpu.VMEM((cells_x + 4, cells_y + 16, depth), f32),
            pltpu.VMEM((cells_x + 2, cells_y + 16, depth), f32),
        ],
        compiler_params=pltpu.CompilerParams(vmem_limit_bytes=32 * MIB),
        cost_estimate=pl.CostEstimate(
            flops=30 * cells, bytes_accessed=8 * cells, transcendentals=0
        ),
        name="prior",
    )(field_late, xlo, xhi, ylo, yhi)

    parts = 8
    new_log_density = pl.pallas_call(
        functools.partial(
            finish_kernel, exchanges=exchanges, capacity=capacity, first_slots=first_slots
        ),
        out_shape=shape(field_shape, f32),
        in_specs=[SMEM, VMEM, ANY, ANY] + [VMEM] * exchanges,
        out_specs=ANY,
        scratch_shapes=[
            pltpu.VMEM((blocks + capacity, 1, width), f32),
            pltpu.VMEM((all_slots, width), f32),
            pltpu.VMEM(field_shape, f32),
            pltpu.VMEM(field_shape, f32),
            pltpu.VMEM(field_shape, f32),
            pltpu.SemaphoreType.DMA((2,)),
            pltpu.SemaphoreType.DMA((parts,)),
        ],
        compiler_params=pltpu.CompilerParams(vmem_limit_bytes=50 * MIB),
        cost_estimate=pl.CostEstimate(
            flops=4 * cells, bytes_accessed=12 * cells, transcendentals=cells
        ),
        name="finish",
    )(wanted, match, log_density, base, *arrived)
    return new_log_density, extinction.reshape(blocks_dev, stars)


def solution(mesh):
    placed = (
        P("gx", "gy", None),
        P(("gx", "gy"), None, None, None),
        P(("gx", "gy"), None),
        P(("gx", "gy"), None),
        P(("gx", "gy")),
        P(("gx", "gy"), None),
    )
    return jax.shard_map(
        on_device,
        mesh=mesh,
        in_specs=placed,
        out_specs=(P("gx", "gy", None), P(("gx", "gy"), None)),
        check_vma=False,
    )
```

```python
import functools

import jax
import jax.numpy as jnp
from jax import lax
from jax.experimental import pallas as pl
from jax.experimental.pallas import tpu as pltpu
from jax.sharding import PartitionSpec as P

shift_kappa = 0.5
prior_weight = 0.05
step_rate = 2.0

LANES = 128
GROUP = 16
MIB = 1 << 20
MARK = 1 << 16

CONTRACT_LANES = (((1,), (1,)), ((), ()))


def split_by(value, size):
    if size & (size - 1) == 0:
        high = value >> (size.bit_length() - 1)
        return high, value & (size - 1)
    high = value // size
    return high, value - high * size


def route_kernel(
    ids_ref, outgoing_ref, position_ref, *, devices, capacity, first_slots, blocks, per_column
):
    half = ids_ref.shape[0] // 2
    ids = jnp.concatenate([ids_ref[:half, :], ids_ref[half:, :]], axis=1)
    lane = lax.broadcasted_iota(jnp.int32, (LANES, LANES), 1)
    row = lax.broadcasted_iota(jnp.int32, (LANES, LANES), 0)
    upper = jnp.where(row <= lane, 1.0, 0.0).astype(jnp.bfloat16)
    tile_no = lax.broadcasted_iota(jnp.int32, (devices, LANES), 0)
    slot_no = lax.broadcasted_iota(jnp.int32, (capacity, LANES), 0)
    before = jnp.zeros((devices, 1), jnp.float32)
    lists = jnp.zeros((2 * devices, capacity), jnp.float32)
    for chunk in range(half):
        target, local = split_by(ids[chunk : chunk + 1, :], blocks)
        column, part = split_by(local, per_column)
        local = ((column >> 3) * per_column + part) * 8 + (column & 7)
        hit = tile_no == target
        onehot = jnp.where(hit, 1.0, 0.0)
        upto = before + jnp.dot(
            onehot.astype(jnp.bfloat16), upper, preferred_element_type=jnp.float32
        )
        before = upto[:, LANES - 1 :]
        rank = jnp.sum(onehot * upto, axis=0, keepdims=True).astype(jnp.int32) - 1
        in_slot = jnp.where(slot_no == rank, 1.0, 0.0).astype(jnp.bfloat16)
        high = ((local >> 7) + 1).astype(jnp.float32)
        low = (local & 127).astype(jnp.float32)
        digits = jnp.concatenate([jnp.where(hit, high, 0.0), jnp.where(hit, low, 0.0)], axis=0)
        lists = lists + lax.dot_general(
            digits.astype(jnp.bfloat16),
            in_slot,
            CONTRACT_LANES,
            preferred_element_type=jnp.float32,
        )
        last_slots = capacity - first_slots
        position_ref[chunk : chunk + 1, :] = jnp.where(
            rank < first_slots,
            target * first_slots + rank,
            devices * first_slots + target * last_slots + rank - first_slots,
        )
    high, low = lists[:devices], lists[devices:]
    wanted = ((high - 1.0) * 128.0 + low).astype(jnp.int32)
    filled = before.astype(jnp.int32)
    me = lax.axis_index("gx") * lax.axis_size("gy") + lax.axis_index("gy")
    fullest = jnp.max(jnp.where(tile_no[:, :1] == me, 0.0, before), axis=0, keepdims=True)
    listed = jnp.where(high > 0.5, wanted, blocks + filled)
    if first_slots < capacity:
        slot = lax.broadcasted_iota(jnp.int32, (devices, capacity), 1)
        mark = fullest.astype(jnp.int32) * MARK
        listed = listed + jnp.where(slot == capacity - 1, mark, 0)
    outgoing_ref[...] = listed


def edges_kernel(
    field_hbm, xfirst_ref, xlast_ref, yfirst_ref, ylast_ref, planes_ref, strips_ref, sems
):
    cells_x, cells_y, _ = field_hbm.shape
    copies = [
        pltpu.make_async_copy(field_hbm.at[pl.ds(0, 2)], planes_ref.at[0], sems.at[0]),
        pltpu.make_async_copy(field_hbm.at[pl.ds(cells_x - 2, 2)], planes_ref.at[1], sems.at[1]),
        pltpu.make_async_copy(field_hbm.at[:, pl.ds(0, 8)], strips_ref.at[0], sems.at[2]),
        pltpu.make_async_copy(
            field_hbm.at[:, pl.ds(cells_y - 8, 8)], strips_ref.at[1], sems.at[3]
        ),
    ]
    for copy in copies:
        copy.start()
    for copy in copies:
        copy.wait()
    xfirst_ref[...] = planes_ref[0].astype(xfirst_ref.dtype)
    xlast_ref[...] = planes_ref[1].astype(xlast_ref.dtype)
    for h in range(2):
        for x in range(cells_x):
            yfirst_ref[h, x : x + 1, :] = strips_ref[0, x, h : h + 1, :]
            ylast_ref[h, x : x + 1, :] = strips_ref[1, x, 6 + h : 7 + h, :]


def copies_in_parts(source, target, sems):
    parts = sems.shape[0]
    size = source.shape[0] // parts
    return [
        pltpu.make_async_copy(
            source.at[pl.ds(i * size, size)], target.at[pl.ds(i * size, size)], sems.at[i]
        )
        for i in range(parts)
    ]


def for_each_group(incoming_ref, visit, capacity, first_slots, blocks):
    sources = incoming_ref.shape[0] // capacity
    last_slots = capacity - first_slots
    together = 4

    def groups_of(source):
        last = incoming_ref[source * capacity + capacity - 1] & (MARK - 1)
        return (jnp.where(last < blocks, capacity, last - blocks) + GROUP - 1) // GROUP

    def some_sources(quad, carry):
        own = [quad * together + i for i in range(together)]
        most = functools.reduce(jnp.maximum, [groups_of(source) for source in own])

        def one_group(group, carry):
            slot = group * GROUP
            for source in own:
                listed = incoming_ref.at[pl.ds(source * capacity + slot, GROUP)]
                wanted = [listed[j] for j in range(GROUP)]
                visit(wanted, pl.multiple_of(source * first_slots + slot, GROUP), 0)
            return carry

        return lax.fori_loop(0, jnp.minimum(most, first_slots // GROUP), one_group, carry)

    lax.fori_loop(0, sources // together, some_sources, 0)
    if last_slots == 0:
        return

    def one_source(source, carry):
        def one_group(group, carry):
            slot = group * GROUP
            listed = incoming_ref.at[pl.ds(source * capacity + slot, GROUP)]
            wanted = [listed[j] & (MARK - 1) for j in range(GROUP)]
            visit(wanted, pl.multiple_of(source * last_slots + slot - first_slots, GROUP), 1)
            return carry

        return lax.fori_loop(first_slots // GROUP, groups_of(source), one_group, carry)

    lax.fori_loop(0, sources, one_source, 0)


def serve_kernel(incoming_ref, field_hbm, *refs, capacity, first_slots):
    *served_refs, crowded_ref, rows_ref, sems = refs
    blocks = field_hbm.shape[0]
    loads = copies_in_parts(field_hbm, rows_ref, sems)
    for load in loads:
        load.start()

    def mark_of(source, most):
        return jnp.maximum(most, incoming_ref[source * capacity + capacity - 1] >> 16)

    fullest = lax.fori_loop(0, incoming_ref.shape[0] // capacity, mark_of, jnp.int32(0))
    crowded_ref[0] = jnp.where(fullest > first_slots, 1, 0)
    rows_ref[blocks:] = jnp.zeros((rows_ref.shape[0] - blocks, 1, LANES), jnp.float32)
    for load in loads:
        load.wait()

    def visit(wanted, row, list_part):
        rows = jnp.concatenate([rows_ref[at] for at in wanted], axis=0)
        served_refs[list_part][pl.ds(row, GROUP), :] = jnp.exp(rows).astype(jnp.bfloat16)

    for_each_group(incoming_ref, visit, capacity, first_slots, blocks)


def match_kernel(incoming_ref, match_ref):
    lane = lax.broadcasted_iota(jnp.int32, (LANES, LANES), 1)
    row = lax.broadcasted_iota(jnp.int32, (LANES, LANES), 0)
    ones = jnp.ones((LANES, LANES), jnp.bfloat16)
    same_group = (lane // GROUP) == (row // GROUP)

    def one_row(i):
        wanted = incoming_ref[pl.ds(i, 1), :]
        high = jnp.where(lane == row, (wanted >> 7).astype(jnp.float32), 0.0).astype(jnp.bfloat16)
        low = jnp.where(lane == row, (wanted & 127).astype(jnp.float32), 0.0).astype(jnp.bfloat16)
        down = 128.0 * jnp.dot(high, ones, preferred_element_type=jnp.float32)
        down = down + jnp.dot(low, ones, preferred_element_type=jnp.float32)
        same = (down == wanted.astype(jnp.float32)) & same_group
        match_ref[pl.ds(pl.multiple_of(i * LANES, LANES), LANES), :] = jnp.where(
            same, 1.0, 0.0
        ).astype(jnp.bfloat16)

    def some_rows(i, carry):
        for j in range(4):
            one_row(4 * i + j)
        return carry

    lax.fori_loop(0, incoming_ref.shape[0] // 4, some_rows, 0)


def star_kernel(position_ref, observed_ref, inverse_ref, weights_hbm, *refs, exchanges):
    returned_refs, refs = refs[:exchanges], refs[exchanges:]
    extinction_ref, refs = refs[0], refs[1:]
    parcel_refs, refs = refs[:exchanges], refs[exchanges:]
    weights_ref, returned_rows, sens_ref, parcel_rows, sems = refs
    held, per, slots, stars, width = weights_ref.shape
    chunks = extinction_ref.shape[0]
    per_chunk = per * slots
    fold = LANES // stars
    all_slots = parcel_rows.shape[0]
    ahead = held // 2
    lane = lax.broadcasted_iota(jnp.int32, (8, LANES), 1)
    row = lax.broadcasted_iota(jnp.int32, (8, LANES), 0)
    star_group = lane // stars
    own_slot = [row == star_group + fold * h for h in range(8 // fold)]

    def load(chunk, u):
        return [
            pltpu.make_async_copy(
                weights_hbm.at[chunk * per + b], weights_ref.at[u, b], sems.at[u, b]
            )
            for b in range(per)
        ]

    def extinctions(u, chunk, places):
        sums = []
        for b in range(per):
            total = jnp.zeros((stars, width), jnp.float32)
            for k in range(slots):
                fetched = returned_rows[places[u * per_chunk + b * slots + k]]
                total = total + weights_ref[u, b, k].astype(jnp.float32) * fetched
            sums.append(total)
        extinction = lax.dot_general(
            jnp.ones((8, width), jnp.float32),
            jnp.concatenate(sums, axis=0),
            CONTRACT_LANES,
            precision=lax.Precision.HIGHEST,
            preferred_element_type=jnp.float32,
        )
        here = pl.ds(chunk, 1)
        extinction_ref[here, :] = extinction[:1]
        return inverse_ref[here, :] * (extinction - observed_ref[here, :])

    def sensitivities(u, weighted):
        for b in range(per):
            spread = jnp.where(star_group == b, weighted, 0.0)
            shift = stars
            while shift < LANES:
                spread = spread + pltpu.roll(spread, shift, 1)
                shift *= 2
            left = jnp.concatenate(
                [jnp.where(own, spread, 0.0) for own in own_slot], axis=1
            ).astype(jnp.bfloat16)
            eights = [weights_ref[u, b, 8 * j : 8 * j + 8] for j in range(slots // 8)]
            right = jnp.concatenate([x.reshape(8 * stars, width) for x in eights], axis=1)
            sens = jnp.dot(left, right, preferred_element_type=jnp.float32)
            for j in range(slots // 8):
                first = u * per_chunk + b * slots + 8 * j
                sens_ref[first : first + 8, :] = sens[:, j * width : (j + 1) * width]

    def scatter(u, places):
        for i in range(u * per_chunk, (u + 1) * per_chunk):
            parcel_rows[places[i]] = sens_ref[i : i + 1, :]

    for u in range(ahead):
        for copy in load(u, u):
            copy.start()
    start = 0
    for returned_ref in returned_refs:
        span = slice(start, start + returned_ref.shape[0])
        returned_rows.reshape(all_slots, width)[span, :] = returned_ref[...].astype(jnp.float32)
        start = span.stop
    parcel_rows.reshape(all_slots, width)[...] = jnp.zeros((all_slots, width), jnp.float32)

    def one_round(i, carry):
        first = i * held
        size = held * per_chunk
        places = position_ref.at[pl.ds(pl.multiple_of(first * per_chunk, size), size)]
        weighted = {}
        for u in range(held + 2):
            if u < held:
                for copy in load(first + u, u):
                    copy.wait()
                following = load(first + u + ahead, (u + ahead) % held)
                if u + ahead < held:
                    for copy in following:
                        copy.start()
                else:

                    @pl.when(first + u + ahead < chunks)
                    def _(following=following):
                        for copy in following:
                            copy.start()

                weighted[u] = extinctions(u, first + u, places)
            if 1 <= u <= held:
                sensitivities(u - 1, weighted[u - 1])
            if u >= 2:
                scatter(u - 2, places)
        return carry

    lax.fori_loop(0, chunks // held, one_round, 0)
    start = 0
    for parcel_ref in parcel_refs:
        span = slice(start, start + parcel_ref.shape[0])
        parcel_ref[...] = parcel_rows.reshape(all_slots, width)[span, :].astype(jnp.bfloat16)
        start = span.stop


def prior_kernel(field_ref, xlo_ref, xhi_ref, ylo_ref, yhi_ref, out_ref, padded, smooth):
    cells_x, cells_y, depth = field_ref.shape
    rows = padded.shape[1]
    gx, gy = lax.axis_index("gx"), lax.axis_index("gy")
    last_gx, last_gy = lax.axis_size("gx") - 1, lax.axis_size("gy") - 1
    z = lax.broadcasted_iota(jnp.int32, (rows, depth), 1)
    y = lax.broadcasted_iota(jnp.int32, (rows, depth), 0) - 8
    inside_y = ((y >= 0) | (gy > 0)) & ((y < cells_y) | (gy < last_gy))

    def operate(center, below, above):
        beside = below + above
        beside = beside + pltpu.roll(center, 1, 0) + pltpu.roll(center, rows - 1, 0)
        beside = beside + jnp.where(z == 0, 0.0, pltpu.roll(center, 1, 1))
        beside = beside + jnp.where(z == depth - 1, 0.0, pltpu.roll(center, depth - 1, 1))
        return (shift_kappa + 6.0) * center - beside

    def fill(plane, source):
        padded[plane, 8 : 8 + cells_y, :] = source
        padded[plane, 0:8, :] = jnp.zeros((8, depth), jnp.float32)
        padded[plane, 8 + cells_y :, :] = jnp.zeros((8, depth), jnp.float32)
        for h in range(2):
            padded[plane, 6 + h : 7 + h, :] = ylo_ref[h, pl.ds(plane, 1), :]
            padded[plane, 8 + cells_y + h : 9 + cells_y + h, :] = yhi_ref[h, pl.ds(plane, 1), :]

    for h in range(2):
        fill(h, xlo_ref[h].astype(jnp.float32))
        fill(cells_x + 2 + h, xhi_ref[h].astype(jnp.float32))

    def fill_own(x, carry):
        fill(x + 2, field_ref[x])
        return carry

    lax.fori_loop(0, cells_x, fill_own, 0)

    def smooth_plane(plane, carry):
        value = operate(padded[plane], padded[plane - 1], padded[plane + 1])
        inside = ((plane > 1) | (gx > 0)) & ((plane < cells_x + 2) | (gx < last_gx))
        smooth[plane - 1] = jnp.where(inside_y & inside, value, 0.0)
        return carry

    lax.fori_loop(1, cells_x + 3, smooth_plane, 0)

    def out_plane(x, carry):
        prior = operate(smooth[x + 1], smooth[x], smooth[x + 2])
        out_ref[x] = field_ref[x] - (step_rate * prior_weight) * prior[8 : 8 + cells_y]
        return carry

    lax.fori_loop(0, cells_x, out_plane, 0)


def finish_kernel(
    incoming_ref, match_ref, field_hbm, base_hbm, *refs, exchanges, capacity, first_slots
):
    arrived_refs, refs = refs[:exchanges], refs[exchanges:]
    out_hbm, collected, rows_ref, field_ref, base_ref, out_ref, in_sems, out_sems = refs
    cells_x, cells_y, depth = field_ref.shape
    per_column = depth // LANES
    parts = out_sems.shape[0]
    planes = cells_x // parts
    blocks = cells_x * cells_y * per_column
    loads = copies_in_parts(field_hbm, field_ref, in_sems.at[0])
    loads += copies_in_parts(base_hbm, base_ref, in_sems.at[1])
    for load in loads:
        load.start()
    collected_rows = collected.reshape(collected.shape[0], LANES)
    start = 0
    for arrived_ref in arrived_refs:
        for i in range(arrived_ref.shape[0] // LANES):
            span = slice(start + i * LANES, start + (i + 1) * LANES)
            rows_ref[span, :] = -step_rate * jnp.dot(
                match_ref[span, :],
                arrived_ref[i * LANES : (i + 1) * LANES, :],
                preferred_element_type=jnp.float32,
            )
        start += arrived_ref.shape[0]
    collected_rows[...] = jnp.zeros_like(collected_rows)

    part_starts = [0, arrived_refs[0].shape[0]]

    def visit(wanted, row, list_part):
        row = pl.multiple_of(row + part_starts[list_part], GROUP)
        rows = rows_ref.at[pl.ds(row, GROUP)]
        sums = [collected[wanted[j]] + rows[j : j + 1, :] for j in range(GROUP)]
        for j in range(GROUP):
            collected[wanted[j]] = sums[j]

    for_each_group(incoming_ref, visit, capacity, first_slots, blocks)
    for load in loads:
        load.wait()

    def store(part):
        span = pl.ds(part * planes, planes)
        return pltpu.make_async_copy(out_ref.at[span], out_hbm.at[span], out_sems.at[part])

    def one_plane(x, carry):
        for yb in range(cells_y // 8):
            for part in range(per_column):
                at = pl.multiple_of(((x * (cells_y // 8) + yb) * per_column + part) * 8, 8)
                here = (x, slice(8 * yb, 8 * yb + 8), slice(part * LANES, (part + 1) * LANES))
                out_ref[here] = base_ref[here] + collected_rows[pl.ds(at, 8), :] * jnp.exp(
                    field_ref[here]
                )
        return carry

    for part in range(parts):
        lax.fori_loop(part * planes, (part + 1) * planes, one_plane, 0)
        store(part).start()
    for part in range(parts):
        store(part).wait()


def both_ways(first, last, axis):
    peers = lax.axis_size(axis)
    up = [(i, i + 1) for i in range(peers - 1)]
    down = [(j, i) for i, j in up]
    return lax.ppermute(last, axis, up), lax.ppermute(first, axis, down)


def halo(xfirst, xlast, yfirst, ylast):
    xlo, xhi = both_ways(xfirst, xlast, "gx")

    def rows(own, at):
        ends = [x[:, at].transpose(1, 0, 2) for x in (xlo, xhi)]
        return jnp.concatenate([ends[0], own.astype(xlo.dtype), ends[1]], axis=1)

    ylo, yhi = both_ways(rows(yfirst, slice(0, 2)), rows(ylast, slice(-2, None)), "gy")
    return xlo, xhi, ylo.astype(jnp.float32), yhi.astype(jnp.float32)


VMEM = pl.BlockSpec(memory_space=pltpu.VMEM)
SMEM = pl.BlockSpec(memory_space=pltpu.SMEM)
ANY = pl.BlockSpec(memory_space=pl.ANY)


def on_device(log_density, weights, observed, inverse_var, star_counts, block_ids):
    cells_x, cells_y, depth = log_density.shape
    blocks_dev, slots, stars, width = weights.shape
    devices = lax.axis_size("gx") * lax.axis_size("gy")
    requests = blocks_dev * slots
    capacity = 2 * requests // devices
    first_slots = min(capacity, -(-3 * capacity // (4 * GROUP)) * GROUP)
    slots_of = [n for n in (first_slots, capacity - first_slots) if n > 0]
    exchanges = len(slots_of)
    all_slots = devices * capacity
    per_column = depth // width
    blocks = cells_x * cells_y * per_column
    cells = log_density.size
    field_shape = (cells_x, cells_y, depth)
    mesh_axes = ("gx", "gy")
    f32, bf16, i32 = jnp.float32, jnp.bfloat16, jnp.int32
    shape = jax.ShapeDtypeStruct

    def to_rows(x):
        x = x.reshape(cells_x, cells_y // 8, 8, per_column, width)
        return x.transpose(0, 1, 3, 2, 4).reshape(blocks, 1, width)

    def exchange(x):
        return lax.all_to_all(x, mesh_axes, split_axis=0, concat_axis=0, tiled=True)

    def exchange_rows(parts, crowded):
        moved = [parts[0].reshape(devices, first_slots, width)]
        moved[0] = exchange(moved[0])
        for part in parts[1:]:
            part = part.reshape(devices, capacity - first_slots, width)
            moved.append(lax.cond(crowded, exchange, lambda x: x, part))
        return [x.reshape(-1, width) for x in moved]

    outgoing, position = pl.pallas_call(
        functools.partial(
            route_kernel,
            devices=devices,
            capacity=capacity,
            first_slots=first_slots,
            blocks=blocks,
            per_column=per_column,
        ),
        out_shape=[shape((devices, capacity), i32), shape((requests // LANES, LANES), i32)],
        in_specs=[VMEM],
        out_specs=[VMEM, VMEM],
        name="route",
    )(block_ids.T)
    incoming = exchange(outgoing)

    field, _ = lax.optimization_barrier((log_density, outgoing))
    xfirst, xlast, yfirst, ylast = pl.pallas_call(
        edges_kernel,
        out_shape=[
            shape((2, cells_y, depth), bf16),
            shape((2, cells_y, depth), bf16),
            shape((2, cells_x, depth), f32),
            shape((2, cells_x, depth), f32),
        ],
        in_specs=[ANY],
        out_specs=[VMEM] * 4,
        scratch_shapes=[
            pltpu.VMEM((2, 2, cells_y, depth), f32),
            pltpu.VMEM((2, cells_x, 8, depth), f32),
            pltpu.SemaphoreType.DMA((4,)),
        ],
        compiler_params=pltpu.CompilerParams(vmem_limit_bytes=56 * MIB),
        cost_estimate=pl.CostEstimate(flops=0, bytes_accessed=2 * MIB, transcendentals=0),
        name="edges",
    )(field)
    incoming, *edges = lax.optimization_barrier((incoming, xfirst, xlast, yfirst, ylast))
    wanted = incoming.reshape(-1)

    *served, crowded = pl.pallas_call(
        functools.partial(serve_kernel, capacity=capacity, first_slots=first_slots),
        out_shape=[shape((devices * n, width), bf16) for n in slots_of] + [shape((1,), i32)],
        in_specs=[SMEM, ANY],
        out_specs=[VMEM] * exchanges + [SMEM],
        scratch_shapes=[
            pltpu.VMEM((blocks + capacity, 1, width), f32),
            pltpu.SemaphoreType.DMA((16,)),
        ],
        compiler_params=pltpu.CompilerParams(vmem_limit_bytes=56 * MIB),
        cost_estimate=pl.CostEstimate(
            flops=cells, bytes_accessed=6 * MIB, transcendentals=cells
        ),
        name="serve",
    )(wanted, to_rows(log_density))
    crowded = crowded[0] != 0

    incoming_late, *edges, _ = lax.optimization_barrier((incoming, *edges, served[0]))
    slot_lists = [
        incoming_late[:, :first_slots].reshape(-1, LANES),
        (incoming_late[:, first_slots:] & (MARK - 1)).reshape(-1, LANES),
    ][:exchanges]
    match = pl.pallas_call(
        match_kernel,
        out_shape=shape((all_slots, LANES), bf16),
        in_specs=[VMEM],
        out_specs=VMEM,
        compiler_params=pltpu.CompilerParams(vmem_limit_bytes=8 * MIB),
        cost_estimate=pl.CostEstimate(flops=10**9, bytes_accessed=MIB, transcendentals=0),
        name="match",
    )(jnp.concatenate(slot_lists, axis=0))
    returned = exchange_rows(served, crowded)
    xlo, xhi, ylo, yhi = halo(*edges)
    *returned, match, ylo, yhi = lax.optimization_barrier((*returned, match, ylo, yhi))

    chunks = blocks_dev * stars // LANES
    held = chunks // 2
    live = jnp.arange(stars)[None, :] < star_counts[:, None]
    live_inverse = jnp.where(live, inverse_var, 0.0)
    extinction, *parcel = pl.pallas_call(
        functools.partial(star_kernel, exchanges=exchanges),
        out_shape=[shape((chunks, LANES), f32)]
        + [shape((devices * n, width), bf16) for n in slots_of],
        in_specs=[SMEM, VMEM, VMEM, ANY] + [VMEM] * exchanges,
        out_specs=[VMEM] * (1 + exchanges),
        scratch_shapes=[
            pltpu.VMEM((held, blocks_dev // chunks, slots, stars, width), bf16),
            pltpu.VMEM((all_slots, 1, width), f32),
            pltpu.VMEM((held * (blocks_dev // chunks) * slots, width), f32),
            pltpu.VMEM((all_slots, 1, width), f32),
            pltpu.SemaphoreType.DMA((held, blocks_dev // chunks)),
        ],
        compiler_params=pltpu.CompilerParams(vmem_limit_bytes=50 * MIB),
        cost_estimate=pl.CostEstimate(
            flops=4 * weights.size, bytes_accessed=2 * weights.size, transcendentals=0
        ),
        name="stars",
    )(
        position.reshape(slots // 2, 2, blocks_dev).transpose(2, 1, 0).reshape(requests),
        observed.reshape(chunks, LANES),
        live_inverse.reshape(chunks, LANES),
        weights,
        *returned,
    )
    arrived = exchange_rows(parcel, crowded)

    field_late, _ = lax.optimization_barrier((log_density, parcel[0]))
    base = pl.pallas_call(
        prior_kernel,
        out_shape=shape(field_shape, f32),
        in_specs=[VMEM] * 5,
        out_specs=VMEM,
        scratch_shapes=[
            pltpu.VMEM((cells_x + 4, cells_y + 16, depth), f32),
            pltpu.VMEM((cells_x + 2, cells_y + 16, depth), f32),
        ],
        compiler_params=pltpu.CompilerParams(vmem_limit_bytes=32 * MIB),
        cost_estimate=pl.CostEstimate(
            flops=30 * cells, bytes_accessed=8 * cells, transcendentals=0
        ),
        name="prior",
    )(field_late, xlo, xhi, ylo, yhi)

    parts = 8
    new_log_density = pl.pallas_call(
        functools.partial(
            finish_kernel, exchanges=exchanges, capacity=capacity, first_slots=first_slots
        ),
        out_shape=shape(field_shape, f32),
        in_specs=[SMEM, VMEM, ANY, ANY] + [VMEM] * exchanges,
        out_specs=ANY,
        scratch_shapes=[
            pltpu.VMEM((blocks + capacity, 1, width), f32),
            pltpu.VMEM((all_slots, width), f32),
            pltpu.VMEM(field_shape, f32),
            pltpu.VMEM(field_shape, f32),
            pltpu.VMEM(field_shape, f32),
            pltpu.SemaphoreType.DMA((2, parts)),
            pltpu.SemaphoreType.DMA((parts,)),
        ],
        compiler_params=pltpu.CompilerParams(vmem_limit_bytes=50 * MIB),
        cost_estimate=pl.CostEstimate(
            flops=4 * cells, bytes_accessed=12 * cells, transcendentals=cells
        ),
        name="finish",
    )(wanted, match, log_density, base, *arrived)
    return new_log_density, extinction.reshape(blocks_dev, stars)


def solution(mesh):
    placed = (
        P("gx", "gy", None),
        P(("gx", "gy"), None, None, None),
        P(("gx", "gy"), None),
        P(("gx", "gy"), None),
        P(("gx", "gy")),
        P(("gx", "gy"), None),
    )
    return jax.shard_map(
        on_device,
        mesh=mesh,
        in_specs=placed,
        out_specs=(P("gx", "gy", None), P(("gx", "gy"), None)),
        check_vma=False,
    )
```

```python
import functools

import jax
import jax.numpy as jnp
from jax import lax
from jax.experimental import pallas as pl
from jax.experimental.pallas import tpu as pltpu
from jax.sharding import PartitionSpec as P

shift_kappa = 0.5
prior_weight = 0.05
step_rate = 2.0

LANES = 128
GROUP = 16
MIB = 1 << 20
MARK = 1 << 16

CONTRACT_LANES = (((1,), (1,)), ((), ()))


def split_by(value, size):
    if size & (size - 1) == 0:
        high = value >> (size.bit_length() - 1)
        return high, value & (size - 1)
    high = value // size
    return high, value - high * size


def route_kernel(
    ids_ref, outgoing_ref, position_ref, *, devices, capacity, first_slots, blocks, per_column
):
    half = ids_ref.shape[0] // 2
    ids = jnp.concatenate([ids_ref[:half, :], ids_ref[half:, :]], axis=1)
    lane = lax.broadcasted_iota(jnp.int32, (LANES, LANES), 1)
    row = lax.broadcasted_iota(jnp.int32, (LANES, LANES), 0)
    upper = jnp.where(row <= lane, 1.0, 0.0).astype(jnp.bfloat16)
    tile_no = lax.broadcasted_iota(jnp.int32, (devices, LANES), 0)
    slot_no = lax.broadcasted_iota(jnp.int32, (capacity, LANES), 0)
    before = jnp.zeros((devices, 1), jnp.float32)
    lists = jnp.zeros((2 * devices, capacity), jnp.float32)
    for chunk in range(half):
        target, local = split_by(ids[chunk : chunk + 1, :], blocks)
        column, part = split_by(local, per_column)
        local = ((column >> 3) * per_column + part) * 8 + (column & 7)
        hit = tile_no == target
        onehot = jnp.where(hit, 1.0, 0.0)
        upto = before + jnp.dot(
            onehot.astype(jnp.bfloat16), upper, preferred_element_type=jnp.float32
        )
        before = upto[:, LANES - 1 :]
        rank = jnp.sum(onehot * upto, axis=0, keepdims=True).astype(jnp.int32) - 1
        in_slot = jnp.where(slot_no == rank, 1.0, 0.0).astype(jnp.bfloat16)
        high = ((local >> 7) + 1).astype(jnp.float32)
        low = (local & 127).astype(jnp.float32)
        digits = jnp.concatenate([jnp.where(hit, high, 0.0), jnp.where(hit, low, 0.0)], axis=0)
        lists = lists + lax.dot_general(
            digits.astype(jnp.bfloat16),
            in_slot,
            CONTRACT_LANES,
            preferred_element_type=jnp.float32,
        )
        last_slots = capacity - first_slots
        position_ref[chunk : chunk + 1, :] = jnp.where(
            rank < first_slots,
            target * first_slots + rank,
            devices * first_slots + target * last_slots + rank - first_slots,
        )
    high, low = lists[:devices], lists[devices:]
    wanted = ((high - 1.0) * 128.0 + low).astype(jnp.int32)
    filled = before.astype(jnp.int32)
    me = lax.axis_index("gx") * lax.axis_size("gy") + lax.axis_index("gy")
    fullest = jnp.max(jnp.where(tile_no[:, :1] == me, 0.0, before), axis=0, keepdims=True)
    listed = jnp.where(high > 0.5, wanted, blocks + filled)
    if first_slots < capacity:
        slot = lax.broadcasted_iota(jnp.int32, (devices, capacity), 1)
        mark = fullest.astype(jnp.int32) * MARK
        listed = listed + jnp.where(slot == capacity - 1, mark, 0)
    outgoing_ref[...] = listed


def edges_kernel(
    field_hbm, xfirst_ref, xlast_ref, yfirst_ref, ylast_ref, planes_ref, strips_ref, sems
):
    cells_x, cells_y, _ = field_hbm.shape
    copies = [
        pltpu.make_async_copy(field_hbm.at[pl.ds(0, 2)], planes_ref.at[0], sems.at[0]),
        pltpu.make_async_copy(field_hbm.at[pl.ds(cells_x - 2, 2)], planes_ref.at[1], sems.at[1]),
        pltpu.make_async_copy(field_hbm.at[:, pl.ds(0, 8)], strips_ref.at[0], sems.at[2]),
        pltpu.make_async_copy(
            field_hbm.at[:, pl.ds(cells_y - 8, 8)], strips_ref.at[1], sems.at[3]
        ),
    ]
    for copy in copies:
        copy.start()
    for copy in copies:
        copy.wait()
    xfirst_ref[...] = planes_ref[0].astype(xfirst_ref.dtype)
    xlast_ref[...] = planes_ref[1].astype(xlast_ref.dtype)
    for h in range(2):
        for x in range(cells_x):
            yfirst_ref[h, x : x + 1, :] = strips_ref[0, x, h : h + 1, :]
            ylast_ref[h, x : x + 1, :] = strips_ref[1, x, 6 + h : 7 + h, :]


def copies_in_parts(source, target, sems):
    parts = sems.shape[0]
    size = source.shape[0] // parts
    return [
        pltpu.make_async_copy(
            source.at[pl.ds(i * size, size)], target.at[pl.ds(i * size, size)], sems.at[i]
        )
        for i in range(parts)
    ]


def for_each_group(incoming_ref, visit, capacity, first_slots, blocks):
    sources = incoming_ref.shape[0] // capacity
    last_slots = capacity - first_slots
    together = 4

    def groups_of(source):
        last = incoming_ref[source * capacity + capacity - 1] & (MARK - 1)
        return (jnp.where(last < blocks, capacity, last - blocks) + GROUP - 1) // GROUP

    def some_sources(quad, carry):
        own = [quad * together + i for i in range(together)]
        most = functools.reduce(jnp.maximum, [groups_of(source) for source in own])

        def one_group(group, carry):
            slot = group * GROUP
            for source in own:
                listed = incoming_ref.at[pl.ds(source * capacity + slot, GROUP)]
                wanted = [listed[j] for j in range(GROUP)]
                visit(wanted, pl.multiple_of(source * first_slots + slot, GROUP), 0)
            return carry

        return lax.fori_loop(0, jnp.minimum(most, first_slots // GROUP), one_group, carry)

    lax.fori_loop(0, sources // together, some_sources, 0)
    if last_slots == 0:
        return

    def one_source(source, carry):
        def one_group(group, carry):
            slot = group * GROUP
            listed = incoming_ref.at[pl.ds(source * capacity + slot, GROUP)]
            wanted = [listed[j] & (MARK - 1) for j in range(GROUP)]
            visit(wanted, pl.multiple_of(source * last_slots + slot - first_slots, GROUP), 1)
            return carry

        return lax.fori_loop(first_slots // GROUP, groups_of(source), one_group, carry)

    lax.fori_loop(0, sources, one_source, 0)


def serve_kernel(incoming_ref, field_hbm, *refs, capacity, first_slots):
    *served_refs, crowded_ref, rows_ref, found_ref, sems = refs
    blocks = field_hbm.shape[0]
    loads = copies_in_parts(field_hbm, rows_ref, sems)
    for load in loads:
        load.start()

    def mark_of(source, most):
        return jnp.maximum(most, incoming_ref[source * capacity + capacity - 1] >> 16)

    fullest = lax.fori_loop(0, incoming_ref.shape[0] // capacity, mark_of, jnp.int32(0))
    crowded_ref[0] = jnp.where(fullest > first_slots, 1, 0)
    rows_ref[blocks:] = jnp.zeros((rows_ref.shape[0] - blocks, 1, LANES), jnp.float32)
    for load in loads:
        load.wait()

    part_starts = [0, served_refs[0].shape[0]]

    def visit(wanted, row, list_part):
        rows = [rows_ref[at] for at in wanted]
        found = found_ref.at[pl.ds(row + part_starts[list_part], GROUP)]
        for j in range(GROUP):
            found[j] = rows[j]

    for_each_group(incoming_ref, visit, capacity, first_slots, blocks)
    found = found_ref.reshape(found_ref.shape[0], LANES)
    for start, served_ref in zip(part_starts, served_refs):
        span = slice(start, start + served_ref.shape[0])
        served_ref[...] = jnp.exp(found[span, :]).astype(jnp.bfloat16)


def match_kernel(incoming_ref, match_ref):
    lane = lax.broadcasted_iota(jnp.int32, (LANES, LANES), 1)
    row = lax.broadcasted_iota(jnp.int32, (LANES, LANES), 0)
    ones = jnp.ones((LANES, LANES), jnp.bfloat16)
    same_group = (lane // GROUP) == (row // GROUP)

    def one_row(i):
        wanted = incoming_ref[pl.ds(i, 1), :]
        high = jnp.where(lane == row, (wanted >> 7).astype(jnp.float32), 0.0).astype(jnp.bfloat16)
        low = jnp.where(lane == row, (wanted & 127).astype(jnp.float32), 0.0).astype(jnp.bfloat16)
        down = 128.0 * jnp.dot(high, ones, preferred_element_type=jnp.float32)
        down = down + jnp.dot(low, ones, preferred_element_type=jnp.float32)
        same = (down == wanted.astype(jnp.float32)) & same_group
        match_ref[pl.ds(pl.multiple_of(i * LANES, LANES), LANES), :] = jnp.where(
            same, 1.0, 0.0
        ).astype(jnp.bfloat16)

    def some_rows(i, carry):
        for j in range(4):
            one_row(4 * i + j)
        return carry

    lax.fori_loop(0, incoming_ref.shape[0] // 4, some_rows, 0)


def star_kernel(position_ref, observed_ref, inverse_ref, weights_hbm, *refs, exchanges):
    returned_refs, refs = refs[:exchanges], refs[exchanges:]
    extinction_ref, refs = refs[0], refs[1:]
    parcel_refs, refs = refs[:exchanges], refs[exchanges:]
    weights_ref, returned_rows, sens_ref, parcel_rows, sems = refs
    sets, in_set, per, slots, stars, width = weights_ref.shape
    chunks = extinction_ref.shape[0]
    rounds = chunks // (sets * in_set)
    per_chunk = per * slots
    fold = LANES // stars
    all_slots = parcel_rows.shape[0]
    sens_blocks = sens_ref.reshape(sens_ref.shape[0], width)
    lane = lax.broadcasted_iota(jnp.int32, (8, LANES), 1)
    row = lax.broadcasted_iota(jnp.int32, (8, LANES), 0)
    star_group = lane // stars
    own_slot = [row == star_group + fold * h for h in range(8 // fold)]

    def load(one_round, one_set):
        return [
            pltpu.make_async_copy(
                weights_hbm.at[pl.ds(((one_round * sets + one_set) * in_set + u) * per, per)],
                weights_ref.at[one_set, u],
                sems.at[one_set, u],
            )
            for u in range(in_set)
        ]

    def extinctions(one_set, u, chunk, places):
        sums = []
        for b in range(per):
            total = jnp.zeros((stars // 8, 8, width), jnp.float32)
            for k in range(slots):
                at = places[u * per_chunk + b * slots + k]
                fetched = returned_rows[pl.ds(at, 8, stride=0), :]
                block = weights_ref[one_set, u, b, k].astype(jnp.float32)
                total = total + block.reshape(stars // 8, 8, width) * fetched
            sums.append(total.reshape(stars, width))
        extinction = lax.dot_general(
            jnp.ones((8, width), jnp.float32),
            jnp.concatenate(sums, axis=0),
            CONTRACT_LANES,
            precision=lax.Precision.HIGHEST,
            preferred_element_type=jnp.float32,
        )
        here = pl.ds(chunk, 1)
        extinction_ref[here, :] = extinction[:1]
        return inverse_ref[here, :] * (extinction - observed_ref[here, :])

    def sensitivities(one_set, u, weighted):
        for b in range(per):
            spread = jnp.where(star_group == b, weighted, 0.0)
            shift = stars
            while shift < LANES:
                spread = spread + pltpu.roll(spread, shift, 1)
                shift *= 2
            left = jnp.concatenate(
                [jnp.where(own, spread, 0.0) for own in own_slot], axis=1
            ).astype(jnp.bfloat16)
            eights = [weights_ref[one_set, u, b, 8 * j : 8 * j + 8] for j in range(slots // 8)]
            right = jnp.concatenate([x.reshape(8 * stars, width) for x in eights], axis=1)
            sens = jnp.dot(left, right, preferred_element_type=jnp.float32)
            for j in range(slots // 8):
                first = u * per_chunk + b * slots + 8 * j
                sens_blocks[first : first + 8, :] = sens[:, j * width : (j + 1) * width]

    def scatter(u, places):
        for i in range(u * per_chunk, (u + 1) * per_chunk):
            parcel_rows[places[i]] = sens_ref[i]

    def work(one_round, one_set):
        first = (one_round * sets + one_set) * in_set
        size = in_set * per_chunk
        places = position_ref.at[pl.ds(pl.multiple_of(first * per_chunk, size), size)]
        weighted = {}
        for u in range(in_set + 2):
            if u < in_set:
                weighted[u] = extinctions(one_set, u, first + u, places)
            if 1 <= u <= in_set:
                sensitivities(one_set, u - 1, weighted[u - 1])
            if u >= 2:
                scatter(u - 2, places)

    for one_set in range(sets):
        for copy in load(0, one_set):
            copy.start()
    start = 0
    for returned_ref in returned_refs:
        span = slice(start, start + returned_ref.shape[0])
        returned_rows[span, :] = returned_ref[...].astype(jnp.float32)
        start = span.stop
    parcel_rows.reshape(all_slots, width)[...] = jnp.zeros((all_slots, width), jnp.float32)

    def one_round(i, carry):
        for one_set in range(sets):
            for copy in load(i, one_set):
                copy.wait()
            work(i, one_set)

            @pl.when(i + 1 < rounds)
            def _():
                for copy in load(i + 1, one_set):
                    copy.start()

        return carry

    lax.fori_loop(0, rounds, one_round, 0)
    start = 0
    for parcel_ref in parcel_refs:
        span = slice(start, start + parcel_ref.shape[0])
        parcel_ref[...] = parcel_rows.reshape(all_slots, width)[span, :].astype(jnp.bfloat16)
        start = span.stop


def prior_kernel(field_ref, xlo_ref, xhi_ref, ylo_ref, yhi_ref, out_ref, padded, smooth):
    cells_x, cells_y, depth = field_ref.shape
    rows = padded.shape[1]
    gx, gy = lax.axis_index("gx"), lax.axis_index("gy")
    last_gx, last_gy = lax.axis_size("gx") - 1, lax.axis_size("gy") - 1
    z = lax.broadcasted_iota(jnp.int32, (rows, depth), 1)
    y = lax.broadcasted_iota(jnp.int32, (rows, depth), 0) - 8
    inside_y = ((y >= 0) | (gy > 0)) & ((y < cells_y) | (gy < last_gy))

    def operate(center, below, above):
        beside = below + above
        beside = beside + pltpu.roll(center, 1, 0) + pltpu.roll(center, rows - 1, 0)
        beside = beside + jnp.where(z == 0, 0.0, pltpu.roll(center, 1, 1))
        beside = beside + jnp.where(z == depth - 1, 0.0, pltpu.roll(center, depth - 1, 1))
        return (shift_kappa + 6.0) * center - beside

    def fill(plane, source):
        padded[plane, 8 : 8 + cells_y, :] = source
        padded[plane, 0:8, :] = jnp.zeros((8, depth), jnp.float32)
        padded[plane, 8 + cells_y :, :] = jnp.zeros((8, depth), jnp.float32)
        for h in range(2):
            padded[plane, 6 + h : 7 + h, :] = ylo_ref[h, pl.ds(plane, 1), :]
            padded[plane, 8 + cells_y + h : 9 + cells_y + h, :] = yhi_ref[h, pl.ds(plane, 1), :]

    for h in range(2):
        fill(h, xlo_ref[h].astype(jnp.float32))
        fill(cells_x + 2 + h, xhi_ref[h].astype(jnp.float32))

    def fill_own(x, carry):
        fill(x + 2, field_ref[x])
        return carry

    lax.fori_loop(0, cells_x, fill_own, 0)

    def smooth_plane(plane, carry):
        value = operate(padded[plane], padded[plane - 1], padded[plane + 1])
        inside = ((plane > 1) | (gx > 0)) & ((plane < cells_x + 2) | (gx < last_gx))
        smooth[plane - 1] = jnp.where(inside_y & inside, value, 0.0)
        return carry

    lax.fori_loop(1, cells_x + 3, smooth_plane, 0)

    def out_plane(x, carry):
        prior = operate(smooth[x + 1], smooth[x], smooth[x + 2])
        out_ref[x] = field_ref[x] - (step_rate * prior_weight) * prior[8 : 8 + cells_y]
        return carry

    lax.fori_loop(0, cells_x, out_plane, 0)


def finish_kernel(
    incoming_ref, match_ref, field_hbm, base_hbm, *refs, exchanges, capacity, first_slots
):
    arrived_refs, refs = refs[:exchanges], refs[exchanges:]
    out_hbm, collected, rows_ref, field_ref, base_ref, out_ref, in_sems, out_sems = refs
    cells_x, cells_y, depth = field_ref.shape
    per_column = depth // LANES
    parts = out_sems.shape[0]
    planes = cells_x // parts
    blocks = cells_x * cells_y * per_column
    loads = copies_in_parts(field_hbm, field_ref, in_sems.at[0])
    loads += copies_in_parts(base_hbm, base_ref, in_sems.at[1])
    for load in loads:
        load.start()
    collected_rows = collected.reshape(collected.shape[0], LANES)
    merged = rows_ref.reshape(rows_ref.shape[0], LANES)
    start = 0
    for arrived_ref in arrived_refs:
        for i in range(arrived_ref.shape[0] // LANES):
            span = slice(start + i * LANES, start + (i + 1) * LANES)
            merged[span, :] = -step_rate * jnp.dot(
                match_ref[span, :],
                arrived_ref[i * LANES : (i + 1) * LANES, :],
                preferred_element_type=jnp.float32,
            )
        start += arrived_ref.shape[0]
    collected_rows[...] = jnp.zeros_like(collected_rows)

    part_starts = [0, arrived_refs[0].shape[0]]

    def visit(wanted, row, list_part):
        row = pl.multiple_of(row + part_starts[list_part], GROUP)
        rows = rows_ref.at[pl.ds(row, GROUP)]
        sums = [collected[wanted[j]] + rows[j] for j in range(GROUP)]
        for j in range(GROUP):
            collected[wanted[j]] = sums[j]

    for_each_group(incoming_ref, visit, capacity, first_slots, blocks)
    for load in loads:
        load.wait()

    def store(part):
        span = pl.ds(part * planes, planes)
        return pltpu.make_async_copy(out_ref.at[span], out_hbm.at[span], out_sems.at[part])

    def one_plane(x, carry):
        for yb in range(cells_y // 8):
            for part in range(per_column):
                at = pl.multiple_of(((x * (cells_y // 8) + yb) * per_column + part) * 8, 8)
                here = (x, slice(8 * yb, 8 * yb + 8), slice(part * LANES, (part + 1) * LANES))
                out_ref[here] = base_ref[here] + collected_rows[pl.ds(at, 8), :] * jnp.exp(
                    field_ref[here]
                )
        return carry

    for part in range(parts):
        lax.fori_loop(part * planes, (part + 1) * planes, one_plane, 0)
        store(part).start()
    for part in range(parts):
        store(part).wait()


def both_ways(first, last, axis):
    peers = lax.axis_size(axis)
    up = [(i, i + 1) for i in range(peers - 1)]
    down = [(j, i) for i, j in up]
    return lax.ppermute(last, axis, up), lax.ppermute(first, axis, down)


def halo(xfirst, xlast, yfirst, ylast):
    xlo, xhi = both_ways(xfirst, xlast, "gx")

    def rows(own, at):
        ends = [x[:, at].transpose(1, 0, 2) for x in (xlo, xhi)]
        return jnp.concatenate([ends[0], own.astype(xlo.dtype), ends[1]], axis=1)

    ylo, yhi = both_ways(rows(yfirst, slice(0, 2)), rows(ylast, slice(-2, None)), "gy")
    return xlo, xhi, ylo.astype(jnp.float32), yhi.astype(jnp.float32)


VMEM = pl.BlockSpec(memory_space=pltpu.VMEM)
SMEM = pl.BlockSpec(memory_space=pltpu.SMEM)
ANY = pl.BlockSpec(memory_space=pl.ANY)


def on_device(log_density, weights, observed, inverse_var, star_counts, block_ids):
    cells_x, cells_y, depth = log_density.shape
    blocks_dev, slots, stars, width = weights.shape
    devices = lax.axis_size("gx") * lax.axis_size("gy")
    requests = blocks_dev * slots
    capacity = 2 * requests // devices
    first_slots = min(capacity, -(-3 * capacity // (4 * GROUP)) * GROUP)
    slots_of = [n for n in (first_slots, capacity - first_slots) if n > 0]
    exchanges = len(slots_of)
    all_slots = devices * capacity
    per_column = depth // width
    blocks = cells_x * cells_y * per_column
    cells = log_density.size
    field_shape = (cells_x, cells_y, depth)
    mesh_axes = ("gx", "gy")
    f32, bf16, i32 = jnp.float32, jnp.bfloat16, jnp.int32
    shape = jax.ShapeDtypeStruct

    def to_rows(x):
        x = x.reshape(cells_x, cells_y // 8, 8, per_column, width)
        return x.transpose(0, 1, 3, 2, 4).reshape(blocks, 1, width)

    def exchange(x):
        return lax.all_to_all(x, mesh_axes, split_axis=0, concat_axis=0, tiled=True)

    def exchange_rows(parts, crowded):
        moved = [parts[0].reshape(devices, first_slots, width)]
        moved[0] = exchange(moved[0])
        for part in parts[1:]:
            part = part.reshape(devices, capacity - first_slots, width)
            moved.append(lax.cond(crowded, exchange, lambda x: x, part))
        return [x.reshape(-1, width) for x in moved]

    outgoing, position = pl.pallas_call(
        functools.partial(
            route_kernel,
            devices=devices,
            capacity=capacity,
            first_slots=first_slots,
            blocks=blocks,
            per_column=per_column,
        ),
        out_shape=[shape((devices, capacity), i32), shape((requests // LANES, LANES), i32)],
        in_specs=[VMEM],
        out_specs=[VMEM, VMEM],
        name="route",
    )(block_ids.T)
    incoming = exchange(outgoing)

    field, _ = lax.optimization_barrier((log_density, outgoing))
    xfirst, xlast, yfirst, ylast = pl.pallas_call(
        edges_kernel,
        out_shape=[
            shape((2, cells_y, depth), bf16),
            shape((2, cells_y, depth), bf16),
            shape((2, cells_x, depth), f32),
            shape((2, cells_x, depth), f32),
        ],
        in_specs=[ANY],
        out_specs=[VMEM] * 4,
        scratch_shapes=[
            pltpu.VMEM((2, 2, cells_y, depth), f32),
            pltpu.VMEM((2, cells_x, 8, depth), f32),
            pltpu.SemaphoreType.DMA((4,)),
        ],
        compiler_params=pltpu.CompilerParams(vmem_limit_bytes=56 * MIB),
        cost_estimate=pl.CostEstimate(flops=0, bytes_accessed=2 * MIB, transcendentals=0),
        name="edges",
    )(field)
    incoming, *edges = lax.optimization_barrier((incoming, xfirst, xlast, yfirst, ylast))
    wanted = incoming.reshape(-1)

    *served, crowded = pl.pallas_call(
        functools.partial(serve_kernel, capacity=capacity, first_slots=first_slots),
        out_shape=[shape((devices * n, width), bf16) for n in slots_of] + [shape((1,), i32)],
        in_specs=[SMEM, ANY],
        out_specs=[VMEM] * exchanges + [SMEM],
        scratch_shapes=[
            pltpu.VMEM((blocks + capacity, 1, width), f32),
            pltpu.VMEM((all_slots, 1, width), f32),
            pltpu.SemaphoreType.DMA((16,)),
        ],
        compiler_params=pltpu.CompilerParams(vmem_limit_bytes=56 * MIB),
        cost_estimate=pl.CostEstimate(
            flops=cells, bytes_accessed=6 * MIB, transcendentals=cells
        ),
        name="serve",
    )(wanted, to_rows(log_density))
    crowded = crowded[0] != 0

    incoming_late, *edges, _ = lax.optimization_barrier((incoming, *edges, served[0]))
    slot_lists = [
        incoming_late[:, :first_slots].reshape(-1, LANES),
        (incoming_late[:, first_slots:] & (MARK - 1)).reshape(-1, LANES),
    ][:exchanges]
    match = pl.pallas_call(
        match_kernel,
        out_shape=shape((all_slots, LANES), bf16),
        in_specs=[VMEM],
        out_specs=VMEM,
        compiler_params=pltpu.CompilerParams(vmem_limit_bytes=8 * MIB),
        cost_estimate=pl.CostEstimate(flops=10**9, bytes_accessed=MIB, transcendentals=0),
        name="match",
    )(jnp.concatenate(slot_lists, axis=0))
    returned = exchange_rows(served, crowded)
    xlo, xhi, ylo, yhi = halo(*edges)
    *returned, match, ylo, yhi = lax.optimization_barrier((*returned, match, ylo, yhi))

    chunks = blocks_dev * stars // LANES
    in_set = chunks // 4
    live = jnp.arange(stars)[None, :] < star_counts[:, None]
    live_inverse = jnp.where(live, inverse_var, 0.0)
    extinction, *parcel = pl.pallas_call(
        functools.partial(star_kernel, exchanges=exchanges),
        out_shape=[shape((chunks, LANES), f32)]
        + [shape((devices * n, width), bf16) for n in slots_of],
        in_specs=[SMEM, VMEM, VMEM, ANY] + [VMEM] * exchanges,
        out_specs=[VMEM] * (1 + exchanges),
        scratch_shapes=[
            pltpu.VMEM((2, in_set, blocks_dev // chunks, slots, stars, width), bf16),
            pltpu.VMEM((all_slots + 8, width), f32),
            pltpu.VMEM((in_set * (blocks_dev // chunks) * slots, 1, width), f32),
            pltpu.VMEM((all_slots, 1, width), f32),
            pltpu.SemaphoreType.DMA((2, in_set)),
        ],
        compiler_params=pltpu.CompilerParams(vmem_limit_bytes=50 * MIB),
        cost_estimate=pl.CostEstimate(
            flops=4 * weights.size, bytes_accessed=2 * weights.size, transcendentals=0
        ),
        name="stars",
    )(
        position.reshape(slots // 2, 2, blocks_dev).transpose(2, 1, 0).reshape(requests),
        observed.reshape(chunks, LANES),
        live_inverse.reshape(chunks, LANES),
        weights,
        *returned,
    )
    arrived = exchange_rows(parcel, crowded)

    field_late, _ = lax.optimization_barrier((log_density, parcel[0]))
    base = pl.pallas_call(
        prior_kernel,
        out_shape=shape(field_shape, f32),
        in_specs=[VMEM] * 5,
        out_specs=VMEM,
        scratch_shapes=[
            pltpu.VMEM((cells_x + 4, cells_y + 16, depth), f32),
            pltpu.VMEM((cells_x + 2, cells_y + 16, depth), f32),
        ],
        compiler_params=pltpu.CompilerParams(vmem_limit_bytes=32 * MIB),
        cost_estimate=pl.CostEstimate(
            flops=30 * cells, bytes_accessed=8 * cells, transcendentals=0
        ),
        name="prior",
    )(field_late, xlo, xhi, ylo, yhi)

    parts = 8
    new_log_density = pl.pallas_call(
        functools.partial(
            finish_kernel, exchanges=exchanges, capacity=capacity, first_slots=first_slots
        ),
        out_shape=shape(field_shape, f32),
        in_specs=[SMEM, VMEM, ANY, ANY] + [VMEM] * exchanges,
        out_specs=ANY,
        scratch_shapes=[
            pltpu.VMEM((blocks + capacity, 1, width), f32),
            pltpu.VMEM((all_slots, 1, width), f32),
            pltpu.VMEM(field_shape, f32),
            pltpu.VMEM(field_shape, f32),
            pltpu.VMEM(field_shape, f32),
            pltpu.SemaphoreType.DMA((2, parts)),
            pltpu.SemaphoreType.DMA((parts,)),
        ],
        compiler_params=pltpu.CompilerParams(vmem_limit_bytes=50 * MIB),
        cost_estimate=pl.CostEstimate(
            flops=4 * cells, bytes_accessed=12 * cells, transcendentals=cells
        ),
        name="finish",
    )(wanted, match, log_density, base, *arrived)
    return new_log_density, extinction.reshape(blocks_dev, stars)


def solution(mesh):
    placed = (
        P("gx", "gy", None),
        P(("gx", "gy"), None, None, None),
        P(("gx", "gy"), None),
        P(("gx", "gy"), None),
        P(("gx", "gy")),
        P(("gx", "gy"), None),
    )
    return jax.shard_map(
        on_device,
        mesh=mesh,
        in_specs=placed,
        out_specs=(P("gx", "gy", None), P(("gx", "gy"), None)),
        check_vma=False,
    )
```

```python
import functools

import jax
import jax.numpy as jnp
from jax import lax
from jax.experimental import pallas as pl
from jax.experimental.pallas import tpu as pltpu
from jax.sharding import PartitionSpec as P

shift_kappa = 0.5
prior_weight = 0.05
step_rate = 2.0

LANES = 128
GROUP = 8
MIB = 1 << 20
MARK = 1 << 16

CONTRACT_LANES = (((1,), (1,)), ((), ()))


def split_by(value, size):
    if size & (size - 1) == 0:
        high = value >> (size.bit_length() - 1)
        return high, value & (size - 1)
    high = value // size
    return high, value - high * size


def route_kernel(
    ids_ref, outgoing_ref, position_ref, *, devices, capacity, first_slots, blocks, per_column
):
    half = ids_ref.shape[0] // 2
    ids = jnp.concatenate([ids_ref[:half, :], ids_ref[half:, :]], axis=1)
    lane = lax.broadcasted_iota(jnp.int32, (LANES, LANES), 1)
    row = lax.broadcasted_iota(jnp.int32, (LANES, LANES), 0)
    upper = jnp.where(row <= lane, 1.0, 0.0).astype(jnp.bfloat16)
    tile_no = lax.broadcasted_iota(jnp.int32, (devices, LANES), 0)
    slot_no = lax.broadcasted_iota(jnp.int32, (capacity, LANES), 0)
    before = jnp.zeros((devices, 1), jnp.float32)
    lists = jnp.zeros((2 * devices, capacity), jnp.float32)
    for chunk in range(half):
        target, local = split_by(ids[chunk : chunk + 1, :], blocks)
        column, part = split_by(local, per_column)
        local = ((column >> 3) * per_column + part) * 8 + (column & 7)
        hit = tile_no == target
        onehot = jnp.where(hit, 1.0, 0.0)
        upto = before + jnp.dot(
            onehot.astype(jnp.bfloat16), upper, preferred_element_type=jnp.float32
        )
        before = upto[:, LANES - 1 :]
        rank = jnp.sum(onehot * upto, axis=0, keepdims=True).astype(jnp.int32) - 1
        in_slot = jnp.where(slot_no == rank, 1.0, 0.0).astype(jnp.bfloat16)
        high = ((local >> 7) + 1).astype(jnp.float32)
        low = (local & 127).astype(jnp.float32)
        digits = jnp.concatenate([jnp.where(hit, high, 0.0), jnp.where(hit, low, 0.0)], axis=0)
        lists = lists + lax.dot_general(
            digits.astype(jnp.bfloat16),
            in_slot,
            CONTRACT_LANES,
            preferred_element_type=jnp.float32,
        )
        last_slots = capacity - first_slots
        position_ref[chunk : chunk + 1, :] = jnp.where(
            rank < first_slots,
            target * first_slots + rank,
            devices * first_slots + target * last_slots + rank - first_slots,
        )
    high, low = lists[:devices], lists[devices:]
    wanted = ((high - 1.0) * 128.0 + low).astype(jnp.int32)
    filled = before.astype(jnp.int32)
    me = lax.axis_index("gx") * lax.axis_size("gy") + lax.axis_index("gy")
    fullest = jnp.max(jnp.where(tile_no[:, :1] == me, 0.0, before), axis=0, keepdims=True)
    listed = jnp.where(high > 0.5, wanted, blocks + filled)
    if first_slots < capacity:
        slot = lax.broadcasted_iota(jnp.int32, (devices, capacity), 1)
        mark = fullest.astype(jnp.int32) * MARK
        listed = listed + jnp.where(slot == capacity - 1, mark, 0)
    outgoing_ref[...] = listed


def edges_kernel(
    field_hbm, xfirst_ref, xlast_ref, yfirst_ref, ylast_ref, planes_ref, strips_ref, sems
):
    cells_x, cells_y, _ = field_hbm.shape
    copies = [
        pltpu.make_async_copy(field_hbm.at[pl.ds(0, 2)], planes_ref.at[0], sems.at[0]),
        pltpu.make_async_copy(field_hbm.at[pl.ds(cells_x - 2, 2)], planes_ref.at[1], sems.at[1]),
        pltpu.make_async_copy(field_hbm.at[:, pl.ds(0, 8)], strips_ref.at[0], sems.at[2]),
        pltpu.make_async_copy(
            field_hbm.at[:, pl.ds(cells_y - 8, 8)], strips_ref.at[1], sems.at[3]
        ),
    ]
    for copy in copies:
        copy.start()
    for copy in copies:
        copy.wait()
    xfirst_ref[...] = planes_ref[0].astype(xfirst_ref.dtype)
    xlast_ref[...] = planes_ref[1].astype(xlast_ref.dtype)
    for h in range(2):
        for x in range(cells_x):
            yfirst_ref[h, x : x + 1, :] = strips_ref[0, x, h : h + 1, :]
            ylast_ref[h, x : x + 1, :] = strips_ref[1, x, 6 + h : 7 + h, :]


def copies_in_parts(source, target, sems):
    parts = sems.shape[0]
    size = source.shape[0] // parts
    return [
        pltpu.make_async_copy(
            source.at[pl.ds(i * size, size)], target.at[pl.ds(i * size, size)], sems.at[i]
        )
        for i in range(parts)
    ]


def for_each_group(incoming_ref, visit, capacity, first_slots, blocks):
    sources = incoming_ref.shape[0] // capacity
    last_slots = capacity - first_slots
    together = 8

    def groups_of(source):
        last = incoming_ref[source * capacity + capacity - 1] & (MARK - 1)
        return (jnp.where(last < blocks, capacity, last - blocks) + GROUP - 1) // GROUP

    def some_sources(quad, carry):
        own = [quad * together + i for i in range(together)]
        most = functools.reduce(jnp.maximum, [groups_of(source) for source in own])

        def one_group(group, carry):
            slot = group * GROUP
            for source in own:
                listed = incoming_ref.at[pl.ds(source * capacity + slot, GROUP)]
                wanted = [listed[j] for j in range(GROUP)]
                visit(wanted, pl.multiple_of(source * first_slots + slot, GROUP), 0)
            return carry

        return lax.fori_loop(0, jnp.minimum(most, first_slots // GROUP), one_group, carry)

    lax.fori_loop(0, sources // together, some_sources, 0)
    if last_slots == 0:
        return

    def one_source(source, carry):
        def one_group(group, carry):
            slot = group * GROUP
            listed = incoming_ref.at[pl.ds(source * capacity + slot, GROUP)]
            wanted = [listed[j] & (MARK - 1) for j in range(GROUP)]
            visit(wanted, pl.multiple_of(source * last_slots + slot - first_slots, GROUP), 1)
            return carry

        return lax.fori_loop(first_slots // GROUP, groups_of(source), one_group, carry)

    lax.fori_loop(0, sources, one_source, 0)


def serve_kernel(incoming_ref, field_hbm, *refs, capacity, first_slots):
    *served_refs, crowded_ref, rows_ref, found_ref, sems = refs
    blocks = field_hbm.shape[0]
    loads = copies_in_parts(field_hbm, rows_ref, sems)
    for load in loads:
        load.start()

    def mark_of(source, most):
        return jnp.maximum(most, incoming_ref[source * capacity + capacity - 1] >> 16)

    fullest = lax.fori_loop(0, incoming_ref.shape[0] // capacity, mark_of, jnp.int32(0))
    crowded_ref[0] = jnp.where(fullest > first_slots, 1, 0)
    rows_ref[blocks:] = jnp.zeros((rows_ref.shape[0] - blocks, 1, LANES), jnp.float32)
    for load in loads:
        load.wait()

    part_starts = [0, served_refs[0].shape[0]]

    def visit(wanted, row, list_part):
        rows = [rows_ref[at] for at in wanted]
        found = found_ref.at[pl.ds(row + part_starts[list_part], GROUP)]
        for j in range(GROUP):
            found[j] = rows[j]

    for_each_group(incoming_ref, visit, capacity, first_slots, blocks)
    found = found_ref.reshape(found_ref.shape[0], LANES)
    for start, served_ref in zip(part_starts, served_refs):
        span = slice(start, start + served_ref.shape[0])
        served_ref[...] = jnp.exp(found[span, :]).astype(jnp.bfloat16)


def match_kernel(incoming_ref, match_ref):
    lane = lax.broadcasted_iota(jnp.int32, (LANES, LANES), 1)
    row = lax.broadcasted_iota(jnp.int32, (LANES, LANES), 0)
    ones = jnp.ones((LANES, LANES), jnp.bfloat16)
    same_group = (lane // GROUP) == (row // GROUP)

    def one_row(i):
        wanted = incoming_ref[pl.ds(i, 1), :]
        high = jnp.where(lane == row, (wanted >> 7).astype(jnp.float32), 0.0).astype(jnp.bfloat16)
        low = jnp.where(lane == row, (wanted & 127).astype(jnp.float32), 0.0).astype(jnp.bfloat16)
        down = 128.0 * jnp.dot(high, ones, preferred_element_type=jnp.float32)
        down = down + jnp.dot(low, ones, preferred_element_type=jnp.float32)
        same = (down == wanted.astype(jnp.float32)) & same_group
        match_ref[pl.ds(pl.multiple_of(i * LANES, LANES), LANES), :] = jnp.where(
            same, 1.0, 0.0
        ).astype(jnp.bfloat16)

    def some_rows(i, carry):
        for j in range(4):
            one_row(4 * i + j)
        return carry

    lax.fori_loop(0, incoming_ref.shape[0] // 4, some_rows, 0)


def star_kernel(position_ref, observed_ref, inverse_ref, weights_hbm, *refs, exchanges):
    returned_refs, refs = refs[:exchanges], refs[exchanges:]
    extinction_ref, refs = refs[0], refs[1:]
    parcel_refs, refs = refs[:exchanges], refs[exchanges:]
    weights_ref, returned_rows, sens_ref, parcel_rows, sems = refs
    sets, in_set, per, slots, stars, width = weights_ref.shape
    chunks = extinction_ref.shape[0]
    rounds = chunks // (sets * in_set)
    per_chunk = per * slots
    fold = LANES // stars
    all_slots = parcel_rows.shape[0]
    sens_blocks = sens_ref.reshape(sens_ref.shape[0], width)
    lane = lax.broadcasted_iota(jnp.int32, (8, LANES), 1)
    row = lax.broadcasted_iota(jnp.int32, (8, LANES), 0)
    star_group = lane // stars
    own_slot = [row == star_group + fold * h for h in range(8 // fold)]

    def load(one_round, one_set):
        return [
            pltpu.make_async_copy(
                weights_hbm.at[pl.ds(((one_round * sets + one_set) * in_set + u) * per, per)],
                weights_ref.at[one_set, u],
                sems.at[one_set, u],
            )
            for u in range(in_set)
        ]

    def extinctions(one_set, u, chunk, places):
        sums = []
        for b in range(per):
            total = jnp.zeros((stars // 8, 8, width), jnp.float32)
            for k in range(slots):
                at = places[u * per_chunk + b * slots + k]
                fetched = returned_rows[pl.ds(at, 8, stride=0), :]
                block = weights_ref[one_set, u, b, k].astype(jnp.float32)
                total = total + block.reshape(stars // 8, 8, width) * fetched
            sums.append(total.reshape(stars, width))
        extinction = lax.dot_general(
            jnp.ones((8, width), jnp.float32),
            jnp.concatenate(sums, axis=0),
            CONTRACT_LANES,
            precision=lax.Precision.HIGHEST,
            preferred_element_type=jnp.float32,
        )
        here = pl.ds(chunk, 1)
        extinction_ref[here, :] = extinction[:1]
        return inverse_ref[here, :] * (extinction - observed_ref[here, :])

    def sensitivities(one_set, u, weighted):
        for b in range(per):
            spread = jnp.where(star_group == b, weighted, 0.0)
            shift = stars
            while shift < LANES:
                spread = spread + pltpu.roll(spread, shift, 1)
                shift *= 2
            left = jnp.concatenate(
                [jnp.where(own, spread, 0.0) for own in own_slot], axis=1
            ).astype(jnp.bfloat16)
            eights = [weights_ref[one_set, u, b, 8 * j : 8 * j + 8] for j in range(slots // 8)]
            right = jnp.concatenate([x.reshape(8 * stars, width) for x in eights], axis=1)
            sens = jnp.dot(left, right, preferred_element_type=jnp.float32)
            for j in range(slots // 8):
                first = u * per_chunk + b * slots + 8 * j
                sens_blocks[first : first + 8, :] = sens[:, j * width : (j + 1) * width]

    def scatter(u, places):
        for i in range(u * per_chunk, (u + 1) * per_chunk):
            parcel_rows[places[i]] = sens_ref[i]

    def work(one_round, one_set):
        first = (one_round * sets + one_set) * in_set
        size = in_set * per_chunk
        places = position_ref.at[pl.ds(pl.multiple_of(first * per_chunk, size), size)]
        weighted = {}
        for u in range(in_set + 2):
            if u < in_set:
                weighted[u] = extinctions(one_set, u, first + u, places)
            if 1 <= u <= in_set:
                sensitivities(one_set, u - 1, weighted[u - 1])
            if u >= 2:
                scatter(u - 2, places)

    for copy in load(0, 0):
        copy.start()
    start = 0
    for returned_ref in returned_refs:
        span = slice(start, start + returned_ref.shape[0])
        returned_rows[span, :] = returned_ref[...].astype(jnp.float32)
        start = span.stop
    parcel_rows.reshape(all_slots, width)[...] = jnp.zeros((all_slots, width), jnp.float32)

    def one_round(i, carry):
        for one_set in range(sets):
            for copy in load(i, one_set):
                copy.wait()
            if one_set + 1 < sets:
                for copy in load(i, one_set + 1):
                    copy.start()
            else:

                @pl.when(i + 1 < rounds)
                def _():
                    for copy in load(i + 1, 0):
                        copy.start()

            work(i, one_set)
        return carry

    lax.fori_loop(0, rounds, one_round, 0)
    start = 0
    for parcel_ref in parcel_refs:
        span = slice(start, start + parcel_ref.shape[0])
        parcel_ref[...] = parcel_rows.reshape(all_slots, width)[span, :].astype(jnp.bfloat16)
        start = span.stop


def prior_kernel(
    field_hbm, xlo_ref, xhi_ref, ylo_ref, yhi_ref, out_hbm, padded, smooth, out_ref, sems, out_sems
):
    cells_x, cells_y, depth = field_hbm.shape
    rows = padded.shape[1]
    parts = sems.shape[0]
    planes = cells_x // parts
    own_rows = pl.ds(8, cells_y)
    loads = [
        pltpu.make_async_copy(
            field_hbm.at[pl.ds(i * planes, planes)],
            padded.at[pl.ds(2 + i * planes, planes), own_rows],
            sems.at[i],
        )
        for i in range(parts)
    ]
    for load in loads:
        load.start()
    gx, gy = lax.axis_index("gx"), lax.axis_index("gy")
    last_gx, last_gy = lax.axis_size("gx") - 1, lax.axis_size("gy") - 1
    z = lax.broadcasted_iota(jnp.int32, (rows, depth), 1)
    y = lax.broadcasted_iota(jnp.int32, (rows, depth), 0) - 8
    inside_y = ((y >= 0) | (gy > 0)) & ((y < cells_y) | (gy < last_gy))

    def operate(center, below, above):
        beside = below + above
        beside = beside + pltpu.roll(center, 1, 0) + pltpu.roll(center, rows - 1, 0)
        beside = beside + jnp.where(z == 0, 0.0, pltpu.roll(center, 1, 1))
        beside = beside + jnp.where(z == depth - 1, 0.0, pltpu.roll(center, depth - 1, 1))
        return (shift_kappa + 6.0) * center - beside

    for h in range(2):
        padded[h, own_rows, :] = xlo_ref[h].astype(jnp.float32)
        padded[cells_x + 2 + h, own_rows, :] = xhi_ref[h].astype(jnp.float32)

    def fill_ends(plane, carry):
        padded[plane, 0:8, :] = jnp.zeros((8, depth), jnp.float32)
        padded[plane, 8 + cells_y :, :] = jnp.zeros((8, depth), jnp.float32)
        for h in range(2):
            padded[plane, 6 + h : 7 + h, :] = ylo_ref[h, pl.ds(plane, 1), :]
            padded[plane, 8 + cells_y + h : 9 + cells_y + h, :] = yhi_ref[h, pl.ds(plane, 1), :]
        return carry

    lax.fori_loop(0, cells_x + 4, fill_ends, 0)
    for load in loads:
        load.wait()

    def smooth_plane(plane, carry):
        value = operate(padded[plane], padded[plane - 1], padded[plane + 1])
        inside = ((plane > 1) | (gx > 0)) & ((plane < cells_x + 2) | (gx < last_gx))
        smooth[plane - 1] = jnp.where(inside_y & inside, value, 0.0)
        return carry

    lax.fori_loop(1, cells_x + 3, smooth_plane, 0)

    def out_plane(x, carry):
        prior = operate(smooth[x + 1], smooth[x], smooth[x + 2])
        change = (step_rate * prior_weight) * prior[8 : 8 + cells_y]
        out_ref[x] = padded[x + 2, own_rows, :] - change
        return carry

    def store(part):
        span = pl.ds(part * planes, planes)
        return pltpu.make_async_copy(out_ref.at[span], out_hbm.at[span], out_sems.at[part])

    for part in range(parts):
        lax.fori_loop(part * planes, (part + 1) * planes, out_plane, 0)
        store(part).start()
    for part in range(parts):
        store(part).wait()


def finish_kernel(
    incoming_ref, match_hbm, field_hbm, base_hbm, *refs, exchanges, capacity, first_slots
):
    arrived_refs, refs = refs[:exchanges], refs[exchanges:]
    out_hbm, collected, rows_ref, match_ref, field_ref, base_ref, out_ref, in_sems, out_sems = refs
    cells_x, cells_y, depth = field_ref.shape
    per_column = depth // LANES
    parts = out_sems.shape[0]
    planes = cells_x // parts
    blocks = cells_x * cells_y * per_column
    matches = copies_in_parts(match_hbm, match_ref, in_sems.at[2])
    loads = copies_in_parts(field_hbm, field_ref, in_sems.at[0])
    loads += copies_in_parts(base_hbm, base_ref, in_sems.at[1])
    for load in matches + loads:
        load.start()
    collected_rows = collected.reshape(collected.shape[0], LANES)
    collected_rows[...] = jnp.zeros_like(collected_rows)
    for load in matches:
        load.wait()
    merged = rows_ref.reshape(rows_ref.shape[0], LANES)
    start = 0
    for arrived_ref in arrived_refs:
        for i in range(arrived_ref.shape[0] // LANES):
            span = slice(start + i * LANES, start + (i + 1) * LANES)
            merged[span, :] = -step_rate * jnp.dot(
                match_ref[span, :],
                arrived_ref[i * LANES : (i + 1) * LANES, :],
                preferred_element_type=jnp.float32,
            )
        start += arrived_ref.shape[0]

    part_starts = [0, arrived_refs[0].shape[0]]

    def visit(wanted, row, list_part):
        row = pl.multiple_of(row + part_starts[list_part], GROUP)
        rows = rows_ref.at[pl.ds(row, GROUP)]
        sums = [collected[wanted[j]] + rows[j] for j in range(GROUP)]
        for j in range(GROUP):
            collected[wanted[j]] = sums[j]

    for_each_group(incoming_ref, visit, capacity, first_slots, blocks)
    for load in loads:
        load.wait()

    def store(part):
        span = pl.ds(part * planes, planes)
        return pltpu.make_async_copy(out_ref.at[span], out_hbm.at[span], out_sems.at[part])

    def one_plane(x, carry):
        for yb in range(cells_y // 8):
            for part in range(per_column):
                at = pl.multiple_of(((x * (cells_y // 8) + yb) * per_column + part) * 8, 8)
                here = (x, slice(8 * yb, 8 * yb + 8), slice(part * LANES, (part + 1) * LANES))
                out_ref[here] = base_ref[here] + collected_rows[pl.ds(at, 8), :] * jnp.exp(
                    field_ref[here]
                )
        return carry

    for part in range(parts):
        lax.fori_loop(part * planes, (part + 1) * planes, one_plane, 0)
        store(part).start()
    for part in range(parts):
        store(part).wait()


def both_ways(first, last, axis):
    peers = lax.axis_size(axis)
    up = [(i, i + 1) for i in range(peers - 1)]
    down = [(j, i) for i, j in up]
    return lax.ppermute(last, axis, up), lax.ppermute(first, axis, down)


def halo(xfirst, xlast, yfirst, ylast):
    xlo, xhi = both_ways(xfirst, xlast, "gx")

    def rows(own, at):
        ends = [x[:, at].transpose(1, 0, 2) for x in (xlo, xhi)]
        return jnp.concatenate([ends[0], own.astype(xlo.dtype), ends[1]], axis=1)

    ylo, yhi = both_ways(rows(yfirst, slice(0, 2)), rows(ylast, slice(-2, None)), "gy")
    return xlo, xhi, ylo.astype(jnp.float32), yhi.astype(jnp.float32)


VMEM = pl.BlockSpec(memory_space=pltpu.VMEM)
SMEM = pl.BlockSpec(memory_space=pltpu.SMEM)
ANY = pl.BlockSpec(memory_space=pl.ANY)


def on_device(log_density, weights, observed, inverse_var, star_counts, block_ids):
    cells_x, cells_y, depth = log_density.shape
    blocks_dev, slots, stars, width = weights.shape
    devices = lax.axis_size("gx") * lax.axis_size("gy")
    requests = blocks_dev * slots
    capacity = 2 * requests // devices
    first_slots = 11 * capacity // 16 if capacity % LANES == 0 else capacity
    slots_of = [n for n in (first_slots, capacity - first_slots) if n > 0]
    exchanges = len(slots_of)
    all_slots = devices * capacity
    per_column = depth // width
    blocks = cells_x * cells_y * per_column
    cells = log_density.size
    field_shape = (cells_x, cells_y, depth)
    mesh_axes = ("gx", "gy")
    f32, bf16, i32 = jnp.float32, jnp.bfloat16, jnp.int32
    shape = jax.ShapeDtypeStruct

    def to_rows(x):
        x = x.reshape(cells_x, cells_y // 8, 8, per_column, width)
        return x.transpose(0, 1, 3, 2, 4).reshape(blocks, 1, width)

    def exchange(x):
        return lax.all_to_all(x, mesh_axes, split_axis=0, concat_axis=0, tiled=True)

    def exchange_rows(parts, crowded):
        moved = [parts[0].reshape(devices, first_slots, width)]
        moved[0] = exchange(moved[0])
        for part in parts[1:]:
            part = part.reshape(devices, capacity - first_slots, width)
            moved.append(lax.cond(crowded, exchange, lambda x: x, part))
        return [x.reshape(-1, width) for x in moved]

    outgoing, position = pl.pallas_call(
        functools.partial(
            route_kernel,
            devices=devices,
            capacity=capacity,
            first_slots=first_slots,
            blocks=blocks,
            per_column=per_column,
        ),
        out_shape=[shape((devices, capacity), i32), shape((requests // LANES, LANES), i32)],
        in_specs=[VMEM],
        out_specs=[VMEM, VMEM],
        name="route",
    )(block_ids.T)
    incoming = exchange(outgoing)

    field, _ = lax.optimization_barrier((log_density, outgoing))
    xfirst, xlast, yfirst, ylast = pl.pallas_call(
        edges_kernel,
        out_shape=[
            shape((2, cells_y, depth), bf16),
            shape((2, cells_y, depth), bf16),
            shape((2, cells_x, depth), f32),
            shape((2, cells_x, depth), f32),
        ],
        in_specs=[ANY],
        out_specs=[VMEM] * 4,
        scratch_shapes=[
            pltpu.VMEM((2, 2, cells_y, depth), f32),
            pltpu.VMEM((2, cells_x, 8, depth), f32),
            pltpu.SemaphoreType.DMA((4,)),
        ],
        compiler_params=pltpu.CompilerParams(vmem_limit_bytes=56 * MIB),
        cost_estimate=pl.CostEstimate(flops=0, bytes_accessed=2 * MIB, transcendentals=0),
        name="edges",
    )(field)
    incoming, *edges = lax.optimization_barrier((incoming, xfirst, xlast, yfirst, ylast))
    wanted = incoming.reshape(-1)

    *served, crowded = pl.pallas_call(
        functools.partial(serve_kernel, capacity=capacity, first_slots=first_slots),
        out_shape=[shape((devices * n, width), bf16) for n in slots_of] + [shape((1,), i32)],
        in_specs=[SMEM, ANY],
        out_specs=[VMEM] * exchanges + [SMEM],
        scratch_shapes=[
            pltpu.VMEM((blocks + capacity, 1, width), f32),
            pltpu.VMEM((all_slots, 1, width), f32),
            pltpu.SemaphoreType.DMA((16,)),
        ],
        compiler_params=pltpu.CompilerParams(vmem_limit_bytes=56 * MIB),
        cost_estimate=pl.CostEstimate(
            flops=cells, bytes_accessed=6 * MIB, transcendentals=cells
        ),
        name="serve",
    )(wanted, to_rows(log_density))
    crowded = crowded[0] != 0

    returned = exchange_rows(served, crowded)
    *edges, _ = lax.optimization_barrier((*edges, served[0]))
    xlo, xhi, ylo, yhi = halo(*edges)
    *returned, ylo, yhi = lax.optimization_barrier((*returned, ylo, yhi))

    chunks = blocks_dev * stars // LANES
    in_set = chunks // 4
    live = jnp.arange(stars)[None, :] < star_counts[:, None]
    live_inverse = jnp.where(live, inverse_var, 0.0)
    extinction, *parcel = pl.pallas_call(
        functools.partial(star_kernel, exchanges=exchanges),
        out_shape=[shape((chunks, LANES), f32)]
        + [shape((devices * n, width), bf16) for n in slots_of],
        in_specs=[SMEM, VMEM, VMEM, ANY] + [VMEM] * exchanges,
        out_specs=[VMEM] * (1 + exchanges),
        scratch_shapes=[
            pltpu.VMEM((2, in_set, blocks_dev // chunks, slots, stars, width), bf16),
            pltpu.VMEM((all_slots + 8, width), f32),
            pltpu.VMEM((in_set * (blocks_dev // chunks) * slots, 1, width), f32),
            pltpu.VMEM((all_slots, 1, width), f32),
            pltpu.SemaphoreType.DMA((2, in_set)),
        ],
        compiler_params=pltpu.CompilerParams(vmem_limit_bytes=50 * MIB),
        cost_estimate=pl.CostEstimate(
            flops=4 * weights.size, bytes_accessed=2 * weights.size, transcendentals=0
        ),
        name="stars",
    )(
        position.reshape(slots // 2, 2, blocks_dev).transpose(2, 1, 0).reshape(requests),
        observed.reshape(chunks, LANES),
        live_inverse.reshape(chunks, LANES),
        weights,
        *returned,
    )
    arrived = exchange_rows(parcel, crowded)

    field_late, incoming_late, _ = lax.optimization_barrier((log_density, incoming, parcel[0]))
    slot_lists = [
        incoming_late[:, :first_slots].reshape(-1, LANES),
        (incoming_late[:, first_slots:] & (MARK - 1)).reshape(-1, LANES),
    ][:exchanges]
    match = pl.pallas_call(
        match_kernel,
        out_shape=shape((all_slots, LANES), bf16),
        in_specs=[VMEM],
        out_specs=VMEM,
        compiler_params=pltpu.CompilerParams(vmem_limit_bytes=8 * MIB),
        cost_estimate=pl.CostEstimate(flops=10**9, bytes_accessed=MIB, transcendentals=0),
        name="match",
    )(jnp.concatenate(slot_lists, axis=0))
    parts = 8
    base = pl.pallas_call(
        prior_kernel,
        out_shape=shape(field_shape, f32),
        in_specs=[ANY] + [VMEM] * 4,
        out_specs=ANY,
        scratch_shapes=[
            pltpu.VMEM((cells_x + 4, cells_y + 16, depth), f32),
            pltpu.VMEM((cells_x + 2, cells_y + 16, depth), f32),
            pltpu.VMEM(field_shape, f32),
            pltpu.SemaphoreType.DMA((parts,)),
            pltpu.SemaphoreType.DMA((parts,)),
        ],
        compiler_params=pltpu.CompilerParams(vmem_limit_bytes=56 * MIB),
        cost_estimate=pl.CostEstimate(
            flops=30 * cells, bytes_accessed=8 * cells, transcendentals=0
        ),
        name="prior",
    )(field_late, xlo, xhi, ylo, yhi)

    new_log_density = pl.pallas_call(
        functools.partial(
            finish_kernel, exchanges=exchanges, capacity=capacity, first_slots=first_slots
        ),
        out_shape=shape(field_shape, f32),
        in_specs=[SMEM, ANY, ANY, ANY] + [VMEM] * exchanges,
        out_specs=ANY,
        scratch_shapes=[
            pltpu.VMEM((blocks + capacity, 1, width), f32),
            pltpu.VMEM((all_slots, 1, width), f32),
            pltpu.VMEM((all_slots, LANES), bf16),
            pltpu.VMEM(field_shape, f32),
            pltpu.VMEM(field_shape, f32),
            pltpu.VMEM(field_shape, f32),
            pltpu.SemaphoreType.DMA((3, parts)),
            pltpu.SemaphoreType.DMA((parts,)),
        ],
        compiler_params=pltpu.CompilerParams(vmem_limit_bytes=50 * MIB),
        cost_estimate=pl.CostEstimate(
            flops=4 * cells, bytes_accessed=12 * cells, transcendentals=cells
        ),
        name="finish",
    )(wanted, match, log_density, base, *arrived)
    return new_log_density, extinction.reshape(blocks_dev, stars)


def solution(mesh):
    placed = (
        P("gx", "gy", None),
        P(("gx", "gy"), None, None, None),
        P(("gx", "gy"), None),
        P(("gx", "gy"), None),
        P(("gx", "gy")),
        P(("gx", "gy"), None),
    )
    return jax.shard_map(
        on_device,
        mesh=mesh,
        in_specs=placed,
        out_specs=(P("gx", "gy", None), P(("gx", "gy"), None)),
        check_vma=False,
    )
```

```python
import functools

import jax
import jax.numpy as jnp
from jax import lax
from jax.experimental import pallas as pl
from jax.experimental.pallas import tpu as pltpu
from jax.sharding import PartitionSpec as P

shift_kappa = 0.5
prior_weight = 0.05
step_rate = 2.0

LANES = 128
GROUP = 8
MIB = 1 << 20
MARK = 1 << 16

CONTRACT_LANES = (((1,), (1,)), ((), ()))


def split_by(value, size):
    if size & (size - 1) == 0:
        high = value >> (size.bit_length() - 1)
        return high, value & (size - 1)
    high = value // size
    return high, value - high * size


def route_kernel(
    ids_ref, outgoing_ref, position_ref, *, devices, capacity, first_slots, blocks, per_column
):
    half = ids_ref.shape[0] // 2
    ids = jnp.concatenate([ids_ref[:half, :], ids_ref[half:, :]], axis=1)
    lane = lax.broadcasted_iota(jnp.int32, (LANES, LANES), 1)
    row = lax.broadcasted_iota(jnp.int32, (LANES, LANES), 0)
    upper = jnp.where(row <= lane, 1.0, 0.0).astype(jnp.bfloat16)
    tile_no = lax.broadcasted_iota(jnp.int32, (devices, LANES), 0)
    slot_no = lax.broadcasted_iota(jnp.int32, (capacity, LANES), 0)
    before = jnp.zeros((devices, 1), jnp.float32)
    lists = jnp.zeros((2 * devices, capacity), jnp.float32)
    for chunk in range(half):
        target, local = split_by(ids[chunk : chunk + 1, :], blocks)
        column, part = split_by(local, per_column)
        local = ((column >> 3) * per_column + part) * 8 + (column & 7)
        hit = tile_no == target
        onehot = jnp.where(hit, 1.0, 0.0)
        upto = before + jnp.dot(
            onehot.astype(jnp.bfloat16), upper, preferred_element_type=jnp.float32
        )
        before = upto[:, LANES - 1 :]
        rank = jnp.sum(onehot * upto, axis=0, keepdims=True).astype(jnp.int32) - 1
        in_slot = jnp.where(slot_no == rank, 1.0, 0.0).astype(jnp.bfloat16)
        high = ((local >> 7) + 1).astype(jnp.float32)
        low = (local & 127).astype(jnp.float32)
        digits = jnp.concatenate([jnp.where(hit, high, 0.0), jnp.where(hit, low, 0.0)], axis=0)
        lists = lists + lax.dot_general(
            digits.astype(jnp.bfloat16),
            in_slot,
            CONTRACT_LANES,
            preferred_element_type=jnp.float32,
        )
        last_slots = capacity - first_slots
        position_ref[chunk : chunk + 1, :] = jnp.where(
            rank < first_slots,
            target * first_slots + rank,
            devices * first_slots + target * last_slots + rank - first_slots,
        )
    high, low = lists[:devices], lists[devices:]
    wanted = ((high - 1.0) * 128.0 + low).astype(jnp.int32)
    filled = before.astype(jnp.int32)
    me = lax.axis_index("gx") * lax.axis_size("gy") + lax.axis_index("gy")
    fullest = jnp.max(jnp.where(tile_no[:, :1] == me, 0.0, before), axis=0, keepdims=True)
    listed = jnp.where(high > 0.5, wanted, blocks + filled)
    if first_slots < capacity:
        slot = lax.broadcasted_iota(jnp.int32, (devices, capacity), 1)
        mark = fullest.astype(jnp.int32) * MARK
        listed = listed + jnp.where(slot == capacity - 1, mark, 0)
    outgoing_ref[...] = listed


def edges_kernel(
    field_hbm, xfirst_ref, xlast_ref, yfirst_ref, ylast_ref, planes_ref, strips_ref, sems
):
    cells_x, cells_y, _ = field_hbm.shape
    copies = [
        pltpu.make_async_copy(field_hbm.at[pl.ds(0, 2)], planes_ref.at[0], sems.at[0]),
        pltpu.make_async_copy(field_hbm.at[pl.ds(cells_x - 2, 2)], planes_ref.at[1], sems.at[1]),
        pltpu.make_async_copy(field_hbm.at[:, pl.ds(0, 8)], strips_ref.at[0], sems.at[2]),
        pltpu.make_async_copy(
            field_hbm.at[:, pl.ds(cells_y - 8, 8)], strips_ref.at[1], sems.at[3]
        ),
    ]
    for copy in copies:
        copy.start()
    for copy in copies:
        copy.wait()
    xfirst_ref[...] = planes_ref[0].astype(xfirst_ref.dtype)
    xlast_ref[...] = planes_ref[1].astype(xlast_ref.dtype)
    for h in range(2):
        for x in range(cells_x):
            yfirst_ref[h, x + 2 : x + 3, :] = strips_ref[0, x, h : h + 1, :]
            ylast_ref[h, x + 2 : x + 3, :] = strips_ref[1, x, 6 + h : 7 + h, :]


def ends_kernel(
    xlo_ref, xhi_ref, yfirst_ref, ylast_ref, first_ref, last_ref, slab_ref
):
    cells_y = xlo_ref.shape[1]
    length = yfirst_ref.shape[1]
    for own_ref, out_ref, start, row in (
        (yfirst_ref, first_ref, 0, 0),
        (ylast_ref, last_ref, cells_y - 16, 14),
    ):
        slab_ref[...] = own_ref[...]
        for e in range(2):
            for x_ref, at in ((xlo_ref, e), (xhi_ref, length - 2 + e)):
                block = x_ref[e, start : start + 16, :].astype(jnp.float32)
                for h in range(2):
                    slab_ref[h, at : at + 1, :] = block[row + h : row + h + 1, :]
        out_ref[...] = slab_ref[...].astype(out_ref.dtype)


def copies_in_parts(source, target, sems):
    parts = sems.shape[0]
    size = source.shape[0] // parts
    return [
        pltpu.make_async_copy(
            source.at[pl.ds(i * size, size)], target.at[pl.ds(i * size, size)], sems.at[i]
        )
        for i in range(parts)
    ]


def for_each_group(incoming_ref, visit, capacity, first_slots, blocks):
    sources = incoming_ref.shape[0] // capacity
    last_slots = capacity - first_slots
    together = 8

    def groups_of(source):
        last = incoming_ref[source * capacity + capacity - 1] & (MARK - 1)
        return (jnp.where(last < blocks, capacity, last - blocks) + GROUP - 1) // GROUP

    def some_sources(quad, carry):
        own = [quad * together + i for i in range(together)]
        most = functools.reduce(jnp.maximum, [groups_of(source) for source in own])

        def one_group(group, carry):
            slot = group * GROUP
            for which, source in enumerate(own):
                listed = incoming_ref.at[pl.ds(source * capacity + slot, GROUP)]
                wanted = [listed[j] for j in range(GROUP)]
                visit(wanted, pl.multiple_of(source * first_slots + slot, GROUP), 0, which)
            return carry

        return lax.fori_loop(0, jnp.minimum(most, first_slots // GROUP), one_group, carry)

    lax.fori_loop(0, sources // together, some_sources, 0)
    if last_slots == 0:
        return

    def one_source(source, carry):
        def one_group(group, carry):
            slot = group * GROUP
            listed = incoming_ref.at[pl.ds(source * capacity + slot, GROUP)]
            wanted = [listed[j] & (MARK - 1) for j in range(GROUP)]
            visit(wanted, pl.multiple_of(source * last_slots + slot - first_slots, GROUP), 1, 0)
            return carry

        return lax.fori_loop(first_slots // GROUP, groups_of(source), one_group, carry)

    lax.fori_loop(0, sources, one_source, 0)


def serve_kernel(incoming_ref, field_hbm, *refs, capacity, first_slots):
    *served_refs, crowded_ref, rows_ref, found_ref, sems = refs
    blocks = field_hbm.shape[0]
    loads = copies_in_parts(field_hbm, rows_ref, sems)
    for load in loads:
        load.start()

    def mark_of(source, most):
        return jnp.maximum(most, incoming_ref[source * capacity + capacity - 1] >> 16)

    fullest = lax.fori_loop(0, incoming_ref.shape[0] // capacity, mark_of, jnp.int32(0))
    crowded_ref[0] = jnp.where(fullest > first_slots, 1, 0)
    rows_ref[blocks:] = jnp.zeros((rows_ref.shape[0] - blocks, 1, LANES), jnp.float32)
    for load in loads:
        load.wait()

    part_starts = [0, served_refs[0].shape[0]]

    def visit(wanted, row, list_part, which):
        rows = [rows_ref[at] for at in wanted]
        found = found_ref.at[pl.ds(row + part_starts[list_part], GROUP)]
        for j in range(GROUP):
            found[j] = rows[j]

    for_each_group(incoming_ref, visit, capacity, first_slots, blocks)
    found = found_ref.reshape(found_ref.shape[0], LANES)
    for start, served_ref in zip(part_starts, served_refs):
        span = slice(start, start + served_ref.shape[0])
        served_ref[...] = jnp.exp(found[span, :]).astype(jnp.bfloat16)


def match_kernel(incoming_ref, match_ref):
    lane = lax.broadcasted_iota(jnp.int32, (LANES, LANES), 1)
    row = lax.broadcasted_iota(jnp.int32, (LANES, LANES), 0)
    ones = jnp.ones((LANES, LANES), jnp.bfloat16)
    same_group = (lane // GROUP) == (row // GROUP)

    def one_row(i):
        wanted = incoming_ref[pl.ds(i, 1), :]
        high = jnp.where(lane == row, (wanted >> 7).astype(jnp.float32), 0.0).astype(jnp.bfloat16)
        low = jnp.where(lane == row, (wanted & 127).astype(jnp.float32), 0.0).astype(jnp.bfloat16)
        down = 128.0 * jnp.dot(high, ones, preferred_element_type=jnp.float32)
        down = down + jnp.dot(low, ones, preferred_element_type=jnp.float32)
        same = (down == wanted.astype(jnp.float32)) & same_group
        match_ref[pl.ds(pl.multiple_of(i * LANES, LANES), LANES), :] = jnp.where(
            same, 1.0, 0.0
        ).astype(jnp.bfloat16)

    def some_rows(i, carry):
        for j in range(4):
            one_row(4 * i + j)
        return carry

    lax.fori_loop(0, incoming_ref.shape[0] // 4, some_rows, 0)


def star_kernel(position_ref, observed_ref, inverse_ref, weights_hbm, *refs, exchanges):
    returned_refs, refs = refs[:exchanges], refs[exchanges:]
    extinction_ref, refs = refs[0], refs[1:]
    parcel_refs, refs = refs[:exchanges], refs[exchanges:]
    weights_ref, returned_rows, sens_ref, parcel_rows, sems = refs
    sets, in_set, per, slots, stars, width = weights_ref.shape
    chunks = extinction_ref.shape[0]
    rounds = chunks // (sets * in_set)
    per_chunk = per * slots
    fold = LANES // stars
    all_slots = parcel_rows.shape[0]
    sens_blocks = sens_ref.reshape(sens_ref.shape[0], width)
    lane = lax.broadcasted_iota(jnp.int32, (8, LANES), 1)
    row = lax.broadcasted_iota(jnp.int32, (8, LANES), 0)
    star_group = lane // stars
    own_slot = [row == star_group + fold * h for h in range(8 // fold)]

    def load(one_round, one_set):
        return [
            pltpu.make_async_copy(
                weights_hbm.at[pl.ds(((one_round * sets + one_set) * in_set + u) * per, per)],
                weights_ref.at[one_set, u],
                sems.at[one_set, u],
            )
            for u in range(in_set)
        ]

    def extinctions(one_set, u, chunk, places):
        sums = []
        for b in range(per):
            total = jnp.zeros((stars // 8, 8, width), jnp.float32)
            for k in range(slots):
                at = places[u * per_chunk + b * slots + k]
                fetched = returned_rows[pl.ds(at, 8, stride=0), :]
                block = weights_ref[one_set, u, b, k].astype(jnp.float32)
                total = total + block.reshape(stars // 8, 8, width) * fetched
            sums.append(total.reshape(stars, width))
        extinction = lax.dot_general(
            jnp.ones((8, width), jnp.float32),
            jnp.concatenate(sums, axis=0),
            CONTRACT_LANES,
            precision=lax.Precision.HIGHEST,
            preferred_element_type=jnp.float32,
        )
        here = pl.ds(chunk, 1)
        extinction_ref[here, :] = extinction[:1]
        return inverse_ref[here, :] * (extinction - observed_ref[here, :])

    def sensitivities(one_set, u, weighted):
        for b in range(per):
            spread = jnp.where(star_group == b, weighted, 0.0)
            shift = stars
            while shift < LANES:
                spread = spread + pltpu.roll(spread, shift, 1)
                shift *= 2
            left = jnp.concatenate(
                [jnp.where(own, spread, 0.0) for own in own_slot], axis=1
            ).astype(jnp.bfloat16)
            eights = [weights_ref[one_set, u, b, 8 * j : 8 * j + 8] for j in range(slots // 8)]
            right = jnp.concatenate([x.reshape(8 * stars, width) for x in eights], axis=1)
            sens = jnp.dot(left, right, preferred_element_type=jnp.float32)
            for j in range(slots // 8):
                first = u * per_chunk + b * slots + 8 * j
                sens_blocks[first : first + 8, :] = sens[:, j * width : (j + 1) * width]

    def scatter(u, places):
        for i in range(u * per_chunk, (u + 1) * per_chunk):
            parcel_rows[places[i]] = sens_ref[i]

    def work(one_round, one_set):
        first = (one_round * sets + one_set) * in_set
        size = in_set * per_chunk
        places = position_ref.at[pl.ds(pl.multiple_of(first * per_chunk, size), size)]
        weighted = {}
        for u in range(in_set + 2):
            if u < in_set:
                weighted[u] = extinctions(one_set, u, first + u, places)
            if 1 <= u <= in_set:
                sensitivities(one_set, u - 1, weighted[u - 1])
            if u >= 2:
                scatter(u - 2, places)

    for copy in load(0, 0):
        copy.start()
    start = 0
    for returned_ref in returned_refs:
        span = slice(start, start + returned_ref.shape[0])
        returned_rows[span, :] = returned_ref[...].astype(jnp.float32)
        start = span.stop
    parcel_rows.reshape(all_slots, width)[...] = jnp.zeros((all_slots, width), jnp.float32)

    def one_round(i, carry):
        for one_set in range(sets):
            for copy in load(i, one_set):
                copy.wait()
            if one_set + 1 < sets:
                for copy in load(i, one_set + 1):
                    copy.start()
            else:

                @pl.when(i + 1 < rounds)
                def _():
                    for copy in load(i + 1, 0):
                        copy.start()

            work(i, one_set)
        return carry

    lax.fori_loop(0, rounds, one_round, 0)
    start = 0
    for parcel_ref in parcel_refs:
        span = slice(start, start + parcel_ref.shape[0])
        parcel_ref[...] = parcel_rows.reshape(all_slots, width)[span, :].astype(jnp.bfloat16)
        start = span.stop


def prior_kernel(
    field_hbm, xlo_ref, xhi_ref, ylo_ref, yhi_ref, out_hbm,
    padded, smooth, out_ref, yends_ref, sems, out_sems,
):
    cells_x, cells_y, depth = field_hbm.shape
    rows = padded.shape[1]
    parts = sems.shape[0]
    planes = cells_x // parts
    own_rows = pl.ds(8, cells_y)
    loads = [
        pltpu.make_async_copy(
            field_hbm.at[pl.ds(i * planes, planes)],
            padded.at[pl.ds(2 + i * planes, planes), own_rows],
            sems.at[i],
        )
        for i in range(parts)
    ]
    for load in loads:
        load.start()
    gx, gy = lax.axis_index("gx"), lax.axis_index("gy")
    last_gx, last_gy = lax.axis_size("gx") - 1, lax.axis_size("gy") - 1
    z = lax.broadcasted_iota(jnp.int32, (rows, depth), 1)
    y = lax.broadcasted_iota(jnp.int32, (rows, depth), 0) - 8
    inside_y = ((y >= 0) | (gy > 0)) & ((y < cells_y) | (gy < last_gy))

    def operate(center, below, above):
        beside = below + above
        beside = beside + pltpu.roll(center, 1, 0) + pltpu.roll(center, rows - 1, 0)
        beside = beside + jnp.where(z == 0, 0.0, pltpu.roll(center, 1, 1))
        beside = beside + jnp.where(z == depth - 1, 0.0, pltpu.roll(center, depth - 1, 1))
        return (shift_kappa + 6.0) * center - beside

    for h in range(2):
        padded[h, own_rows, :] = xlo_ref[h].astype(jnp.float32)
        padded[cells_x + 2 + h, own_rows, :] = xhi_ref[h].astype(jnp.float32)

    yends_ref[0] = ylo_ref[...].astype(jnp.float32)
    yends_ref[1] = yhi_ref[...].astype(jnp.float32)

    def fill_ends(plane, carry):
        padded[plane, 0:8, :] = jnp.zeros((8, depth), jnp.float32)
        padded[plane, 8 + cells_y :, :] = jnp.zeros((8, depth), jnp.float32)
        for h in range(2):
            padded[plane, 6 + h : 7 + h, :] = yends_ref[0, h, pl.ds(plane, 1), :]
            padded[plane, 8 + cells_y + h : 9 + cells_y + h, :] = yends_ref[1, h, pl.ds(plane, 1), :]
        return carry

    lax.fori_loop(0, cells_x + 4, fill_ends, 0)

    def smooth_plane(plane, carry):
        value = operate(padded[plane], padded[plane - 1], padded[plane + 1])
        inside = ((plane > 1) | (gx > 0)) & ((plane < cells_x + 2) | (gx < last_gx))
        smooth[plane - 1] = jnp.where(inside_y & inside, value, 0.0)
        return carry

    def out_plane(x, carry):
        prior = operate(smooth[x + 1], smooth[x], smooth[x + 2])
        change = (step_rate * prior_weight) * prior[8 : 8 + cells_y]
        out_ref[x] = padded[x + 2, own_rows, :] - change
        return carry

    def store(part):
        span = pl.ds(part * planes, planes)
        return pltpu.make_async_copy(out_ref.at[span], out_hbm.at[span], out_sems.at[part])

    smoothed, done = 1, 0
    for part in range(parts):
        loads[part].wait()
        ready = cells_x + 3 if part + 1 == parts else 1 + (part + 1) * planes
        lax.fori_loop(smoothed, ready, smooth_plane, 0)
        smoothed = ready
        lax.fori_loop(done, ready - 3, out_plane, 0)
        done = ready - 3
        for whole in range(parts):
            if part * planes - 2 < (whole + 1) * planes <= done:
                store(whole).start()
    for part in range(parts):
        store(part).wait()


def finish_kernel(
    incoming_ref, match_hbm, field_hbm, base_hbm, *refs, exchanges, capacity, first_slots
):
    arrived_refs, refs = refs[:exchanges], refs[exchanges:]
    out_hbm, *collected, rows_ref, match_ref, field_ref, base_ref, out_ref, in_sems, out_sems = refs
    cells_x, cells_y, depth = field_ref.shape
    per_column = depth // LANES
    parts = out_sems.shape[0]
    planes = cells_x // parts
    blocks = cells_x * cells_y * per_column
    matches = copies_in_parts(match_hbm, match_ref, in_sems.at[2])
    loads = copies_in_parts(field_hbm, field_ref, in_sems.at[0])
    loads += copies_in_parts(base_hbm, base_ref, in_sems.at[1])
    for load in matches + loads:
        load.start()
    collected_rows = [ref.reshape(ref.shape[0], LANES) for ref in collected]
    for ref in collected_rows:
        ref[...] = jnp.zeros_like(ref)
    for load in matches:
        load.wait()
    merged = rows_ref.reshape(rows_ref.shape[0], LANES)
    start = 0
    for arrived_ref in arrived_refs:
        for i in range(arrived_ref.shape[0] // LANES):
            span = slice(start + i * LANES, start + (i + 1) * LANES)
            merged[span, :] = -step_rate * jnp.dot(
                match_ref[span, :],
                arrived_ref[i * LANES : (i + 1) * LANES, :],
                preferred_element_type=jnp.float32,
            )
        start += arrived_ref.shape[0]

    part_starts = [0, arrived_refs[0].shape[0]]

    def visit(wanted, row, list_part, which):
        row = pl.multiple_of(row + part_starts[list_part], GROUP)
        rows = rows_ref.at[pl.ds(row, GROUP)]
        into = collected[which % len(collected)]
        sums = [into[wanted[j]] + rows[j] for j in range(GROUP)]
        for j in range(GROUP):
            into[wanted[j]] = sums[j]

    for_each_group(incoming_ref, visit, capacity, first_slots, blocks)
    for load in loads:
        load.wait()

    def store(part):
        span = pl.ds(part * planes, planes)
        return pltpu.make_async_copy(out_ref.at[span], out_hbm.at[span], out_sems.at[part])

    def one_plane(x, carry):
        for yb in range(cells_y // 8):
            for part in range(per_column):
                at = pl.multiple_of(((x * (cells_y // 8) + yb) * per_column + part) * 8, 8)
                here = (x, slice(8 * yb, 8 * yb + 8), slice(part * LANES, (part + 1) * LANES))
                grad = collected_rows[0][pl.ds(at, 8), :] + collected_rows[1][pl.ds(at, 8), :]
                out_ref[here] = base_ref[here] + grad * jnp.exp(field_ref[here])
        return carry

    for part in range(parts):
        lax.fori_loop(part * planes, (part + 1) * planes, one_plane, 0)
        store(part).start()
    for part in range(parts):
        store(part).wait()


def both_ways(first, last, axis):
    peers = lax.axis_size(axis)
    up = [(i, i + 1) for i in range(peers - 1)]
    down = [(j, i) for i, j in up]
    return lax.ppermute(last, axis, up), lax.ppermute(first, axis, down)


VMEM = pl.BlockSpec(memory_space=pltpu.VMEM)
SMEM = pl.BlockSpec(memory_space=pltpu.SMEM)
ANY = pl.BlockSpec(memory_space=pl.ANY)


def on_device(log_density, weights, observed, inverse_var, star_counts, block_ids):
    cells_x, cells_y, depth = log_density.shape
    blocks_dev, slots, stars, width = weights.shape
    devices = lax.axis_size("gx") * lax.axis_size("gy")
    requests = blocks_dev * slots
    capacity = 2 * requests // devices
    first_slots = 11 * capacity // 16 if capacity % LANES == 0 else capacity
    slots_of = [n for n in (first_slots, capacity - first_slots) if n > 0]
    exchanges = len(slots_of)
    all_slots = devices * capacity
    per_column = depth // width
    blocks = cells_x * cells_y * per_column
    cells = log_density.size
    field_shape = (cells_x, cells_y, depth)
    mesh_axes = ("gx", "gy")
    f32, bf16, i32 = jnp.float32, jnp.bfloat16, jnp.int32
    shape = jax.ShapeDtypeStruct

    def to_rows(x):
        x = x.reshape(cells_x, cells_y // 8, 8, per_column, width)
        return x.transpose(0, 1, 3, 2, 4).reshape(blocks, 1, width)

    def exchange(x):
        return lax.all_to_all(x, mesh_axes, split_axis=0, concat_axis=0, tiled=True)

    def exchange_rows(parts, crowded):
        moved = [parts[0].reshape(devices, first_slots, width)]
        moved[0] = exchange(moved[0])
        for part in parts[1:]:
            part = part.reshape(devices, capacity - first_slots, width)
            moved.append(lax.cond(crowded, exchange, lambda x: x, part))
        return [x.reshape(-1, width) for x in moved]

    outgoing, position = pl.pallas_call(
        functools.partial(
            route_kernel,
            devices=devices,
            capacity=capacity,
            first_slots=first_slots,
            blocks=blocks,
            per_column=per_column,
        ),
        out_shape=[shape((devices, capacity), i32), shape((requests // LANES, LANES), i32)],
        in_specs=[VMEM],
        out_specs=[VMEM, VMEM],
        name="route",
    )(block_ids.T)
    incoming = exchange(outgoing)

    field, _ = lax.optimization_barrier((log_density, outgoing))
    xfirst, xlast, yfirst, ylast = pl.pallas_call(
        edges_kernel,
        out_shape=[
            shape((2, cells_y, depth), bf16),
            shape((2, cells_y, depth), bf16),
            shape((2, cells_x + 4, depth), f32),
            shape((2, cells_x + 4, depth), f32),
        ],
        in_specs=[ANY],
        out_specs=[VMEM] * 4,
        scratch_shapes=[
            pltpu.VMEM((2, 2, cells_y, depth), f32),
            pltpu.VMEM((2, cells_x, 8, depth), f32),
            pltpu.SemaphoreType.DMA((4,)),
        ],
        compiler_params=pltpu.CompilerParams(vmem_limit_bytes=56 * MIB),
        cost_estimate=pl.CostEstimate(flops=0, bytes_accessed=2 * MIB, transcendentals=0),
        name="edges",
    )(field)
    xlo, xhi = both_ways(xfirst, xlast, "gx")
    incoming, *edges = lax.optimization_barrier((incoming, xlo, xhi, yfirst, ylast))
    wanted = incoming.reshape(-1)

    *served, crowded = pl.pallas_call(
        functools.partial(serve_kernel, capacity=capacity, first_slots=first_slots),
        out_shape=[shape((devices * n, width), bf16) for n in slots_of] + [shape((1,), i32)],
        in_specs=[SMEM, ANY],
        out_specs=[VMEM] * exchanges + [SMEM],
        scratch_shapes=[
            pltpu.VMEM((blocks + capacity, 1, width), f32),
            pltpu.VMEM((all_slots, 1, width), f32),
            pltpu.SemaphoreType.DMA((16,)),
        ],
        compiler_params=pltpu.CompilerParams(vmem_limit_bytes=56 * MIB),
        cost_estimate=pl.CostEstimate(
            flops=cells, bytes_accessed=6 * MIB, transcendentals=cells
        ),
        name="serve",
    )(wanted, to_rows(log_density))
    crowded = crowded[0] != 0

    returned = exchange_rows(served, crowded)
    *edges, incoming_late, _ = lax.optimization_barrier((*edges, incoming, served[0]))
    slabs = pl.pallas_call(
        ends_kernel,
        out_shape=[shape((2, cells_x + 4, depth), bf16)] * 2,
        in_specs=[VMEM] * 4,
        out_specs=[VMEM] * 2,
        scratch_shapes=[pltpu.VMEM((2, cells_x + 4, depth), f32)],
        compiler_params=pltpu.CompilerParams(vmem_limit_bytes=8 * MIB),
        cost_estimate=pl.CostEstimate(flops=0, bytes_accessed=MIB, transcendentals=0),
        name="ends",
    )(*edges)
    ylo, yhi = both_ways(*slabs, "gy")
    xlo, xhi, *_ = edges
    slot_lists = [
        incoming_late[:, :first_slots].reshape(-1, LANES),
        (incoming_late[:, first_slots:] & (MARK - 1)).reshape(-1, LANES),
    ][:exchanges]
    match = pl.pallas_call(
        match_kernel,
        out_shape=shape((all_slots, LANES), bf16),
        in_specs=[VMEM],
        out_specs=VMEM,
        compiler_params=pltpu.CompilerParams(vmem_limit_bytes=8 * MIB),
        cost_estimate=pl.CostEstimate(flops=10**9, bytes_accessed=MIB, transcendentals=0),
        name="match",
    )(jnp.concatenate(slot_lists, axis=0))
    *returned, match, ylo, yhi = lax.optimization_barrier((*returned, match, ylo, yhi))

    chunks = blocks_dev * stars // LANES
    in_set = chunks // 4
    live = jnp.arange(stars)[None, :] < star_counts[:, None]
    live_inverse = jnp.where(live, inverse_var, 0.0)
    extinction, *parcel = pl.pallas_call(
        functools.partial(star_kernel, exchanges=exchanges),
        out_shape=[shape((chunks, LANES), f32)]
        + [shape((devices * n, width), bf16) for n in slots_of],
        in_specs=[SMEM, VMEM, VMEM, ANY] + [VMEM] * exchanges,
        out_specs=[VMEM] * (1 + exchanges),
        scratch_shapes=[
            pltpu.VMEM((2, in_set, blocks_dev // chunks, slots, stars, width), bf16),
            pltpu.VMEM((all_slots + 8, width), f32),
            pltpu.VMEM((in_set * (blocks_dev // chunks) * slots, 1, width), f32),
            pltpu.VMEM((all_slots, 1, width), f32),
            pltpu.SemaphoreType.DMA((2, in_set)),
        ],
        compiler_params=pltpu.CompilerParams(vmem_limit_bytes=50 * MIB),
        cost_estimate=pl.CostEstimate(
            flops=4 * weights.size, bytes_accessed=2 * weights.size, transcendentals=0
        ),
        name="stars",
    )(
        position.reshape(slots // 2, 2, blocks_dev).transpose(2, 1, 0).reshape(requests),
        observed.reshape(chunks, LANES),
        live_inverse.reshape(chunks, LANES),
        weights,
        *returned,
    )
    arrived = exchange_rows(parcel, crowded)

    field_late, _ = lax.optimization_barrier((log_density, parcel[0]))
    parts = 8
    base = pl.pallas_call(
        prior_kernel,
        out_shape=shape(field_shape, f32),
        in_specs=[ANY] + [VMEM] * 4,
        out_specs=ANY,
        scratch_shapes=[
            pltpu.VMEM((cells_x + 4, cells_y + 16, depth), f32),
            pltpu.VMEM((cells_x + 2, cells_y + 16, depth), f32),
            pltpu.VMEM(field_shape, f32),
            pltpu.VMEM((2, 2, cells_x + 4, depth), f32),
            pltpu.SemaphoreType.DMA((parts,)),
            pltpu.SemaphoreType.DMA((parts,)),
        ],
        compiler_params=pltpu.CompilerParams(vmem_limit_bytes=56 * MIB),
        cost_estimate=pl.CostEstimate(
            flops=30 * cells, bytes_accessed=8 * cells, transcendentals=0
        ),
        name="prior",
    )(field_late, xlo, xhi, ylo, yhi)

    new_log_density = pl.pallas_call(
        functools.partial(
            finish_kernel, exchanges=exchanges, capacity=capacity, first_slots=first_slots
        ),
        out_shape=shape(field_shape, f32),
        in_specs=[SMEM, ANY, ANY, ANY] + [VMEM] * exchanges,
        out_specs=ANY,
        scratch_shapes=[
            pltpu.VMEM((blocks + capacity, 1, width), f32),
            pltpu.VMEM((blocks + capacity, 1, width), f32),
            pltpu.VMEM((all_slots, 1, width), f32),
            pltpu.VMEM((all_slots, LANES), bf16),
            pltpu.VMEM(field_shape, f32),
            pltpu.VMEM(field_shape, f32),
            pltpu.VMEM(field_shape, f32),
            pltpu.SemaphoreType.DMA((3, parts)),
            pltpu.SemaphoreType.DMA((parts,)),
        ],
        compiler_params=pltpu.CompilerParams(vmem_limit_bytes=50 * MIB),
        cost_estimate=pl.CostEstimate(
            flops=4 * cells, bytes_accessed=12 * cells, transcendentals=cells
        ),
        name="finish",
    )(wanted, match, log_density, base, *arrived)
    return new_log_density, extinction.reshape(blocks_dev, stars)


def solution(mesh):
    placed = (
        P("gx", "gy", None),
        P(("gx", "gy"), None, None, None),
        P(("gx", "gy"), None),
        P(("gx", "gy"), None),
        P(("gx", "gy")),
        P(("gx", "gy"), None),
    )
    return jax.shard_map(
        on_device,
        mesh=mesh,
        in_specs=placed,
        out_specs=(P("gx", "gy", None), P(("gx", "gy"), None)),
        check_vma=False,
    )
```

```python
import functools

import jax
import jax.numpy as jnp
from jax import lax
from jax.experimental import pallas as pl
from jax.experimental.pallas import tpu as pltpu
from jax.sharding import PartitionSpec as P

shift_kappa = 0.5
prior_weight = 0.05
step_rate = 2.0

LANES = 128
GROUP = 8
MIB = 1 << 20
MARK = 1 << 16

CONTRACT_LANES = (((1,), (1,)), ((), ()))


def split_by(value, size):
    if size & (size - 1) == 0:
        high = value >> (size.bit_length() - 1)
        return high, value & (size - 1)
    high = value // size
    return high, value - high * size


def route_kernel(
    ids_ref, outgoing_ref, position_ref, *, devices, capacity, first_slots, blocks, per_column
):
    half = ids_ref.shape[0] // 2
    ids = jnp.concatenate([ids_ref[:half, :], ids_ref[half:, :]], axis=1)
    lane = lax.broadcasted_iota(jnp.int32, (LANES, LANES), 1)
    row = lax.broadcasted_iota(jnp.int32, (LANES, LANES), 0)
    upper = jnp.where(row <= lane, 1.0, 0.0).astype(jnp.bfloat16)
    tile_no = lax.broadcasted_iota(jnp.int32, (devices, LANES), 0)
    slot_no = lax.broadcasted_iota(jnp.int32, (capacity, LANES), 0)
    before = jnp.zeros((devices, 1), jnp.float32)
    lists = jnp.zeros((2 * devices, capacity), jnp.float32)
    for chunk in range(half):
        target, local = split_by(ids[chunk : chunk + 1, :], blocks)
        column, part = split_by(local, per_column)
        local = ((column >> 3) * per_column + part) * 8 + (column & 7)
        hit = tile_no == target
        onehot = jnp.where(hit, 1.0, 0.0)
        upto = before + jnp.dot(
            onehot.astype(jnp.bfloat16), upper, preferred_element_type=jnp.float32
        )
        before = upto[:, LANES - 1 :]
        rank = jnp.sum(onehot * upto, axis=0, keepdims=True).astype(jnp.int32) - 1
        in_slot = jnp.where(slot_no == rank, 1.0, 0.0).astype(jnp.bfloat16)
        high = ((local >> 7) + 1).astype(jnp.float32)
        low = (local & 127).astype(jnp.float32)
        digits = jnp.concatenate([jnp.where(hit, high, 0.0), jnp.where(hit, low, 0.0)], axis=0)
        lists = lists + lax.dot_general(
            digits.astype(jnp.bfloat16),
            in_slot,
            CONTRACT_LANES,
            preferred_element_type=jnp.float32,
        )
        last_slots = capacity - first_slots
        position_ref[chunk : chunk + 1, :] = jnp.where(
            rank < first_slots,
            target * first_slots + rank,
            devices * first_slots + target * last_slots + rank - first_slots,
        )
    high, low = lists[:devices], lists[devices:]
    wanted = ((high - 1.0) * 128.0 + low).astype(jnp.int32)
    filled = before.astype(jnp.int32)
    me = lax.axis_index("gx") * lax.axis_size("gy") + lax.axis_index("gy")
    fullest = jnp.max(jnp.where(tile_no[:, :1] == me, 0.0, before), axis=0, keepdims=True)
    listed = jnp.where(high > 0.5, wanted, blocks + filled)
    if first_slots < capacity:
        slot = lax.broadcasted_iota(jnp.int32, (devices, capacity), 1)
        mark = fullest.astype(jnp.int32) * MARK
        listed = listed + jnp.where(slot == capacity - 1, mark, 0)
    outgoing_ref[...] = listed


def edges_kernel(
    field_hbm, xfirst_ref, xlast_ref, yfirst_ref, ylast_ref, planes_ref, strips_ref, sems
):
    cells_x, cells_y, _ = field_hbm.shape
    copies = [
        pltpu.make_async_copy(field_hbm.at[pl.ds(0, 2)], planes_ref.at[0], sems.at[0]),
        pltpu.make_async_copy(field_hbm.at[pl.ds(cells_x - 2, 2)], planes_ref.at[1], sems.at[1]),
        pltpu.make_async_copy(field_hbm.at[:, pl.ds(0, 8)], strips_ref.at[0], sems.at[2]),
        pltpu.make_async_copy(
            field_hbm.at[:, pl.ds(cells_y - 8, 8)], strips_ref.at[1], sems.at[3]
        ),
    ]
    for copy in copies:
        copy.start()
    for copy in copies:
        copy.wait()
    xfirst_ref[...] = planes_ref[0].astype(xfirst_ref.dtype)
    xlast_ref[...] = planes_ref[1].astype(xlast_ref.dtype)
    for h in range(2):
        for x in range(cells_x):
            yfirst_ref[h, x + 2 : x + 3, :] = strips_ref[0, x, h : h + 1, :]
            ylast_ref[h, x + 2 : x + 3, :] = strips_ref[1, x, 6 + h : 7 + h, :]


def ends_kernel(
    xlo_ref, xhi_ref, yfirst_ref, ylast_ref, first_ref, last_ref, slab_ref
):
    cells_y = xlo_ref.shape[1]
    length = yfirst_ref.shape[1]
    for own_ref, out_ref, start, row in (
        (yfirst_ref, first_ref, 0, 0),
        (ylast_ref, last_ref, cells_y - 16, 14),
    ):
        slab_ref[...] = own_ref[...]
        for e in range(2):
            for x_ref, at in ((xlo_ref, e), (xhi_ref, length - 2 + e)):
                block = x_ref[e, start : start + 16, :].astype(jnp.float32)
                for h in range(2):
                    slab_ref[h, at : at + 1, :] = block[row + h : row + h + 1, :]
        out_ref[...] = slab_ref[...].astype(out_ref.dtype)


def copies_in_parts(source, target, sems):
    parts = sems.shape[0]
    size = source.shape[0] // parts
    return [
        pltpu.make_async_copy(
            source.at[pl.ds(i * size, size)], target.at[pl.ds(i * size, size)], sems.at[i]
        )
        for i in range(parts)
    ]


def for_each_group(incoming_ref, visit, capacity, first_slots, blocks):
    sources = incoming_ref.shape[0] // capacity
    last_slots = capacity - first_slots
    together = 8

    def groups_of(source):
        last = incoming_ref[source * capacity + capacity - 1] & (MARK - 1)
        return (jnp.where(last < blocks, capacity, last - blocks) + GROUP - 1) // GROUP

    def some_sources(quad, carry):
        own = [quad * together + i for i in range(together)]
        most = functools.reduce(jnp.maximum, [groups_of(source) for source in own])

        def one_group(group, carry):
            slot = group * GROUP
            for which, source in enumerate(own):
                listed = incoming_ref.at[pl.ds(source * capacity + slot, GROUP)]
                wanted = [listed[j] for j in range(GROUP)]
                visit(wanted, pl.multiple_of(source * first_slots + slot, GROUP), 0, which)
            return carry

        return lax.fori_loop(0, jnp.minimum(most, first_slots // GROUP), one_group, carry)

    lax.fori_loop(0, sources // together, some_sources, 0)
    if last_slots == 0:
        return

    def one_source(source, carry):
        def one_group(group, carry):
            slot = group * GROUP
            listed = incoming_ref.at[pl.ds(source * capacity + slot, GROUP)]
            wanted = [listed[j] & (MARK - 1) for j in range(GROUP)]
            visit(wanted, pl.multiple_of(source * last_slots + slot - first_slots, GROUP), 1, 0)
            return carry

        return lax.fori_loop(first_slots // GROUP, groups_of(source), one_group, carry)

    lax.fori_loop(0, sources, one_source, 0)


def serve_kernel(incoming_ref, field_hbm, *refs, capacity, first_slots):
    *served_refs, crowded_ref, rows_ref, found_ref, sems = refs
    blocks = field_hbm.shape[0]
    loads = copies_in_parts(field_hbm, rows_ref, sems)
    for load in loads:
        load.start()

    def mark_of(source, most):
        return jnp.maximum(most, incoming_ref[source * capacity + capacity - 1] >> 16)

    fullest = lax.fori_loop(0, incoming_ref.shape[0] // capacity, mark_of, jnp.int32(0))
    crowded_ref[0] = jnp.where(fullest > first_slots, 1, 0)
    rows_ref[blocks:] = jnp.zeros((rows_ref.shape[0] - blocks, 1, LANES), jnp.float32)
    for load in loads:
        load.wait()

    part_starts = [0, served_refs[0].shape[0]]

    def visit(wanted, row, list_part, which):
        rows = [rows_ref[at] for at in wanted]
        found = found_ref.at[pl.ds(row + part_starts[list_part], GROUP)]
        for j in range(GROUP):
            found[j] = rows[j]

    for_each_group(incoming_ref, visit, capacity, first_slots, blocks)
    found = found_ref.reshape(found_ref.shape[0], LANES)
    for start, served_ref in zip(part_starts, served_refs):
        span = slice(start, start + served_ref.shape[0])
        served_ref[...] = jnp.exp(found[span, :]).astype(jnp.bfloat16)


def match_kernel(incoming_ref, match_ref):
    lane = lax.broadcasted_iota(jnp.int32, (LANES, LANES), 1)
    row = lax.broadcasted_iota(jnp.int32, (LANES, LANES), 0)
    ones = jnp.ones((LANES, LANES), jnp.bfloat16)
    same_group = (lane // GROUP) == (row // GROUP)

    def one_row(i):
        wanted = incoming_ref[pl.ds(i, 1), :]
        high = jnp.where(lane == row, (wanted >> 7).astype(jnp.float32), 0.0).astype(jnp.bfloat16)
        low = jnp.where(lane == row, (wanted & 127).astype(jnp.float32), 0.0).astype(jnp.bfloat16)
        down = 128.0 * jnp.dot(high, ones, preferred_element_type=jnp.float32)
        down = down + jnp.dot(low, ones, preferred_element_type=jnp.float32)
        same = (down == wanted.astype(jnp.float32)) & same_group
        match_ref[pl.ds(pl.multiple_of(i * LANES, LANES), LANES), :] = jnp.where(
            same, 1.0, 0.0
        ).astype(jnp.bfloat16)

    def some_rows(i, carry):
        for j in range(4):
            one_row(4 * i + j)
        return carry

    lax.fori_loop(0, incoming_ref.shape[0] // 4, some_rows, 0)


def star_kernel(position_ref, observed_ref, inverse_ref, weights_hbm, *refs, exchanges):
    returned_refs, refs = refs[:exchanges], refs[exchanges:]
    extinction_ref, refs = refs[0], refs[1:]
    parcel_refs, refs = refs[:exchanges], refs[exchanges:]
    weights_ref, returned_rows, sens_ref, parcel_rows, sems = refs
    sets, in_set, per, slots, stars, width = weights_ref.shape
    chunks = extinction_ref.shape[0]
    rounds = chunks // (sets * in_set)
    per_chunk = per * slots
    fold = LANES // stars
    all_slots = parcel_rows.shape[0]
    sens_blocks = sens_ref.reshape(sens_ref.shape[0], width)
    lane = lax.broadcasted_iota(jnp.int32, (8, LANES), 1)
    row = lax.broadcasted_iota(jnp.int32, (8, LANES), 0)
    star_group = lane // stars
    own_slot = [row == star_group + fold * h for h in range(8 // fold)]

    def load(one_round, one_set):
        return [
            pltpu.make_async_copy(
                weights_hbm.at[pl.ds(((one_round * sets + one_set) * in_set + u) * per, per)],
                weights_ref.at[one_set, u],
                sems.at[one_set, u],
            )
            for u in range(in_set)
        ]

    def extinctions(one_set, u, chunk, places):
        sums = []
        for b in range(per):
            total = jnp.zeros((stars // 8, 8, width), jnp.float32)
            for k in range(slots):
                at = places[u * per_chunk + b * slots + k]
                fetched = returned_rows[pl.ds(at, 8, stride=0), :]
                block = weights_ref[one_set, u, b, k].astype(jnp.float32)
                total = total + block.reshape(stars // 8, 8, width) * fetched
            sums.append(total.reshape(stars, width))
        extinction = lax.dot_general(
            jnp.ones((8, width), jnp.float32),
            jnp.concatenate(sums, axis=0),
            CONTRACT_LANES,
            precision=lax.Precision.HIGHEST,
            preferred_element_type=jnp.float32,
        )
        here = pl.ds(chunk, 1)
        extinction_ref[here, :] = extinction[:1]
        return inverse_ref[here, :] * (extinction - observed_ref[here, :])

    def sensitivities(one_set, u, weighted):
        for b in range(per):
            spread = jnp.where(star_group == b, weighted, 0.0)
            shift = stars
            while shift < LANES:
                spread = spread + pltpu.roll(spread, shift, 1)
                shift *= 2
            left = jnp.concatenate(
                [jnp.where(own, spread, 0.0) for own in own_slot], axis=1
            ).astype(jnp.bfloat16)
            eights = [weights_ref[one_set, u, b, 8 * j : 8 * j + 8] for j in range(slots // 8)]
            right = jnp.concatenate([x.reshape(8 * stars, width) for x in eights], axis=1)
            sens = jnp.dot(left, right, preferred_element_type=jnp.float32)
            for j in range(slots // 8):
                first = u * per_chunk + b * slots + 8 * j
                sens_blocks[first : first + 8, :] = sens[:, j * width : (j + 1) * width]

    def scatter(u, places):
        for i in range(u * per_chunk, (u + 1) * per_chunk):
            parcel_rows[places[i]] = sens_ref[i]

    def work(one_round, one_set):
        first = (one_round * sets + one_set) * in_set
        size = in_set * per_chunk
        places = position_ref.at[pl.ds(pl.multiple_of(first * per_chunk, size), size)]
        weighted = {}
        for u in range(in_set + 2):
            if u < in_set:
                weighted[u] = extinctions(one_set, u, first + u, places)
            if 1 <= u <= in_set:
                sensitivities(one_set, u - 1, weighted[u - 1])
            if u >= 2:
                scatter(u - 2, places)

    for copy in load(0, 0):
        copy.start()
    start = 0
    for returned_ref in returned_refs:
        span = slice(start, start + returned_ref.shape[0])
        returned_rows[span, :] = returned_ref[...].astype(jnp.float32)
        start = span.stop
    parcel_rows.reshape(all_slots, width)[...] = jnp.zeros((all_slots, width), jnp.float32)

    def one_round(i, carry):
        for one_set in range(sets):
            for copy in load(i, one_set):
                copy.wait()
            if one_set + 1 < sets:
                for copy in load(i, one_set + 1):
                    copy.start()
            else:

                @pl.when(i + 1 < rounds)
                def _():
                    for copy in load(i + 1, 0):
                        copy.start()

            work(i, one_set)
        return carry

    lax.fori_loop(0, rounds, one_round, 0)
    start = 0
    for parcel_ref in parcel_refs:
        span = slice(start, start + parcel_ref.shape[0])
        parcel_ref[...] = parcel_rows.reshape(all_slots, width)[span, :].astype(jnp.bfloat16)
        start = span.stop


def prior_kernel(
    field_hbm, xlo_ref, xhi_ref, ylo_ref, yhi_ref, out_hbm,
    padded, smooth, out_ref, yends_ref, sems, out_sems,
):
    cells_x, cells_y, depth = field_hbm.shape
    rows = padded.shape[1]
    parts = sems.shape[0]
    planes = cells_x // parts
    own_rows = pl.ds(8, cells_y)
    loads = [
        pltpu.make_async_copy(
            field_hbm.at[pl.ds(i * planes, planes)],
            padded.at[pl.ds(2 + i * planes, planes), own_rows],
            sems.at[i],
        )
        for i in range(parts)
    ]
    for load in loads:
        load.start()
    gx, gy = lax.axis_index("gx"), lax.axis_index("gy")
    last_gx, last_gy = lax.axis_size("gx") - 1, lax.axis_size("gy") - 1
    z = lax.broadcasted_iota(jnp.int32, (rows, depth), 1)
    y = lax.broadcasted_iota(jnp.int32, (rows, depth), 0) - 8
    inside_y = ((y >= 0) | (gy > 0)) & ((y < cells_y) | (gy < last_gy))

    def operate(center, below, above):
        beside = below + above
        beside = beside + pltpu.roll(center, 1, 0) + pltpu.roll(center, rows - 1, 0)
        beside = beside + jnp.where(z == 0, 0.0, pltpu.roll(center, 1, 1))
        beside = beside + jnp.where(z == depth - 1, 0.0, pltpu.roll(center, depth - 1, 1))
        return (shift_kappa + 6.0) * center - beside

    for h in range(2):
        padded[h, own_rows, :] = xlo_ref[h].astype(jnp.float32)
        padded[cells_x + 2 + h, own_rows, :] = xhi_ref[h].astype(jnp.float32)

    yends_ref[0] = ylo_ref[...].astype(jnp.float32)
    yends_ref[1] = yhi_ref[...].astype(jnp.float32)

    def fill_ends(plane, carry):
        padded[plane, 0:8, :] = jnp.zeros((8, depth), jnp.float32)
        padded[plane, 8 + cells_y :, :] = jnp.zeros((8, depth), jnp.float32)
        for h in range(2):
            padded[plane, 6 + h : 7 + h, :] = yends_ref[0, h, pl.ds(plane, 1), :]
            padded[plane, 8 + cells_y + h : 9 + cells_y + h, :] = yends_ref[1, h, pl.ds(plane, 1), :]
        return carry

    lax.fori_loop(0, cells_x + 4, fill_ends, 0)

    def smooth_plane(plane, carry):
        value = operate(padded[plane], padded[plane - 1], padded[plane + 1])
        inside = ((plane > 1) | (gx > 0)) & ((plane < cells_x + 2) | (gx < last_gx))
        smooth[plane - 1] = jnp.where(inside_y & inside, value, 0.0)
        return carry

    def out_plane(x, carry):
        prior = operate(smooth[x + 1], smooth[x], smooth[x + 2])
        change = (step_rate * prior_weight) * prior[8 : 8 + cells_y]
        out_ref[x] = padded[x + 2, own_rows, :] - change
        return carry

    def store(part):
        span = pl.ds(part * planes, planes)
        return pltpu.make_async_copy(out_ref.at[span], out_hbm.at[span], out_sems.at[part])

    smoothed, done = 1, 0
    for part in range(parts):
        loads[part].wait()
        ready = cells_x + 3 if part + 1 == parts else 1 + (part + 1) * planes
        lax.fori_loop(smoothed, ready, smooth_plane, 0)
        smoothed = ready
        lax.fori_loop(done, ready - 3, out_plane, 0)
        done = ready - 3
        for whole in range(parts):
            if part * planes - 2 < (whole + 1) * planes <= done:
                store(whole).start()
    for part in range(parts):
        store(part).wait()


def finish_kernel(
    incoming_ref, match_hbm, field_hbm, base_hbm, *refs, exchanges, capacity, first_slots
):
    arrived_refs, refs = refs[:exchanges], refs[exchanges:]
    out_hbm, *collected, rows_ref, match_ref, field_ref, base_ref, out_ref, in_sems, out_sems = refs
    cells_x, cells_y, depth = field_ref.shape
    per_column = depth // LANES
    parts = out_sems.shape[0]
    planes = cells_x // parts
    blocks = cells_x * cells_y * per_column
    matches = copies_in_parts(match_hbm, match_ref, in_sems.at[2])
    loads = copies_in_parts(field_hbm, field_ref, in_sems.at[0])
    loads += copies_in_parts(base_hbm, base_ref, in_sems.at[1])
    for load in matches + loads:
        load.start()
    collected_rows = [ref.reshape(ref.shape[0], LANES) for ref in collected]
    for ref in collected_rows:
        ref[...] = jnp.zeros_like(ref)
    for load in matches:
        load.wait()
    merged = rows_ref.reshape(rows_ref.shape[0], LANES)
    start = 0
    for arrived_ref in arrived_refs:
        for i in range(arrived_ref.shape[0] // LANES):
            span = slice(start + i * LANES, start + (i + 1) * LANES)
            merged[span, :] = -step_rate * jnp.dot(
                match_ref[span, :],
                arrived_ref[i * LANES : (i + 1) * LANES, :],
                preferred_element_type=jnp.float32,
            )
        start += arrived_ref.shape[0]

    part_starts = [0, arrived_refs[0].shape[0]]

    def visit(wanted, row, list_part, which):
        row = pl.multiple_of(row + part_starts[list_part], GROUP)
        rows = rows_ref.at[pl.ds(row, GROUP)]
        into = collected[which % len(collected)]
        sums = [into[wanted[j]] + rows[j] for j in range(GROUP)]
        for j in range(GROUP):
            into[wanted[j]] = sums[j]

    for_each_group(incoming_ref, visit, capacity, first_slots, blocks)
    for load in loads:
        load.wait()

    def store(part):
        span = pl.ds(part * planes, planes)
        return pltpu.make_async_copy(out_ref.at[span], out_hbm.at[span], out_sems.at[part])

    def one_plane(x, carry):
        for yb in range(cells_y // 8):
            for part in range(per_column):
                at = pl.multiple_of(((x * (cells_y // 8) + yb) * per_column + part) * 8, 8)
                here = (x, slice(8 * yb, 8 * yb + 8), slice(part * LANES, (part + 1) * LANES))
                grad = collected_rows[0][pl.ds(at, 8), :] + collected_rows[1][pl.ds(at, 8), :]
                out_ref[here] = base_ref[here] + grad * jnp.exp(field_ref[here])
        return carry

    for part in range(parts):
        lax.fori_loop(part * planes, (part + 1) * planes, one_plane, 0)
        store(part).start()
    for part in range(parts):
        store(part).wait()


def both_ways(first, last, axis):
    peers = lax.axis_size(axis)
    up = [(i, i + 1) for i in range(peers - 1)]
    down = [(j, i) for i, j in up]
    return lax.ppermute(last, axis, up), lax.ppermute(first, axis, down)


VMEM = pl.BlockSpec(memory_space=pltpu.VMEM)
SMEM = pl.BlockSpec(memory_space=pltpu.SMEM)
ANY = pl.BlockSpec(memory_space=pl.ANY)


def on_device(log_density, weights, observed, inverse_var, star_counts, block_ids):
    cells_x, cells_y, depth = log_density.shape
    blocks_dev, slots, stars, width = weights.shape
    devices = lax.axis_size("gx") * lax.axis_size("gy")
    requests = blocks_dev * slots
    capacity = 2 * requests // devices
    first_slots = 11 * capacity // 16 if capacity % LANES == 0 else capacity
    slots_of = [n for n in (first_slots, capacity - first_slots) if n > 0]
    exchanges = len(slots_of)
    all_slots = devices * capacity
    per_column = depth // width
    blocks = cells_x * cells_y * per_column
    cells = log_density.size
    field_shape = (cells_x, cells_y, depth)
    mesh_axes = ("gx", "gy")
    f32, bf16, i32 = jnp.float32, jnp.bfloat16, jnp.int32
    shape = jax.ShapeDtypeStruct

    def to_rows(x):
        x = x.reshape(cells_x, cells_y // 8, 8, per_column, width)
        return x.transpose(0, 1, 3, 2, 4).reshape(blocks, 1, width)

    def exchange(x):
        return lax.all_to_all(x, mesh_axes, split_axis=0, concat_axis=0, tiled=True)

    def exchange_rows(parts, crowded):
        moved = [parts[0].reshape(devices, first_slots, width)]
        moved[0] = exchange(moved[0])
        for part in parts[1:]:
            part = part.reshape(devices, capacity - first_slots, width)
            moved.append(lax.cond(crowded, exchange, lambda x: x, part))
        return [x.reshape(-1, width) for x in moved]

    outgoing, position = pl.pallas_call(
        functools.partial(
            route_kernel,
            devices=devices,
            capacity=capacity,
            first_slots=first_slots,
            blocks=blocks,
            per_column=per_column,
        ),
        out_shape=[shape((devices, capacity), i32), shape((requests // LANES, LANES), i32)],
        in_specs=[VMEM],
        out_specs=[VMEM, VMEM],
        name="route",
    )(block_ids.T)
    incoming = exchange(outgoing)

    field, _ = lax.optimization_barrier((log_density, outgoing))
    xfirst, xlast, yfirst, ylast = pl.pallas_call(
        edges_kernel,
        out_shape=[
            shape((2, cells_y, depth), bf16),
            shape((2, cells_y, depth), bf16),
            shape((2, cells_x + 4, depth), f32),
            shape((2, cells_x + 4, depth), f32),
        ],
        in_specs=[ANY],
        out_specs=[VMEM] * 4,
        scratch_shapes=[
            pltpu.VMEM((2, 2, cells_y, depth), f32),
            pltpu.VMEM((2, cells_x, 8, depth), f32),
            pltpu.SemaphoreType.DMA((4,)),
        ],
        compiler_params=pltpu.CompilerParams(vmem_limit_bytes=56 * MIB),
        cost_estimate=pl.CostEstimate(flops=0, bytes_accessed=2 * MIB, transcendentals=0),
        name="edges",
    )(field)
    incoming, *edges = lax.optimization_barrier((incoming, xfirst, xlast, yfirst, ylast))
    wanted = incoming.reshape(-1)

    *served, crowded = pl.pallas_call(
        functools.partial(serve_kernel, capacity=capacity, first_slots=first_slots),
        out_shape=[shape((devices * n, width), bf16) for n in slots_of] + [shape((1,), i32)],
        in_specs=[SMEM, ANY],
        out_specs=[VMEM] * exchanges + [SMEM],
        scratch_shapes=[
            pltpu.VMEM((blocks + capacity, 1, width), f32),
            pltpu.VMEM((all_slots, 1, width), f32),
            pltpu.SemaphoreType.DMA((16,)),
        ],
        compiler_params=pltpu.CompilerParams(vmem_limit_bytes=56 * MIB),
        cost_estimate=pl.CostEstimate(
            flops=cells, bytes_accessed=6 * MIB, transcendentals=cells
        ),
        name="serve",
    )(wanted, to_rows(log_density))
    crowded = crowded[0] != 0

    returned = exchange_rows(served, crowded)
    *edges, incoming_late, _ = lax.optimization_barrier((*edges, incoming, served[0]))
    xlo, xhi = both_ways(*edges[:2], "gx")
    slabs = pl.pallas_call(
        ends_kernel,
        out_shape=[shape((2, cells_x + 4, depth), bf16)] * 2,
        in_specs=[VMEM] * 4,
        out_specs=[VMEM] * 2,
        scratch_shapes=[pltpu.VMEM((2, cells_x + 4, depth), f32)],
        compiler_params=pltpu.CompilerParams(vmem_limit_bytes=8 * MIB),
        cost_estimate=pl.CostEstimate(flops=0, bytes_accessed=MIB, transcendentals=0),
        name="ends",
    )(xlo, xhi, *edges[2:])
    ylo, yhi = both_ways(*slabs, "gy")
    slot_lists = [
        incoming_late[:, :first_slots].reshape(-1, LANES),
        (incoming_late[:, first_slots:] & (MARK - 1)).reshape(-1, LANES),
    ][:exchanges]
    match = pl.pallas_call(
        match_kernel,
        out_shape=shape((all_slots, LANES), bf16),
        in_specs=[VMEM],
        out_specs=VMEM,
        compiler_params=pltpu.CompilerParams(vmem_limit_bytes=8 * MIB),
        cost_estimate=pl.CostEstimate(flops=10**9, bytes_accessed=MIB, transcendentals=0),
        name="match",
    )(jnp.concatenate(slot_lists, axis=0))
    *returned, match, ylo, yhi = lax.optimization_barrier((*returned, match, ylo, yhi))

    chunks = blocks_dev * stars // LANES
    in_set = chunks // 4
    live = jnp.arange(stars)[None, :] < star_counts[:, None]
    live_inverse = jnp.where(live, inverse_var, 0.0)
    extinction, *parcel = pl.pallas_call(
        functools.partial(star_kernel, exchanges=exchanges),
        out_shape=[shape((chunks, LANES), f32)]
        + [shape((devices * n, width), bf16) for n in slots_of],
        in_specs=[SMEM, VMEM, VMEM, ANY] + [VMEM] * exchanges,
        out_specs=[VMEM] * (1 + exchanges),
        scratch_shapes=[
            pltpu.VMEM((2, in_set, blocks_dev // chunks, slots, stars, width), bf16),
            pltpu.VMEM((all_slots + 8, width), f32),
            pltpu.VMEM((in_set * (blocks_dev // chunks) * slots, 1, width), f32),
            pltpu.VMEM((all_slots, 1, width), f32),
            pltpu.SemaphoreType.DMA((2, in_set)),
        ],
        compiler_params=pltpu.CompilerParams(vmem_limit_bytes=50 * MIB),
        cost_estimate=pl.CostEstimate(
            flops=4 * weights.size, bytes_accessed=2 * weights.size, transcendentals=0
        ),
        name="stars",
    )(
        position.reshape(slots // 2, 2, blocks_dev).transpose(2, 1, 0).reshape(requests),
        observed.reshape(chunks, LANES),
        live_inverse.reshape(chunks, LANES),
        weights,
        *returned,
    )
    arrived = exchange_rows(parcel, crowded)

    field_late, _ = lax.optimization_barrier((log_density, parcel[0]))
    parts = 8
    base = pl.pallas_call(
        prior_kernel,
        out_shape=shape(field_shape, f32),
        in_specs=[ANY] + [VMEM] * 4,
        out_specs=ANY,
        scratch_shapes=[
            pltpu.VMEM((cells_x + 4, cells_y + 16, depth), f32),
            pltpu.VMEM((cells_x + 2, cells_y + 16, depth), f32),
            pltpu.VMEM(field_shape, f32),
            pltpu.VMEM((2, 2, cells_x + 4, depth), f32),
            pltpu.SemaphoreType.DMA((parts,)),
            pltpu.SemaphoreType.DMA((parts,)),
        ],
        compiler_params=pltpu.CompilerParams(vmem_limit_bytes=56 * MIB),
        cost_estimate=pl.CostEstimate(
            flops=30 * cells, bytes_accessed=8 * cells, transcendentals=0
        ),
        name="prior",
    )(field_late, xlo, xhi, ylo, yhi)

    new_log_density = pl.pallas_call(
        functools.partial(
            finish_kernel, exchanges=exchanges, capacity=capacity, first_slots=first_slots
        ),
        out_shape=shape(field_shape, f32),
        in_specs=[SMEM, ANY, ANY, ANY] + [VMEM] * exchanges,
        out_specs=ANY,
        scratch_shapes=[
            pltpu.VMEM((blocks + capacity, 1, width), f32),
            pltpu.VMEM((blocks + capacity, 1, width), f32),
            pltpu.VMEM((all_slots, 1, width), f32),
            pltpu.VMEM((all_slots, LANES), bf16),
            pltpu.VMEM(field_shape, f32),
            pltpu.VMEM(field_shape, f32),
            pltpu.VMEM(field_shape, f32),
            pltpu.SemaphoreType.DMA((3, parts)),
            pltpu.SemaphoreType.DMA((parts,)),
        ],
        compiler_params=pltpu.CompilerParams(vmem_limit_bytes=50 * MIB),
        cost_estimate=pl.CostEstimate(
            flops=4 * cells, bytes_accessed=12 * cells, transcendentals=cells
        ),
        name="finish",
    )(wanted, match, log_density, base, *arrived)
    return new_log_density, extinction.reshape(blocks_dev, stars)


def solution(mesh):
    placed = (
        P("gx", "gy", None),
        P(("gx", "gy"), None, None, None),
        P(("gx", "gy"), None),
        P(("gx", "gy"), None),
        P(("gx", "gy")),
        P(("gx", "gy"), None),
    )
    return jax.shard_map(
        on_device,
        mesh=mesh,
        in_specs=placed,
        out_specs=(P("gx", "gy", None), P(("gx", "gy"), None)),
        check_vma=False,
    )
```

```python
import functools

import jax
import jax.numpy as jnp
from jax import lax
from jax.experimental import pallas as pl
from jax.experimental.pallas import tpu as pltpu
from jax.sharding import PartitionSpec as P

shift_kappa = 0.5
prior_weight = 0.05
step_rate = 2.0

LANES = 128
GROUP = 8
MIB = 1 << 20
MARK = 1 << 16

CONTRACT_LANES = (((1,), (1,)), ((), ()))


def split_by(value, size):
    if size & (size - 1) == 0:
        high = value >> (size.bit_length() - 1)
        return high, value & (size - 1)
    high = value // size
    return high, value - high * size


def route_kernel(
    ids_ref, outgoing_ref, position_ref, *, devices, capacity, first_slots, blocks, per_column
):
    half = ids_ref.shape[0] // 2
    ids = jnp.concatenate([ids_ref[:half, :], ids_ref[half:, :]], axis=1)
    lane = lax.broadcasted_iota(jnp.int32, (LANES, LANES), 1)
    row = lax.broadcasted_iota(jnp.int32, (LANES, LANES), 0)
    upper = jnp.where(row <= lane, 1.0, 0.0).astype(jnp.bfloat16)
    tile_no = lax.broadcasted_iota(jnp.int32, (devices, LANES), 0)
    slot_no = lax.broadcasted_iota(jnp.int32, (capacity, LANES), 0)
    before = jnp.zeros((devices, 1), jnp.float32)
    lists = jnp.zeros((2 * devices, capacity), jnp.float32)
    for chunk in range(half):
        target, local = split_by(ids[chunk : chunk + 1, :], blocks)
        column, part = split_by(local, per_column)
        local = ((column >> 3) * per_column + part) * 8 + (column & 7)
        hit = tile_no == target
        onehot = jnp.where(hit, 1.0, 0.0)
        upto = before + jnp.dot(
            onehot.astype(jnp.bfloat16), upper, preferred_element_type=jnp.float32
        )
        before = upto[:, LANES - 1 :]
        rank = jnp.sum(onehot * upto, axis=0, keepdims=True).astype(jnp.int32) - 1
        in_slot = jnp.where(slot_no == rank, 1.0, 0.0).astype(jnp.bfloat16)
        high = ((local >> 7) + 1).astype(jnp.float32)
        low = (local & 127).astype(jnp.float32)
        digits = jnp.concatenate([jnp.where(hit, high, 0.0), jnp.where(hit, low, 0.0)], axis=0)
        lists = lists + lax.dot_general(
            digits.astype(jnp.bfloat16),
            in_slot,
            CONTRACT_LANES,
            preferred_element_type=jnp.float32,
        )
        last_slots = capacity - first_slots
        position_ref[chunk : chunk + 1, :] = jnp.where(
            rank < first_slots,
            target * first_slots + rank,
            devices * first_slots + target * last_slots + rank - first_slots,
        )
    high, low = lists[:devices], lists[devices:]
    wanted = ((high - 1.0) * 128.0 + low).astype(jnp.int32)
    filled = before.astype(jnp.int32)
    me = lax.axis_index("gx") * lax.axis_size("gy") + lax.axis_index("gy")
    fullest = jnp.max(jnp.where(tile_no[:, :1] == me, 0.0, before), axis=0, keepdims=True)
    listed = jnp.where(high > 0.5, wanted, blocks + filled)
    if first_slots < capacity:
        slot = lax.broadcasted_iota(jnp.int32, (devices, capacity), 1)
        mark = fullest.astype(jnp.int32) * MARK
        listed = listed + jnp.where(slot == capacity - 1, mark, 0)
    outgoing_ref[...] = listed


def edges_kernel(
    field_hbm, xfirst_ref, xlast_ref, yfirst_ref, ylast_ref, planes_ref, strips_ref, sems
):
    cells_x, cells_y, _ = field_hbm.shape
    copies = [
        pltpu.make_async_copy(field_hbm.at[pl.ds(0, 2)], planes_ref.at[0], sems.at[0]),
        pltpu.make_async_copy(field_hbm.at[pl.ds(cells_x - 2, 2)], planes_ref.at[1], sems.at[1]),
        pltpu.make_async_copy(field_hbm.at[:, pl.ds(0, 8)], strips_ref.at[0], sems.at[2]),
        pltpu.make_async_copy(
            field_hbm.at[:, pl.ds(cells_y - 8, 8)], strips_ref.at[1], sems.at[3]
        ),
    ]
    for copy in copies:
        copy.start()
    for copy in copies:
        copy.wait()
    xfirst_ref[...] = planes_ref[0].astype(xfirst_ref.dtype)
    xlast_ref[...] = planes_ref[1].astype(xlast_ref.dtype)
    for h in range(2):
        for x in range(cells_x):
            yfirst_ref[h, x + 2 : x + 3, :] = strips_ref[0, x, h : h + 1, :]
            ylast_ref[h, x + 2 : x + 3, :] = strips_ref[1, x, 6 + h : 7 + h, :]


def ends_kernel(
    xlo_ref, xhi_ref, yfirst_ref, ylast_ref, first_ref, last_ref, slab_ref
):
    cells_y = xlo_ref.shape[1]
    length = yfirst_ref.shape[1]
    for own_ref, out_ref, start, row in (
        (yfirst_ref, first_ref, 0, 0),
        (ylast_ref, last_ref, cells_y - 16, 14),
    ):
        slab_ref[...] = own_ref[...]
        for e in range(2):
            for x_ref, at in ((xlo_ref, e), (xhi_ref, length - 2 + e)):
                block = x_ref[e, start : start + 16, :].astype(jnp.float32)
                for h in range(2):
                    slab_ref[h, at : at + 1, :] = block[row + h : row + h + 1, :]
        out_ref[...] = slab_ref[...].astype(out_ref.dtype)


def copies_in_parts(source, target, sems):
    parts = sems.shape[0]
    size = source.shape[0] // parts
    return [
        pltpu.make_async_copy(
            source.at[pl.ds(i * size, size)], target.at[pl.ds(i * size, size)], sems.at[i]
        )
        for i in range(parts)
    ]


def for_each_group(incoming_ref, visit, capacity, first_slots, blocks):
    sources = incoming_ref.shape[0] // capacity
    last_slots = capacity - first_slots
    together = 8

    def groups_of(source):
        last = incoming_ref[source * capacity + capacity - 1] & (MARK - 1)
        return (jnp.where(last < blocks, capacity, last - blocks) + GROUP - 1) // GROUP

    def some_sources(quad, carry):
        own = [quad * together + i for i in range(together)]
        most = functools.reduce(jnp.maximum, [groups_of(source) for source in own])

        def one_group(group, carry):
            slot = group * GROUP
            for which, source in enumerate(own):
                listed = incoming_ref.at[pl.ds(source * capacity + slot, GROUP)]
                wanted = [listed[j] for j in range(GROUP)]
                visit(wanted, pl.multiple_of(source * first_slots + slot, GROUP), 0, which)
            return carry

        return lax.fori_loop(0, jnp.minimum(most, first_slots // GROUP), one_group, carry)

    lax.fori_loop(0, sources // together, some_sources, 0)
    if last_slots == 0:
        return

    def one_source(source, carry):
        def one_group(group, carry):
            slot = group * GROUP
            listed = incoming_ref.at[pl.ds(source * capacity + slot, GROUP)]
            wanted = [listed[j] & (MARK - 1) for j in range(GROUP)]
            visit(wanted, pl.multiple_of(source * last_slots + slot - first_slots, GROUP), 1, 0)
            return carry

        return lax.fori_loop(first_slots // GROUP, groups_of(source), one_group, carry)

    lax.fori_loop(0, sources, one_source, 0)


def serve_kernel(incoming_ref, field_hbm, *refs, capacity, first_slots):
    *served_refs, crowded_ref, rows_ref, found_ref, sems = refs
    blocks = field_hbm.shape[0]
    loads = copies_in_parts(field_hbm, rows_ref, sems)
    for load in loads:
        load.start()

    def mark_of(source, most):
        return jnp.maximum(most, incoming_ref[source * capacity + capacity - 1] >> 16)

    fullest = lax.fori_loop(0, incoming_ref.shape[0] // capacity, mark_of, jnp.int32(0))
    crowded_ref[0] = jnp.where(fullest > first_slots, 1, 0)
    rows_ref[blocks:] = jnp.zeros((rows_ref.shape[0] - blocks, 1, LANES), jnp.float32)
    for load in loads:
        load.wait()

    part_starts = [0, served_refs[0].shape[0]]

    def visit(wanted, row, list_part, which):
        rows = [rows_ref[at] for at in wanted]
        found = found_ref.at[pl.ds(row + part_starts[list_part], GROUP)]
        for j in range(GROUP):
            found[j] = rows[j]

    for_each_group(incoming_ref, visit, capacity, first_slots, blocks)
    found = found_ref.reshape(found_ref.shape[0], LANES)
    for start, served_ref in zip(part_starts, served_refs):
        span = slice(start, start + served_ref.shape[0])
        served_ref[...] = jnp.exp(found[span, :]).astype(jnp.bfloat16)


def match_kernel(incoming_ref, match_ref):
    lane = lax.broadcasted_iota(jnp.int32, (LANES, LANES), 1)
    row = lax.broadcasted_iota(jnp.int32, (LANES, LANES), 0)
    ones = jnp.ones((LANES, LANES), jnp.bfloat16)
    same_group = (lane // GROUP) == (row // GROUP)

    def one_row(i):
        wanted = incoming_ref[pl.ds(i, 1), :]
        high = jnp.where(lane == row, (wanted >> 7).astype(jnp.float32), 0.0).astype(jnp.bfloat16)
        low = jnp.where(lane == row, (wanted & 127).astype(jnp.float32), 0.0).astype(jnp.bfloat16)
        down = 128.0 * jnp.dot(high, ones, preferred_element_type=jnp.float32)
        down = down + jnp.dot(low, ones, preferred_element_type=jnp.float32)
        same = (down == wanted.astype(jnp.float32)) & same_group
        match_ref[pl.ds(pl.multiple_of(i * LANES, LANES), LANES), :] = jnp.where(
            same, 1.0, 0.0
        ).astype(jnp.bfloat16)

    def some_rows(i, carry):
        for j in range(4):
            one_row(4 * i + j)
        return carry

    lax.fori_loop(0, incoming_ref.shape[0] // 4, some_rows, 0)


def star_kernel(position_ref, observed_ref, inverse_ref, weights_hbm, *refs, exchanges):
    returned_refs, refs = refs[:exchanges], refs[exchanges:]
    extinction_ref, refs = refs[0], refs[1:]
    parcel_refs, refs = refs[:exchanges], refs[exchanges:]
    weights_ref, returned_rows, sens_ref, parcel_rows, sems = refs
    sets, in_set, per, slots, stars, width = weights_ref.shape
    chunks = extinction_ref.shape[0]
    rounds = chunks // (sets * in_set)
    per_chunk = per * slots
    fold = LANES // stars
    all_slots = parcel_rows.shape[0]
    sens_blocks = sens_ref.reshape(sens_ref.shape[0], width)
    lane = lax.broadcasted_iota(jnp.int32, (8, LANES), 1)
    row = lax.broadcasted_iota(jnp.int32, (8, LANES), 0)
    star_group = lane // stars
    own_slot = [row == star_group + fold * h for h in range(8 // fold)]

    def load(one_round, one_set):
        return [
            pltpu.make_async_copy(
                weights_hbm.at[pl.ds(((one_round * sets + one_set) * in_set + u) * per, per)],
                weights_ref.at[one_set, u],
                sems.at[one_set, u],
            )
            for u in range(in_set)
        ]

    def extinctions(one_set, u, chunk, places):
        sums = []
        for b in range(per):
            total = jnp.zeros((stars // 8, 8, width), jnp.float32)
            for k in range(slots):
                at = places[u * per_chunk + b * slots + k]
                fetched = returned_rows[pl.ds(at, 8, stride=0), :]
                block = weights_ref[one_set, u, b, k].astype(jnp.float32)
                total = total + block.reshape(stars // 8, 8, width) * fetched
            sums.append(total.reshape(stars, width))
        extinction = lax.dot_general(
            jnp.ones((8, width), jnp.float32),
            jnp.concatenate(sums, axis=0),
            CONTRACT_LANES,
            precision=lax.Precision.HIGHEST,
            preferred_element_type=jnp.float32,
        )
        here = pl.ds(chunk, 1)
        extinction_ref[here, :] = extinction[:1]
        return inverse_ref[here, :] * (extinction - observed_ref[here, :])

    def sensitivities(one_set, u, weighted):
        for b in range(per):
            spread = jnp.where(star_group == b, weighted, 0.0)
            shift = stars
            while shift < LANES:
                spread = spread + pltpu.roll(spread, shift, 1)
                shift *= 2
            left = jnp.concatenate(
                [jnp.where(own, spread, 0.0) for own in own_slot], axis=1
            ).astype(jnp.bfloat16)
            eights = [weights_ref[one_set, u, b, 8 * j : 8 * j + 8] for j in range(slots // 8)]
            right = jnp.concatenate([x.reshape(8 * stars, width) for x in eights], axis=1)
            sens = jnp.dot(left, right, preferred_element_type=jnp.float32)
            for j in range(slots // 8):
                first = u * per_chunk + b * slots + 8 * j
                sens_blocks[first : first + 8, :] = sens[:, j * width : (j + 1) * width]

    def scatter(u, places):
        for i in range(u * per_chunk, (u + 1) * per_chunk):
            parcel_rows[places[i]] = sens_ref[i]

    def work(one_round, one_set):
        first = (one_round * sets + one_set) * in_set
        size = in_set * per_chunk
        places = position_ref.at[pl.ds(pl.multiple_of(first * per_chunk, size), size)]
        weighted = {}
        for u in range(in_set + 2):
            if u < in_set:
                weighted[u] = extinctions(one_set, u, first + u, places)
            if 1 <= u <= in_set:
                sensitivities(one_set, u - 1, weighted[u - 1])
            if u >= 2:
                scatter(u - 2, places)

    for copy in load(0, 0):
        copy.start()
    start = 0
    for returned_ref in returned_refs:
        span = slice(start, start + returned_ref.shape[0])
        returned_rows[span, :] = returned_ref[...].astype(jnp.float32)
        start = span.stop
    parcel_rows.reshape(all_slots, width)[...] = jnp.zeros((all_slots, width), jnp.float32)

    def one_round(i, carry):
        for one_set in range(sets):
            for copy in load(i, one_set):
                copy.wait()
            if one_set + 1 < sets:
                for copy in load(i, one_set + 1):
                    copy.start()
            else:

                @pl.when(i + 1 < rounds)
                def _():
                    for copy in load(i + 1, 0):
                        copy.start()

            work(i, one_set)
        return carry

    lax.fori_loop(0, rounds, one_round, 0)
    start = 0
    for parcel_ref in parcel_refs:
        span = slice(start, start + parcel_ref.shape[0])
        parcel_ref[...] = parcel_rows.reshape(all_slots, width)[span, :].astype(jnp.bfloat16)
        start = span.stop


def prior_kernel(
    field_hbm, xlo_ref, xhi_ref, ylo_ref, yhi_ref, out_hbm,
    padded, smooth, out_ref, yends_ref, sems, out_sems,
):
    cells_x, cells_y, depth = field_hbm.shape
    rows = padded.shape[1]
    parts = sems.shape[0]
    planes = cells_x // parts
    own_rows = pl.ds(8, cells_y)
    loads = [
        pltpu.make_async_copy(
            field_hbm.at[pl.ds(i * planes, planes)],
            padded.at[pl.ds(2 + i * planes, planes), own_rows],
            sems.at[i],
        )
        for i in range(parts)
    ]
    for load in loads:
        load.start()
    gx, gy = lax.axis_index("gx"), lax.axis_index("gy")
    last_gx, last_gy = lax.axis_size("gx") - 1, lax.axis_size("gy") - 1
    z = lax.broadcasted_iota(jnp.int32, (rows, depth), 1)
    y = lax.broadcasted_iota(jnp.int32, (rows, depth), 0) - 8
    inside_y = ((y >= 0) | (gy > 0)) & ((y < cells_y) | (gy < last_gy))

    def operate(center, below, above):
        beside = below + above
        beside = beside + pltpu.roll(center, 1, 0) + pltpu.roll(center, rows - 1, 0)
        beside = beside + jnp.where(z == 0, 0.0, pltpu.roll(center, 1, 1))
        beside = beside + jnp.where(z == depth - 1, 0.0, pltpu.roll(center, depth - 1, 1))
        return (shift_kappa + 6.0) * center - beside

    for h in range(2):
        padded[h, own_rows, :] = xlo_ref[h].astype(jnp.float32)
        padded[cells_x + 2 + h, own_rows, :] = xhi_ref[h].astype(jnp.float32)

    yends_ref[0] = ylo_ref[...].astype(jnp.float32)
    yends_ref[1] = yhi_ref[...].astype(jnp.float32)

    def fill_ends(plane, carry):
        padded[plane, 0:8, :] = jnp.zeros((8, depth), jnp.float32)
        padded[plane, 8 + cells_y :, :] = jnp.zeros((8, depth), jnp.float32)
        for h in range(2):
            padded[plane, 6 + h : 7 + h, :] = yends_ref[0, h, pl.ds(plane, 1), :]
            padded[plane, 8 + cells_y + h : 9 + cells_y + h, :] = yends_ref[1, h, pl.ds(plane, 1), :]
        return carry

    lax.fori_loop(0, cells_x + 4, fill_ends, 0)

    def smooth_plane(plane, carry):
        value = operate(padded[plane], padded[plane - 1], padded[plane + 1])
        inside = ((plane > 1) | (gx > 0)) & ((plane < cells_x + 2) | (gx < last_gx))
        smooth[plane - 1] = jnp.where(inside_y & inside, value, 0.0)
        return carry

    def out_plane(x, carry):
        prior = operate(smooth[x + 1], smooth[x], smooth[x + 2])
        change = (step_rate * prior_weight) * prior[8 : 8 + cells_y]
        out_ref[x] = padded[x + 2, own_rows, :] - change
        return carry

    def store(part):
        span = pl.ds(part * planes, planes)
        return pltpu.make_async_copy(out_ref.at[span], out_hbm.at[span], out_sems.at[part])

    smoothed, done = 1, 0
    for part in range(parts):
        loads[part].wait()
        ready = cells_x + 3 if part + 1 == parts else 1 + (part + 1) * planes
        lax.fori_loop(smoothed, ready, smooth_plane, 0)
        smoothed = ready
        lax.fori_loop(done, ready - 3, out_plane, 0)
        done = ready - 3
        for whole in range(parts):
            if part * planes - 2 < (whole + 1) * planes <= done:
                store(whole).start()
    for part in range(parts):
        store(part).wait()


def finish_kernel(
    incoming_ref, match_hbm, field_hbm, base_hbm, *refs, exchanges, capacity, first_slots
):
    arrived_refs, refs = refs[:exchanges], refs[exchanges:]
    out_hbm, *collected, rows_ref, match_ref, field_ref, base_ref, out_ref, in_sems, out_sems = refs
    cells_x, cells_y, depth = field_ref.shape
    per_column = depth // LANES
    parts = out_sems.shape[0]
    planes = cells_x // parts
    blocks = cells_x * cells_y * per_column
    matches = copies_in_parts(match_hbm, match_ref, in_sems.at[2])
    loads = copies_in_parts(field_hbm, field_ref, in_sems.at[0])
    loads += copies_in_parts(base_hbm, base_ref, in_sems.at[1])
    for load in matches:
        load.start()
    collected_rows = [ref.reshape(ref.shape[0], LANES) for ref in collected]
    for ref in collected_rows:
        ref[...] = jnp.zeros_like(ref)
    for load in matches:
        load.wait()
    for load in loads:
        load.start()
    merged = rows_ref.reshape(rows_ref.shape[0], LANES)
    start = 0
    for arrived_ref in arrived_refs:
        for i in range(arrived_ref.shape[0] // LANES):
            span = slice(start + i * LANES, start + (i + 1) * LANES)
            merged[span, :] = -step_rate * jnp.dot(
                match_ref[span, :],
                arrived_ref[i * LANES : (i + 1) * LANES, :],
                preferred_element_type=jnp.float32,
            )
        start += arrived_ref.shape[0]

    part_starts = [0, arrived_refs[0].shape[0]]

    def visit(wanted, row, list_part, which):
        row = pl.multiple_of(row + part_starts[list_part], GROUP)
        rows = rows_ref.at[pl.ds(row, GROUP)]
        into = collected[which % len(collected)]
        sums = [into[wanted[j]] + rows[j] for j in range(GROUP)]
        for j in range(GROUP):
            into[wanted[j]] = sums[j]

    for_each_group(incoming_ref, visit, capacity, first_slots, blocks)
    for load in loads:
        load.wait()

    def store(part):
        span = pl.ds(part * planes, planes)
        return pltpu.make_async_copy(out_ref.at[span], out_hbm.at[span], out_sems.at[part])

    def one_plane(x, carry):
        for yb in range(cells_y // 8):
            for part in range(per_column):
                at = pl.multiple_of(((x * (cells_y // 8) + yb) * per_column + part) * 8, 8)
                here = (x, slice(8 * yb, 8 * yb + 8), slice(part * LANES, (part + 1) * LANES))
                grad = collected_rows[0][pl.ds(at, 8), :] + collected_rows[1][pl.ds(at, 8), :]
                out_ref[here] = base_ref[here] + grad * jnp.exp(field_ref[here])
        return carry

    for part in range(parts):
        lax.fori_loop(part * planes, (part + 1) * planes, one_plane, 0)
        store(part).start()
    for part in range(parts):
        store(part).wait()


def both_ways(first, last, axis):
    peers = lax.axis_size(axis)
    up = [(i, i + 1) for i in range(peers - 1)]
    down = [(j, i) for i, j in up]
    return lax.ppermute(last, axis, up), lax.ppermute(first, axis, down)


VMEM = pl.BlockSpec(memory_space=pltpu.VMEM)
SMEM = pl.BlockSpec(memory_space=pltpu.SMEM)
ANY = pl.BlockSpec(memory_space=pl.ANY)


def on_device(log_density, weights, observed, inverse_var, star_counts, block_ids):
    cells_x, cells_y, depth = log_density.shape
    blocks_dev, slots, stars, width = weights.shape
    devices = lax.axis_size("gx") * lax.axis_size("gy")
    requests = blocks_dev * slots
    capacity = 2 * requests // devices
    first_slots = 11 * capacity // 16 if capacity % LANES == 0 else capacity
    slots_of = [n for n in (first_slots, capacity - first_slots) if n > 0]
    exchanges = len(slots_of)
    all_slots = devices * capacity
    per_column = depth // width
    blocks = cells_x * cells_y * per_column
    cells = log_density.size
    field_shape = (cells_x, cells_y, depth)
    mesh_axes = ("gx", "gy")
    f32, bf16, i32 = jnp.float32, jnp.bfloat16, jnp.int32
    shape = jax.ShapeDtypeStruct

    def to_rows(x):
        x = x.reshape(cells_x, cells_y // 8, 8, per_column, width)
        return x.transpose(0, 1, 3, 2, 4).reshape(blocks, 1, width)

    def exchange(x):
        return lax.all_to_all(x, mesh_axes, split_axis=0, concat_axis=0, tiled=True)

    def exchange_rows(parts, crowded):
        moved = [parts[0].reshape(devices, first_slots, width)]
        moved[0] = exchange(moved[0])
        for part in parts[1:]:
            part = part.reshape(devices, capacity - first_slots, width)
            moved.append(lax.cond(crowded, exchange, lambda x: x, part))
        return [x.reshape(-1, width) for x in moved]

    outgoing, position = pl.pallas_call(
        functools.partial(
            route_kernel,
            devices=devices,
            capacity=capacity,
            first_slots=first_slots,
            blocks=blocks,
            per_column=per_column,
        ),
        out_shape=[shape((devices, capacity), i32), shape((requests // LANES, LANES), i32)],
        in_specs=[VMEM],
        out_specs=[VMEM, VMEM],
        name="route",
    )(block_ids.T)
    gathered = lax.all_gather(outgoing, mesh_axes, axis=0, tiled=False)
    me = lax.axis_index("gx") * lax.axis_size("gy") + lax.axis_index("gy")
    incoming = lax.dynamic_index_in_dim(gathered, me, axis=1, keepdims=False)

    field, _ = lax.optimization_barrier((log_density, outgoing))
    xfirst, xlast, yfirst, ylast = pl.pallas_call(
        edges_kernel,
        out_shape=[
            shape((2, cells_y, depth), bf16),
            shape((2, cells_y, depth), bf16),
            shape((2, cells_x + 4, depth), f32),
            shape((2, cells_x + 4, depth), f32),
        ],
        in_specs=[ANY],
        out_specs=[VMEM] * 4,
        scratch_shapes=[
            pltpu.VMEM((2, 2, cells_y, depth), f32),
            pltpu.VMEM((2, cells_x, 8, depth), f32),
            pltpu.SemaphoreType.DMA((4,)),
        ],
        compiler_params=pltpu.CompilerParams(vmem_limit_bytes=56 * MIB),
        cost_estimate=pl.CostEstimate(flops=0, bytes_accessed=2 * MIB, transcendentals=0),
        name="edges",
    )(field)
    incoming, *edges = lax.optimization_barrier((incoming, xfirst, xlast, yfirst, ylast))
    wanted = incoming.reshape(-1)

    *served, crowded = pl.pallas_call(
        functools.partial(serve_kernel, capacity=capacity, first_slots=first_slots),
        out_shape=[shape((devices * n, width), bf16) for n in slots_of] + [shape((1,), i32)],
        in_specs=[SMEM, ANY],
        out_specs=[VMEM] * exchanges + [SMEM],
        scratch_shapes=[
            pltpu.VMEM((blocks + capacity, 1, width), f32),
            pltpu.VMEM((all_slots, 1, width), f32),
            pltpu.SemaphoreType.DMA((16,)),
        ],
        compiler_params=pltpu.CompilerParams(vmem_limit_bytes=56 * MIB),
        cost_estimate=pl.CostEstimate(
            flops=cells, bytes_accessed=6 * MIB, transcendentals=cells
        ),
        name="serve",
    )(wanted, to_rows(log_density))
    crowded = crowded[0] != 0

    returned = exchange_rows(served, crowded)
    *edges, incoming_late, _ = lax.optimization_barrier((*edges, incoming, served[0]))
    xlo, xhi = both_ways(*edges[:2], "gx")
    slabs = pl.pallas_call(
        ends_kernel,
        out_shape=[shape((2, cells_x + 4, depth), bf16)] * 2,
        in_specs=[VMEM] * 4,
        out_specs=[VMEM] * 2,
        scratch_shapes=[pltpu.VMEM((2, cells_x + 4, depth), f32)],
        compiler_params=pltpu.CompilerParams(vmem_limit_bytes=8 * MIB),
        cost_estimate=pl.CostEstimate(flops=0, bytes_accessed=MIB, transcendentals=0),
        name="ends",
    )(xlo, xhi, *edges[2:])
    ylo, yhi = both_ways(*slabs, "gy")
    slot_lists = [
        incoming_late[:, :first_slots].reshape(-1, LANES),
        (incoming_late[:, first_slots:] & (MARK - 1)).reshape(-1, LANES),
    ][:exchanges]
    match = pl.pallas_call(
        match_kernel,
        out_shape=shape((all_slots, LANES), bf16),
        in_specs=[VMEM],
        out_specs=VMEM,
        compiler_params=pltpu.CompilerParams(vmem_limit_bytes=8 * MIB),
        cost_estimate=pl.CostEstimate(flops=10**9, bytes_accessed=MIB, transcendentals=0),
        name="match",
    )(jnp.concatenate(slot_lists, axis=0))
    *returned, match, ylo, yhi = lax.optimization_barrier((*returned, match, ylo, yhi))

    chunks = blocks_dev * stars // LANES
    in_set = chunks // 4
    live = jnp.arange(stars)[None, :] < star_counts[:, None]
    live_inverse = jnp.where(live, inverse_var, 0.0)
    extinction, *parcel = pl.pallas_call(
        functools.partial(star_kernel, exchanges=exchanges),
        out_shape=[shape((chunks, LANES), f32)]
        + [shape((devices * n, width), bf16) for n in slots_of],
        in_specs=[SMEM, VMEM, VMEM, ANY] + [VMEM] * exchanges,
        out_specs=[VMEM] * (1 + exchanges),
        scratch_shapes=[
            pltpu.VMEM((2, in_set, blocks_dev // chunks, slots, stars, width), bf16),
            pltpu.VMEM((all_slots + 8, width), f32),
            pltpu.VMEM((in_set * (blocks_dev // chunks) * slots, 1, width), f32),
            pltpu.VMEM((all_slots, 1, width), f32),
            pltpu.SemaphoreType.DMA((2, in_set)),
        ],
        compiler_params=pltpu.CompilerParams(vmem_limit_bytes=50 * MIB),
        cost_estimate=pl.CostEstimate(
            flops=4 * weights.size, bytes_accessed=2 * weights.size, transcendentals=0
        ),
        name="stars",
    )(
        position.reshape(slots // 2, 2, blocks_dev).transpose(2, 1, 0).reshape(requests),
        observed.reshape(chunks, LANES),
        live_inverse.reshape(chunks, LANES),
        weights,
        *returned,
    )
    arrived = exchange_rows(parcel, crowded)

    field_late, _ = lax.optimization_barrier((log_density, parcel[0]))
    parts = 8
    base = pl.pallas_call(
        prior_kernel,
        out_shape=shape(field_shape, f32),
        in_specs=[ANY] + [VMEM] * 4,
        out_specs=ANY,
        scratch_shapes=[
            pltpu.VMEM((cells_x + 4, cells_y + 16, depth), f32),
            pltpu.VMEM((cells_x + 2, cells_y + 16, depth), f32),
            pltpu.VMEM(field_shape, f32),
            pltpu.VMEM((2, 2, cells_x + 4, depth), f32),
            pltpu.SemaphoreType.DMA((parts,)),
            pltpu.SemaphoreType.DMA((parts,)),
        ],
        compiler_params=pltpu.CompilerParams(vmem_limit_bytes=56 * MIB),
        cost_estimate=pl.CostEstimate(
            flops=30 * cells, bytes_accessed=8 * cells, transcendentals=0
        ),
        name="prior",
    )(field_late, xlo, xhi, ylo, yhi)

    new_log_density = pl.pallas_call(
        functools.partial(
            finish_kernel, exchanges=exchanges, capacity=capacity, first_slots=first_slots
        ),
        out_shape=shape(field_shape, f32),
        in_specs=[SMEM, ANY, ANY, ANY] + [VMEM] * exchanges,
        out_specs=ANY,
        scratch_shapes=[
            pltpu.VMEM((blocks + capacity, 1, width), f32),
            pltpu.VMEM((blocks + capacity, 1, width), f32),
            pltpu.VMEM((all_slots, 1, width), f32),
            pltpu.VMEM((all_slots, LANES), bf16),
            pltpu.VMEM(field_shape, f32),
            pltpu.VMEM(field_shape, f32),
            pltpu.VMEM(field_shape, f32),
            pltpu.SemaphoreType.DMA((3, parts)),
            pltpu.SemaphoreType.DMA((parts,)),
        ],
        compiler_params=pltpu.CompilerParams(vmem_limit_bytes=50 * MIB),
        cost_estimate=pl.CostEstimate(
            flops=4 * cells, bytes_accessed=12 * cells, transcendentals=cells
        ),
        name="finish",
    )(wanted, match, log_density, base, *arrived)
    return new_log_density, extinction.reshape(blocks_dev, stars)


def solution(mesh):
    placed = (
        P("gx", "gy", None),
        P(("gx", "gy"), None, None, None),
        P(("gx", "gy"), None),
        P(("gx", "gy"), None),
        P(("gx", "gy")),
        P(("gx", "gy"), None),
    )
    return jax.shard_map(
        on_device,
        mesh=mesh,
        in_specs=placed,
        out_specs=(P("gx", "gy", None), P(("gx", "gy"), None)),
        check_vma=False,
    )
```

```python
import functools

import jax
import jax.numpy as jnp
from jax import lax
from jax.experimental import pallas as pl
from jax.experimental.pallas import tpu as pltpu
from jax.sharding import PartitionSpec as P

shift_kappa = 0.5
prior_weight = 0.05
step_rate = 2.0

LANES = 128
GROUP = 8
MIB = 1 << 20
MARK = 1 << 16

CONTRACT_LANES = (((1,), (1,)), ((), ()))


def split_by(value, size):
    if size & (size - 1) == 0:
        high = value >> (size.bit_length() - 1)
        return high, value & (size - 1)
    high = value // size
    return high, value - high * size


def route_kernel(
    ids_ref, outgoing_ref, position_ref, *, devices, capacity, first_slots, blocks, per_column
):
    half = ids_ref.shape[0] // 2
    ids = jnp.concatenate([ids_ref[:half, :], ids_ref[half:, :]], axis=1)
    lane = lax.broadcasted_iota(jnp.int32, (LANES, LANES), 1)
    row = lax.broadcasted_iota(jnp.int32, (LANES, LANES), 0)
    upper = jnp.where(row <= lane, 1.0, 0.0).astype(jnp.bfloat16)
    tile_no = lax.broadcasted_iota(jnp.int32, (devices, LANES), 0)
    slot_no = lax.broadcasted_iota(jnp.int32, (capacity, LANES), 0)
    before = jnp.zeros((devices, 1), jnp.float32)
    lists = jnp.zeros((2 * devices, capacity), jnp.float32)
    for chunk in range(half):
        target, local = split_by(ids[chunk : chunk + 1, :], blocks)
        column, part = split_by(local, per_column)
        local = ((column >> 3) * per_column + part) * 8 + (column & 7)
        hit = tile_no == target
        onehot = jnp.where(hit, 1.0, 0.0)
        upto = before + jnp.dot(
            onehot.astype(jnp.bfloat16), upper, preferred_element_type=jnp.float32
        )
        before = upto[:, LANES - 1 :]
        rank = jnp.sum(onehot * upto, axis=0, keepdims=True).astype(jnp.int32) - 1
        in_slot = jnp.where(slot_no == rank, 1.0, 0.0).astype(jnp.bfloat16)
        high = ((local >> 7) + 1).astype(jnp.float32)
        low = (local & 127).astype(jnp.float32)
        digits = jnp.concatenate([jnp.where(hit, high, 0.0), jnp.where(hit, low, 0.0)], axis=0)
        lists = lists + lax.dot_general(
            digits.astype(jnp.bfloat16),
            in_slot,
            CONTRACT_LANES,
            preferred_element_type=jnp.float32,
        )
        last_slots = capacity - first_slots
        position_ref[chunk : chunk + 1, :] = jnp.where(
            rank < first_slots,
            target * first_slots + rank,
            devices * first_slots + target * last_slots + rank - first_slots,
        )
    high, low = lists[:devices], lists[devices:]
    wanted = ((high - 1.0) * 128.0 + low).astype(jnp.int32)
    filled = before.astype(jnp.int32)
    me = lax.axis_index("gx") * lax.axis_size("gy") + lax.axis_index("gy")
    fullest = jnp.max(jnp.where(tile_no[:, :1] == me, 0.0, before), axis=0, keepdims=True)
    listed = jnp.where(high > 0.5, wanted, blocks + filled)
    if first_slots < capacity:
        slot = lax.broadcasted_iota(jnp.int32, (devices, capacity), 1)
        mark = fullest.astype(jnp.int32) * MARK
        listed = listed + jnp.where(slot == capacity - 1, mark, 0)
    outgoing_ref[...] = listed


def table_kernel(field_ref, table_ref, xfirst_ref, xlast_ref, yfirst_ref, ylast_ref):
    cells_x, cells_y, depth = field_ref.shape
    per_column = depth // LANES
    blocks = cells_x * cells_y * per_column
    xfirst_ref[...] = field_ref[:2].astype(xfirst_ref.dtype)
    xlast_ref[...] = field_ref[cells_x - 2 :].astype(xlast_ref.dtype)

    def one_plane(x, carry):
        for yb in range(cells_y // 8):
            for part in range(0, per_column, 2):
                at = pl.multiple_of(((x * (cells_y // 8) + yb) * per_column + part) * 8, 16)
                both = [
                    field_ref[x, 8 * yb : 8 * yb + 8, p * LANES : (p + 1) * LANES]
                    for p in (part, part + 1)
                ]
                rows = jnp.exp(jnp.concatenate(both, axis=0))
                table_ref[pl.ds(at, 16), :] = rows.astype(table_ref.dtype)
        for h in range(2):
            yfirst_ref[h, pl.ds(x + 2, 1), :] = field_ref[x, h : h + 1, :]
            ylast_ref[h, pl.ds(x + 2, 1), :] = field_ref[x, cells_y - 2 + h : cells_y - 1 + h, :]
        return carry

    lax.fori_loop(0, cells_x, one_plane, 0)
    pad = table_ref.shape[0] - blocks
    table_ref[blocks:, :] = jnp.zeros((pad, LANES), table_ref.dtype)


def ends_kernel(
    xlo_ref, xhi_ref, yfirst_ref, ylast_ref, first_ref, last_ref, slab_ref
):
    cells_y = xlo_ref.shape[1]
    length = yfirst_ref.shape[1]
    for own_ref, out_ref, start, row in (
        (yfirst_ref, first_ref, 0, 0),
        (ylast_ref, last_ref, cells_y - 16, 14),
    ):
        slab_ref[...] = own_ref[...]
        for e in range(2):
            for x_ref, at in ((xlo_ref, e), (xhi_ref, length - 2 + e)):
                block = x_ref[e, start : start + 16, :].astype(jnp.float32)
                for h in range(2):
                    slab_ref[h, at : at + 1, :] = block[row + h : row + h + 1, :]
        out_ref[...] = slab_ref[...].astype(out_ref.dtype)


def copies_in_parts(source, target, sems):
    parts = sems.shape[0]
    size = source.shape[0] // parts
    return [
        pltpu.make_async_copy(
            source.at[pl.ds(i * size, size)], target.at[pl.ds(i * size, size)], sems.at[i]
        )
        for i in range(parts)
    ]


def for_each_group(incoming_ref, visit, capacity, first_slots, blocks):
    sources = incoming_ref.shape[0] // capacity
    last_slots = capacity - first_slots
    together = 8

    def groups_of(source):
        last = incoming_ref[source * capacity + capacity - 1] & (MARK - 1)
        return (jnp.where(last < blocks, capacity, last - blocks) + GROUP - 1) // GROUP

    def some_sources(quad, carry):
        own = [quad * together + i for i in range(together)]
        most = functools.reduce(jnp.maximum, [groups_of(source) for source in own])

        def one_group(group, carry):
            slot = group * GROUP
            for which, source in enumerate(own):
                listed = incoming_ref.at[pl.ds(source * capacity + slot, GROUP)]
                wanted = [listed[j] for j in range(GROUP)]
                visit(wanted, pl.multiple_of(source * first_slots + slot, GROUP), 0, which)
            return carry

        return lax.fori_loop(0, jnp.minimum(most, first_slots // GROUP), one_group, carry)

    lax.fori_loop(0, sources // together, some_sources, 0)
    if last_slots == 0:
        return

    def one_source(source, carry):
        def one_group(group, carry):
            slot = group * GROUP
            listed = incoming_ref.at[pl.ds(source * capacity + slot, GROUP)]
            wanted = [listed[j] & (MARK - 1) for j in range(GROUP)]
            visit(wanted, pl.multiple_of(source * last_slots + slot - first_slots, GROUP), 1, 0)
            return carry

        return lax.fori_loop(first_slots // GROUP, groups_of(source), one_group, carry)

    lax.fori_loop(0, sources, one_source, 0)


def serve_kernel(incoming_ref, table_ref, *refs, capacity, first_slots, blocks):
    *served_refs, crowded_ref, rows_ref, found_ref = refs

    def mark_of(source, most):
        return jnp.maximum(most, incoming_ref[source * capacity + capacity - 1] >> 16)

    fullest = lax.fori_loop(0, incoming_ref.shape[0] // capacity, mark_of, jnp.int32(0))
    crowded_ref[0] = jnp.where(fullest > first_slots, 1, 0)
    rows_ref.reshape(rows_ref.shape[0], LANES)[...] = table_ref[...].astype(jnp.float32)
    part_starts = [0, served_refs[0].shape[0]]

    def visit(wanted, row, list_part, which):
        rows = [rows_ref[at] for at in wanted]
        found = found_ref.at[pl.ds(row + part_starts[list_part], GROUP)]
        for j in range(GROUP):
            found[j] = rows[j]

    for_each_group(incoming_ref, visit, capacity, first_slots, blocks)
    found = found_ref.reshape(found_ref.shape[0], LANES)
    for start, served_ref in zip(part_starts, served_refs):
        span = slice(start, start + served_ref.shape[0])
        served_ref[...] = found[span, :].astype(jnp.bfloat16)


def match_kernel(incoming_ref, match_ref):
    lane = lax.broadcasted_iota(jnp.int32, (LANES, LANES), 1)
    row = lax.broadcasted_iota(jnp.int32, (LANES, LANES), 0)
    ones = jnp.ones((LANES, LANES), jnp.bfloat16)
    same_group = (lane // GROUP) == (row // GROUP)

    def one_row(i):
        wanted = incoming_ref[pl.ds(i, 1), :]
        high = jnp.where(lane == row, (wanted >> 7).astype(jnp.float32), 0.0).astype(jnp.bfloat16)
        low = jnp.where(lane == row, (wanted & 127).astype(jnp.float32), 0.0).astype(jnp.bfloat16)
        down = 128.0 * jnp.dot(high, ones, preferred_element_type=jnp.float32)
        down = down + jnp.dot(low, ones, preferred_element_type=jnp.float32)
        same = (down == wanted.astype(jnp.float32)) & same_group
        match_ref[pl.ds(pl.multiple_of(i * LANES, LANES), LANES), :] = jnp.where(
            same, 1.0, 0.0
        ).astype(jnp.bfloat16)

    def some_rows(i, carry):
        for j in range(4):
            one_row(4 * i + j)
        return carry

    lax.fori_loop(0, incoming_ref.shape[0] // 4, some_rows, 0)


def star_kernel(position_ref, observed_ref, inverse_ref, weights_hbm, *refs, exchanges):
    returned_refs, refs = refs[:exchanges], refs[exchanges:]
    extinction_ref, refs = refs[0], refs[1:]
    parcel_refs, refs = refs[:exchanges], refs[exchanges:]
    weights_ref, returned_rows, sens_ref, parcel_rows, sems = refs
    sets, in_set, per, slots, stars, width = weights_ref.shape
    chunks = extinction_ref.shape[0]
    rounds = chunks // (sets * in_set)
    per_chunk = per * slots
    fold = LANES // stars
    all_slots = parcel_rows.shape[0]
    sens_blocks = sens_ref.reshape(sens_ref.shape[0], width)
    lane = lax.broadcasted_iota(jnp.int32, (8, LANES), 1)
    row = lax.broadcasted_iota(jnp.int32, (8, LANES), 0)
    star_group = lane // stars
    own_slot = [row == star_group + fold * h for h in range(8 // fold)]

    def load(one_round, one_set):
        return [
            pltpu.make_async_copy(
                weights_hbm.at[pl.ds(((one_round * sets + one_set) * in_set + u) * per, per)],
                weights_ref.at[one_set, u],
                sems.at[one_set, u],
            )
            for u in range(in_set)
        ]

    def extinctions(one_set, u, chunk, places):
        sums = []
        for b in range(per):
            total = jnp.zeros((stars // 8, 8, width), jnp.float32)
            for k in range(slots):
                at = places[u * per_chunk + b * slots + k]
                fetched = returned_rows[pl.ds(at, 8, stride=0), :]
                block = weights_ref[one_set, u, b, k].astype(jnp.float32)
                total = total + block.reshape(stars // 8, 8, width) * fetched
            sums.append(total.reshape(stars, width))
        extinction = lax.dot_general(
            jnp.ones((8, width), jnp.float32),
            jnp.concatenate(sums, axis=0),
            CONTRACT_LANES,
            precision=lax.Precision.HIGHEST,
            preferred_element_type=jnp.float32,
        )
        here = pl.ds(chunk, 1)
        extinction_ref[here, :] = extinction[:1]
        return inverse_ref[here, :] * (extinction - observed_ref[here, :])

    def sensitivities(one_set, u, weighted):
        for b in range(per):
            spread = jnp.where(star_group == b, weighted, 0.0)
            shift = stars
            while shift < LANES:
                spread = spread + pltpu.roll(spread, shift, 1)
                shift *= 2
            left = jnp.concatenate(
                [jnp.where(own, spread, 0.0) for own in own_slot], axis=1
            ).astype(jnp.bfloat16)
            eights = [weights_ref[one_set, u, b, 8 * j : 8 * j + 8] for j in range(slots // 8)]
            right = jnp.concatenate([x.reshape(8 * stars, width) for x in eights], axis=1)
            sens = jnp.dot(left, right, preferred_element_type=jnp.float32)
            for j in range(slots // 8):
                first = u * per_chunk + b * slots + 8 * j
                sens_blocks[first : first + 8, :] = sens[:, j * width : (j + 1) * width]

    def scatter(u, places):
        for i in range(u * per_chunk, (u + 1) * per_chunk):
            parcel_rows[places[i]] = sens_ref[i]

    def work(one_round, one_set):
        first = (one_round * sets + one_set) * in_set
        size = in_set * per_chunk
        places = position_ref.at[pl.ds(pl.multiple_of(first * per_chunk, size), size)]
        weighted = {}
        for u in range(in_set + 2):
            if u < in_set:
                weighted[u] = extinctions(one_set, u, first + u, places)
            if 1 <= u <= in_set:
                sensitivities(one_set, u - 1, weighted[u - 1])
            if u >= 2:
                scatter(u - 2, places)

    for copy in load(0, 0):
        copy.start()
    start = 0
    for returned_ref in returned_refs:
        span = slice(start, start + returned_ref.shape[0])
        returned_rows[span, :] = returned_ref[...].astype(jnp.float32)
        start = span.stop
    parcel_rows.reshape(all_slots, width)[...] = jnp.zeros((all_slots, width), jnp.float32)

    def one_round(i, carry):
        for one_set in range(sets):
            for copy in load(i, one_set):
                copy.wait()
            if one_set + 1 < sets:
                for copy in load(i, one_set + 1):
                    copy.start()
            else:

                @pl.when(i + 1 < rounds)
                def _():
                    for copy in load(i + 1, 0):
                        copy.start()

            work(i, one_set)
        return carry

    lax.fori_loop(0, rounds, one_round, 0)
    start = 0
    for parcel_ref in parcel_refs:
        span = slice(start, start + parcel_ref.shape[0])
        parcel_ref[...] = parcel_rows.reshape(all_slots, width)[span, :].astype(jnp.bfloat16)
        start = span.stop


def prior_kernel(
    field_hbm, xlo_ref, xhi_ref, ylo_ref, yhi_ref, out_hbm,
    padded, smooth, out_ref, yends_ref, sems, out_sems,
):
    cells_x, cells_y, depth = field_hbm.shape
    rows = padded.shape[1]
    parts = sems.shape[0]
    planes = cells_x // parts
    own_rows = pl.ds(8, cells_y)
    loads = [
        pltpu.make_async_copy(
            field_hbm.at[pl.ds(i * planes, planes)],
            padded.at[pl.ds(2 + i * planes, planes), own_rows],
            sems.at[i],
        )
        for i in range(parts)
    ]
    for load in loads:
        load.start()
    gx, gy = lax.axis_index("gx"), lax.axis_index("gy")
    last_gx, last_gy = lax.axis_size("gx") - 1, lax.axis_size("gy") - 1
    z = lax.broadcasted_iota(jnp.int32, (rows, depth), 1)
    y = lax.broadcasted_iota(jnp.int32, (rows, depth), 0) - 8
    inside_y = ((y >= 0) | (gy > 0)) & ((y < cells_y) | (gy < last_gy))

    def operate(center, below, above):
        beside = below + above
        beside = beside + pltpu.roll(center, 1, 0) + pltpu.roll(center, rows - 1, 0)
        beside = beside + jnp.where(z == 0, 0.0, pltpu.roll(center, 1, 1))
        beside = beside + jnp.where(z == depth - 1, 0.0, pltpu.roll(center, depth - 1, 1))
        return (shift_kappa + 6.0) * center - beside

    for h in range(2):
        padded[h, own_rows, :] = xlo_ref[h].astype(jnp.float32)
        padded[cells_x + 2 + h, own_rows, :] = xhi_ref[h].astype(jnp.float32)

    yends_ref[0] = ylo_ref[...].astype(jnp.float32)
    yends_ref[1] = yhi_ref[...].astype(jnp.float32)

    def fill_ends(plane, carry):
        padded[plane, 0:8, :] = jnp.zeros((8, depth), jnp.float32)
        padded[plane, 8 + cells_y :, :] = jnp.zeros((8, depth), jnp.float32)
        for h in range(2):
            padded[plane, 6 + h : 7 + h, :] = yends_ref[0, h, pl.ds(plane, 1), :]
            padded[plane, 8 + cells_y + h : 9 + cells_y + h, :] = yends_ref[1, h, pl.ds(plane, 1), :]
        return carry

    lax.fori_loop(0, cells_x + 4, fill_ends, 0)

    def smooth_plane(plane, carry):
        value = operate(padded[plane], padded[plane - 1], padded[plane + 1])
        inside = ((plane > 1) | (gx > 0)) & ((plane < cells_x + 2) | (gx < last_gx))
        smooth[plane - 1] = jnp.where(inside_y & inside, value, 0.0)
        return carry

    def out_plane(x, carry):
        prior = operate(smooth[x + 1], smooth[x], smooth[x + 2])
        change = (step_rate * prior_weight) * prior[8 : 8 + cells_y]
        out_ref[x] = padded[x + 2, own_rows, :] - change
        return carry

    def store(part):
        span = pl.ds(part * planes, planes)
        return pltpu.make_async_copy(out_ref.at[span], out_hbm.at[span], out_sems.at[part])

    smoothed, done = 1, 0
    for part in range(parts):
        loads[part].wait()
        ready = cells_x + 3 if part + 1 == parts else 1 + (part + 1) * planes
        lax.fori_loop(smoothed, ready, smooth_plane, 0)
        smoothed = ready
        lax.fori_loop(done, ready - 3, out_plane, 0)
        done = ready - 3
        for whole in range(parts):
            if part * planes - 2 < (whole + 1) * planes <= done:
                store(whole).start()
    for part in range(parts):
        store(part).wait()


def finish_kernel(
    incoming_ref, match_hbm, field_hbm, base_hbm, *refs, exchanges, capacity, first_slots
):
    arrived_refs, refs = refs[:exchanges], refs[exchanges:]
    out_hbm, *collected, rows_ref, match_ref, field_ref, base_ref, out_ref, in_sems, out_sems = refs
    cells_x, cells_y, depth = field_ref.shape
    per_column = depth // LANES
    parts = out_sems.shape[0]
    planes = cells_x // parts
    blocks = cells_x * cells_y * per_column
    matches = copies_in_parts(match_hbm, match_ref, in_sems.at[2])
    loads = copies_in_parts(field_hbm, field_ref, in_sems.at[0])
    loads += copies_in_parts(base_hbm, base_ref, in_sems.at[1])
    for load in matches + loads:
        load.start()
    collected_rows = [ref.reshape(ref.shape[0], LANES) for ref in collected]
    for ref in collected_rows:
        ref[...] = jnp.zeros_like(ref)
    for load in matches:
        load.wait()
    merged = rows_ref.reshape(rows_ref.shape[0], LANES)
    start = 0
    for arrived_ref in arrived_refs:
        for i in range(arrived_ref.shape[0] // LANES):
            span = slice(start + i * LANES, start + (i + 1) * LANES)
            merged[span, :] = -step_rate * jnp.dot(
                match_ref[span, :],
                arrived_ref[i * LANES : (i + 1) * LANES, :],
                preferred_element_type=jnp.float32,
            )
        start += arrived_ref.shape[0]

    part_starts = [0, arrived_refs[0].shape[0]]

    def visit(wanted, row, list_part, which):
        row = pl.multiple_of(row + part_starts[list_part], GROUP)
        rows = rows_ref.at[pl.ds(row, GROUP)]
        into = collected[which % len(collected)]
        sums = [into[wanted[j]] + rows[j] for j in range(GROUP)]
        for j in range(GROUP):
            into[wanted[j]] = sums[j]

    for_each_group(incoming_ref, visit, capacity, first_slots, blocks)
    for load in loads:
        load.wait()

    def store(part):
        span = pl.ds(part * planes, planes)
        return pltpu.make_async_copy(out_ref.at[span], out_hbm.at[span], out_sems.at[part])

    def one_plane(x, carry):
        for yb in range(cells_y // 8):
            for part in range(per_column):
                at = pl.multiple_of(((x * (cells_y // 8) + yb) * per_column + part) * 8, 8)
                here = (x, slice(8 * yb, 8 * yb + 8), slice(part * LANES, (part + 1) * LANES))
                grad = collected_rows[0][pl.ds(at, 8), :] + collected_rows[1][pl.ds(at, 8), :]
                out_ref[here] = base_ref[here] + grad * jnp.exp(field_ref[here])
        return carry

    for part in range(parts):
        lax.fori_loop(part * planes, (part + 1) * planes, one_plane, 0)
        store(part).start()
    for part in range(parts):
        store(part).wait()


def both_ways(first, last, axis):
    peers = lax.axis_size(axis)
    up = [(i, i + 1) for i in range(peers - 1)]
    down = [(j, i) for i, j in up]
    return lax.ppermute(last, axis, up), lax.ppermute(first, axis, down)


VMEM = pl.BlockSpec(memory_space=pltpu.VMEM)
SMEM = pl.BlockSpec(memory_space=pltpu.SMEM)
ANY = pl.BlockSpec(memory_space=pl.ANY)


def on_device(log_density, weights, observed, inverse_var, star_counts, block_ids):
    cells_x, cells_y, depth = log_density.shape
    blocks_dev, slots, stars, width = weights.shape
    devices = lax.axis_size("gx") * lax.axis_size("gy")
    requests = blocks_dev * slots
    capacity = 2 * requests // devices
    first_slots = 11 * capacity // 16 if capacity % LANES == 0 else capacity
    slots_of = [n for n in (first_slots, capacity - first_slots) if n > 0]
    exchanges = len(slots_of)
    all_slots = devices * capacity
    per_column = depth // width
    blocks = cells_x * cells_y * per_column
    cells = log_density.size
    field_shape = (cells_x, cells_y, depth)
    mesh_axes = ("gx", "gy")
    f32, bf16, i32 = jnp.float32, jnp.bfloat16, jnp.int32
    shape = jax.ShapeDtypeStruct

    def exchange(x):
        return lax.all_to_all(x, mesh_axes, split_axis=0, concat_axis=0, tiled=True)

    def exchange_rows(parts, crowded):
        moved = [parts[0].reshape(devices, first_slots, width)]
        moved[0] = exchange(moved[0])
        for part in parts[1:]:
            part = part.reshape(devices, capacity - first_slots, width)
            moved.append(lax.cond(crowded, exchange, lambda x: x, part))
        return [x.reshape(-1, width) for x in moved]

    outgoing, position = pl.pallas_call(
        functools.partial(
            route_kernel,
            devices=devices,
            capacity=capacity,
            first_slots=first_slots,
            blocks=blocks,
            per_column=per_column,
        ),
        out_shape=[shape((devices, capacity), i32), shape((requests // LANES, LANES), i32)],
        in_specs=[VMEM],
        out_specs=[VMEM, VMEM],
        name="route",
    )(block_ids.T)
    incoming = exchange(outgoing)

    field, _ = lax.optimization_barrier((log_density, outgoing))
    table, xfirst, xlast, yfirst, ylast = pl.pallas_call(
        table_kernel,
        out_shape=[
            shape((blocks + capacity, width), bf16),
            shape((2, cells_y, depth), bf16),
            shape((2, cells_y, depth), bf16),
            shape((2, cells_x + 4, depth), f32),
            shape((2, cells_x + 4, depth), f32),
        ],
        in_specs=[VMEM],
        out_specs=[VMEM] * 5,
        compiler_params=pltpu.CompilerParams(vmem_limit_bytes=16 * MIB),
        cost_estimate=pl.CostEstimate(
            flops=8 * cells, bytes_accessed=8 * cells, transcendentals=cells
        ),
        name="table",
    )(field)
    incoming, *edges = lax.optimization_barrier((incoming, xfirst, xlast, yfirst, ylast))
    wanted = incoming.reshape(-1)

    *served, crowded = pl.pallas_call(
        functools.partial(
            serve_kernel, capacity=capacity, first_slots=first_slots, blocks=blocks
        ),
        out_shape=[shape((devices * n, width), bf16) for n in slots_of] + [shape((1,), i32)],
        in_specs=[SMEM, VMEM],
        out_specs=[VMEM] * exchanges + [SMEM],
        scratch_shapes=[
            pltpu.VMEM((blocks + capacity, 1, width), f32),
            pltpu.VMEM((all_slots, 1, width), f32),
        ],
        compiler_params=pltpu.CompilerParams(vmem_limit_bytes=24 * MIB),
        cost_estimate=pl.CostEstimate(
            flops=cells, bytes_accessed=6 * MIB, transcendentals=cells
        ),
        name="serve",
    )(wanted, table)
    crowded = crowded[0] != 0

    returned = exchange_rows(served, crowded)
    *edges, incoming_late, _ = lax.optimization_barrier((*edges, incoming, served[0]))
    xlo, xhi = both_ways(*edges[:2], "gx")
    slabs = pl.pallas_call(
        ends_kernel,
        out_shape=[shape((2, cells_x + 4, depth), bf16)] * 2,
        in_specs=[VMEM] * 4,
        out_specs=[VMEM] * 2,
        scratch_shapes=[pltpu.VMEM((2, cells_x + 4, depth), f32)],
        compiler_params=pltpu.CompilerParams(vmem_limit_bytes=8 * MIB),
        cost_estimate=pl.CostEstimate(flops=0, bytes_accessed=MIB, transcendentals=0),
        name="ends",
    )(xlo, xhi, *edges[2:])
    ylo, yhi = both_ways(*slabs, "gy")
    slot_lists = [
        incoming_late[:, :first_slots].reshape(-1, LANES),
        (incoming_late[:, first_slots:] & (MARK - 1)).reshape(-1, LANES),
    ][:exchanges]
    match = pl.pallas_call(
        match_kernel,
        out_shape=shape((all_slots, LANES), bf16),
        in_specs=[VMEM],
        out_specs=VMEM,
        compiler_params=pltpu.CompilerParams(vmem_limit_bytes=8 * MIB),
        cost_estimate=pl.CostEstimate(flops=10**9, bytes_accessed=MIB, transcendentals=0),
        name="match",
    )(jnp.concatenate(slot_lists, axis=0))
    *returned, match, ylo, yhi = lax.optimization_barrier((*returned, match, ylo, yhi))

    chunks = blocks_dev * stars // LANES
    in_set = chunks // 4
    live = jnp.arange(stars)[None, :] < star_counts[:, None]
    live_inverse = jnp.where(live, inverse_var, 0.0)
    extinction, *parcel = pl.pallas_call(
        functools.partial(star_kernel, exchanges=exchanges),
        out_shape=[shape((chunks, LANES), f32)]
        + [shape((devices * n, width), bf16) for n in slots_of],
        in_specs=[SMEM, VMEM, VMEM, ANY] + [VMEM] * exchanges,
        out_specs=[VMEM] * (1 + exchanges),
        scratch_shapes=[
            pltpu.VMEM((2, in_set, blocks_dev // chunks, slots, stars, width), bf16),
            pltpu.VMEM((all_slots + 8, width), f32),
            pltpu.VMEM((in_set * (blocks_dev // chunks) * slots, 1, width), f32),
            pltpu.VMEM((all_slots, 1, width), f32),
            pltpu.SemaphoreType.DMA((2, in_set)),
        ],
        compiler_params=pltpu.CompilerParams(vmem_limit_bytes=50 * MIB),
        cost_estimate=pl.CostEstimate(
            flops=4 * weights.size, bytes_accessed=2 * weights.size, transcendentals=0
        ),
        name="stars",
    )(
        position.reshape(slots // 2, 2, blocks_dev).transpose(2, 1, 0).reshape(requests),
        observed.reshape(chunks, LANES),
        live_inverse.reshape(chunks, LANES),
        weights,
        *returned,
    )
    arrived = exchange_rows(parcel, crowded)

    field_late, _ = lax.optimization_barrier((log_density, parcel[0]))
    parts = 8
    base = pl.pallas_call(
        prior_kernel,
        out_shape=shape(field_shape, f32),
        in_specs=[ANY] + [VMEM] * 4,
        out_specs=ANY,
        scratch_shapes=[
            pltpu.VMEM((cells_x + 4, cells_y + 16, depth), f32),
            pltpu.VMEM((cells_x + 2, cells_y + 16, depth), f32),
            pltpu.VMEM(field_shape, f32),
            pltpu.VMEM((2, 2, cells_x + 4, depth), f32),
            pltpu.SemaphoreType.DMA((parts,)),
            pltpu.SemaphoreType.DMA((parts,)),
        ],
        compiler_params=pltpu.CompilerParams(vmem_limit_bytes=56 * MIB),
        cost_estimate=pl.CostEstimate(
            flops=30 * cells, bytes_accessed=8 * cells, transcendentals=0
        ),
        name="prior",
    )(field_late, xlo, xhi, ylo, yhi)

    new_log_density = pl.pallas_call(
        functools.partial(
            finish_kernel, exchanges=exchanges, capacity=capacity, first_slots=first_slots
        ),
        out_shape=shape(field_shape, f32),
        in_specs=[SMEM, ANY, ANY, ANY] + [VMEM] * exchanges,
        out_specs=ANY,
        scratch_shapes=[
            pltpu.VMEM((blocks + capacity, 1, width), f32),
            pltpu.VMEM((blocks + capacity, 1, width), f32),
            pltpu.VMEM((all_slots, 1, width), f32),
            pltpu.VMEM((all_slots, LANES), bf16),
            pltpu.VMEM(field_shape, f32),
            pltpu.VMEM(field_shape, f32),
            pltpu.VMEM(field_shape, f32),
            pltpu.SemaphoreType.DMA((3, parts)),
            pltpu.SemaphoreType.DMA((parts,)),
        ],
        compiler_params=pltpu.CompilerParams(vmem_limit_bytes=50 * MIB),
        cost_estimate=pl.CostEstimate(
            flops=4 * cells, bytes_accessed=12 * cells, transcendentals=cells
        ),
        name="finish",
    )(wanted, match, log_density, base, *arrived)
    return new_log_density, extinction.reshape(blocks_dev, stars)


def solution(mesh):
    placed = (
        P("gx", "gy", None),
        P(("gx", "gy"), None, None, None),
        P(("gx", "gy"), None),
        P(("gx", "gy"), None),
        P(("gx", "gy")),
        P(("gx", "gy"), None),
    )
    return jax.shard_map(
        on_device,
        mesh=mesh,
        in_specs=placed,
        out_specs=(P("gx", "gy", None), P(("gx", "gy"), None)),
        check_vma=False,
    )
```

```python
import functools

import jax
import jax.numpy as jnp
from jax import lax
from jax.experimental import pallas as pl
from jax.experimental.pallas import tpu as pltpu
from jax.sharding import PartitionSpec as P

shift_kappa = 0.5
prior_weight = 0.05
step_rate = 2.0

LANES = 128
GROUP = 8
MIB = 1 << 20
MARK = 1 << 16

CONTRACT_LANES = (((1,), (1,)), ((), ()))


def split_by(value, size):
    if size & (size - 1) == 0:
        high = value >> (size.bit_length() - 1)
        return high, value & (size - 1)
    high = value // size
    return high, value - high * size


def route_kernel(
    ids_ref, outgoing_ref, position_ref, *, devices, capacity, first_slots, blocks, per_column
):
    half = ids_ref.shape[0] // 2
    ids = jnp.concatenate([ids_ref[:half, :], ids_ref[half:, :]], axis=1)
    target, local = split_by(ids, blocks)
    column, part = split_by(local, per_column)
    local = ((column >> 3) * per_column + part) * 8 + (column & 7)
    high = ((local >> 7) + 1).astype(jnp.float32)
    low = (local & 127).astype(jnp.float32)
    lane = lax.broadcasted_iota(jnp.int32, (LANES, LANES), 1)
    row = lax.broadcasted_iota(jnp.int32, (LANES, LANES), 0)
    upper = jnp.where(row <= lane, 1.0, 0.0)
    sums = jnp.concatenate([upper, jnp.ones_like(upper)], axis=1).astype(jnp.bfloat16)
    tile_no = lax.broadcasted_iota(jnp.int32, (devices, LANES), 0)
    slot_no = lax.broadcasted_iota(jnp.int32, (capacity, LANES), 0)
    hits = [tile_no == target[c : c + 1, :] for c in range(half)]
    onehots = [jnp.where(hit, 1.0, 0.0) for hit in hits]
    counts = jnp.dot(
        jnp.concatenate(onehots, axis=0).astype(jnp.bfloat16),
        sums,
        preferred_element_type=jnp.float32,
    )
    before = jnp.zeros((devices, LANES), jnp.float32)
    ranks, digits, in_slots = [], [], []
    for c in range(half):
        here = slice(c * devices, (c + 1) * devices)
        upto = before + counts[here, :LANES]
        before = before + counts[here, LANES:]
        rank = jnp.sum(onehots[c] * upto, axis=0, keepdims=True).astype(jnp.int32) - 1
        ranks.append(rank)
        in_slots.append(jnp.where(slot_no == rank, 1.0, 0.0))
        digits.append(
            jnp.concatenate(
                [jnp.where(hits[c], x[c : c + 1, :], 0.0) for x in (high, low)], axis=0
            )
        )
    lists = lax.dot_general(
        jnp.concatenate(digits, axis=1).astype(jnp.bfloat16),
        jnp.concatenate(in_slots, axis=1).astype(jnp.bfloat16),
        CONTRACT_LANES,
        preferred_element_type=jnp.float32,
    )
    rank = jnp.concatenate(ranks, axis=0)
    last_slots = capacity - first_slots
    position_ref[...] = jnp.where(
        rank < first_slots,
        target * first_slots + rank,
        devices * first_slots + target * last_slots + rank - first_slots,
    )
    before = before[:, :1]
    high, low = lists[:devices], lists[devices:]
    wanted = ((high - 1.0) * 128.0 + low).astype(jnp.int32)
    filled = before.astype(jnp.int32)
    me = lax.axis_index("gx") * lax.axis_size("gy") + lax.axis_index("gy")
    fullest = jnp.max(jnp.where(tile_no[:, :1] == me, 0.0, before), axis=0, keepdims=True)
    listed = jnp.where(high > 0.5, wanted, blocks + filled)
    if first_slots < capacity:
        slot = lax.broadcasted_iota(jnp.int32, (devices, capacity), 1)
        mark = fullest.astype(jnp.int32) * MARK
        listed = listed + jnp.where(slot == capacity - 1, mark, 0)
    outgoing_ref[...] = listed


def table_kernel(field_ref, table_ref, xfirst_ref, xlast_ref, yfirst_ref, ylast_ref):
    cells_x, cells_y, depth = field_ref.shape
    per_column = depth // LANES
    blocks = cells_x * cells_y * per_column
    xfirst_ref[...] = field_ref[:2].astype(xfirst_ref.dtype)
    xlast_ref[...] = field_ref[cells_x - 2 :].astype(xlast_ref.dtype)

    def one_plane(x, carry):
        for yb in range(cells_y // 8):
            for part in range(0, per_column, 2):
                at = pl.multiple_of(((x * (cells_y // 8) + yb) * per_column + part) * 8, 16)
                both = [
                    field_ref[x, 8 * yb : 8 * yb + 8, p * LANES : (p + 1) * LANES]
                    for p in (part, part + 1)
                ]
                rows = jnp.exp(jnp.concatenate(both, axis=0))
                table_ref[pl.ds(at, 16), :] = rows.astype(table_ref.dtype)
        for h in range(2):
            yfirst_ref[h, pl.ds(x + 2, 1), :] = field_ref[x, h : h + 1, :]
            ylast_ref[h, pl.ds(x + 2, 1), :] = field_ref[x, cells_y - 2 + h : cells_y - 1 + h, :]
        return carry

    lax.fori_loop(0, cells_x, one_plane, 0)
    pad = table_ref.shape[0] - blocks
    table_ref[blocks:, :] = jnp.zeros((pad, LANES), table_ref.dtype)


def ends_kernel(
    xlo_ref, xhi_ref, yfirst_ref, ylast_ref, first_ref, last_ref, slab_ref
):
    cells_y = xlo_ref.shape[1]
    length = yfirst_ref.shape[1]
    for own_ref, out_ref, start, row in (
        (yfirst_ref, first_ref, 0, 0),
        (ylast_ref, last_ref, cells_y - 16, 14),
    ):
        slab_ref[...] = own_ref[...]
        for e in range(2):
            for x_ref, at in ((xlo_ref, e), (xhi_ref, length - 2 + e)):
                block = x_ref[e, start : start + 16, :].astype(jnp.float32)
                for h in range(2):
                    slab_ref[h, at : at + 1, :] = block[row + h : row + h + 1, :]
        out_ref[...] = slab_ref[...].astype(out_ref.dtype)


def copies_in_parts(source, target, sems):
    parts = sems.shape[0]
    size = source.shape[0] // parts
    return [
        pltpu.make_async_copy(
            source.at[pl.ds(i * size, size)], target.at[pl.ds(i * size, size)], sems.at[i]
        )
        for i in range(parts)
    ]


def for_each_group(incoming_ref, visit, capacity, first_slots, blocks):
    sources = incoming_ref.shape[0] // capacity
    last_slots = capacity - first_slots
    together = 8

    def groups_of(source):
        last = incoming_ref[source * capacity + capacity - 1] & (MARK - 1)
        return (jnp.where(last < blocks, capacity, last - blocks) + GROUP - 1) // GROUP

    def some_sources(quad, carry):
        own = [quad * together + i for i in range(together)]
        most = functools.reduce(jnp.maximum, [groups_of(source) for source in own])

        def one_group(group, carry):
            slot = group * GROUP
            for which, source in enumerate(own):
                listed = incoming_ref.at[pl.ds(source * capacity + slot, GROUP)]
                wanted = [listed[j] for j in range(GROUP)]
                visit(wanted, pl.multiple_of(source * first_slots + slot, GROUP), 0, which)
            return carry

        return lax.fori_loop(0, jnp.minimum(most, first_slots // GROUP), one_group, carry)

    lax.fori_loop(0, sources // together, some_sources, 0)
    if last_slots == 0:
        return

    def one_source(source, carry):
        def one_group(group, carry):
            slot = group * GROUP
            listed = incoming_ref.at[pl.ds(source * capacity + slot, GROUP)]
            wanted = [listed[j] & (MARK - 1) for j in range(GROUP)]
            visit(wanted, pl.multiple_of(source * last_slots + slot - first_slots, GROUP), 1, 0)
            return carry

        return lax.fori_loop(first_slots // GROUP, groups_of(source), one_group, carry)

    lax.fori_loop(0, sources, one_source, 0)


def serve_kernel(incoming_ref, table_ref, *refs, capacity, first_slots, blocks):
    *served_refs, crowded_ref, rows_ref, found_ref = refs

    def mark_of(source, most):
        return jnp.maximum(most, incoming_ref[source * capacity + capacity - 1] >> 16)

    fullest = lax.fori_loop(0, incoming_ref.shape[0] // capacity, mark_of, jnp.int32(0))
    crowded_ref[0] = jnp.where(fullest > first_slots, 1, 0)
    rows_ref.reshape(rows_ref.shape[0], LANES)[...] = table_ref[...].astype(jnp.float32)
    part_starts = [0, served_refs[0].shape[0]]

    def visit(wanted, row, list_part, which):
        rows = [rows_ref[at] for at in wanted]
        found = found_ref.at[pl.ds(row + part_starts[list_part], GROUP)]
        for j in range(GROUP):
            found[j] = rows[j]

    for_each_group(incoming_ref, visit, capacity, first_slots, blocks)
    found = found_ref.reshape(found_ref.shape[0], LANES)
    for start, served_ref in zip(part_starts, served_refs):
        span = slice(start, start + served_ref.shape[0])
        served_ref[...] = found[span, :].astype(jnp.bfloat16)


def match_kernel(incoming_ref, match_ref):
    lane = lax.broadcasted_iota(jnp.int32, (LANES, LANES), 1)
    row = lax.broadcasted_iota(jnp.int32, (LANES, LANES), 0)
    ones = jnp.ones((LANES, LANES), jnp.bfloat16)
    same_group = (lane // GROUP) == (row // GROUP)

    def one_row(i):
        wanted = incoming_ref[pl.ds(i, 1), :]
        high = jnp.where(lane == row, (wanted >> 7).astype(jnp.float32), 0.0).astype(jnp.bfloat16)
        low = jnp.where(lane == row, (wanted & 127).astype(jnp.float32), 0.0).astype(jnp.bfloat16)
        down = 128.0 * jnp.dot(high, ones, preferred_element_type=jnp.float32)
        down = down + jnp.dot(low, ones, preferred_element_type=jnp.float32)
        same = (down == wanted.astype(jnp.float32)) & same_group
        match_ref[pl.ds(pl.multiple_of(i * LANES, LANES), LANES), :] = jnp.where(
            same, 1.0, 0.0
        ).astype(jnp.bfloat16)

    def some_rows(i, carry):
        for j in range(4):
            one_row(4 * i + j)
        return carry

    lax.fori_loop(0, incoming_ref.shape[0] // 4, some_rows, 0)


def star_kernel(position_ref, observed_ref, inverse_ref, weights_hbm, *refs, exchanges):
    returned_refs, refs = refs[:exchanges], refs[exchanges:]
    extinction_ref, refs = refs[0], refs[1:]
    parcel_refs, refs = refs[:exchanges], refs[exchanges:]
    weights_ref, returned_rows, sens_ref, parcel_rows, sems = refs
    sets, in_set, per, slots, stars, width = weights_ref.shape
    chunks = extinction_ref.shape[0]
    rounds = chunks // (sets * in_set)
    per_chunk = per * slots
    fold = LANES // stars
    all_slots = parcel_rows.shape[0]
    sens_blocks = sens_ref.reshape(sens_ref.shape[0], width)
    lane = lax.broadcasted_iota(jnp.int32, (8, LANES), 1)
    row = lax.broadcasted_iota(jnp.int32, (8, LANES), 0)
    star_group = lane // stars
    own_slot = [row == star_group + fold * h for h in range(8 // fold)]

    def load(one_round, one_set):
        return [
            pltpu.make_async_copy(
                weights_hbm.at[pl.ds(((one_round * sets + one_set) * in_set + u) * per, per)],
                weights_ref.at[one_set, u],
                sems.at[one_set, u],
            )
            for u in range(in_set)
        ]

    def extinctions(one_set, u, chunk, places):
        sums = []
        for b in range(per):
            total = jnp.zeros((stars // 8, 8, width), jnp.float32)
            for k in range(slots):
                at = places[u * per_chunk + b * slots + k]
                fetched = returned_rows[pl.ds(at, 8, stride=0), :]
                block = weights_ref[one_set, u, b, k].astype(jnp.float32)
                total = total + block.reshape(stars // 8, 8, width) * fetched
            sums.append(total.reshape(stars, width))
        extinction = lax.dot_general(
            jnp.ones((8, width), jnp.float32),
            jnp.concatenate(sums, axis=0),
            CONTRACT_LANES,
            precision=lax.Precision.HIGHEST,
            preferred_element_type=jnp.float32,
        )
        here = pl.ds(chunk, 1)
        extinction_ref[here, :] = extinction[:1]
        return inverse_ref[here, :] * (extinction - observed_ref[here, :])

    def sensitivities(one_set, u, weighted):
        for b in range(per):
            spread = jnp.where(star_group == b, weighted, 0.0)
            shift = stars
            while shift < LANES:
                spread = spread + pltpu.roll(spread, shift, 1)
                shift *= 2
            left = jnp.concatenate(
                [jnp.where(own, spread, 0.0) for own in own_slot], axis=1
            ).astype(jnp.bfloat16)
            eights = [weights_ref[one_set, u, b, 8 * j : 8 * j + 8] for j in range(slots // 8)]
            right = jnp.concatenate([x.reshape(8 * stars, width) for x in eights], axis=1)
            sens = jnp.dot(left, right, preferred_element_type=jnp.float32)
            for j in range(slots // 8):
                first = u * per_chunk + b * slots + 8 * j
                sens_blocks[first : first + 8, :] = sens[:, j * width : (j + 1) * width]

    def scatter(u, places):
        for i in range(u * per_chunk, (u + 1) * per_chunk):
            parcel_rows[places[i]] = sens_ref[i]

    def work(one_round, one_set):
        first = (one_round * sets + one_set) * in_set
        size = in_set * per_chunk
        places = position_ref.at[pl.ds(pl.multiple_of(first * per_chunk, size), size)]
        weighted = {}
        for u in range(in_set + 2):
            if u < in_set:
                weighted[u] = extinctions(one_set, u, first + u, places)
            if 1 <= u <= in_set:
                sensitivities(one_set, u - 1, weighted[u - 1])
            if u >= 2:
                scatter(u - 2, places)

    for copy in load(0, 0):
        copy.start()
    start = 0
    for returned_ref in returned_refs:
        span = slice(start, start + returned_ref.shape[0])
        returned_rows[span, :] = returned_ref[...].astype(jnp.float32)
        start = span.stop
    parcel_rows.reshape(all_slots, width)[...] = jnp.zeros((all_slots, width), jnp.float32)

    def one_round(i, carry):
        for one_set in range(sets):
            for copy in load(i, one_set):
                copy.wait()
            if one_set + 1 < sets:
                for copy in load(i, one_set + 1):
                    copy.start()
            else:

                @pl.when(i + 1 < rounds)
                def _():
                    for copy in load(i + 1, 0):
                        copy.start()

            work(i, one_set)
        return carry

    lax.fori_loop(0, rounds, one_round, 0)
    start = 0
    for parcel_ref in parcel_refs:
        span = slice(start, start + parcel_ref.shape[0])
        parcel_ref[...] = parcel_rows.reshape(all_slots, width)[span, :].astype(jnp.bfloat16)
        start = span.stop


def prior_kernel(
    field_hbm, xlo_ref, xhi_ref, ylo_ref, yhi_ref, out_hbm,
    padded, smooth, out_ref, yends_ref, sems, out_sems,
):
    cells_x, cells_y, depth = field_hbm.shape
    rows = padded.shape[1]
    parts = sems.shape[0]
    planes = cells_x // parts
    own_rows = pl.ds(8, cells_y)
    loads = [
        pltpu.make_async_copy(
            field_hbm.at[pl.ds(i * planes, planes)],
            padded.at[pl.ds(2 + i * planes, planes), own_rows],
            sems.at[i],
        )
        for i in range(parts)
    ]
    for load in loads:
        load.start()
    gx, gy = lax.axis_index("gx"), lax.axis_index("gy")
    last_gx, last_gy = lax.axis_size("gx") - 1, lax.axis_size("gy") - 1
    z = lax.broadcasted_iota(jnp.int32, (rows, depth), 1)
    y = lax.broadcasted_iota(jnp.int32, (rows, depth), 0) - 8
    inside_y = ((y >= 0) | (gy > 0)) & ((y < cells_y) | (gy < last_gy))

    def operate(center, below, above):
        beside = below + above
        beside = beside + pltpu.roll(center, 1, 0) + pltpu.roll(center, rows - 1, 0)
        beside = beside + jnp.where(z == 0, 0.0, pltpu.roll(center, 1, 1))
        beside = beside + jnp.where(z == depth - 1, 0.0, pltpu.roll(center, depth - 1, 1))
        return (shift_kappa + 6.0) * center - beside

    for h in range(2):
        padded[h, own_rows, :] = xlo_ref[h].astype(jnp.float32)
        padded[cells_x + 2 + h, own_rows, :] = xhi_ref[h].astype(jnp.float32)

    yends_ref[0] = ylo_ref[...].astype(jnp.float32)
    yends_ref[1] = yhi_ref[...].astype(jnp.float32)

    def fill_ends(plane, carry):
        padded[plane, 0:8, :] = jnp.zeros((8, depth), jnp.float32)
        padded[plane, 8 + cells_y :, :] = jnp.zeros((8, depth), jnp.float32)
        for h in range(2):
            padded[plane, 6 + h : 7 + h, :] = yends_ref[0, h, pl.ds(plane, 1), :]
            padded[plane, 8 + cells_y + h : 9 + cells_y + h, :] = yends_ref[1, h, pl.ds(plane, 1), :]
        return carry

    lax.fori_loop(0, cells_x + 4, fill_ends, 0)

    def smooth_plane(plane, carry):
        value = operate(padded[plane], padded[plane - 1], padded[plane + 1])
        inside = ((plane > 1) | (gx > 0)) & ((plane < cells_x + 2) | (gx < last_gx))
        smooth[plane - 1] = jnp.where(inside_y & inside, value, 0.0)
        return carry

    def out_plane(x, carry):
        prior = operate(smooth[x + 1], smooth[x], smooth[x + 2])
        change = (step_rate * prior_weight) * prior[8 : 8 + cells_y]
        out_ref[x] = padded[x + 2, own_rows, :] - change
        return carry

    def store(part):
        span = pl.ds(part * planes, planes)
        return pltpu.make_async_copy(out_ref.at[span], out_hbm.at[span], out_sems.at[part])

    smoothed, done = 1, 0
    for part in range(parts):
        loads[part].wait()
        ready = cells_x + 3 if part + 1 == parts else 1 + (part + 1) * planes
        lax.fori_loop(smoothed, ready, smooth_plane, 0)
        smoothed = ready
        lax.fori_loop(done, ready - 3, out_plane, 0)
        done = ready - 3
        for whole in range(parts):
            if part * planes - 2 < (whole + 1) * planes <= done:
                store(whole).start()
    for part in range(parts):
        store(part).wait()


def finish_kernel(
    incoming_ref, match_hbm, field_hbm, base_hbm, *refs, exchanges, capacity, first_slots
):
    arrived_refs, refs = refs[:exchanges], refs[exchanges:]
    out_hbm, *collected, rows_ref, match_ref, field_ref, base_ref, out_ref, in_sems, out_sems = refs
    cells_x, cells_y, depth = field_ref.shape
    per_column = depth // LANES
    parts = out_sems.shape[0]
    planes = cells_x // parts
    blocks = cells_x * cells_y * per_column
    matches = copies_in_parts(match_hbm, match_ref, in_sems.at[2])
    loads = copies_in_parts(field_hbm, field_ref, in_sems.at[0])
    loads += copies_in_parts(base_hbm, base_ref, in_sems.at[1])
    for load in matches + loads:
        load.start()
    collected_rows = [ref.reshape(ref.shape[0], LANES) for ref in collected]
    for ref in collected_rows:
        ref[...] = jnp.zeros_like(ref)
    for load in matches:
        load.wait()
    merged = rows_ref.reshape(rows_ref.shape[0], LANES)
    start = 0
    for arrived_ref in arrived_refs:
        for i in range(arrived_ref.shape[0] // LANES):
            span = slice(start + i * LANES, start + (i + 1) * LANES)
            merged[span, :] = -step_rate * jnp.dot(
                match_ref[span, :],
                arrived_ref[i * LANES : (i + 1) * LANES, :],
                preferred_element_type=jnp.float32,
            )
        start += arrived_ref.shape[0]

    part_starts = [0, arrived_refs[0].shape[0]]

    def visit(wanted, row, list_part, which):
        row = pl.multiple_of(row + part_starts[list_part], GROUP)
        rows = rows_ref.at[pl.ds(row, GROUP)]
        into = collected[which % len(collected)]
        sums = [into[wanted[j]] + rows[j] for j in range(GROUP)]
        for j in range(GROUP):
            into[wanted[j]] = sums[j]

    for_each_group(incoming_ref, visit, capacity, first_slots, blocks)
    for load in loads:
        load.wait()

    def store(part):
        span = pl.ds(part * planes, planes)
        return pltpu.make_async_copy(out_ref.at[span], out_hbm.at[span], out_sems.at[part])

    def one_plane(x, carry):
        for yb in range(cells_y // 8):
            for part in range(per_column):
                at = pl.multiple_of(((x * (cells_y // 8) + yb) * per_column + part) * 8, 8)
                here = (x, slice(8 * yb, 8 * yb + 8), slice(part * LANES, (part + 1) * LANES))
                grad = collected_rows[0][pl.ds(at, 8), :] + collected_rows[1][pl.ds(at, 8), :]
                out_ref[here] = base_ref[here] + grad * jnp.exp(field_ref[here])
        return carry

    for part in range(parts):
        lax.fori_loop(part * planes, (part + 1) * planes, one_plane, 0)
        store(part).start()
    for part in range(parts):
        store(part).wait()


def both_ways(first, last, axis):
    peers = lax.axis_size(axis)
    up = [(i, i + 1) for i in range(peers - 1)]
    down = [(j, i) for i, j in up]
    return lax.ppermute(last, axis, up), lax.ppermute(first, axis, down)


VMEM = pl.BlockSpec(memory_space=pltpu.VMEM)
SMEM = pl.BlockSpec(memory_space=pltpu.SMEM)
ANY = pl.BlockSpec(memory_space=pl.ANY)


def on_device(log_density, weights, observed, inverse_var, star_counts, block_ids):
    cells_x, cells_y, depth = log_density.shape
    blocks_dev, slots, stars, width = weights.shape
    devices = lax.axis_size("gx") * lax.axis_size("gy")
    requests = blocks_dev * slots
    capacity = 2 * requests // devices
    first_slots = 11 * capacity // 16 if capacity % LANES == 0 else capacity
    slots_of = [n for n in (first_slots, capacity - first_slots) if n > 0]
    exchanges = len(slots_of)
    all_slots = devices * capacity
    per_column = depth // width
    blocks = cells_x * cells_y * per_column
    cells = log_density.size
    field_shape = (cells_x, cells_y, depth)
    mesh_axes = ("gx", "gy")
    f32, bf16, i32 = jnp.float32, jnp.bfloat16, jnp.int32
    shape = jax.ShapeDtypeStruct

    def exchange(x):
        return lax.all_to_all(x, mesh_axes, split_axis=0, concat_axis=0, tiled=True)

    def exchange_rows(parts, crowded):
        moved = [parts[0].reshape(devices, first_slots, width)]
        moved[0] = exchange(moved[0])
        for part in parts[1:]:
            part = part.reshape(devices, capacity - first_slots, width)
            moved.append(lax.cond(crowded, exchange, lambda x: x, part))
        return [x.reshape(-1, width) for x in moved]

    outgoing, position = pl.pallas_call(
        functools.partial(
            route_kernel,
            devices=devices,
            capacity=capacity,
            first_slots=first_slots,
            blocks=blocks,
            per_column=per_column,
        ),
        out_shape=[shape((devices, capacity), i32), shape((requests // LANES, LANES), i32)],
        in_specs=[VMEM],
        out_specs=[VMEM, VMEM],
        name="route",
    )(block_ids.T)
    incoming = exchange(outgoing)

    field, _ = lax.optimization_barrier((log_density, outgoing))
    table, xfirst, xlast, yfirst, ylast = pl.pallas_call(
        table_kernel,
        out_shape=[
            shape((blocks + capacity, width), bf16),
            shape((2, cells_y, depth), bf16),
            shape((2, cells_y, depth), bf16),
            shape((2, cells_x + 4, depth), f32),
            shape((2, cells_x + 4, depth), f32),
        ],
        in_specs=[VMEM],
        out_specs=[VMEM] * 5,
        compiler_params=pltpu.CompilerParams(vmem_limit_bytes=16 * MIB),
        cost_estimate=pl.CostEstimate(
            flops=8 * cells, bytes_accessed=8 * cells, transcendentals=cells
        ),
        name="table",
    )(field)
    incoming, *edges = lax.optimization_barrier((incoming, xfirst, xlast, yfirst, ylast))
    wanted = incoming.reshape(-1)

    *served, crowded = pl.pallas_call(
        functools.partial(
            serve_kernel, capacity=capacity, first_slots=first_slots, blocks=blocks
        ),
        out_shape=[shape((devices * n, width), bf16) for n in slots_of] + [shape((1,), i32)],
        in_specs=[SMEM, VMEM],
        out_specs=[VMEM] * exchanges + [SMEM],
        scratch_shapes=[
            pltpu.VMEM((blocks + capacity, 1, width), f32),
            pltpu.VMEM((all_slots, 1, width), f32),
        ],
        compiler_params=pltpu.CompilerParams(vmem_limit_bytes=24 * MIB),
        cost_estimate=pl.CostEstimate(
            flops=cells, bytes_accessed=6 * MIB, transcendentals=cells
        ),
        name="serve",
    )(wanted, table)
    crowded = crowded[0] != 0

    returned = exchange_rows(served, crowded)
    *edges, incoming_late, _ = lax.optimization_barrier((*edges, incoming, served[0]))
    xlo, xhi = both_ways(*edges[:2], "gx")
    slabs = pl.pallas_call(
        ends_kernel,
        out_shape=[shape((2, cells_x + 4, depth), bf16)] * 2,
        in_specs=[VMEM] * 4,
        out_specs=[VMEM] * 2,
        scratch_shapes=[pltpu.VMEM((2, cells_x + 4, depth), f32)],
        compiler_params=pltpu.CompilerParams(vmem_limit_bytes=8 * MIB),
        cost_estimate=pl.CostEstimate(flops=0, bytes_accessed=MIB, transcendentals=0),
        name="ends",
    )(xlo, xhi, *edges[2:])
    ylo, yhi = both_ways(*slabs, "gy")
    slot_lists = [
        incoming_late[:, :first_slots].reshape(-1, LANES),
        (incoming_late[:, first_slots:] & (MARK - 1)).reshape(-1, LANES),
    ][:exchanges]
    match = pl.pallas_call(
        match_kernel,
        out_shape=shape((all_slots, LANES), bf16),
        in_specs=[VMEM],
        out_specs=VMEM,
        compiler_params=pltpu.CompilerParams(vmem_limit_bytes=8 * MIB),
        cost_estimate=pl.CostEstimate(flops=10**9, bytes_accessed=MIB, transcendentals=0),
        name="match",
    )(jnp.concatenate(slot_lists, axis=0))
    *returned, match, ylo, yhi = lax.optimization_barrier((*returned, match, ylo, yhi))

    chunks = blocks_dev * stars // LANES
    in_set = chunks // 4
    live = jnp.arange(stars)[None, :] < star_counts[:, None]
    live_inverse = jnp.where(live, inverse_var, 0.0)
    extinction, *parcel = pl.pallas_call(
        functools.partial(star_kernel, exchanges=exchanges),
        out_shape=[shape((chunks, LANES), f32)]
        + [shape((devices * n, width), bf16) for n in slots_of],
        in_specs=[SMEM, VMEM, VMEM, ANY] + [VMEM] * exchanges,
        out_specs=[VMEM] * (1 + exchanges),
        scratch_shapes=[
            pltpu.VMEM((2, in_set, blocks_dev // chunks, slots, stars, width), bf16),
            pltpu.VMEM((all_slots + 8, width), f32),
            pltpu.VMEM((in_set * (blocks_dev // chunks) * slots, 1, width), f32),
            pltpu.VMEM((all_slots, 1, width), f32),
            pltpu.SemaphoreType.DMA((2, in_set)),
        ],
        compiler_params=pltpu.CompilerParams(vmem_limit_bytes=50 * MIB),
        cost_estimate=pl.CostEstimate(
            flops=4 * weights.size, bytes_accessed=2 * weights.size, transcendentals=0
        ),
        name="stars",
    )(
        position.reshape(slots // 2, 2, blocks_dev).transpose(2, 1, 0).reshape(requests),
        observed.reshape(chunks, LANES),
        live_inverse.reshape(chunks, LANES),
        weights,
        *returned,
    )
    arrived = exchange_rows(parcel, crowded)

    field_late, _ = lax.optimization_barrier((log_density, parcel[0]))
    parts = 8
    base = pl.pallas_call(
        prior_kernel,
        out_shape=shape(field_shape, f32),
        in_specs=[ANY] + [VMEM] * 4,
        out_specs=ANY,
        scratch_shapes=[
            pltpu.VMEM((cells_x + 4, cells_y + 16, depth), f32),
            pltpu.VMEM((cells_x + 2, cells_y + 16, depth), f32),
            pltpu.VMEM(field_shape, f32),
            pltpu.VMEM((2, 2, cells_x + 4, depth), f32),
            pltpu.SemaphoreType.DMA((parts,)),
            pltpu.SemaphoreType.DMA((parts,)),
        ],
        compiler_params=pltpu.CompilerParams(vmem_limit_bytes=56 * MIB),
        cost_estimate=pl.CostEstimate(
            flops=30 * cells, bytes_accessed=8 * cells, transcendentals=0
        ),
        name="prior",
    )(field_late, xlo, xhi, ylo, yhi)

    new_log_density = pl.pallas_call(
        functools.partial(
            finish_kernel, exchanges=exchanges, capacity=capacity, first_slots=first_slots
        ),
        out_shape=shape(field_shape, f32),
        in_specs=[SMEM, ANY, ANY, ANY] + [VMEM] * exchanges,
        out_specs=ANY,
        scratch_shapes=[
            pltpu.VMEM((blocks + capacity, 1, width), f32),
            pltpu.VMEM((blocks + capacity, 1, width), f32),
            pltpu.VMEM((all_slots, 1, width), f32),
            pltpu.VMEM((all_slots, LANES), bf16),
            pltpu.VMEM(field_shape, f32),
            pltpu.VMEM(field_shape, f32),
            pltpu.VMEM(field_shape, f32),
            pltpu.SemaphoreType.DMA((3, parts)),
            pltpu.SemaphoreType.DMA((parts,)),
        ],
        compiler_params=pltpu.CompilerParams(vmem_limit_bytes=50 * MIB),
        cost_estimate=pl.CostEstimate(
            flops=4 * cells, bytes_accessed=12 * cells, transcendentals=cells
        ),
        name="finish",
    )(wanted, match, log_density, base, *arrived)
    return new_log_density, extinction.reshape(blocks_dev, stars)


def solution(mesh):
    placed = (
        P("gx", "gy", None),
        P(("gx", "gy"), None, None, None),
        P(("gx", "gy"), None),
        P(("gx", "gy"), None),
        P(("gx", "gy")),
        P(("gx", "gy"), None),
    )
    return jax.shard_map(
        on_device,
        mesh=mesh,
        in_specs=placed,
        out_specs=(P("gx", "gy", None), P(("gx", "gy"), None)),
        check_vma=False,
    )
```

```python
import functools

import jax
import jax.numpy as jnp
from jax import lax
from jax.experimental import pallas as pl
from jax.experimental.pallas import tpu as pltpu
from jax.sharding import PartitionSpec as P

shift_kappa = 0.5
prior_weight = 0.05
step_rate = 2.0

LANES = 128
GROUP = 8
MIB = 1 << 20
MARK = 1 << 16

CONTRACT_LANES = (((1,), (1,)), ((), ()))


def split_by(value, size):
    if size & (size - 1) == 0:
        high = value >> (size.bit_length() - 1)
        return high, value & (size - 1)
    high = value // size
    return high, value - high * size


def route_kernel(
    ids_ref, outgoing_ref, position_ref, *, devices, capacity, first_slots, blocks, per_column
):
    half = ids_ref.shape[0] // 2
    ids = jnp.concatenate([ids_ref[:half, :], ids_ref[half:, :]], axis=1)
    target, local = split_by(ids, blocks)
    column, part = split_by(local, per_column)
    local = ((column >> 3) * per_column + part) * 8 + (column & 7)
    high = ((local >> 7) + 1).astype(jnp.float32)
    low = (local & 127).astype(jnp.float32)
    lane = lax.broadcasted_iota(jnp.int32, (LANES, LANES), 1)
    row = lax.broadcasted_iota(jnp.int32, (LANES, LANES), 0)
    upper = jnp.where(row <= lane, 1.0, 0.0)
    sums = jnp.concatenate([upper, jnp.ones_like(upper)], axis=1).astype(jnp.bfloat16)
    tile_no = lax.broadcasted_iota(jnp.int32, (devices, LANES), 0)
    slot_no = lax.broadcasted_iota(jnp.int32, (capacity, LANES), 0)
    hits = [tile_no == target[c : c + 1, :] for c in range(half)]
    onehots = [jnp.where(hit, 1.0, 0.0) for hit in hits]
    counts = jnp.dot(
        jnp.concatenate(onehots, axis=0).astype(jnp.bfloat16),
        sums,
        preferred_element_type=jnp.float32,
    )
    before = jnp.zeros((devices, LANES), jnp.float32)
    ranks, digits, in_slots = [], [], []
    for c in range(half):
        here = slice(c * devices, (c + 1) * devices)
        upto = before + counts[here, :LANES]
        before = before + counts[here, LANES:]
        rank = jnp.sum(onehots[c] * upto, axis=0, keepdims=True).astype(jnp.int32) - 1
        ranks.append(rank)
        in_slots.append(jnp.where(slot_no == rank, 1.0, 0.0))
        digits.append(
            jnp.concatenate(
                [jnp.where(hits[c], x[c : c + 1, :], 0.0) for x in (high, low)], axis=0
            )
        )
    lists = lax.dot_general(
        jnp.concatenate(digits, axis=1).astype(jnp.bfloat16),
        jnp.concatenate(in_slots, axis=1).astype(jnp.bfloat16),
        CONTRACT_LANES,
        preferred_element_type=jnp.float32,
    )
    rank = jnp.concatenate(ranks, axis=0)
    last_slots = capacity - first_slots
    position_ref[...] = jnp.where(
        rank < first_slots,
        target * first_slots + rank,
        devices * first_slots + target * last_slots + rank - first_slots,
    )
    before = before[:, :1]
    high, low = lists[:devices], lists[devices:]
    wanted = ((high - 1.0) * 128.0 + low).astype(jnp.int32)
    filled = before.astype(jnp.int32)
    me = lax.axis_index("gx") * lax.axis_size("gy") + lax.axis_index("gy")
    fullest = jnp.max(jnp.where(tile_no[:, :1] == me, 0.0, before), axis=0, keepdims=True)
    listed = jnp.where(high > 0.5, wanted, blocks + filled)
    if first_slots < capacity:
        slot = lax.broadcasted_iota(jnp.int32, (devices, capacity), 1)
        mark = fullest.astype(jnp.int32) * MARK
        listed = listed + jnp.where(slot == capacity - 1, mark, 0)
    outgoing_ref[...] = listed


def table_kernel(field_ref, table_ref, xfirst_ref, xlast_ref, yfirst_ref, ylast_ref):
    cells_x, cells_y, depth = field_ref.shape
    per_column = depth // LANES
    blocks = cells_x * cells_y * per_column
    xfirst_ref[...] = field_ref[:2].astype(xfirst_ref.dtype)
    xlast_ref[...] = field_ref[cells_x - 2 :].astype(xlast_ref.dtype)

    def one_plane(x, carry):
        for yb in range(cells_y // 8):
            for part in range(0, per_column, 2):
                at = pl.multiple_of(((x * (cells_y // 8) + yb) * per_column + part) * 8, 16)
                both = [
                    field_ref[x, 8 * yb : 8 * yb + 8, p * LANES : (p + 1) * LANES]
                    for p in (part, part + 1)
                ]
                rows = jnp.exp(jnp.concatenate(both, axis=0))
                table_ref[pl.ds(at, 16), :] = rows.astype(table_ref.dtype)
        for h in range(2):
            yfirst_ref[h, pl.ds(x + 2, 1), :] = field_ref[x, h : h + 1, :]
            ylast_ref[h, pl.ds(x + 2, 1), :] = field_ref[x, cells_y - 2 + h : cells_y - 1 + h, :]
        return carry

    lax.fori_loop(0, cells_x, one_plane, 0)
    pad = table_ref.shape[0] - blocks
    table_ref[blocks:, :] = jnp.zeros((pad, LANES), table_ref.dtype)


def ends_kernel(
    xlo_ref, xhi_ref, yfirst_ref, ylast_ref, first_ref, last_ref, slab_ref
):
    cells_y = xlo_ref.shape[1]
    length = yfirst_ref.shape[1]
    for own_ref, out_ref, start, row in (
        (yfirst_ref, first_ref, 0, 0),
        (ylast_ref, last_ref, cells_y - 16, 14),
    ):
        slab_ref[...] = own_ref[...]
        for e in range(2):
            for x_ref, at in ((xlo_ref, e), (xhi_ref, length - 2 + e)):
                block = x_ref[e, start : start + 16, :].astype(jnp.float32)
                for h in range(2):
                    slab_ref[h, at : at + 1, :] = block[row + h : row + h + 1, :]
        out_ref[...] = slab_ref[...].astype(out_ref.dtype)


def copies_in_parts(source, target, sems):
    parts = sems.shape[0]
    size = source.shape[0] // parts
    return [
        pltpu.make_async_copy(
            source.at[pl.ds(i * size, size)], target.at[pl.ds(i * size, size)], sems.at[i]
        )
        for i in range(parts)
    ]


def for_each_group(incoming_ref, visit, capacity, first_slots, blocks):
    sources = incoming_ref.shape[0] // capacity
    last_slots = capacity - first_slots
    together = 8

    def groups_of(source):
        last = incoming_ref[source * capacity + capacity - 1] & (MARK - 1)
        return (jnp.where(last < blocks, capacity, last - blocks) + GROUP - 1) // GROUP

    def some_sources(quad, carry):
        own = [quad * together + i for i in range(together)]
        most = functools.reduce(jnp.maximum, [groups_of(source) for source in own])

        def one_group(group, carry):
            slot = group * GROUP
            for which, source in enumerate(own):
                listed = incoming_ref.at[pl.ds(source * capacity + slot, GROUP)]
                wanted = [listed[j] for j in range(GROUP)]
                visit(wanted, pl.multiple_of(source * first_slots + slot, GROUP), 0, which)
            return carry

        return lax.fori_loop(0, jnp.minimum(most, first_slots // GROUP), one_group, carry)

    lax.fori_loop(0, sources // together, some_sources, 0)
    if last_slots == 0:
        return

    def one_source(source, carry):
        def one_group(group, carry):
            slot = group * GROUP
            listed = incoming_ref.at[pl.ds(source * capacity + slot, GROUP)]
            wanted = [listed[j] & (MARK - 1) for j in range(GROUP)]
            visit(wanted, pl.multiple_of(source * last_slots + slot - first_slots, GROUP), 1, 0)
            return carry

        return lax.fori_loop(first_slots // GROUP, groups_of(source), one_group, carry)

    lax.fori_loop(0, sources, one_source, 0)


def serve_kernel(incoming_ref, table_ref, *refs, capacity, first_slots, blocks):
    *served_refs, crowded_ref, rows_ref, found_ref = refs

    def mark_of(source, most):
        return jnp.maximum(most, incoming_ref[source * capacity + capacity - 1] >> 16)

    fullest = lax.fori_loop(0, incoming_ref.shape[0] // capacity, mark_of, jnp.int32(0))
    crowded_ref[0] = jnp.where(fullest > first_slots, 1, 0)
    rows_ref.reshape(rows_ref.shape[0], LANES)[...] = table_ref[...].astype(jnp.float32)
    part_starts = [0, served_refs[0].shape[0]]

    def visit(wanted, row, list_part, which):
        rows = [rows_ref[at] for at in wanted]
        found = found_ref.at[pl.ds(row + part_starts[list_part], GROUP)]
        for j in range(GROUP):
            found[j] = rows[j]

    for_each_group(incoming_ref, visit, capacity, first_slots, blocks)
    found = found_ref.reshape(found_ref.shape[0], LANES)
    for start, served_ref in zip(part_starts, served_refs):
        span = slice(start, start + served_ref.shape[0])
        served_ref[...] = found[span, :].astype(jnp.bfloat16)


def match_kernel(incoming_ref, match_ref):
    lane = lax.broadcasted_iota(jnp.int32, (LANES, LANES), 1)
    row = lax.broadcasted_iota(jnp.int32, (LANES, LANES), 0)
    ones = jnp.ones((LANES, LANES), jnp.bfloat16)
    same_group = (lane // GROUP) == (row // GROUP)

    def one_row(i):
        wanted = incoming_ref[pl.ds(i, 1), :]
        high = jnp.where(lane == row, (wanted >> 7).astype(jnp.float32), 0.0).astype(jnp.bfloat16)
        low = jnp.where(lane == row, (wanted & 127).astype(jnp.float32), 0.0).astype(jnp.bfloat16)
        down = 128.0 * jnp.dot(high, ones, preferred_element_type=jnp.float32)
        down = down + jnp.dot(low, ones, preferred_element_type=jnp.float32)
        same = (down == wanted.astype(jnp.float32)) & same_group
        match_ref[pl.ds(pl.multiple_of(i * LANES, LANES), LANES), :] = jnp.where(
            same, 1.0, 0.0
        ).astype(jnp.bfloat16)

    def some_rows(i, carry):
        for j in range(4):
            one_row(4 * i + j)
        return carry

    lax.fori_loop(0, incoming_ref.shape[0] // 4, some_rows, 0)


def star_kernel(position_ref, observed_ref, inverse_ref, weights_hbm, *refs, exchanges):
    returned_refs, refs = refs[:exchanges], refs[exchanges:]
    extinction_ref, refs = refs[0], refs[1:]
    parcel_refs, refs = refs[:exchanges], refs[exchanges:]
    weights_ref, returned_rows, sens_ref, parcel_rows, sems = refs
    chunks, per, slots, stars, width = weights_ref.shape
    quarter = chunks // 4
    bounds = [0, quarter // 2, quarter, 2 * quarter, 3 * quarter, chunks]
    per_chunk = per * slots
    held = sens_ref.shape[0] // per_chunk
    fold = LANES // stars
    all_slots = parcel_rows.shape[0]
    sens_blocks = sens_ref.reshape(sens_ref.shape[0], width)
    lane = lax.broadcasted_iota(jnp.int32, (8, LANES), 1)
    row = lax.broadcasted_iota(jnp.int32, (8, LANES), 0)
    star_group = lane // stars
    own_slot = [row == star_group + fold * h for h in range(8 // fold)]

    loads = [
        [
            pltpu.make_async_copy(
                weights_hbm.at[pl.ds(c * per, per)], weights_ref.at[c], sems.at[c]
            )
            for c in range(first, last)
        ]
        for first, last in zip(bounds[:-1], bounds[1:])
    ]

    def extinctions(chunk):
        sums = []
        for b in range(per):
            total = jnp.zeros((stars // 8, 8, width), jnp.float32)
            for k in range(slots):
                at = position_ref[chunk * per_chunk + b * slots + k]
                fetched = returned_rows[pl.ds(at, 8, stride=0), :]
                block = weights_ref[chunk, b, k].astype(jnp.float32)
                total = total + block.reshape(stars // 8, 8, width) * fetched
            sums.append(total.reshape(stars, width))
        extinction = lax.dot_general(
            jnp.ones((8, width), jnp.float32),
            jnp.concatenate(sums, axis=0),
            CONTRACT_LANES,
            precision=lax.Precision.HIGHEST,
            preferred_element_type=jnp.float32,
        )
        here = slice(chunk, chunk + 1)
        extinction_ref[here, :] = extinction[:1]
        return inverse_ref[here, :] * (extinction - observed_ref[here, :])

    def sensitivities(chunk, weighted):
        for b in range(per):
            spread = jnp.where(star_group == b, weighted, 0.0)
            shift = stars
            while shift < LANES:
                spread = spread + pltpu.roll(spread, shift, 1)
                shift *= 2
            left = jnp.concatenate(
                [jnp.where(own, spread, 0.0) for own in own_slot], axis=1
            ).astype(jnp.bfloat16)
            eights = [weights_ref[chunk, b, 8 * j : 8 * j + 8] for j in range(slots // 8)]
            right = jnp.concatenate([x.reshape(8 * stars, width) for x in eights], axis=1)
            sens = jnp.dot(left, right, preferred_element_type=jnp.float32)
            for j in range(slots // 8):
                first = chunk % held * per_chunk + b * slots + 8 * j
                sens_blocks[first : first + 8, :] = sens[:, j * width : (j + 1) * width]

    def scatter(chunk):
        for i in range(per_chunk):
            at = position_ref[chunk * per_chunk + i]
            parcel_rows[at] = sens_ref[chunk % held * per_chunk + i]

    for one_set in loads[:2]:
        for copy in one_set:
            copy.start()
    start = 0
    for returned_ref in returned_refs:
        span = slice(start, start + returned_ref.shape[0])
        returned_rows[span, :] = returned_ref[...].astype(jnp.float32)
        start = span.stop
    parcel_rows.reshape(all_slots, width)[...] = jnp.zeros((all_slots, width), jnp.float32)

    weighted = {}
    for chunk in range(chunks + 2):
        if chunk in bounds[:-1]:
            which = bounds.index(chunk)
            for copy in loads[which]:
                copy.wait()
            for copy in loads[which + 2] if which + 2 < len(loads) else []:
                copy.start()
        if chunk < chunks:
            weighted[chunk] = extinctions(chunk)
        if 1 <= chunk <= chunks:
            sensitivities(chunk - 1, weighted[chunk - 1])
        if chunk >= 2:
            scatter(chunk - 2)
    start = 0
    for parcel_ref in parcel_refs:
        span = slice(start, start + parcel_ref.shape[0])
        parcel_ref[...] = parcel_rows.reshape(all_slots, width)[span, :].astype(jnp.bfloat16)
        start = span.stop


def prior_kernel(
    field_hbm, xlo_ref, xhi_ref, ylo_ref, yhi_ref, out_hbm,
    padded, smooth, out_ref, yends_ref, sems, out_sems,
):
    cells_x, cells_y, depth = field_hbm.shape
    rows = padded.shape[1]
    parts = sems.shape[0]
    planes = cells_x // parts
    own_rows = pl.ds(8, cells_y)
    loads = [
        pltpu.make_async_copy(
            field_hbm.at[pl.ds(i * planes, planes)],
            padded.at[pl.ds(2 + i * planes, planes), own_rows],
            sems.at[i],
        )
        for i in range(parts)
    ]
    for load in loads:
        load.start()
    gx, gy = lax.axis_index("gx"), lax.axis_index("gy")
    last_gx, last_gy = lax.axis_size("gx") - 1, lax.axis_size("gy") - 1
    z = lax.broadcasted_iota(jnp.int32, (rows, depth), 1)
    y = lax.broadcasted_iota(jnp.int32, (rows, depth), 0) - 8
    inside_y = ((y >= 0) | (gy > 0)) & ((y < cells_y) | (gy < last_gy))

    def operate(center, below, above):
        beside = below + above
        beside = beside + pltpu.roll(center, 1, 0) + pltpu.roll(center, rows - 1, 0)
        beside = beside + jnp.where(z == 0, 0.0, pltpu.roll(center, 1, 1))
        beside = beside + jnp.where(z == depth - 1, 0.0, pltpu.roll(center, depth - 1, 1))
        return (shift_kappa + 6.0) * center - beside

    for h in range(2):
        padded[h, own_rows, :] = xlo_ref[h].astype(jnp.float32)
        padded[cells_x + 2 + h, own_rows, :] = xhi_ref[h].astype(jnp.float32)

    yends_ref[0] = ylo_ref[...].astype(jnp.float32)
    yends_ref[1] = yhi_ref[...].astype(jnp.float32)

    def fill_ends(plane, carry):
        padded[plane, 0:8, :] = jnp.zeros((8, depth), jnp.float32)
        padded[plane, 8 + cells_y :, :] = jnp.zeros((8, depth), jnp.float32)
        for h in range(2):
            padded[plane, 6 + h : 7 + h, :] = yends_ref[0, h, pl.ds(plane, 1), :]
            padded[plane, 8 + cells_y + h : 9 + cells_y + h, :] = yends_ref[1, h, pl.ds(plane, 1), :]
        return carry

    lax.fori_loop(0, cells_x + 4, fill_ends, 0)

    def smooth_plane(plane, carry):
        value = operate(padded[plane], padded[plane - 1], padded[plane + 1])
        inside = ((plane > 1) | (gx > 0)) & ((plane < cells_x + 2) | (gx < last_gx))
        smooth[plane - 1] = jnp.where(inside_y & inside, value, 0.0)
        return carry

    def out_plane(x, carry):
        prior = operate(smooth[x + 1], smooth[x], smooth[x + 2])
        change = (step_rate * prior_weight) * prior[8 : 8 + cells_y]
        out_ref[x] = padded[x + 2, own_rows, :] - change
        return carry

    def store(part):
        span = pl.ds(part * planes, planes)
        return pltpu.make_async_copy(out_ref.at[span], out_hbm.at[span], out_sems.at[part])

    smoothed, done = 1, 0
    for part in range(parts):
        loads[part].wait()
        ready = cells_x + 3 if part + 1 == parts else 1 + (part + 1) * planes
        lax.fori_loop(smoothed, ready, smooth_plane, 0)
        smoothed = ready
        lax.fori_loop(done, ready - 3, out_plane, 0)
        done = ready - 3
        for whole in range(parts):
            if part * planes - 2 < (whole + 1) * planes <= done:
                store(whole).start()
    for part in range(parts):
        store(part).wait()


def finish_kernel(
    incoming_ref, match_hbm, field_hbm, base_hbm, *refs, exchanges, capacity, first_slots
):
    arrived_refs, refs = refs[:exchanges], refs[exchanges:]
    out_hbm, *collected, rows_ref, match_ref, field_ref, base_ref, out_ref, in_sems, out_sems = refs
    cells_x, cells_y, depth = field_ref.shape
    per_column = depth // LANES
    parts = out_sems.shape[0]
    planes = cells_x // parts
    blocks = cells_x * cells_y * per_column
    matches = copies_in_parts(match_hbm, match_ref, in_sems.at[2])
    loads = copies_in_parts(field_hbm, field_ref, in_sems.at[0])
    loads += copies_in_parts(base_hbm, base_ref, in_sems.at[1])
    for load in matches + loads:
        load.start()
    collected_rows = [ref.reshape(ref.shape[0], LANES) for ref in collected]
    for ref in collected_rows:
        ref[...] = jnp.zeros_like(ref)
    for load in matches:
        load.wait()
    merged = rows_ref.reshape(rows_ref.shape[0], LANES)
    start = 0
    for arrived_ref in arrived_refs:
        for i in range(arrived_ref.shape[0] // LANES):
            span = slice(start + i * LANES, start + (i + 1) * LANES)
            merged[span, :] = -step_rate * jnp.dot(
                match_ref[span, :],
                arrived_ref[i * LANES : (i + 1) * LANES, :],
                preferred_element_type=jnp.float32,
            )
        start += arrived_ref.shape[0]

    part_starts = [0, arrived_refs[0].shape[0]]

    def visit(wanted, row, list_part, which):
        row = pl.multiple_of(row + part_starts[list_part], GROUP)
        rows = rows_ref.at[pl.ds(row, GROUP)]
        into = collected[which % len(collected)]
        sums = [into[wanted[j]] + rows[j] for j in range(GROUP)]
        for j in range(GROUP):
            into[wanted[j]] = sums[j]

    for_each_group(incoming_ref, visit, capacity, first_slots, blocks)
    for load in loads:
        load.wait()

    def store(part):
        span = pl.ds(part * planes, planes)
        return pltpu.make_async_copy(out_ref.at[span], out_hbm.at[span], out_sems.at[part])

    def one_plane(x, carry):
        for yb in range(cells_y // 8):
            for part in range(per_column):
                at = pl.multiple_of(((x * (cells_y // 8) + yb) * per_column + part) * 8, 8)
                here = (x, slice(8 * yb, 8 * yb + 8), slice(part * LANES, (part + 1) * LANES))
                grad = collected_rows[0][pl.ds(at, 8), :] + collected_rows[1][pl.ds(at, 8), :]
                out_ref[here] = base_ref[here] + grad * jnp.exp(field_ref[here])
        return carry

    for part in range(parts):
        lax.fori_loop(part * planes, (part + 1) * planes, one_plane, 0)
        store(part).start()
    for part in range(parts):
        store(part).wait()


def both_ways(first, last, axis):
    peers = lax.axis_size(axis)
    up = [(i, i + 1) for i in range(peers - 1)]
    down = [(j, i) for i, j in up]
    return lax.ppermute(last, axis, up), lax.ppermute(first, axis, down)


VMEM = pl.BlockSpec(memory_space=pltpu.VMEM)
SMEM = pl.BlockSpec(memory_space=pltpu.SMEM)
ANY = pl.BlockSpec(memory_space=pl.ANY)


def on_device(log_density, weights, observed, inverse_var, star_counts, block_ids):
    cells_x, cells_y, depth = log_density.shape
    blocks_dev, slots, stars, width = weights.shape
    devices = lax.axis_size("gx") * lax.axis_size("gy")
    requests = blocks_dev * slots
    capacity = 2 * requests // devices
    first_slots = 11 * capacity // 16 if capacity % LANES == 0 else capacity
    slots_of = [n for n in (first_slots, capacity - first_slots) if n > 0]
    exchanges = len(slots_of)
    all_slots = devices * capacity
    per_column = depth // width
    blocks = cells_x * cells_y * per_column
    cells = log_density.size
    field_shape = (cells_x, cells_y, depth)
    mesh_axes = ("gx", "gy")
    f32, bf16, i32 = jnp.float32, jnp.bfloat16, jnp.int32
    shape = jax.ShapeDtypeStruct

    def exchange(x):
        return lax.all_to_all(x, mesh_axes, split_axis=0, concat_axis=0, tiled=True)

    def exchange_rows(parts, crowded):
        moved = [parts[0].reshape(devices, first_slots, width)]
        moved[0] = exchange(moved[0])
        for part in parts[1:]:
            part = part.reshape(devices, capacity - first_slots, width)
            moved.append(lax.cond(crowded, exchange, lambda x: x, part))
        return [x.reshape(-1, width) for x in moved]

    outgoing, position = pl.pallas_call(
        functools.partial(
            route_kernel,
            devices=devices,
            capacity=capacity,
            first_slots=first_slots,
            blocks=blocks,
            per_column=per_column,
        ),
        out_shape=[shape((devices, capacity), i32), shape((requests // LANES, LANES), i32)],
        in_specs=[VMEM],
        out_specs=[VMEM, VMEM],
        name="route",
    )(block_ids.T)
    incoming = exchange(outgoing)

    field, _ = lax.optimization_barrier((log_density, outgoing))
    table, xfirst, xlast, yfirst, ylast = pl.pallas_call(
        table_kernel,
        out_shape=[
            shape((blocks + capacity, width), bf16),
            shape((2, cells_y, depth), bf16),
            shape((2, cells_y, depth), bf16),
            shape((2, cells_x + 4, depth), f32),
            shape((2, cells_x + 4, depth), f32),
        ],
        in_specs=[VMEM],
        out_specs=[VMEM] * 5,
        compiler_params=pltpu.CompilerParams(vmem_limit_bytes=16 * MIB),
        cost_estimate=pl.CostEstimate(
            flops=8 * cells, bytes_accessed=8 * cells, transcendentals=cells
        ),
        name="table",
    )(field)
    incoming, *edges = lax.optimization_barrier((incoming, xfirst, xlast, yfirst, ylast))
    wanted = incoming.reshape(-1)

    *served, crowded = pl.pallas_call(
        functools.partial(
            serve_kernel, capacity=capacity, first_slots=first_slots, blocks=blocks
        ),
        out_shape=[shape((devices * n, width), bf16) for n in slots_of] + [shape((1,), i32)],
        in_specs=[SMEM, VMEM],
        out_specs=[VMEM] * exchanges + [SMEM],
        scratch_shapes=[
            pltpu.VMEM((blocks + capacity, 1, width), f32),
            pltpu.VMEM((all_slots, 1, width), f32),
        ],
        compiler_params=pltpu.CompilerParams(vmem_limit_bytes=24 * MIB),
        cost_estimate=pl.CostEstimate(
            flops=cells, bytes_accessed=6 * MIB, transcendentals=cells
        ),
        name="serve",
    )(wanted, table)
    crowded = crowded[0] != 0

    returned = exchange_rows(served, crowded)
    *edges, incoming_late, _ = lax.optimization_barrier((*edges, incoming, served[0]))
    xlo, xhi = both_ways(*edges[:2], "gx")
    slabs = pl.pallas_call(
        ends_kernel,
        out_shape=[shape((2, cells_x + 4, depth), bf16)] * 2,
        in_specs=[VMEM] * 4,
        out_specs=[VMEM] * 2,
        scratch_shapes=[pltpu.VMEM((2, cells_x + 4, depth), f32)],
        compiler_params=pltpu.CompilerParams(vmem_limit_bytes=8 * MIB),
        cost_estimate=pl.CostEstimate(flops=0, bytes_accessed=MIB, transcendentals=0),
        name="ends",
    )(xlo, xhi, *edges[2:])
    ylo, yhi = both_ways(*slabs, "gy")
    slot_lists = [
        incoming_late[:, :first_slots].reshape(-1, LANES),
        (incoming_late[:, first_slots:] & (MARK - 1)).reshape(-1, LANES),
    ][:exchanges]
    match = pl.pallas_call(
        match_kernel,
        out_shape=shape((all_slots, LANES), bf16),
        in_specs=[VMEM],
        out_specs=VMEM,
        compiler_params=pltpu.CompilerParams(vmem_limit_bytes=8 * MIB),
        cost_estimate=pl.CostEstimate(flops=10**9, bytes_accessed=MIB, transcendentals=0),
        name="match",
    )(jnp.concatenate(slot_lists, axis=0))
    *returned, match, ylo, yhi = lax.optimization_barrier((*returned, match, ylo, yhi))

    chunks = blocks_dev * stars // LANES
    live = jnp.arange(stars)[None, :] < star_counts[:, None]
    live_inverse = jnp.where(live, inverse_var, 0.0)
    extinction, *parcel = pl.pallas_call(
        functools.partial(star_kernel, exchanges=exchanges),
        out_shape=[shape((chunks, LANES), f32)]
        + [shape((devices * n, width), bf16) for n in slots_of],
        in_specs=[SMEM, VMEM, VMEM, ANY] + [VMEM] * exchanges,
        out_specs=[VMEM] * (1 + exchanges),
        scratch_shapes=[
            pltpu.VMEM((chunks, blocks_dev // chunks, slots, stars, width), bf16),
            pltpu.VMEM((all_slots + 8, width), f32),
            pltpu.VMEM((4 * (blocks_dev // chunks) * slots, 1, width), f32),
            pltpu.VMEM((all_slots, 1, width), f32),
            pltpu.SemaphoreType.DMA((chunks,)),
        ],
        compiler_params=pltpu.CompilerParams(vmem_limit_bytes=50 * MIB),
        cost_estimate=pl.CostEstimate(
            flops=4 * weights.size, bytes_accessed=2 * weights.size, transcendentals=0
        ),
        name="stars",
    )(
        position.reshape(slots // 2, 2, blocks_dev).transpose(2, 1, 0).reshape(requests),
        observed.reshape(chunks, LANES),
        live_inverse.reshape(chunks, LANES),
        weights,
        *returned,
    )
    arrived = exchange_rows(parcel, crowded)

    field_late, _ = lax.optimization_barrier((log_density, parcel[0]))
    parts = 8
    base = pl.pallas_call(
        prior_kernel,
        out_shape=shape(field_shape, f32),
        in_specs=[ANY] + [VMEM] * 4,
        out_specs=ANY,
        scratch_shapes=[
            pltpu.VMEM((cells_x + 4, cells_y + 16, depth), f32),
            pltpu.VMEM((cells_x + 2, cells_y + 16, depth), f32),
            pltpu.VMEM(field_shape, f32),
            pltpu.VMEM((2, 2, cells_x + 4, depth), f32),
            pltpu.SemaphoreType.DMA((parts,)),
            pltpu.SemaphoreType.DMA((parts,)),
        ],
        compiler_params=pltpu.CompilerParams(vmem_limit_bytes=56 * MIB),
        cost_estimate=pl.CostEstimate(
            flops=30 * cells, bytes_accessed=8 * cells, transcendentals=0
        ),
        name="prior",
    )(field_late, xlo, xhi, ylo, yhi)

    new_log_density = pl.pallas_call(
        functools.partial(
            finish_kernel, exchanges=exchanges, capacity=capacity, first_slots=first_slots
        ),
        out_shape=shape(field_shape, f32),
        in_specs=[SMEM, ANY, ANY, ANY] + [VMEM] * exchanges,
        out_specs=ANY,
        scratch_shapes=[
            pltpu.VMEM((blocks + capacity, 1, width), f32),
            pltpu.VMEM((blocks + capacity, 1, width), f32),
            pltpu.VMEM((all_slots, 1, width), f32),
            pltpu.VMEM((all_slots, LANES), bf16),
            pltpu.VMEM(field_shape, f32),
            pltpu.VMEM(field_shape, f32),
            pltpu.VMEM(field_shape, f32),
            pltpu.SemaphoreType.DMA((3, parts)),
            pltpu.SemaphoreType.DMA((parts,)),
        ],
        compiler_params=pltpu.CompilerParams(vmem_limit_bytes=50 * MIB),
        cost_estimate=pl.CostEstimate(
            flops=4 * cells, bytes_accessed=12 * cells, transcendentals=cells
        ),
        name="finish",
    )(wanted, match, log_density, base, *arrived)
    return new_log_density, extinction.reshape(blocks_dev, stars)


def solution(mesh):
    placed = (
        P("gx", "gy", None),
        P(("gx", "gy"), None, None, None),
        P(("gx", "gy"), None),
        P(("gx", "gy"), None),
        P(("gx", "gy")),
        P(("gx", "gy"), None),
    )
    return jax.shard_map(
        on_device,
        mesh=mesh,
        in_specs=placed,
        out_specs=(P("gx", "gy", None), P(("gx", "gy"), None)),
        check_vma=False,
    )
```

```python
import functools

import jax
import jax.numpy as jnp
from jax import lax
from jax.experimental import pallas as pl
from jax.experimental.pallas import tpu as pltpu
from jax.sharding import PartitionSpec as P

shift_kappa = 0.5
prior_weight = 0.05
step_rate = 2.0

LANES = 128
GROUP = 8
MIB = 1 << 20
MARK = 1 << 16

CONTRACT_LANES = (((1,), (1,)), ((), ()))


def split_by(value, size):
    if size & (size - 1) == 0:
        high = value >> (size.bit_length() - 1)
        return high, value & (size - 1)
    high = value // size
    return high, value - high * size


def route_kernel(
    ids_ref, outgoing_ref, position_ref, *, devices, capacity, first_slots, blocks, per_column
):
    half = ids_ref.shape[0] // 2
    ids = jnp.concatenate([ids_ref[:half, :], ids_ref[half:, :]], axis=1)
    target, local = split_by(ids, blocks)
    column, part = split_by(local, per_column)
    local = ((column >> 3) * per_column + part) * 8 + (column & 7)
    high = ((local >> 7) + 1).astype(jnp.float32)
    low = (local & 127).astype(jnp.float32)
    lane = lax.broadcasted_iota(jnp.int32, (LANES, LANES), 1)
    row = lax.broadcasted_iota(jnp.int32, (LANES, LANES), 0)
    upper = jnp.where(row <= lane, 1.0, 0.0)
    sums = jnp.concatenate([upper, jnp.ones_like(upper)], axis=1).astype(jnp.bfloat16)
    tile_no = lax.broadcasted_iota(jnp.int32, (devices, LANES), 0)
    slot_no = lax.broadcasted_iota(jnp.int32, (capacity, LANES), 0)
    hits = [tile_no == target[c : c + 1, :] for c in range(half)]
    onehots = [jnp.where(hit, 1.0, 0.0) for hit in hits]
    counts = jnp.dot(
        jnp.concatenate(onehots, axis=0).astype(jnp.bfloat16),
        sums,
        preferred_element_type=jnp.float32,
    )
    before = jnp.zeros((devices, LANES), jnp.float32)
    ranks, digits, in_slots = [], [], []
    for c in range(half):
        here = slice(c * devices, (c + 1) * devices)
        upto = before + counts[here, :LANES]
        before = before + counts[here, LANES:]
        rank = jnp.sum(onehots[c] * upto, axis=0, keepdims=True).astype(jnp.int32) - 1
        ranks.append(rank)
        in_slots.append(jnp.where(slot_no == rank, 1.0, 0.0))
        digits.append(
            jnp.concatenate(
                [jnp.where(hits[c], x[c : c + 1, :], 0.0) for x in (high, low)], axis=0
            )
        )
    lists = lax.dot_general(
        jnp.concatenate(digits, axis=1).astype(jnp.bfloat16),
        jnp.concatenate(in_slots, axis=1).astype(jnp.bfloat16),
        CONTRACT_LANES,
        preferred_element_type=jnp.float32,
    )
    rank = jnp.concatenate(ranks, axis=0)
    last_slots = capacity - first_slots
    position_ref[...] = jnp.where(
        rank < first_slots,
        target * first_slots + rank,
        devices * first_slots + target * last_slots + rank - first_slots,
    )
    before = before[:, :1]
    high, low = lists[:devices], lists[devices:]
    wanted = ((high - 1.0) * 128.0 + low).astype(jnp.int32)
    filled = before.astype(jnp.int32)
    me = lax.axis_index("gx") * lax.axis_size("gy") + lax.axis_index("gy")
    fullest = jnp.max(jnp.where(tile_no[:, :1] == me, 0.0, before), axis=0, keepdims=True)
    listed = jnp.where(high > 0.5, wanted, blocks + filled)
    if first_slots < capacity:
        slot = lax.broadcasted_iota(jnp.int32, (devices, capacity), 1)
        mark = fullest.astype(jnp.int32) * MARK
        listed = listed + jnp.where(slot == capacity - 1, mark, 0)
    outgoing_ref[...] = listed


def table_kernel(field_ref, table_ref, xfirst_ref, xlast_ref, yfirst_ref, ylast_ref):
    cells_x, cells_y, depth = field_ref.shape
    per_column = depth // LANES
    blocks = cells_x * cells_y * per_column
    xfirst_ref[...] = field_ref[:2].astype(xfirst_ref.dtype)
    xlast_ref[...] = field_ref[cells_x - 2 :].astype(xlast_ref.dtype)

    def one_plane(x, carry):
        for yb in range(cells_y // 8):
            for part in range(0, per_column, 2):
                at = pl.multiple_of(((x * (cells_y // 8) + yb) * per_column + part) * 8, 16)
                both = [
                    field_ref[x, 8 * yb : 8 * yb + 8, p * LANES : (p + 1) * LANES]
                    for p in (part, part + 1)
                ]
                rows = jnp.exp(jnp.concatenate(both, axis=0))
                table_ref[pl.ds(at, 16), :] = rows.astype(table_ref.dtype)
        for h in range(2):
            yfirst_ref[h, pl.ds(x + 2, 1), :] = field_ref[x, h : h + 1, :]
            ylast_ref[h, pl.ds(x + 2, 1), :] = field_ref[x, cells_y - 2 + h : cells_y - 1 + h, :]
        return carry

    lax.fori_loop(0, cells_x, one_plane, 0)
    pad = table_ref.shape[0] - blocks
    table_ref[blocks:, :] = jnp.zeros((pad, LANES), table_ref.dtype)


def ends_kernel(
    xlo_ref, xhi_ref, yfirst_ref, ylast_ref, first_ref, last_ref, slab_ref
):
    cells_y = xlo_ref.shape[1]
    length = yfirst_ref.shape[1]
    for own_ref, out_ref, start, row in (
        (yfirst_ref, first_ref, 0, 0),
        (ylast_ref, last_ref, cells_y - 16, 14),
    ):
        slab_ref[...] = own_ref[...]
        for e in range(2):
            for x_ref, at in ((xlo_ref, e), (xhi_ref, length - 2 + e)):
                block = x_ref[e, start : start + 16, :].astype(jnp.float32)
                for h in range(2):
                    slab_ref[h, at : at + 1, :] = block[row + h : row + h + 1, :]
        out_ref[...] = slab_ref[...].astype(out_ref.dtype)


def copies_in_parts(source, target, sems):
    parts = sems.shape[0]
    size = source.shape[0] // parts
    return [
        pltpu.make_async_copy(
            source.at[pl.ds(i * size, size)], target.at[pl.ds(i * size, size)], sems.at[i]
        )
        for i in range(parts)
    ]


def for_each_group(incoming_ref, visit, capacity, first_slots, blocks):
    sources = incoming_ref.shape[0] // capacity
    last_slots = capacity - first_slots
    together = 8

    def groups_of(source):
        last = incoming_ref[source * capacity + capacity - 1] & (MARK - 1)
        return (jnp.where(last < blocks, capacity, last - blocks) + GROUP - 1) // GROUP

    def some_sources(quad, carry):
        own = [quad * together + i for i in range(together)]
        most = functools.reduce(jnp.maximum, [groups_of(source) for source in own])

        def one_group(group, carry):
            slot = group * GROUP
            for which, source in enumerate(own):
                listed = incoming_ref.at[pl.ds(source * capacity + slot, GROUP)]
                wanted = [listed[j] for j in range(GROUP)]
                visit(wanted, pl.multiple_of(source * first_slots + slot, GROUP), 0, which)
            return carry

        return lax.fori_loop(0, jnp.minimum(most, first_slots // GROUP), one_group, carry)

    lax.fori_loop(0, sources // together, some_sources, 0)
    if last_slots == 0:
        return

    def one_source(source, carry):
        def one_group(group, carry):
            slot = group * GROUP
            listed = incoming_ref.at[pl.ds(source * capacity + slot, GROUP)]
            wanted = [listed[j] & (MARK - 1) for j in range(GROUP)]
            visit(wanted, pl.multiple_of(source * last_slots + slot - first_slots, GROUP), 1, 0)
            return carry

        return lax.fori_loop(first_slots // GROUP, groups_of(source), one_group, carry)

    lax.fori_loop(0, sources, one_source, 0)


def serve_kernel(incoming_ref, table_ref, *refs, capacity, first_slots, blocks):
    *served_refs, crowded_ref, rows_ref, found_ref = refs

    def mark_of(source, most):
        return jnp.maximum(most, incoming_ref[source * capacity + capacity - 1] >> 16)

    fullest = lax.fori_loop(0, incoming_ref.shape[0] // capacity, mark_of, jnp.int32(0))
    crowded_ref[0] = jnp.where(fullest > first_slots, 1, 0)
    rows_ref.reshape(rows_ref.shape[0], LANES)[...] = table_ref[...].astype(jnp.float32)
    part_starts = [0, served_refs[0].shape[0]]

    def visit(wanted, row, list_part, which):
        rows = [rows_ref[at] for at in wanted]
        found = found_ref.at[pl.ds(row + part_starts[list_part], GROUP)]
        for j in range(GROUP):
            found[j] = rows[j]

    for_each_group(incoming_ref, visit, capacity, first_slots, blocks)
    found = found_ref.reshape(found_ref.shape[0], LANES)
    for start, served_ref in zip(part_starts, served_refs):
        span = slice(start, start + served_ref.shape[0])
        served_ref[...] = found[span, :].astype(jnp.bfloat16)


def match_kernel(incoming_ref, match_ref):
    lane = lax.broadcasted_iota(jnp.int32, (LANES, LANES), 1)
    row = lax.broadcasted_iota(jnp.int32, (LANES, LANES), 0)
    ones = jnp.ones((LANES, LANES), jnp.bfloat16)
    same_group = (lane // GROUP) == (row // GROUP)

    def one_row(i):
        wanted = incoming_ref[pl.ds(i, 1), :]
        high = jnp.where(lane == row, (wanted >> 7).astype(jnp.float32), 0.0).astype(jnp.bfloat16)
        low = jnp.where(lane == row, (wanted & 127).astype(jnp.float32), 0.0).astype(jnp.bfloat16)
        down = 128.0 * jnp.dot(high, ones, preferred_element_type=jnp.float32)
        down = down + jnp.dot(low, ones, preferred_element_type=jnp.float32)
        same = (down == wanted.astype(jnp.float32)) & same_group
        match_ref[pl.ds(pl.multiple_of(i * LANES, LANES), LANES), :] = jnp.where(
            same, 1.0, 0.0
        ).astype(jnp.bfloat16)

    def some_rows(i, carry):
        for j in range(4):
            one_row(4 * i + j)
        return carry

    lax.fori_loop(0, incoming_ref.shape[0] // 4, some_rows, 0)


def star_kernel(position_ref, observed_ref, inverse_ref, weights_hbm, *refs, exchanges):
    returned_refs, refs = refs[:exchanges], refs[exchanges:]
    extinction_ref, refs = refs[0], refs[1:]
    parcel_refs, refs = refs[:exchanges], refs[exchanges:]
    weights_ref, returned_rows, sens_ref, parcel_rows, sems = refs
    chunks, per, slots, stars, width = weights_ref.shape
    quarter = chunks // 4
    bounds = [0, quarter // 2, quarter, 2 * quarter, 3 * quarter, chunks]
    per_chunk = per * slots
    held = sens_ref.shape[0] // per_chunk
    fold = LANES // stars
    all_slots = parcel_rows.shape[0]
    sens_blocks = sens_ref.reshape(sens_ref.shape[0], width)
    lane = lax.broadcasted_iota(jnp.int32, (8, LANES), 1)
    row = lax.broadcasted_iota(jnp.int32, (8, LANES), 0)
    star_group = lane // stars
    own_slot = [row == star_group + fold * h for h in range(8 // fold)]

    loads = [
        [
            pltpu.make_async_copy(
                weights_hbm.at[pl.ds(c * per, per)], weights_ref.at[c], sems.at[c]
            )
            for c in range(first, last)
        ]
        for first, last in zip(bounds[:-1], bounds[1:])
    ]

    def extinctions(chunk):
        sums = []
        for b in range(per):
            total = jnp.zeros((stars // 8, 8, width), jnp.float32)
            for k in range(slots):
                at = position_ref[chunk * per_chunk + b * slots + k]
                fetched = returned_rows[pl.ds(at, 8, stride=0), :]
                block = weights_ref[chunk, b, k].astype(jnp.float32)
                total = total + block.reshape(stars // 8, 8, width) * fetched
            sums.append(total.reshape(stars, width))
        extinction = lax.dot_general(
            jnp.ones((8, width), jnp.float32),
            jnp.concatenate(sums, axis=0),
            CONTRACT_LANES,
            precision=lax.Precision.HIGHEST,
            preferred_element_type=jnp.float32,
        )
        here = slice(chunk, chunk + 1)
        extinction_ref[here, :] = extinction[:1]
        return inverse_ref[here, :] * (extinction - observed_ref[here, :])

    def sensitivities(chunk, weighted):
        for b in range(per):
            spread = jnp.where(star_group == b, weighted, 0.0)
            shift = stars
            while shift < LANES:
                spread = spread + pltpu.roll(spread, shift, 1)
                shift *= 2
            left = jnp.concatenate(
                [jnp.where(own, spread, 0.0) for own in own_slot], axis=1
            ).astype(jnp.bfloat16)
            eights = [weights_ref[chunk, b, 8 * j : 8 * j + 8] for j in range(slots // 8)]
            right = jnp.concatenate([x.reshape(8 * stars, width) for x in eights], axis=1)
            sens = jnp.dot(left, right, preferred_element_type=jnp.float32)
            for j in range(slots // 8):
                first = chunk % held * per_chunk + b * slots + 8 * j
                sens_blocks[first : first + 8, :] = sens[:, j * width : (j + 1) * width]

    def scatter(chunk):
        for i in range(per_chunk):
            at = position_ref[chunk * per_chunk + i]
            parcel_rows[at] = sens_ref[chunk % held * per_chunk + i]

    for one_set in loads[:2]:
        for copy in one_set:
            copy.start()
    start = 0
    for returned_ref in returned_refs:
        span = slice(start, start + returned_ref.shape[0])
        returned_rows[span, :] = returned_ref[...].astype(jnp.float32)
        start = span.stop
    parcel_rows.reshape(all_slots, width)[...] = jnp.zeros((all_slots, width), jnp.float32)

    weighted = {}
    for chunk in range(chunks + 2):
        if chunk in bounds[:-1]:
            which = bounds.index(chunk)
            for copy in loads[which]:
                copy.wait()
            for copy in loads[which + 2] if which + 2 < len(loads) else []:
                copy.start()
        if chunk < chunks:
            weighted[chunk] = extinctions(chunk)
        if 1 <= chunk <= chunks:
            sensitivities(chunk - 1, weighted[chunk - 1])
        if chunk >= 2:
            scatter(chunk - 2)
    start = 0
    for parcel_ref in parcel_refs:
        span = slice(start, start + parcel_ref.shape[0])
        parcel_ref[...] = parcel_rows.reshape(all_slots, width)[span, :].astype(jnp.bfloat16)
        start = span.stop


def prior_kernel(
    field_hbm, xlo_ref, xhi_ref, ylo_ref, yhi_ref, out_hbm,
    padded, smooth, out_ref, yends_ref, sems, out_sems,
):
    cells_x, cells_y, depth = field_hbm.shape
    rows = padded.shape[1]
    parts = sems.shape[0]
    planes = cells_x // parts
    own_rows = pl.ds(8, cells_y)
    loads = [
        pltpu.make_async_copy(
            field_hbm.at[pl.ds(i * planes, planes)],
            padded.at[pl.ds(2 + i * planes, planes), own_rows],
            sems.at[i],
        )
        for i in range(parts)
    ]
    for load in loads:
        load.start()
    gx, gy = lax.axis_index("gx"), lax.axis_index("gy")
    last_gx, last_gy = lax.axis_size("gx") - 1, lax.axis_size("gy") - 1
    z = lax.broadcasted_iota(jnp.int32, (rows, depth), 1)
    y = lax.broadcasted_iota(jnp.int32, (rows, depth), 0) - 8
    inside_y = ((y >= 0) | (gy > 0)) & ((y < cells_y) | (gy < last_gy))

    def operate(center, below, above):
        beside = below + above
        beside = beside + pltpu.roll(center, 1, 0) + pltpu.roll(center, rows - 1, 0)
        beside = beside + jnp.where(z == 0, 0.0, pltpu.roll(center, 1, 1))
        beside = beside + jnp.where(z == depth - 1, 0.0, pltpu.roll(center, depth - 1, 1))
        return (shift_kappa + 6.0) * center - beside

    for h in range(2):
        padded[h, own_rows, :] = xlo_ref[h].astype(jnp.float32)
        padded[cells_x + 2 + h, own_rows, :] = xhi_ref[h].astype(jnp.float32)

    yends_ref[0] = ylo_ref[...].astype(jnp.float32)
    yends_ref[1] = yhi_ref[...].astype(jnp.float32)

    def fill_ends(plane, carry):
        padded[plane, 0:8, :] = jnp.zeros((8, depth), jnp.float32)
        padded[plane, 8 + cells_y :, :] = jnp.zeros((8, depth), jnp.float32)
        for h in range(2):
            padded[plane, 6 + h : 7 + h, :] = yends_ref[0, h, pl.ds(plane, 1), :]
            padded[plane, 8 + cells_y + h : 9 + cells_y + h, :] = yends_ref[1, h, pl.ds(plane, 1), :]
        return carry

    lax.fori_loop(0, cells_x + 4, fill_ends, 0)

    def smooth_plane(plane, carry):
        value = operate(padded[plane], padded[plane - 1], padded[plane + 1])
        inside = ((plane > 1) | (gx > 0)) & ((plane < cells_x + 2) | (gx < last_gx))
        smooth[plane - 1] = jnp.where(inside_y & inside, value, 0.0)
        return carry

    def out_plane(x, carry):
        prior = operate(smooth[x + 1], smooth[x], smooth[x + 2])
        change = (step_rate * prior_weight) * prior[8 : 8 + cells_y]
        out_ref[x] = padded[x + 2, own_rows, :] - change
        return carry

    def store(part):
        span = pl.ds(part * planes, planes)
        return pltpu.make_async_copy(out_ref.at[span], out_hbm.at[span], out_sems.at[part])

    smoothed, done = 1, 0
    for part in range(parts):
        loads[part].wait()
        ready = cells_x + 3 if part + 1 == parts else 1 + (part + 1) * planes
        lax.fori_loop(smoothed, ready, smooth_plane, 0)
        smoothed = ready
        lax.fori_loop(done, ready - 3, out_plane, 0)
        done = ready - 3
        for whole in range(parts):
            if part * planes - 2 < (whole + 1) * planes <= done:
                store(whole).start()
    for part in range(parts):
        store(part).wait()


def finish_kernel(
    incoming_ref, match_hbm, field_hbm, base_hbm, *refs, exchanges, capacity, first_slots
):
    arrived_refs, refs = refs[:exchanges], refs[exchanges:]
    out_hbm, *collected, rows_ref, match_ref, field_ref, base_ref, out_ref, in_sems, out_sems = refs
    cells_x, cells_y, depth = field_ref.shape
    per_column = depth // LANES
    parts = out_sems.shape[0]
    planes = cells_x // parts
    blocks = cells_x * cells_y * per_column
    matches = copies_in_parts(match_hbm, match_ref, in_sems.at[2])
    loads = copies_in_parts(field_hbm, field_ref, in_sems.at[0])
    loads += copies_in_parts(base_hbm, base_ref, in_sems.at[1])
    for load in matches + loads:
        load.start()
    collected_rows = [ref.reshape(ref.shape[0], LANES) for ref in collected]
    for ref in collected_rows:
        ref[...] = jnp.zeros_like(ref)
    for load in matches:
        load.wait()
    merged = rows_ref.reshape(rows_ref.shape[0], LANES)
    start = 0
    for arrived_ref in arrived_refs:
        for i in range(arrived_ref.shape[0] // LANES):
            span = slice(start + i * LANES, start + (i + 1) * LANES)
            merged[span, :] = -step_rate * jnp.dot(
                match_ref[span, :],
                arrived_ref[i * LANES : (i + 1) * LANES, :],
                preferred_element_type=jnp.float32,
            )
        start += arrived_ref.shape[0]

    part_starts = [0, arrived_refs[0].shape[0]]

    def visit(wanted, row, list_part, which):
        row = pl.multiple_of(row + part_starts[list_part], GROUP)
        rows = rows_ref.at[pl.ds(row, GROUP)]
        into = collected[which % len(collected)]
        sums = [into[wanted[j]] + rows[j] for j in range(GROUP)]
        for j in range(GROUP):
            into[wanted[j]] = sums[j]

    for_each_group(incoming_ref, visit, capacity, first_slots, blocks)
    for load in loads:
        load.wait()

    def store(part):
        span = pl.ds(part * planes, planes)
        return pltpu.make_async_copy(out_ref.at[span], out_hbm.at[span], out_sems.at[part])

    def one_plane(x, carry):
        for yb in range(cells_y // 8):
            for part in range(per_column):
                at = pl.multiple_of(((x * (cells_y // 8) + yb) * per_column + part) * 8, 8)
                here = (x, slice(8 * yb, 8 * yb + 8), slice(part * LANES, (part + 1) * LANES))
                grad = collected_rows[0][pl.ds(at, 8), :] + collected_rows[1][pl.ds(at, 8), :]
                out_ref[here] = base_ref[here] + grad * jnp.exp(field_ref[here])
        return carry

    for part in range(parts):
        lax.fori_loop(part * planes, (part + 1) * planes, one_plane, 0)
        store(part).start()
    for part in range(parts):
        store(part).wait()


def both_ways(first, last, axis):
    peers = lax.axis_size(axis)
    up = [(i, i + 1) for i in range(peers - 1)]
    down = [(j, i) for i, j in up]
    return lax.ppermute(last, axis, up), lax.ppermute(first, axis, down)


VMEM = pl.BlockSpec(memory_space=pltpu.VMEM)
SMEM = pl.BlockSpec(memory_space=pltpu.SMEM)
ANY = pl.BlockSpec(memory_space=pl.ANY)


def on_device(log_density, weights, observed, inverse_var, star_counts, block_ids):
    cells_x, cells_y, depth = log_density.shape
    blocks_dev, slots, stars, width = weights.shape
    devices = lax.axis_size("gx") * lax.axis_size("gy")
    requests = blocks_dev * slots
    capacity = 2 * requests // devices
    first_slots = 11 * capacity // 16 if capacity % LANES == 0 else capacity
    slots_of = [n for n in (first_slots, capacity - first_slots) if n > 0]
    exchanges = len(slots_of)
    all_slots = devices * capacity
    per_column = depth // width
    blocks = cells_x * cells_y * per_column
    cells = log_density.size
    field_shape = (cells_x, cells_y, depth)
    mesh_axes = ("gx", "gy")
    f32, bf16, i32 = jnp.float32, jnp.bfloat16, jnp.int32
    shape = jax.ShapeDtypeStruct

    def exchange(x):
        return lax.all_to_all(x, mesh_axes, split_axis=0, concat_axis=0, tiled=True)

    def exchange_rows(parts, crowded):
        moved = [parts[0].reshape(devices, first_slots, width)]
        moved[0] = exchange(moved[0])
        for part in parts[1:]:
            part = part.reshape(devices, capacity - first_slots, width)
            moved.append(lax.cond(crowded, exchange, lambda x: x, part))
        return [x.reshape(-1, width) for x in moved]

    outgoing, position = pl.pallas_call(
        functools.partial(
            route_kernel,
            devices=devices,
            capacity=capacity,
            first_slots=first_slots,
            blocks=blocks,
            per_column=per_column,
        ),
        out_shape=[shape((devices, capacity), i32), shape((requests // LANES, LANES), i32)],
        in_specs=[VMEM],
        out_specs=[VMEM, VMEM],
        name="route",
    )(block_ids.T)
    incoming = exchange(outgoing)

    field, _ = lax.optimization_barrier((log_density, outgoing))
    table, xfirst, xlast, yfirst, ylast = pl.pallas_call(
        table_kernel,
        out_shape=[
            shape((blocks + capacity, width), bf16),
            shape((2, cells_y, depth), bf16),
            shape((2, cells_y, depth), bf16),
            shape((2, cells_x + 4, depth), f32),
            shape((2, cells_x + 4, depth), f32),
        ],
        in_specs=[VMEM],
        out_specs=[VMEM] * 5,
        compiler_params=pltpu.CompilerParams(vmem_limit_bytes=16 * MIB),
        cost_estimate=pl.CostEstimate(
            flops=8 * cells, bytes_accessed=8 * cells, transcendentals=cells
        ),
        name="table",
    )(field)
    incoming, *edges = lax.optimization_barrier((incoming, xfirst, xlast, yfirst, ylast))
    wanted = incoming.reshape(-1)

    *served, crowded = pl.pallas_call(
        functools.partial(
            serve_kernel, capacity=capacity, first_slots=first_slots, blocks=blocks
        ),
        out_shape=[shape((devices * n, width), bf16) for n in slots_of] + [shape((1,), i32)],
        in_specs=[SMEM, VMEM],
        out_specs=[VMEM] * exchanges + [SMEM],
        scratch_shapes=[
            pltpu.VMEM((blocks + capacity, 1, width), f32),
            pltpu.VMEM((all_slots, 1, width), f32),
        ],
        compiler_params=pltpu.CompilerParams(vmem_limit_bytes=24 * MIB),
        cost_estimate=pl.CostEstimate(
            flops=cells, bytes_accessed=6 * MIB, transcendentals=cells
        ),
        name="serve",
    )(wanted, table)
    crowded = crowded[0] != 0

    returned = exchange_rows(served, crowded)
    *edges, incoming_late, _ = lax.optimization_barrier((*edges, incoming, served[0]))
    xlo, xhi = both_ways(*edges[:2], "gx")
    slabs = pl.pallas_call(
        ends_kernel,
        out_shape=[shape((2, cells_x + 4, depth), bf16)] * 2,
        in_specs=[VMEM] * 4,
        out_specs=[VMEM] * 2,
        scratch_shapes=[pltpu.VMEM((2, cells_x + 4, depth), f32)],
        compiler_params=pltpu.CompilerParams(vmem_limit_bytes=8 * MIB),
        cost_estimate=pl.CostEstimate(flops=0, bytes_accessed=MIB, transcendentals=0),
        name="ends",
    )(xlo, xhi, *edges[2:])
    ylo, yhi = both_ways(*slabs, "gy")
    slot_lists = [
        incoming_late[:, :first_slots].reshape(-1, LANES),
        (incoming_late[:, first_slots:] & (MARK - 1)).reshape(-1, LANES),
    ][:exchanges]
    *returned, slot_rows, ylo, yhi = lax.optimization_barrier(
        (*returned, jnp.concatenate(slot_lists, axis=0), ylo, yhi)
    )

    chunks = blocks_dev * stars // LANES
    live = jnp.arange(stars)[None, :] < star_counts[:, None]
    live_inverse = jnp.where(live, inverse_var, 0.0)
    extinction, *parcel = pl.pallas_call(
        functools.partial(star_kernel, exchanges=exchanges),
        out_shape=[shape((chunks, LANES), f32)]
        + [shape((devices * n, width), bf16) for n in slots_of],
        in_specs=[SMEM, VMEM, VMEM, ANY] + [VMEM] * exchanges,
        out_specs=[VMEM] * (1 + exchanges),
        scratch_shapes=[
            pltpu.VMEM((chunks, blocks_dev // chunks, slots, stars, width), bf16),
            pltpu.VMEM((all_slots + 8, width), f32),
            pltpu.VMEM((4 * (blocks_dev // chunks) * slots, 1, width), f32),
            pltpu.VMEM((all_slots, 1, width), f32),
            pltpu.SemaphoreType.DMA((chunks,)),
        ],
        compiler_params=pltpu.CompilerParams(vmem_limit_bytes=50 * MIB),
        cost_estimate=pl.CostEstimate(
            flops=4 * weights.size, bytes_accessed=2 * weights.size, transcendentals=0
        ),
        name="stars",
    )(
        position.reshape(slots // 2, 2, blocks_dev).transpose(2, 1, 0).reshape(requests),
        observed.reshape(chunks, LANES),
        live_inverse.reshape(chunks, LANES),
        weights,
        *returned,
    )
    arrived = exchange_rows(parcel, crowded)

    field_late, slot_rows, _ = lax.optimization_barrier((log_density, slot_rows, parcel[0]))
    match = pl.pallas_call(
        match_kernel,
        out_shape=shape((all_slots, LANES), bf16),
        in_specs=[VMEM],
        out_specs=VMEM,
        compiler_params=pltpu.CompilerParams(vmem_limit_bytes=8 * MIB),
        cost_estimate=pl.CostEstimate(flops=10**9, bytes_accessed=MIB, transcendentals=0),
        name="match",
    )(slot_rows)
    parts = 8
    base = pl.pallas_call(
        prior_kernel,
        out_shape=shape(field_shape, f32),
        in_specs=[ANY] + [VMEM] * 4,
        out_specs=ANY,
        scratch_shapes=[
            pltpu.VMEM((cells_x + 4, cells_y + 16, depth), f32),
            pltpu.VMEM((cells_x + 2, cells_y + 16, depth), f32),
            pltpu.VMEM(field_shape, f32),
            pltpu.VMEM((2, 2, cells_x + 4, depth), f32),
            pltpu.SemaphoreType.DMA((parts,)),
            pltpu.SemaphoreType.DMA((parts,)),
        ],
        compiler_params=pltpu.CompilerParams(vmem_limit_bytes=56 * MIB),
        cost_estimate=pl.CostEstimate(
            flops=30 * cells, bytes_accessed=8 * cells, transcendentals=0
        ),
        name="prior",
    )(field_late, xlo, xhi, ylo, yhi)

    new_log_density = pl.pallas_call(
        functools.partial(
            finish_kernel, exchanges=exchanges, capacity=capacity, first_slots=first_slots
        ),
        out_shape=shape(field_shape, f32),
        in_specs=[SMEM, ANY, ANY, ANY] + [VMEM] * exchanges,
        out_specs=ANY,
        scratch_shapes=[
            pltpu.VMEM((blocks + capacity, 1, width), f32),
            pltpu.VMEM((blocks + capacity, 1, width), f32),
            pltpu.VMEM((all_slots, 1, width), f32),
            pltpu.VMEM((all_slots, LANES), bf16),
            pltpu.VMEM(field_shape, f32),
            pltpu.VMEM(field_shape, f32),
            pltpu.VMEM(field_shape, f32),
            pltpu.SemaphoreType.DMA((3, parts)),
            pltpu.SemaphoreType.DMA((parts,)),
        ],
        compiler_params=pltpu.CompilerParams(vmem_limit_bytes=50 * MIB),
        cost_estimate=pl.CostEstimate(
            flops=4 * cells, bytes_accessed=12 * cells, transcendentals=cells
        ),
        name="finish",
    )(wanted, match, log_density, base, *arrived)
    return new_log_density, extinction.reshape(blocks_dev, stars)


def solution(mesh):
    placed = (
        P("gx", "gy", None),
        P(("gx", "gy"), None, None, None),
        P(("gx", "gy"), None),
        P(("gx", "gy"), None),
        P(("gx", "gy")),
        P(("gx", "gy"), None),
    )
    return jax.shard_map(
        on_device,
        mesh=mesh,
        in_specs=placed,
        out_specs=(P("gx", "gy", None), P(("gx", "gy"), None)),
        check_vma=False,
    )
```
